32 devices in a mesh: batch: 8 (over y, x, core), head: 4 (over z).
Axes of the slice: x: 2, y: 2, z: 4, core: 2. Of those that a mesh axis runs over, the one named last changes fastest.
Arguments:
- tokens: bfloat16 [16384, 768], P(('batch', 'head')), may hold values from -6 to 6
- lengths: int32 [16], P('batch'), may hold values from 513 to 1024, as said below
- block_swap: int32 [12], P('head'), may hold values from 0 to 1
- input_weight: bfloat16 [3, 768, 768], P(None, None, 'head'), may hold values from -0.21875 to 0.21875
- input_bias: float32 [2, 768], P(None, 'head'), may hold values from -3 to 3
- out_weight: bfloat16 [768, 768], replicated, may hold values from -1.25 to 1.25
- out_bias: float32 [768], replicated, may hold values from -3 to 3
- gain_one: float32 [768], replicated, may hold values from 0.25 to 1.75
- shift_one: float32 [768], replicated, may hold values from -3 to 3
- up_weight: bfloat16 [768, 3072], P(None, 'head'), may hold values from -0.21875 to 0.21875
- up_bias: float32 [3072], replicated, may hold values from -3 to 3
- down_weight: bfloat16 [3072, 768], P('head'), may hold values from -0.109375 to 0.109375
- down_bias: float32 [768], replicated, may hold values from -3 to 3
- gain_two: float32 [768], replicated, may hold values from 0.25 to 1.75
- shift_two: float32 [768], replicated, may hold values from -3 to 3
- cotangent: bfloat16 [16384, 768], P(('batch', 'head')), may hold values from -6 to 6
Outputs:
- mixed_out: bfloat16 [16384, 768], P(('batch', 'head'))
- grad_tokens: float32 [16384, 768], P(('batch', 'head'))
- grad_input_weight: float32 [3, 768, 768], P(None, None, 'head')
- grad_input_bias: float32 [2, 768], P(None, 'head')
- grad_out_weight: float32 [768, 768], replicated
- grad_out_bias: float32 [768], replicated
- grad_gain_one: float32 [768], replicated
- grad_shift_one: float32 [768], replicated
- grad_up_weight: float32 [768, 3072], P(None, 'head')
- grad_up_bias: float32 [3072], P('head')
- grad_down_weight: float32 [3072, 768], P('head')
- grad_down_bias: float32 [768], replicated
- grad_gain_two: float32 [768], replicated
- grad_shift_two: float32 [768], replicated
The draws below stay inside these ranges and needn't reach their ends.
Inputs may be any that keep to these rules, and one draw needn't show every extreme that they name: `lengths`: one sequence has exactly 1024 tokens.
All inputs are finite; a program needn't handle non-finite values.
Results may differ from the reference program's by a relative error of at most 0.015.
Values may be sent and summed in bfloat16 or wider, within the bound.
No kernel may reach another device: no remote copies, remote signals or barrier semaphores. Data moves between devices by JAX's collectives and lax.ppermute only.
A program may use at most 128 MiB of HBM per device.

```python
import jax
import jax.numpy as jnp
from jax import lax

D = 768
HEADS = 12
HEAD_DIM = 64
FF = 3072
SEQ_LEN = 1024
SEQ_DEV = 2
BLOCK = 512
SEQS = 16
TOKENS = 16384
N_HEAD = 4


def draw_lengths(key, part):
    key = jax.random.fold_in(key, 7)
    first_key, second_key = jax.random.split(key)
    shortest = max(SEQ_LEN // 8, SEQ_LEN - SEQ_DEV * SEQ_LEN // N_HEAD + 1)
    drawn = jax.random.randint(first_key, (SEQS,), shortest, SEQ_LEN + 1)
    chosen = jax.random.randint(second_key, (), 0, SEQS)
    return jnp.where(jnp.arange(SEQS) == chosen, SEQ_LEN, drawn).astype(jnp.int32)


def place_ends(entries, stream_key, low, high):
    longest = entries.shape.index(max(entries.shape))
    spots = []
    for shift in (0, 1):
        where = [jax.random.randint(jax.random.fold_in(stream_key, axis), (), 0, length) for axis, length in enumerate(entries.shape)]
        where[longest] = (where[longest] + shift) % entries.shape[longest]
        spots.append(tuple(where))
    return entries.at[spots[0]].set(low).at[spots[1]].set(high)


def steps_of(own_key, extent, cuts, least, top_value):
    loudness = 1.0
    for dim, blocks in cuts:
        heights = jax.random.uniform(jax.random.fold_in(jax.random.fold_in(own_key, 6), dim), (blocks,), jnp.float32, least / len(cuts), top_value / len(cuts))
        loudness = loudness * jnp.repeat(jnp.exp(heights), extent[dim] // blocks).reshape((-1,) + (1,) * (len(extent) - 1 - dim))
    return loudness


def gaussian(key, dims, deviation, bound, cuts=(), held_as=jnp.bfloat16):
    entries = jax.random.normal(key, dims, jnp.float32) * deviation
    if len(cuts) > 0:
        entries = steps_of(key, dims, cuts, -0.22, 0.18) * entries
    return jnp.clip(entries, min=-bound, max=bound).astype(held_as)


def setup_inputs(seed: int = 0) -> dict:
    splits = jax.random.split(jax.random.key(seed), 17)
    return {
        "tokens": gaussian(splits[0], (TOKENS, D), 1.0, 6.0, ((0, 32),)),
        "lengths": draw_lengths(jax.random.fold_in(splits[16], 71), 0),
        "block_swap": place_ends(jax.random.randint(splits[2], (HEADS,), 0, 2), jax.random.fold_in(splits[2], 1), 0, 1).astype(jnp.int32),
        "input_weight": gaussian(splits[3], (3, D, D), D ** -0.5, 0.21875, ((2, 4),)),
        "input_bias": gaussian(splits[4], (2, D), 0.5, 3.0, ((1, 4),), jnp.float32),
        "out_weight": gaussian(splits[5], (D, D), (D // 32) ** -0.5, 1.25),
        "out_bias": gaussian(splits[6], (D,), 0.5, 3.0, (), jnp.float32),
        "gain_one": jnp.clip(1.0 + 0.15 * jax.random.normal(splits[7], (D,), jnp.float32), 0.25, 1.75),
        "shift_one": gaussian(splits[8], (D,), 0.5, 3.0, (), jnp.float32),
        "up_weight": gaussian(splits[9], (D, FF), D ** -0.5, 0.21875, ((1, 4),)),
        "up_bias": gaussian(splits[10], (FF,), 0.5, 3.0, (), jnp.float32),
        "down_weight": gaussian(splits[11], (FF, D), FF ** -0.5, 0.109375, ((0, 4),)),
        "down_bias": gaussian(splits[12], (D,), 0.5, 3.0, (), jnp.float32),
        "gain_two": jnp.clip(1.0 + 0.15 * jax.random.normal(splits[13], (D,), jnp.float32), 0.25, 1.75),
        "shift_two": gaussian(splits[14], (D,), 0.5, 3.0, (), jnp.float32),
        "cotangent": gaussian(splits[15], (TOKENS, D), 1.0, 6.0, ((0, 32),)),
    }


@jax.custom_vjp
def low(v):
    return lax.optimization_barrier(v.astype(jnp.bfloat16)).astype(jnp.float32)

@jax.custom_vjp
def low_back(v):
    return v

def low_keep(v):
    return (low(v), None)

def low_pass(kept, grad):
    return (grad,)

def back_keep(v):
    return (v, None)

def back_low(kept, grad):
    return (low(grad),)
low.defvjp(low_keep, low_pass)
low_back.defvjp(back_keep, back_low)

def norm_rows(values, gain_row, shift_row):
    centred = values - lax.optimization_barrier(jnp.mean(values, axis=-1, keepdims=True))
    variance = lax.optimization_barrier(jnp.mean(centred * centred, axis=-1, keepdims=True))
    return centred * lax.rsqrt(variance + 1e-05) * gain_row + shift_row

def forward(tokens, input_weight, input_bias, out_weight, out_bias, gain_one, shift_one, up_weight, up_bias, down_weight, down_bias, gain_two, shift_two, present, block_swap):
    highest = lax.Precision.HIGHEST
    seq_count = present.shape[0]
    queries = low(low_back(jnp.dot(tokens, input_weight[0], precision=highest) + input_bias[0]))
    key_rows = low(low_back(jnp.dot(tokens, input_weight[1], precision=highest)))
    value_rows = low(low_back(jnp.dot(tokens, input_weight[2], precision=highest) + input_bias[1]))
    layout = (seq_count, 2, BLOCK, HEADS, HEAD_DIM)
    queries = queries.reshape(layout)
    key_rows = key_rows.reshape(layout)
    value_rows = value_rows.reshape(layout)
    swapped = block_swap == 1
    flipped = swapped[None, None, None, :, None]
    key_rows = jnp.where(flipped, key_rows[:, ::-1], key_rows)
    value_rows = jnp.where(flipped, value_rows[:, ::-1], value_rows)
    blocks = present.reshape(seq_count, 2, BLOCK)
    live_keys = jnp.where(swapped[None, None, :, None], blocks[:, ::-1, None, :], blocks[:, :, None, :])
    scores = low_back(jnp.einsum('sciha,scjha->schij', queries, key_rows, precision=highest) * HEAD_DIM ** (-0.5))
    open_keys = live_keys[:, :, :, None, :] > 0.5
    anyone = lax.optimization_barrier(jnp.max(live_keys, axis=-1))[:, :, :, None, None]
    largest = lax.optimization_barrier(jnp.max(jnp.where(open_keys, scores, -1e+30), axis=-1, keepdims=True))
    largest = jnp.where(anyone > 0.5, largest, 0.0)
    weights = jnp.exp(jnp.where(open_keys, scores - largest, -10000.0))
    totals = lax.optimization_barrier(jnp.sum(weights, axis=-1, keepdims=True)) + (1.0 - anyone)
    mixing = low(weights / totals)
    context = jnp.einsum('schij,scjha->sciha', mixing, value_rows, precision=highest)
    context = low(low_back(context.reshape(seq_count * SEQ_LEN, HEADS * HEAD_DIM)))
    projected = low_back(jnp.dot(context, out_weight, precision=highest) + out_bias)
    first_norm = norm_rows(tokens + projected, gain_one, shift_one)
    pre = low_back(jnp.dot(low(first_norm), up_weight, precision=highest) + up_bias)
    hidden = low(jax.nn.gelu(pre, approximate=False))
    branch = low_back(jnp.dot(hidden, down_weight, precision=highest) + down_bias)
    return norm_rows(first_norm + branch, gain_two, shift_two) * present.reshape(-1, 1)

def reference(tokens, lengths, block_swap, input_weight, input_bias, out_weight, out_bias, gain_one, shift_one, up_weight, up_bias, down_weight, down_bias, gain_two, shift_two, cotangent):
    parameters = tuple((weight.astype(jnp.float32) for weight in (input_weight, input_bias, out_weight, out_bias, gain_one, shift_one, up_weight, up_bias, down_weight, down_bias, gain_two, shift_two)))
    scan_steps = SEQS // SEQ_DEV
    group_rows = SEQ_DEV * SEQ_LEN
    inputs = tokens.astype(jnp.float32).reshape(scan_steps, group_rows, D)
    cotangents = cotangent.astype(jnp.float32).reshape(scan_steps, group_rows, D)
    seq_lengths = lengths.reshape(scan_steps, SEQ_DEV)
    positions = jnp.arange(SEQ_LEN, dtype=jnp.int32)

    def one_step(running, element):
        inputs_now, cotangent_now, lengths_now = element
        present = (positions[None, :] < lengths_now[:, None]).astype(jnp.float32)

        def applied(rows_in, *weight_list):
            return forward(rows_in, *weight_list, present, block_swap)
        result, pullback = jax.vjp(applied, inputs_now, *parameters)
        gradients = pullback(cotangent_now)
        running = tuple((left_side + right_side for left_side, right_side in zip(running, gradients[1:])))
        return (running, (result.astype(jnp.bfloat16), gradients[0]))
    initial = tuple((jnp.zeros_like(weight) for weight in parameters))
    summed, (mixed_out, grad_tokens) = lax.scan(one_step, initial, (inputs, cotangents, seq_lengths))
    return (mixed_out.reshape(TOKENS, D), grad_tokens.reshape(TOKENS, D), summed[0], summed[1], summed[2], summed[3], summed[4], summed[5], summed[6], summed[7], summed[8], summed[9], summed[10], summed[11])
```

```python
import functools

import jax
import jax.numpy as jnp
from jax import lax
from jax.experimental import pallas as pl
from jax.experimental.pallas import tpu as pltpu
from jax.sharding import PartitionSpec as P

SEQ_LEN = 1024
EPSILON = 1e-05
F32 = jnp.float32
BF16 = jnp.bfloat16
VMEM_LIMIT = 48 * 1024 * 1024


def norm_parts(values, gain_row, shift_row):
    centred = values - jnp.mean(values, axis=-1, keepdims=True)
    inverse = lax.rsqrt(jnp.mean(centred * centred, axis=-1, keepdims=True) + EPSILON)
    unit_rows = centred * inverse
    return (unit_rows * gain_row + shift_row, unit_rows, inverse)


def norm_back(grad_rows, unit_rows, inverse, gain_row):
    scaled = grad_rows * gain_row
    grad_in = inverse * (
        scaled
        - jnp.mean(scaled, axis=-1, keepdims=True)
        - unit_rows * jnp.mean(scaled * unit_rows, axis=-1, keepdims=True)
    )
    return (grad_in, jnp.sum(grad_rows * unit_rows, axis=0), jnp.sum(grad_rows, axis=0))


def dot(left_side, right_side, left_dim=1, right_dim=0):
    return lax.dot_general(
        left_side,
        right_side,
        (((left_dim,), (right_dim,)), ((), ())),
        preferred_element_type=F32,
    )


def lane_pick(values, heads, depth):
    lane = lax.broadcasted_iota(jnp.int32, (1, len(values) * depth), 1)
    picked = jnp.full(lane.shape, values[0], jnp.int32)
    for j in range(1, len(values)):
        picked = jnp.where(lane >= j * depth, values[j], picked)
    return picked


def attend_kernel(
    heads, depth, info, tokens, partner, weight, bias, q_out, k_out, v_out, context_out, stats_out
):
    shard = pl.program_id(0)
    total_heads = heads * pl.num_programs(0)
    swaps = [info[shard * heads + j] for j in range(heads)]
    own_live, partner_live = info[total_heads], info[total_heads + 1]
    rows = tokens.shape[0]
    width = heads * depth
    x, xp = tokens[...], partner[...]
    swapped = lane_pick(swaps, heads, depth) == 1
    q = (dot(x, weight[0, 0]) + bias[0, 0]).astype(BF16)
    k = jnp.where(swapped, dot(xp, weight[1, 0]), dot(x, weight[1, 0])).astype(BF16)
    v = (jnp.where(swapped, dot(xp, weight[2, 0]), dot(x, weight[2, 0])) + bias[1, 0]).astype(BF16)
    q = q * (depth**-0.5)
    q_out[0], k_out[0], v_out[0] = q, k, v
    key_index = lax.broadcasted_iota(jnp.int32, (rows, 1), 0)
    stats = []
    pieces = []
    for j in range(heads):
        cut = slice(j * depth, (j + 1) * depth)
        live = jnp.where(swaps[j] == 1, partner_live, own_live)
        open_keys = key_index < live
        anyone = jnp.where(live > 0, 1.0, 0.0).astype(F32)
        scores = dot(k[:, cut], q[:, cut], 1, 1)
        largest = jnp.max(jnp.where(open_keys, scores, -1e30), axis=0, keepdims=True)
        largest = jnp.where(anyone > 0.5, largest, 0.0)
        weights = jnp.exp(jnp.where(open_keys, scores - largest, -10000.0))
        totals = jnp.sum(weights, axis=0, keepdims=True) + (1.0 - anyone)
        mixing = (weights * (1.0 / totals)).astype(BF16)
        stats.append(largest + jnp.log(totals))
        pieces.append(dot(v[:, cut], mixing, 0, 0))
    context_out[0] = jnp.concatenate(pieces, axis=0).T.astype(BF16)
    stats_out[0] = jnp.concatenate(
        stats + [jnp.zeros((8 - heads, rows), F32)], axis=0
    )


def attend_back_kernel(
    heads,
    depth,
    info,
    tokens_t,
    partner_t,
    weight,
    q_in,
    k_in,
    v_in,
    grad_in,
    stats_in,
    own_out,
    partner_out,
    weight_out,
    bias_out,
):
    shard = pl.program_id(0)
    total_heads = heads * pl.num_programs(0)
    swaps = [info[shard * heads + j] for j in range(heads)]
    own_live, partner_live = info[total_heads], info[total_heads + 1]
    rows = q_in.shape[1]
    q, k, v, grad = q_in[0], k_in[0], v_in[0], grad_in[0]
    stats = stats_in[0]
    key_index = lax.broadcasted_iota(jnp.int32, (rows, 1), 0)
    gq, gk, gv = [], [], []
    for j in range(heads):
        cut = slice(j * depth, (j + 1) * depth)
        live = jnp.where(swaps[j] == 1, partner_live, own_live)
        open_keys = key_index < live
        scores = dot(k[:, cut], q[:, cut], 1, 1)
        chances = jnp.exp(jnp.where(open_keys, scores - stats[j : j + 1, :], -10000.0))
        grad_mix = dot(v[:, cut], grad[:, cut], 1, 1)
        shared = jnp.sum(grad_mix * chances, axis=0, keepdims=True)
        grad_scores = (chances * (grad_mix - shared)).astype(BF16)
        gk.append(dot(grad_scores, q[:, cut]))
        gv.append(dot(chances.astype(BF16), grad[:, cut]))
        gq.append(dot(k[:, cut], grad_scores, 0, 0))
    grad_q = (jnp.concatenate(gq, axis=0).T * (depth**-0.5)).astype(BF16)
    grad_k = jnp.concatenate(gk, axis=1).astype(BF16)
    grad_v = jnp.concatenate(gv, axis=1).astype(BF16)
    swapped = lane_pick(swaps, heads, depth) == 1
    nothing = jnp.zeros((), BF16)
    k_own, k_far = jnp.where(swapped, nothing, grad_k), jnp.where(swapped, grad_k, nothing)
    v_own, v_far = jnp.where(swapped, nothing, grad_v), jnp.where(swapped, grad_v, nothing)
    own = (
        dot(grad_q, weight[0, 0], 1, 1)
        + dot(k_own, weight[1, 0], 1, 1)
        + dot(v_own, weight[2, 0], 1, 1)
    )
    far = dot(k_far, weight[1, 0], 1, 1) + dot(v_far, weight[2, 0], 1, 1)

    @pl.when(shard == 0)
    def first():
        own_out[...] = own
        partner_out[...] = far

    @pl.when(shard > 0)
    def later():
        own_out[...] += own
        partner_out[...] += far

    xt, xpt = tokens_t[...], partner_t[...]
    weight_out[0, 0] = dot(xt, grad_q).astype(BF16)
    weight_out[1, 0] = (dot(xt, k_own) + dot(xpt, k_far)).astype(BF16)
    weight_out[2, 0] = (dot(xt, v_own) + dot(xpt, v_far)).astype(BF16)
    bias_out[0] = jnp.concatenate(
        [
            jnp.sum(grad_q.astype(F32), axis=0, keepdims=True),
            jnp.sum(grad_v.astype(F32), axis=0, keepdims=True),
            jnp.zeros((6, grad_q.shape[1]), F32),
        ],
        axis=0,
    )


def attend(info, tokens, partner, weight, bias, shards, heads, depth):
    rows, dim = tokens.shape
    width = heads * depth
    per_shard = pl.BlockSpec((1, rows, width), lambda s: (s, 0, 0))
    items = jax.ShapeDtypeStruct((shards, rows, width), BF16)
    return pl.pallas_call(
        functools.partial(attend_kernel, heads, depth),
        grid=(shards,),
        in_specs=[
            pl.BlockSpec(memory_space=pltpu.SMEM),
            pl.BlockSpec((rows, dim), lambda s: (0, 0)),
            pl.BlockSpec((rows, dim), lambda s: (0, 0)),
            pl.BlockSpec((3, 1, dim, width), lambda s: (0, s, 0, 0)),
            pl.BlockSpec((2, 1, 1, width), lambda s: (0, s, 0, 0)),
        ],
        out_specs=[per_shard] * 4 + [pl.BlockSpec((1, 8, rows), lambda s: (s, 0, 0))],
        out_shape=[items] * 4 + [jax.ShapeDtypeStruct((shards, 8, rows), F32)],
        compiler_params=pltpu.CompilerParams(vmem_limit_bytes=VMEM_LIMIT),
        cost_estimate=pl.CostEstimate(
            flops=10 * rows * dim * dim + 4 * rows * rows * dim,
            bytes_accessed=20 * rows * dim,
            transcendentals=shards * heads * rows * rows,
        ),
        name="attend",
    )(info, tokens, partner, weight, bias)


def attend_back(info, tokens_t, partner_t, weight, q, k, v, grad, stats, shards, heads, depth):
    dim, rows = tokens_t.shape
    width = heads * depth
    per_shard = pl.BlockSpec((1, rows, width), lambda s: (s, 0, 0))
    weight_spec = pl.BlockSpec((3, 1, dim, width), lambda s: (0, s, 0, 0))
    whole = pl.BlockSpec((rows, dim), lambda s: (0, 0))
    return pl.pallas_call(
        functools.partial(attend_back_kernel, heads, depth),
        grid=(shards,),
        in_specs=[
            pl.BlockSpec(memory_space=pltpu.SMEM),
            pl.BlockSpec((dim, rows), lambda s: (0, 0)),
            pl.BlockSpec((dim, rows), lambda s: (0, 0)),
            weight_spec,
            per_shard,
            per_shard,
            per_shard,
            per_shard,
            pl.BlockSpec((1, 8, rows), lambda s: (s, 0, 0)),
        ],
        out_specs=[
            whole,
            whole,
            weight_spec,
            pl.BlockSpec((1, 8, width), lambda s: (s, 0, 0)),
        ],
        out_shape=[
            jax.ShapeDtypeStruct((rows, dim), F32),
            jax.ShapeDtypeStruct((rows, dim), F32),
            jax.ShapeDtypeStruct((3, shards, dim, width), BF16),
            jax.ShapeDtypeStruct((shards, 8, width), F32),
        ],
        compiler_params=pltpu.CompilerParams(vmem_limit_bytes=VMEM_LIMIT),
        cost_estimate=pl.CostEstimate(
            flops=20 * rows * dim * dim + 10 * rows * rows * dim,
            bytes_accessed=32 * rows * dim,
            transcendentals=shards * heads * rows * rows,
        ),
        name="attend_back",
    )(info, tokens_t, partner_t, weight, q, k, v, grad, stats)


def local(
    batch_size,
    shards,
    tokens,
    lengths,
    block_swap,
    input_weight,
    input_bias,
    out_weight,
    out_bias,
    gain_one,
    shift_one,
    up_weight,
    up_bias,
    down_weight,
    down_bias,
    gain_two,
    shift_two,
    cotangent,
):
    heads = block_swap.shape[0]
    rows, dim = tokens.shape
    width = input_weight.shape[2]
    depth = width // heads
    hidden_own = up_weight.shape[1]
    both = ("head", "batch")
    batch_at, head_at = lax.axis_index("batch"), lax.axis_index("head")
    blocks = SEQ_LEN // rows
    length = lax.dynamic_index_in_dim(lengths, head_at // blocks, 0, keepdims=False)
    block_at = head_at % blocks
    own_live = jnp.clip(length - block_at * rows, 0, rows)
    partner_live = jnp.clip(length - (blocks - 1 - block_at) * rows, 0, rows)
    row_mask = (jnp.arange(rows, dtype=jnp.int32) < own_live).astype(F32)[:, None]

    partner = lax.ppermute(tokens, "head", [(i, i ^ 1) for i in range(shards)])
    part = dim // batch_size

    def share(weight, axis):
        piece = lax.dynamic_slice_in_dim(weight, batch_at * part, part, axis)
        return lax.all_gather(piece, both, axis=axis, tiled=True)

    weight_all = share(input_weight, 1).reshape(3, shards, dim, width)
    up_all = share(up_weight, 0).reshape(shards, dim, hidden_own)
    down_all = share(down_weight, 0).reshape(shards, hidden_own, dim)
    small = jnp.concatenate([input_bias.reshape(-1), block_swap.astype(F32)])
    small = lax.all_gather(small, "head")
    bias_all = small[:, : 2 * width].reshape(shards, 2, 1, width).transpose(1, 0, 2, 3)
    info = jnp.concatenate(
        [
            small[:, 2 * width :].reshape(-1).astype(jnp.int32),
            jnp.stack([own_live, partner_live]).astype(jnp.int32),
        ]
    )

    q, k, v, context, stats = attend(
        info, tokens, partner, weight_all, bias_all, shards, heads, depth
    )
    out_parts = out_weight.reshape(shards, width, dim)
    projected = (
        jnp.einsum("sta,sad->td", context, out_parts, preferred_element_type=F32) + out_bias
    )
    first_norm, unit_one, inverse_one = norm_parts(
        tokens.astype(F32) + projected, gain_one, shift_one
    )
    normed_low = first_norm.astype(BF16)
    up_bias_parts = up_bias.reshape(shards, 1, hidden_own)
    pre = jnp.einsum("td,sdh->sth", normed_low, up_all, preferred_element_type=F32) + up_bias_parts
    hidden, activation_back = jax.vjp(lambda inner: jax.nn.gelu(inner, approximate=False), pre)
    hidden = hidden.astype(BF16)
    branch = jnp.einsum("sth,shd->td", hidden, down_all, preferred_element_type=F32) + down_bias
    second, unit_two, inverse_two = norm_parts(first_norm + branch, gain_two, shift_two)
    mixed_out = (second * row_mask).astype(BF16)
    grad_output = cotangent.astype(F32) * row_mask
    grad_second, grad_gain_two, grad_shift_two = norm_back(
        grad_output, unit_two, inverse_two, gain_two
    )
    grad_branch = grad_second.astype(BF16)
    grad_down_bias = jnp.sum(grad_branch.astype(F32), axis=0)
    grad_down = jnp.einsum("sth,td->shd", hidden, grad_branch, preferred_element_type=F32)
    grad_hidden = jnp.einsum("td,shd->sth", grad_branch, down_all, preferred_element_type=F32)
    grad_pre = activation_back(grad_hidden)[0].astype(BF16)
    grad_up_bias = jnp.sum(grad_pre.astype(F32), axis=1)
    grad_up = jnp.einsum("td,sth->sdh", normed_low, grad_pre, preferred_element_type=F32)
    grad_normed = grad_second + jnp.einsum(
        "sth,sdh->td", grad_pre, up_all, preferred_element_type=F32
    )
    grad_first, grad_gain_one, grad_shift_one = norm_back(
        grad_normed, unit_one, inverse_one, gain_one
    )
    grad_proj = grad_first.astype(BF16)
    grad_out_bias = jnp.sum(grad_proj.astype(F32), axis=0)
    grad_out = jnp.einsum("sta,td->sad", context, grad_proj, preferred_element_type=F32)
    grad_context = jnp.einsum(
        "td,sad->sta", grad_proj, out_parts, preferred_element_type=F32
    ).astype(BF16)

    own_rows, partner_rows, grad_weight, grad_bias = attend_back(
        info, tokens.T, partner.T, weight_all, q, k, v, grad_context, stats, shards, heads, depth
    )
    from_partner = lax.ppermute(
        partner_rows.astype(BF16), "head", [(i, i ^ 1) for i in range(shards)]
    )
    grad_tokens = grad_first + own_rows + from_partner.astype(F32)

    def collect(grads, axis):
        piece = lax.psum_scatter(grads, both, scatter_dimension=axis, tiled=True)
        return lax.all_gather(piece, "batch", axis=axis, tiled=True).astype(F32)

    grad_down_own = collect(grad_down.astype(BF16).reshape(shards * hidden_own, dim), 0)
    grad_up_own = collect(grad_up.astype(BF16).reshape(shards * dim, hidden_own), 0)
    grad_out_piece = lax.psum_scatter(
        grad_out.astype(BF16).reshape(shards * width, dim), both, scatter_dimension=0, tiled=True
    )
    grad_out_all = lax.all_gather(grad_out_piece, both, axis=0, tiled=True).astype(F32)
    grad_input_weight = collect(grad_weight.reshape(3, shards * dim, width), 1)

    bias_sums = grad_bias[:, :2].transpose(1, 0, 2).reshape(2, dim)
    vectors = jnp.concatenate(
        [
            jnp.stack(
                [
                    grad_out_bias,
                    grad_gain_one,
                    grad_shift_one,
                    grad_down_bias,
                    grad_gain_two,
                    grad_shift_two,
                ]
            ),
            bias_sums,
            grad_up_bias.reshape(-1, dim),
        ],
        axis=0,
    )
    vectors = jnp.sum(lax.all_gather(vectors, both), axis=0)
    grad_input_bias = lax.dynamic_slice_in_dim(vectors[6:8], head_at * width, width, 1)
    grad_up_bias_own = lax.dynamic_slice_in_dim(
        vectors[8:].reshape(-1), head_at * hidden_own, hidden_own
    )
    return (
        mixed_out,
        grad_tokens,
        grad_input_weight,
        grad_input_bias,
        grad_out_all,
        vectors[0],
        vectors[1],
        vectors[2],
        grad_up_own,
        grad_up_bias_own,
        grad_down_own,
        vectors[3],
        vectors[4],
        vectors[5],
    )


def solution(mesh):
    rows_spec = P(("batch", "head"), None)
    placed = (
        rows_spec,
        P("batch"),
        P("head"),
        P(None, None, "head"),
        P(None, "head"),
        P(),
        P(),
        P(),
        P(),
        P(None, "head"),
        P(),
        P("head", None),
        P(),
        P(),
        P(),
        rows_spec,
    )
    return jax.shard_map(
        functools.partial(local, mesh.shape["batch"], mesh.shape["head"]),
        mesh=mesh,
        in_specs=placed,
        out_specs=(
            rows_spec,
            rows_spec,
            P(None, None, "head"),
            P(None, "head"),
            P(),
            P(),
            P(),
            P(),
            P(None, "head"),
            P("head"),
            P("head", None),
            P(),
            P(),
            P(),
        ),
        check_vma=False,
    )
```

```python
import functools

import jax
import jax.numpy as jnp
from jax import lax
from jax.experimental import pallas as pl
from jax.experimental.pallas import tpu as pltpu
from jax.sharding import PartitionSpec as P

SEQ_LEN = 1024
EPSILON = 1e-05
F32 = jnp.float32
BF16 = jnp.bfloat16
VMEM_LIMIT = 56 * 1024 * 1024
PARAMS = pltpu.CompilerParams(vmem_limit_bytes=VMEM_LIMIT)
CORE, NEAR_X, NEAR_Y = 1, 2, 4
PARTS = 8


def dot(left_side, right_side, left_dim=1, right_dim=0):
    return lax.dot_general(
        left_side,
        right_side,
        (((left_dim,), (right_dim,)), ((), ())),
        preferred_element_type=F32,
    )


def unit_parts(values):
    centred = values - jnp.mean(values, axis=-1, keepdims=True)
    inverse = lax.rsqrt(jnp.mean(centred * centred, axis=-1, keepdims=True) + EPSILON)
    return centred * inverse, inverse


def norm_back(grad_rows, unit_rows, inverse, gain_row):
    scaled = grad_rows * gain_row
    return inverse * (
        scaled
        - jnp.mean(scaled, axis=-1, keepdims=True)
        - unit_rows * jnp.mean(scaled * unit_rows, axis=-1, keepdims=True)
    )


def column_sum(values):
    return jnp.sum(values, axis=0, keepdims=True)


def gelu_parts(inner):
    bell = jnp.exp(inner * inner * -0.5)
    t = 1.0 / (1.0 + jnp.abs(inner) * (0.3275911 * 0.5**0.5))
    poly = t * (
        0.254829592
        + t * (-0.284496736 + t * (1.421413741 + t * (-1.453152027 + t * 1.061405429)))
    )
    tail = 0.5 * poly * bell
    below = jnp.where(inner < 0.0, tail, 1.0 - tail)
    return inner * below, below + inner * bell * 0.3989422804014327


def lane_pick(values, depth):
    lane = lax.broadcasted_iota(jnp.int32, (1, len(values) * depth), 1)
    picked = jnp.full(lane.shape, values[0], jnp.int32)
    for j in range(1, len(values)):
        picked = jnp.where(lane >= j * depth, values[j], picked)
    return picked


class Info:
    def __init__(self, ref, heads, shards):
        self.ref, self.heads, self.base = ref, heads, heads * shards

    def swaps(self, shard):
        return [self.ref[shard * self.heads + j] for j in range(self.heads)]

    own_live = property(lambda self: self.ref[self.base])
    partner_live = property(lambda self: self.ref[self.base + 1])
    part = property(lambda self: self.ref[self.base + 2])
    head_at = property(lambda self: self.ref[self.base + 3])


def fill_weight(info, near, far, scratch):
    for spot in range(PARTS // 2):
        scratch[info.part ^ (2 * spot)] = near[spot, 0]
        scratch[info.part ^ (2 * spot + 1)] = far[spot, 0]


def attend_kernel(
    heads,
    depth,
    info_ref,
    tokens,
    partner,
    near,
    far,
    bias,
    out_weight,
    vectors,
    qkv_out,
    context_out,
    stats_out,
    rows_out,
    normed_out,
    weight_scratch,
    total,
):
    shard, shards = pl.program_id(0), pl.num_programs(0)
    info = Info(info_ref, heads, shards)
    swaps = info.swaps(shard)
    rows, dim = tokens.shape
    width = heads * depth
    fill_weight(info, near, far, weight_scratch)
    weight = weight_scratch[...].reshape(dim, 3 * width)
    own = dot(tokens[...], weight) + bias[0, 0:1]
    other = dot(partner[...], weight[:, : 2 * width]) + bias[0, 0:1, : 2 * width]
    swapped = lane_pick(swaps + swaps, depth) == 1
    kv = jnp.where(swapped, other, own[:, : 2 * width]).astype(BF16)
    q = own[:, 2 * width :].astype(BF16) * (depth**-0.5)
    qkv_out[0, :, : 2 * width] = kv
    qkv_out[0, :, 2 * width :] = q
    key_index = lax.broadcasted_iota(jnp.int32, (rows, 1), 0)
    stats = []
    pieces = []
    for j in range(heads):
        cut = slice(j * depth, (j + 1) * depth)
        live = jnp.where(swaps[j] == 1, info.partner_live, info.own_live)
        open_keys = key_index < live
        anyone = jnp.where(live > 0, 1.0, 0.0).astype(F32)
        scores = dot(kv[:, cut], q[:, cut], 1, 1)
        largest = jnp.max(jnp.where(open_keys, scores, -1e30), axis=0, keepdims=True)
        largest = jnp.where(anyone > 0.5, largest, 0.0)
        weights = jnp.exp(jnp.where(open_keys, scores - largest, -10000.0))
        totals = column_sum(weights) + (1.0 - anyone)
        mixing = (weights * (1.0 / totals)).astype(BF16)
        stats.append(largest + jnp.log(totals))
        pieces.append(dot(kv[:, width + j * depth : width + (j + 1) * depth], mixing, 0, 0))
    context = jnp.concatenate(pieces, axis=0).T.astype(BF16)
    context_out[0] = context
    stats_out[0] = jnp.concatenate(stats + [jnp.zeros((8 - heads, rows), F32)], axis=0)
    projected = dot(context, out_weight[info.head_at ^ shard])

    @pl.when(shard == 0)
    def first():
        total[...] = projected

    @pl.when(shard > 0)
    def later():
        total[...] += projected

    @pl.when(shard == shards - 1)
    def finish():
        values = tokens[...].astype(F32) + (total[...] + vectors[0:1])
        rows_out[...] = values
        unit, _ = unit_parts(values)
        normed_out[...] = (unit * vectors[1:2] + vectors[2:3]).astype(BF16)


def forward_kernel(last, normed, weight, bias, *refs):
    step, steps = pl.program_id(0), pl.num_programs(0)
    if last:
        (info, branch_in, rows_in, cotangent, vectors) = refs[:5]
        (hidden_out, slope_out, mixed_out, second_out, grad_out, sums_out, total) = refs[5:]
    else:
        (hidden_out, slope_out, total) = refs
    dim = normed.shape[1]
    block = weight[0].reshape(-1, 2 * dim)
    pre = dot(normed[...], block[:, :dim], 1, 1) + bias[0]
    hidden, slope = gelu_parts(pre)
    hidden = hidden.astype(BF16)
    hidden_out[...] = hidden
    slope_out[...] = slope
    partial = dot(hidden, block[:, dim:])

    @pl.when(step == 0)
    def first():
        total[...] = partial

    @pl.when(step > 0)
    def later():
        total[...] += partial

    if not last:
        return

    @pl.when(step == steps - 1)
    def finish():
        unit_one, _ = unit_parts(rows_in[...])
        first_norm = unit_one * vectors[0:1] + vectors[1:2]
        unit, inverse = unit_parts(first_norm + (branch_in[...] + total[...] + vectors[2:3]))
        present = lax.broadcasted_iota(jnp.int32, (normed.shape[0], 1), 0) < info[0]
        mask = jnp.where(present, 1.0, 0.0).astype(F32)
        mixed_out[...] = ((unit * vectors[3:4] + vectors[4:5]) * mask).astype(BF16)
        incoming = cotangent[...].astype(F32) * mask
        grad = norm_back(incoming, unit, inverse, vectors[3:4])
        second_out[...] = grad
        low = grad.astype(BF16)
        grad_out[...] = low
        sums_out[...] = jnp.concatenate(
            [
                column_sum(low.astype(F32)),
                column_sum(incoming * unit),
                column_sum(incoming),
                jnp.zeros((5, dim), F32),
            ],
            axis=0,
        )


def backward_kernel(last, normed, grad_branch, weight, hidden, slope, *refs):
    step, steps = pl.program_id(0), pl.num_programs(0)
    if last:
        (info, normed_in, rows_in, second_in, context, vectors) = refs[:6]
        (grads_out, bias_out, first_out, proj_out, sums_out, near_out, far_out) = refs[6:13]
        (total, chunks) = refs[13:]
    else:
        (grads_out, bias_out, total) = refs
    dim = normed.shape[1]
    shards, piece = weight.shape[1], weight.shape[2]
    block = weight[0].reshape(-1, 2 * dim)
    grad_rows = grad_branch[...]
    grad_pre = dot(grad_rows, block[:, dim:], 1, 1) * slope[...]
    grad_pre = grad_pre.astype(BF16)
    bias_out[0] = jnp.broadcast_to(column_sum(grad_pre.astype(F32)), bias_out.shape[1:])
    up = dot(grad_pre, normed[...], 0, 0)
    grads_out[0, :, :, :dim] = up.astype(BF16).reshape(shards, piece, dim)
    down = dot(hidden[...], grad_rows, 0, 0)
    grads_out[0, :, :, dim:] = down.astype(BF16).reshape(shards, piece, dim)
    partial = dot(grad_pre, block[:, :dim])

    @pl.when(step == 0)
    def first():
        total[...] = partial

    @pl.when(step > 0)
    def later():
        total[...] += partial

    if not last:
        return

    @pl.when(step == steps - 1)
    def finish():
        unit, inverse = unit_parts(rows_in[...])
        grad_normed = second_in[...] + (normed_in[...] + total[...])
        grad = norm_back(grad_normed, unit, inverse, vectors[0:1])
        first_out[...] = grad
        low = grad.astype(BF16)
        proj_out[...] = low
        sums_out[...] = jnp.concatenate(
            [
                column_sum(low.astype(F32)),
                column_sum(grad_normed * unit),
                column_sum(grad_normed),
                jnp.zeros((5, dim), F32),
            ],
            axis=0,
        )
        low_t = low.T
        part = info[1]
        for q in range(shards):
            value = dot(low_t, context[q]).astype(BF16)
            chunks[...] = value.reshape(chunks.shape)
            for spot in range(PARTS // 2):
                near_out[spot, q] = chunks[part ^ (2 * spot)]
                far_out[spot, q] = chunks[part ^ (2 * spot + 1)]


def attend_back_kernel(
    heads,
    depth,
    info_ref,
    tokens,
    partner,
    grad_proj,
    near,
    far,
    out_weight,
    qkv_in,
    stats_in,
    own_out,
    partner_out,
    near_out,
    far_out,
    bias_out,
    weight_scratch,
    tokens_t,
    partner_t,
    total,
    chunks,
):
    shard, shards = pl.program_id(0), pl.num_programs(0)
    info = Info(info_ref, heads, shards)
    swaps = info.swaps(shard)
    rows, dim = tokens.shape
    width = heads * depth

    @pl.when(shard == 0)
    def turn():
        tokens_t[...] = tokens[...].T
        partner_t[...] = partner[...].T

    fill_weight(info, near, far, weight_scratch)
    weight = weight_scratch[...].reshape(dim, 3 * width)
    grad = dot(grad_proj[...], out_weight[info.head_at ^ shard], 1, 1).astype(BF16)
    k, v, q = (qkv_in[0, :, i * width : (i + 1) * width] for i in range(3))
    stats = stats_in[0]
    key_index = lax.broadcasted_iota(jnp.int32, (rows, 1), 0)
    gq, gk, gv = [], [], []
    for j in range(heads):
        cut = slice(j * depth, (j + 1) * depth)
        live = jnp.where(swaps[j] == 1, info.partner_live, info.own_live)
        open_keys = key_index < live
        scores = dot(k[:, cut], q[:, cut], 1, 1)
        chances = jnp.exp(jnp.where(open_keys, scores - stats[j : j + 1, :], -10000.0))
        grad_mix = dot(v[:, cut], grad[:, cut], 1, 1)
        shared = column_sum(grad_mix * chances)
        grad_scores = (chances * (grad_mix - shared)).astype(BF16)
        gk.append(dot(grad_scores, q[:, cut]))
        gv.append(dot(chances.astype(BF16), grad[:, cut]))
        gq.append(dot(k[:, cut], grad_scores, 0, 0))
    grad_q = (jnp.concatenate(gq, axis=0).T * (depth**-0.5)).astype(BF16)
    grad_kv = jnp.concatenate(gk + gv, axis=1).astype(BF16)
    swapped = lane_pick(swaps + swaps, depth) == 1
    nothing = jnp.zeros((), BF16)
    grad_own = jnp.concatenate([jnp.where(swapped, nothing, grad_kv), grad_q], axis=1)
    grad_far = jnp.where(swapped, grad_kv, nothing)
    own = dot(grad_own, weight, 1, 1)
    other = dot(grad_far, weight[:, : 2 * width], 1, 1)

    @pl.when(shard == 0)
    def first():
        own_out[...] = own
        total[...] = other

    @pl.when(shard > 0)
    def later():
        own_out[...] += own
        total[...] += other

    @pl.when(shard == shards - 1)
    def finish():
        partner_out[...] = total[...].astype(BF16)

    grads = dot(tokens_t[...], grad_own)
    grads_kv = grads[:, : 2 * width] + dot(partner_t[...], grad_far)
    grads = jnp.concatenate([grads_kv, grads[:, 2 * width :]], axis=1).astype(BF16)
    chunks[...] = grads.reshape(chunks.shape)
    for spot in range(PARTS // 2):
        near_out[spot, 0] = chunks[info.part ^ (2 * spot)]
        far_out[spot, 0] = chunks[info.part ^ (2 * spot + 1)]
    bias_out[0] = jnp.broadcast_to(
        jnp.concatenate(
            [column_sum(grad_kv.astype(F32)), column_sum(grad_q.astype(F32))], axis=1
        ),
        bias_out.shape[1:],
    )


def fold_core_kernel(*refs):
    count = (len(refs) - 4) // 2
    mine, received, outs = refs[:count], refs[count : 2 * count], refs[2 * count :]
    for spot in range(4):
        parts = [a[spot, 0].astype(F32) + b[spot, 0].astype(F32) for a, b in zip(mine, received)]
        used = sum(part.shape[1] for part in parts)
        if used < outs[spot].shape[2]:
            parts.append(jnp.zeros((parts[0].shape[0], outs[spot].shape[2] - used), F32))
        value = jnp.concatenate(parts, axis=1) if len(parts) > 1 else parts[0]
        outs[spot][0] = value.astype(outs[spot].dtype)


def fold_chips_kernel(own, a, b, c, *outs):
    for q, out in enumerate(outs):
        value = own[q] + (a[q].astype(F32) + b[q].astype(F32)) + c[q].astype(F32)
        out[...] = value.astype(out.dtype)


def settle_feed_kernel(info, near, far, up_out, down_out, out_out, up_scratch, out_scratch):
    dim = down_out.shape[2]
    for core, source in enumerate((near, far)):
        for spot in range(PARTS // 2):
            place = info[1] ^ (2 * spot + core)
            value = source[spot].astype(F32)
            up_scratch[place] = value[:, :dim]
            down_out[place] = value[:, dim : 2 * dim]
            out_scratch[place] = value[:, 2 * dim :]
    up_out[...] = up_scratch[...].reshape(-1, dim).T
    shards = out_out.shape[0]
    turned = out_scratch[...].reshape(-1, dim).T.reshape(shards, -1, dim)
    for q in range(shards):
        out_out[info[2] ^ q] = turned[q]


def settle_input_kernel(info, near, far, out):
    width = out.shape[3]
    for core, source in enumerate((near, far)):
        for spot in range(PARTS // 2):
            place = info[1] ^ (2 * spot + core)
            value = source[spot].astype(F32)
            for i in range(3):
                out[(i + 1) % 3, place] = value[:, i * width : (i + 1) * width]


def shape(dims, dtype):
    return jax.ShapeDtypeStruct(dims, dtype)


def whole(*dims):
    return pl.BlockSpec(dims, lambda *_: (0,) * len(dims))


SMEM = pl.BlockSpec(memory_space=pltpu.SMEM)


def attend(info, tokens, partner, near, far, bias, out_weight, vectors, heads, depth):
    rows, dim = tokens.shape
    spots, shards, piece, lanes = near.shape
    width = heads * depth
    weight_spec = pl.BlockSpec((spots, 1, piece, lanes), lambda s: (0, s, 0, 0))
    return pl.pallas_call(
        functools.partial(attend_kernel, heads, depth),
        grid=(shards,),
        in_specs=[
            SMEM,
            whole(rows, dim),
            whole(rows, dim),
            weight_spec,
            weight_spec,
            pl.BlockSpec((1, 8, lanes), lambda s: (s, 0, 0)),
            whole(shards, width, dim),
            whole(8, dim),
        ],
        out_specs=[
            pl.BlockSpec((1, rows, lanes), lambda s: (s, 0, 0)),
            pl.BlockSpec((1, rows, width), lambda s: (s, 0, 0)),
            pl.BlockSpec((1, 8, rows), lambda s: (s, 0, 0)),
            whole(rows, dim),
            whole(rows, dim),
        ],
        out_shape=[
            shape((shards, rows, lanes), BF16),
            shape((shards, rows, width), BF16),
            shape((shards, 8, rows), F32),
            shape((rows, dim), F32),
            shape((rows, dim), BF16),
        ],
        scratch_shapes=[pltpu.VMEM((PARTS, piece, lanes), BF16), pltpu.VMEM((rows, dim), F32)],
        compiler_params=PARAMS,
        cost_estimate=pl.CostEstimate(
            flops=12 * rows * dim * dim + 16 * rows * rows * dim,
            bytes_accessed=24 * rows * dim,
            transcendentals=shards * heads * rows * rows,
        ),
        name="attend",
    )(info, tokens, partner, near, far, bias, out_weight, vectors)


def feed_forward(last, normed, weight, bias, *extra):
    rows, dim = normed.shape
    spots, shards, piece, lanes = weight.shape
    tile = shards * piece
    in_specs = [
        whole(rows, dim),
        pl.BlockSpec((1, shards, piece, lanes), lambda s: (s, 0, 0, 0)),
        pl.BlockSpec((1, 1, tile), lambda s: (s, 0, 0)),
    ]
    out_specs = [pl.BlockSpec((rows, tile), lambda s: (0, s))] * 2
    out_shape = [shape((rows, spots * tile), BF16), shape((rows, spots * tile), F32)]
    scratch = []
    if last:
        in_specs += [SMEM] + [whole(rows, dim)] * 3 + [whole(8, dim)]
        out_specs += [whole(rows, dim)] * 3 + [whole(8, dim)]
        out_shape += [
            shape((rows, dim), BF16),
            shape((rows, dim), F32),
            shape((rows, dim), BF16),
            shape((8, dim), F32),
        ]
        scratch = [pltpu.VMEM((rows, dim), F32)]
    else:
        out_specs.append(whole(rows, dim))
        out_shape.append(shape((rows, dim), F32))
    return pl.pallas_call(
        functools.partial(forward_kernel, last),
        grid=(spots,),
        in_specs=in_specs,
        out_specs=out_specs,
        out_shape=out_shape,
        scratch_shapes=scratch,
        compiler_params=PARAMS,
        cost_estimate=pl.CostEstimate(
            flops=4 * rows * dim * tile * spots,
            bytes_accessed=24 * rows * dim,
            transcendentals=2 * rows * tile * spots,
        ),
        name="feed_last" if last else "feed_first",
    )(normed, weight, bias, *extra)


def feed_back(last, normed, grad_branch, weight, hidden, slope, *extra):
    rows, dim = normed.shape
    spots, shards, piece, lanes = weight.shape
    tile = shards * piece
    weight_spec = pl.BlockSpec((1, shards, piece, lanes), lambda s: (s, 0, 0, 0))
    in_specs = [
        whole(rows, dim),
        whole(rows, dim),
        weight_spec,
        pl.BlockSpec((rows, tile), lambda s: (0, s)),
        pl.BlockSpec((rows, tile), lambda s: (0, s)),
    ]
    out_specs = [weight_spec, pl.BlockSpec((1, 8, tile), lambda s: (s, 0, 0))]
    out_shape = [shape(weight.shape, BF16), shape((spots, 8, tile), F32)]
    scratch = []
    if last:
        width = extra[4].shape[2]
        in_specs += [SMEM] + [whole(rows, dim)] * 3 + [whole(shards, rows, width), whole(8, dim)]
        out_specs += [whole(rows, dim)] * 2 + [whole(8, dim)]
        out_specs += [whole(spots, shards, piece, width)] * 2
        out_shape += [
            shape((rows, dim), F32),
            shape((rows, dim), BF16),
            shape((8, dim), F32),
            shape((spots, shards, piece, width), BF16),
            shape((spots, shards, piece, width), BF16),
        ]
        scratch = [pltpu.VMEM((rows, dim), F32), pltpu.VMEM((PARTS, piece, width), BF16)]
    else:
        out_specs.append(whole(rows, dim))
        out_shape.append(shape((rows, dim), F32))
    return pl.pallas_call(
        functools.partial(backward_kernel, last),
        grid=(spots,),
        in_specs=in_specs,
        out_specs=out_specs,
        out_shape=out_shape,
        scratch_shapes=scratch,
        compiler_params=PARAMS,
        cost_estimate=pl.CostEstimate(
            flops=8 * rows * dim * tile * spots,
            bytes_accessed=36 * rows * dim,
            transcendentals=0,
        ),
        name="feed_back_last" if last else "feed_back_first",
    )(normed, grad_branch, weight, hidden, slope, *extra)


def attend_back(
    info, tokens, partner, grad_proj, near, far, out_weight, qkv, stats, heads, depth
):
    rows, dim = tokens.shape
    spots, shards, piece, lanes = near.shape
    width = heads * depth
    weight_spec = pl.BlockSpec((spots, 1, piece, lanes), lambda s: (0, s, 0, 0))
    return pl.pallas_call(
        functools.partial(attend_back_kernel, heads, depth),
        grid=(shards,),
        in_specs=[
            SMEM,
            whole(rows, dim),
            whole(rows, dim),
            whole(rows, dim),
            weight_spec,
            weight_spec,
            whole(shards, width, dim),
            pl.BlockSpec((1, rows, lanes), lambda s: (s, 0, 0)),
            pl.BlockSpec((1, 8, rows), lambda s: (s, 0, 0)),
        ],
        out_specs=[
            whole(rows, dim),
            whole(rows, dim),
            weight_spec,
            weight_spec,
            pl.BlockSpec((1, 8, lanes), lambda s: (s, 0, 0)),
        ],
        out_shape=[
            shape((rows, dim), F32),
            shape((rows, dim), BF16),
            shape(near.shape, BF16),
            shape(far.shape, BF16),
            shape((shards, 8, lanes), F32),
        ],
        scratch_shapes=[
            pltpu.VMEM((PARTS, piece, lanes), BF16),
            pltpu.VMEM((dim, rows), BF16),
            pltpu.VMEM((dim, rows), BF16),
            pltpu.VMEM((rows, dim), F32),
            pltpu.VMEM((PARTS, piece, lanes), BF16),
        ],
        compiler_params=PARAMS,
        cost_estimate=pl.CostEstimate(
            flops=24 * rows * dim * dim + 40 * rows * rows * dim,
            bytes_accessed=32 * rows * dim,
            transcendentals=shards * heads * rows * rows,
        ),
        name="attend_back",
    )(info, tokens, partner, grad_proj, near, far, out_weight, qkv, stats)


def fold_core(mine, received, lanes):
    spots, shards, piece = mine[0].shape[:3]
    specs = [
        pl.BlockSpec((spots, 1, piece, a.shape[3]), lambda s: (0, s, 0, 0))
        for a in mine + received
    ]
    return pl.pallas_call(
        fold_core_kernel,
        grid=(shards,),
        in_specs=specs,
        out_specs=[pl.BlockSpec((1, piece, lanes), lambda s: (s, 0, 0))] * spots,
        out_shape=[shape((shards, piece, lanes), F32)]
        + [shape((shards, piece, lanes), BF16)] * (spots - 1),
        compiler_params=PARAMS,
        cost_estimate=pl.CostEstimate(
            flops=spots * shards * piece * lanes,
            bytes_accessed=8 * spots * shards * piece * lanes,
            transcendentals=0,
        ),
        name="fold_core",
    )(*mine, *received)


def fold_chips(own, received):
    shards, piece, lanes = own.shape
    cut = 256 if lanes % 256 == 0 else lanes
    spec = pl.BlockSpec((shards, piece, cut), lambda s: (0, 0, s))
    return pl.pallas_call(
        fold_chips_kernel,
        grid=(lanes // cut,),
        in_specs=[spec] * 4,
        out_specs=[pl.BlockSpec((piece, cut), lambda s: (0, s))] * shards,
        out_shape=[shape((piece, lanes), F32)] + [shape((piece, lanes), BF16)] * (shards - 1),
        compiler_params=PARAMS,
        cost_estimate=pl.CostEstimate(
            flops=4 * shards * piece * lanes,
            bytes_accessed=12 * shards * piece * lanes,
            transcendentals=0,
        ),
        name="fold_chips",
    )(own, *received)


class Mover:
    def __init__(self, batch_size, shards):
        self.batch_size, self.shards = batch_size, shards

    def batch(self, value, mask):
        return lax.ppermute(value, "batch", [(i, i ^ mask) for i in range(self.batch_size)])

    def head(self, value, mask):
        return lax.ppermute(value, "head", [(i, i ^ mask) for i in range(self.shards)])

    def around(self, value):
        return [self.batch(value, mask) for mask in (NEAR_X, NEAR_Y, NEAR_X | NEAR_Y)]

    def along(self, values):
        return [self.head(value, q) for q, value in enumerate(values, 1)]

    def gather(self, piece):
        column = jnp.stack([piece] + self.along([piece] * (self.shards - 1)))
        near = jnp.stack([column] + self.around(column))
        return near, self.batch(near, CORE)

    def reduce(self, own, send):
        masks = (NEAR_X, NEAR_Y, NEAR_X | NEAR_Y)
        received = [self.batch(value, mask) for value, mask in zip(send, masks)]
        sums = fold_chips(own, received)
        total = sums[0]
        for value in self.along(sums[1:]):
            total = total + value.astype(F32)
        total = total.astype(BF16)
        mask = PARTS
        while mask < self.batch_size:
            total = (total.astype(F32) + self.batch(total, mask).astype(F32)).astype(BF16)
            mask *= 2
        return total

    def spread(self, piece):
        near = jnp.stack([piece] + self.around(piece))
        return near, self.batch(near, CORE)

    def total(self, value):
        mask = 1
        while mask < self.batch_size:
            value = value + self.batch(value, mask)
            mask *= 2
        mask = 1
        while mask < self.shards:
            value = value + self.head(value, mask)
            mask *= 2
        return value


def exchange_bits(value, axes):
    for axis, bit in axes:
        value = jnp.where(bit == 1, jnp.flip(value, axis), value)
    return value


def stack8(*rows):
    rows = [row.reshape(1, -1) for row in rows]
    return jnp.concatenate(rows + [jnp.zeros((8 - len(rows), rows[0].shape[1]), F32)], axis=0)


def local(
    batch_size,
    shards,
    tokens,
    lengths,
    block_swap,
    input_weight,
    input_bias,
    out_weight,
    out_bias,
    gain_one,
    shift_one,
    up_weight,
    up_bias,
    down_weight,
    down_bias,
    gain_two,
    shift_two,
    cotangent,
):
    move = Mover(batch_size, shards)
    heads = block_swap.shape[0]
    rows, dim = tokens.shape
    width = input_weight.shape[2]
    depth = width // heads
    hidden_own = up_weight.shape[1]
    piece = dim // PARTS
    batch_at, head_at = lax.axis_index("batch"), lax.axis_index("head")
    part = batch_at % PARTS
    part_bits = [(part >> i) & 1 for i in range(3)]
    head_bits = [(head_at >> i) & 1 for i in range(2)]
    blocks = SEQ_LEN // rows
    length = lax.dynamic_index_in_dim(lengths, head_at // blocks, 0, keepdims=False)
    block_at = head_at % blocks
    own_live = jnp.clip(length - block_at * rows, 0, rows)
    partner_live = jnp.clip(length - (blocks - 1 - block_at) * rows, 0, rows)

    input_piece = lax.dynamic_slice_in_dim(input_weight, part * piece, piece, 1)
    input_piece = jnp.concatenate([input_piece[1], input_piece[2], input_piece[0]], axis=1)
    small = jnp.concatenate([input_bias.reshape(-1), block_swap.astype(F32)])
    small = jnp.stack([small] + move.along([small] * (shards - 1)))
    input_near, input_far = move.gather(input_piece)
    partner = move.head(tokens, 1)
    up_piece = lax.dynamic_slice_in_dim(up_weight, part * piece, piece, 1).T
    down_piece = lax.dynamic_slice_in_dim(down_weight, part * piece, piece, 0)
    feed_piece = jnp.concatenate([up_piece, down_piece], axis=1)
    feed_piece, partner = lax.optimization_barrier((feed_piece, partner))
    feed_near, feed_far = move.gather(feed_piece)

    info = jnp.concatenate(
        [
            small[:, 2 * width :].reshape(-1).astype(jnp.int32),
            jnp.stack([own_live, partner_live, part, head_at]).astype(jnp.int32),
        ]
    )
    short_info = jnp.stack([own_live, part, head_at]).astype(jnp.int32)
    bias = jnp.concatenate(
        [jnp.zeros((shards, width), F32), small[:, width : 2 * width], small[:, :width]], axis=1
    )
    bias = jnp.broadcast_to(bias[:, None], (shards, 8, 3 * width))
    bits = [(0, head_bits[1]), (1, head_bits[0])]
    bits += [(2, part_bits[2]), (3, part_bits[1]), (4, part_bits[0])]
    up_bias_rel = exchange_bits(up_bias.reshape(2, 2, 2, 2, 2, piece), bits)
    up_bias_rel = up_bias_rel.transpose(4, 2, 3, 0, 1, 5).reshape(2, 4, 1, shards * piece)
    out_parts = out_weight.reshape(shards, width, dim)

    qkv, context, stats, rows_one, normed = attend(
        info,
        tokens,
        partner,
        input_near,
        input_far,
        bias,
        out_parts,
        stack8(out_bias, gain_one, shift_one),
        heads,
        depth,
    )
    hidden_near, slope_near, branch = feed_forward(False, normed, feed_near, up_bias_rel[0])
    hidden_far, slope_far, mixed_out, grad_second, grad_branch, sums_two = feed_forward(
        True,
        normed,
        feed_far,
        up_bias_rel[1],
        short_info,
        branch,
        rows_one,
        cotangent,
        stack8(gain_one, shift_one, down_bias, gain_two, shift_two),
    )

    feed_grads_far, up_bias_far, grad_normed = feed_back(
        False, normed, grad_branch, feed_far, hidden_far, slope_far
    )
    feed_received = move.batch(feed_grads_far, CORE)
    (
        feed_grads_near,
        up_bias_near,
        grad_first,
        grad_proj,
        sums_one,
        out_grads_near,
        out_grads_far,
    ) = feed_back(
        True,
        normed,
        grad_branch,
        feed_near,
        hidden_near,
        slope_near,
        short_info,
        grad_normed,
        rows_one,
        grad_second,
        context,
        stack8(gain_one),
    )
    out_received = move.batch(out_grads_far, CORE)
    lanes = -(-(2 * dim + width) // 256) * 256
    feed_own, *feed_send = fold_core(
        [feed_grads_near, out_grads_near], [feed_received, out_received], lanes
    )
    own_rows, partner_rows, input_grads_near, input_grads_far, bias_sums = attend_back(
        info,
        tokens,
        partner,
        grad_proj,
        input_near,
        input_far,
        out_parts,
        qkv,
        stats,
        heads,
        depth,
    )
    feed_total = move.reduce(feed_own, feed_send)
    out_total = feed_total[:, 2 * dim : 2 * dim + width]
    out_total = [out_total] + move.along([out_total] * (shards - 1))
    feed_total = jnp.concatenate([feed_total[:, : 2 * dim]] + out_total, axis=1)
    feed_done = move.spread(feed_total)

    from_partner = move.head(partner_rows, 1)
    input_received = move.batch(input_grads_far, CORE)
    input_own, *input_send = fold_core([input_grads_near], [input_received], 3 * width)
    input_total = move.reduce(input_own, input_send)
    input_done = move.spread(input_total)
    grad_tokens = grad_first + own_rows + from_partner.astype(F32)

    up_bias_grad = jnp.stack([up_bias_near[:, 0], up_bias_far[:, 0]])
    up_bias_grad = up_bias_grad.reshape(2, 2, 2, 2, 2, piece).transpose(3, 4, 1, 2, 0, 5)
    up_bias_grad = exchange_bits(up_bias_grad, bits).reshape(-1, dim)
    bias_sums = exchange_bits(bias_sums[:, 0].reshape(2, 2, 3, width), bits[:2])
    bias_sums = bias_sums.reshape(shards, 3, width).transpose(1, 0, 2).reshape(3, dim)
    vectors = move.total(
        jnp.concatenate([sums_one[:3], sums_two[:3], bias_sums[2:], bias_sums[1:2], up_bias_grad])
    )
    grad_input_bias = lax.dynamic_slice_in_dim(vectors[6:8], head_at * width, width, 1)
    grad_up_bias = lax.dynamic_slice_in_dim(
        vectors[8:].reshape(-1), head_at * hidden_own, hidden_own
    )

    grad_up, grad_down, grad_out = pl.pallas_call(
        settle_feed_kernel,
        in_specs=[SMEM] + [whole(4, piece, 2 * dim + shards * width)] * 2,
        out_shape=[
            shape((dim, hidden_own), F32),
            shape((PARTS, piece, dim), F32),
            shape((shards, width, dim), F32),
        ],
        scratch_shapes=[pltpu.VMEM((PARTS, piece, dim), F32)] * 2,
        compiler_params=PARAMS,
        name="settle_feed",
    )(short_info, *feed_done)
    grad_input_weight = pl.pallas_call(
        settle_input_kernel,
        in_specs=[SMEM] + [whole(4, piece, 3 * width)] * 2,
        out_shape=shape((3, PARTS, piece, width), F32),
        compiler_params=PARAMS,
        name="settle_input",
    )(short_info, *input_done)
    return (
        mixed_out,
        grad_tokens,
        grad_input_weight.reshape(3, dim, width),
        grad_input_bias,
        grad_out.reshape(dim, dim),
        vectors[0],
        vectors[1],
        vectors[2],
        grad_up,
        grad_up_bias,
        grad_down.reshape(hidden_own, dim),
        vectors[3],
        vectors[4],
        vectors[5],
    )


def solution(mesh):
    rows_spec = P(("batch", "head"), None)
    placed = (
        rows_spec,
        P("batch"),
        P("head"),
        P(None, None, "head"),
        P(None, "head"),
        P(),
        P(),
        P(),
        P(),
        P(None, "head"),
        P(),
        P("head", None),
        P(),
        P(),
        P(),
        rows_spec,
    )
    return jax.shard_map(
        functools.partial(local, mesh.shape["batch"], mesh.shape["head"]),
        mesh=mesh,
        in_specs=placed,
        out_specs=(
            rows_spec,
            rows_spec,
            P(None, None, "head"),
            P(None, "head"),
            P(),
            P(),
            P(),
            P(),
            P(None, "head"),
            P("head"),
            P("head", None),
            P(),
            P(),
            P(),
        ),
        check_vma=False,
    )
```

```python
import functools

import jax
import jax.numpy as jnp
from jax import lax
from jax.experimental import pallas as pl
from jax.experimental.pallas import tpu as pltpu
from jax.sharding import PartitionSpec as P

SEQ_LEN = 1024
EPSILON = 1e-05
F32 = jnp.float32
BF16 = jnp.bfloat16
VMEM_LIMIT = 56 * 1024 * 1024
PARAMS = pltpu.CompilerParams(vmem_limit_bytes=VMEM_LIMIT)
CORE, NEAR_X, NEAR_Y = 1, 2, 4
PARTS = 8


def dot(left_side, right_side, left_dim=1, right_dim=0):
    return lax.dot_general(
        left_side,
        right_side,
        (((left_dim,), (right_dim,)), ((), ())),
        preferred_element_type=F32,
    )


def unit_parts(values):
    centred = values - jnp.mean(values, axis=-1, keepdims=True)
    inverse = lax.rsqrt(jnp.mean(centred * centred, axis=-1, keepdims=True) + EPSILON)
    return centred * inverse, inverse


def norm_back(grad_rows, unit_rows, inverse, gain_row):
    scaled = grad_rows * gain_row
    return inverse * (
        scaled
        - jnp.mean(scaled, axis=-1, keepdims=True)
        - unit_rows * jnp.mean(scaled * unit_rows, axis=-1, keepdims=True)
    )


def column_sum(values):
    return jnp.sum(values, axis=0, keepdims=True)


def gelu_parts(inner):
    bell = jnp.exp(inner * inner * -0.5)
    t = 1.0 / (1.0 + jnp.abs(inner) * (0.3275911 * 0.5**0.5))
    poly = t * (
        0.254829592
        + t * (-0.284496736 + t * (1.421413741 + t * (-1.453152027 + t * 1.061405429)))
    )
    tail = 0.5 * poly * bell
    below = jnp.where(inner < 0.0, tail, 1.0 - tail)
    return inner * below, below + inner * bell * 0.3989422804014327


def lane_pick(values, depth):
    lane = lax.broadcasted_iota(jnp.int32, (1, len(values) * depth), 1)
    picked = jnp.full(lane.shape, values[0], jnp.int32)
    for j in range(1, len(values)):
        picked = jnp.where(lane >= j * depth, values[j], picked)
    return picked


class Info:
    def __init__(self, ref, heads, shards):
        self.ref, self.heads, self.base = ref, heads, heads * shards

    def swaps(self, shard):
        return [self.ref[shard * self.heads + j] for j in range(self.heads)]

    own_live = property(lambda self: self.ref[self.base])
    partner_live = property(lambda self: self.ref[self.base + 1])
    part = property(lambda self: self.ref[self.base + 2])
    head_at = property(lambda self: self.ref[self.base + 3])


def fill_weight(info, near, far, scratch):
    for spot in range(PARTS // 2):
        scratch[info.part ^ (2 * spot)] = near[spot, 0]
        scratch[info.part ^ (2 * spot + 1)] = far[spot, 0]


def attend_kernel(
    heads,
    depth,
    info_ref,
    tokens,
    partner,
    near,
    far,
    bias,
    out_weight,
    vectors,
    qkv_out,
    context_out,
    stats_out,
    rows_out,
    normed_out,
    weight_scratch,
    total,
):
    shard, shards = pl.program_id(0), pl.num_programs(0)
    info = Info(info_ref, heads, shards)
    swaps = info.swaps(shard)
    rows, dim = tokens.shape
    width = heads * depth
    fill_weight(info, near, far, weight_scratch)
    weight = weight_scratch[...].reshape(dim, 3 * width)
    own = dot(tokens[...], weight) + bias[0, 0:1]
    other = dot(partner[...], weight[:, : 2 * width]) + bias[0, 0:1, : 2 * width]
    swapped = lane_pick(swaps + swaps, depth) == 1
    kv = jnp.where(swapped, other, own[:, : 2 * width]).astype(BF16)
    q = own[:, 2 * width :].astype(BF16) * (depth**-0.5)
    qkv_out[0, :, : 2 * width] = kv
    qkv_out[0, :, 2 * width :] = q
    key_index = lax.broadcasted_iota(jnp.int32, (rows, 1), 0)
    stats = []
    pieces = []
    for j in range(heads):
        cut = slice(j * depth, (j + 1) * depth)
        live = jnp.where(swaps[j] == 1, info.partner_live, info.own_live)
        open_keys = key_index < live
        anyone = jnp.where(live > 0, 1.0, 0.0).astype(F32)
        scores = dot(kv[:, cut], q[:, cut], 1, 1)
        largest = jnp.max(jnp.where(open_keys, scores, -1e30), axis=0, keepdims=True)
        largest = jnp.where(anyone > 0.5, largest, 0.0)
        weights = jnp.exp(jnp.where(open_keys, scores - largest, -10000.0))
        totals = column_sum(weights) + (1.0 - anyone)
        mixing = (weights * (1.0 / totals)).astype(BF16)
        stats.append(largest + jnp.log(totals))
        pieces.append(dot(kv[:, width + j * depth : width + (j + 1) * depth], mixing, 0, 0))
    context = jnp.concatenate(pieces, axis=0).T.astype(BF16)
    context_out[0] = context
    stats_out[0] = jnp.concatenate(stats + [jnp.zeros((8 - heads, rows), F32)], axis=0)
    projected = dot(context, out_weight[info.head_at ^ shard])

    @pl.when(shard == 0)
    def first():
        total[...] = projected

    @pl.when(shard > 0)
    def later():
        total[...] += projected

    @pl.when(shard == shards - 1)
    def finish():
        values = tokens[...].astype(F32) + (total[...] + vectors[0:1])
        rows_out[...] = values
        unit, _ = unit_parts(values)
        normed_out[...] = (unit * vectors[1:2] + vectors[2:3]).astype(BF16)


def tile_of(near, far):
    step, half = pl.program_id(0), pl.num_programs(0) // 2
    return jnp.where(step < half, near[0], far[0]).reshape(-1, near.shape[3])


def add_up(total, partial):
    @pl.when(pl.program_id(0) == 0)
    def first():
        total[...] = partial

    @pl.when(pl.program_id(0) > 0)
    def later():
        total[...] += partial


def at_end(run):
    pl.when(pl.program_id(0) == pl.num_programs(0) - 1)(run)


def eight_rows(*rows):
    width = rows[0].shape[1]
    return jnp.concatenate([*rows, jnp.zeros((8 - len(rows), width), F32)], axis=0)


def feed_up_kernel(normed, near, far, bias, hidden_out, slope_out):
    pre = dot(normed[...], tile_of(near, far), 1, 1) + bias[0]
    hidden, slope = gelu_parts(pre)
    hidden_out[...] = hidden.astype(BF16)
    slope_out[...] = slope


def feed_down_kernel(
    info,
    hidden,
    near,
    far,
    rows_in,
    cotangent,
    vectors,
    mixed_out,
    second_out,
    grad_out,
    sums_out,
    total,
):
    add_up(total, dot(hidden[...], tile_of(near, far)))

    @at_end
    def finish():
        unit_one, _ = unit_parts(rows_in[...])
        first_norm = unit_one * vectors[0:1] + vectors[1:2]
        unit, inverse = unit_parts(first_norm + (total[...] + vectors[2:3]))
        present = lax.broadcasted_iota(jnp.int32, (hidden.shape[0], 1), 0) < info[0]
        mask = jnp.where(present, 1.0, 0.0).astype(F32)
        mixed_out[...] = ((unit * vectors[3:4] + vectors[4:5]) * mask).astype(BF16)
        incoming = cotangent[...].astype(F32) * mask
        grad = norm_back(incoming, unit, inverse, vectors[3:4])
        second_out[...] = grad
        low = grad.astype(BF16)
        grad_out[...] = low
        sums_out[...] = eight_rows(
            column_sum(low.astype(F32)), column_sum(incoming * unit), column_sum(incoming)
        )


def down_back_kernel(grad_branch, weight, hidden, slope, pre_out, grads_out, bias_out):
    shards, piece, dim = grads_out.shape[1:]
    grad_rows = grad_branch[...]
    grad_pre = dot(grad_rows, weight[0].reshape(-1, dim), 1, 1) * slope[...]
    grad_pre = grad_pre.astype(BF16)
    pre_out[...] = grad_pre
    bias_out[0] = jnp.broadcast_to(column_sum(grad_pre.astype(F32)), bias_out.shape[1:])
    down = dot(hidden[...], grad_rows, 0, 0)
    grads_out[0] = down.astype(BF16).reshape(shards, piece, dim)


def up_back_kernel(last, normed, grad_pre, weight, *refs):
    if last:
        (info, normed_in, rows_in, second_in, context, vectors) = refs[:6]
        (grads_out, first_out, proj_out, sums_out, near_out, far_out, total, chunks) = refs[6:]
    else:
        (grads_out, total) = refs
    shards, piece, dim = grads_out.shape[1:]
    up = dot(grad_pre[...], normed[...], 0, 0)
    grads_out[0] = up.astype(BF16).reshape(shards, piece, dim)
    add_up(total, dot(grad_pre[...], weight[0].reshape(-1, dim)))

    if not last:
        return

    @at_end
    def finish():
        unit, inverse = unit_parts(rows_in[...])
        grad_normed = second_in[...] + (normed_in[...] + total[...])
        grad = norm_back(grad_normed, unit, inverse, vectors[0:1])
        first_out[...] = grad
        low = grad.astype(BF16)
        proj_out[...] = low
        sums_out[...] = eight_rows(
            column_sum(low.astype(F32)), column_sum(grad_normed * unit), column_sum(grad_normed)
        )
        low_t = low.T
        part = info[1]
        for q in range(shards):
            value = dot(low_t, context[q]).astype(BF16)
            chunks[...] = value.reshape(chunks.shape)
            for spot in range(PARTS // 2):
                near_out[spot, q] = chunks[part ^ (2 * spot)]
                far_out[spot, q] = chunks[part ^ (2 * spot + 1)]


def attend_back_kernel(
    heads,
    depth,
    first_shard,
    info_ref,
    tokens,
    partner,
    grad_proj,
    near,
    far,
    out_weight,
    qkv_in,
    stats_in,
    own_in,
    partner_in,
    own_out,
    partner_out,
    near_out,
    far_out,
    bias_out,
    weight_scratch,
    tokens_t,
    partner_t,
    chunks,
):
    step = pl.program_id(0)
    shard = step + first_shard
    info = Info(info_ref, heads, out_weight.shape[0])
    swaps = info.swaps(shard)
    rows, dim = tokens.shape
    width = heads * depth

    @pl.when(step == 0)
    def turn():
        tokens_t[...] = tokens[...].T
        partner_t[...] = partner[...].T

    fill_weight(info, near, far, weight_scratch)
    weight = weight_scratch[...].reshape(dim, 3 * width)
    grad = dot(grad_proj[...], out_weight[info.head_at ^ shard], 1, 1).astype(BF16)
    k, v, q = (qkv_in[0, :, i * width : (i + 1) * width] for i in range(3))
    stats = stats_in[0]
    key_index = lax.broadcasted_iota(jnp.int32, (rows, 1), 0)
    gq, gk, gv = [], [], []
    for j in range(heads):
        cut = slice(j * depth, (j + 1) * depth)
        live = jnp.where(swaps[j] == 1, info.partner_live, info.own_live)
        open_keys = key_index < live
        scores = dot(k[:, cut], q[:, cut], 1, 1)
        chances = jnp.exp(jnp.where(open_keys, scores - stats[j : j + 1, :], -10000.0))
        grad_mix = dot(v[:, cut], grad[:, cut], 1, 1)
        shared = column_sum(grad_mix * chances)
        grad_scores = (chances * (grad_mix - shared)).astype(BF16)
        gk.append(dot(grad_scores, q[:, cut]))
        gv.append(dot(chances.astype(BF16), grad[:, cut]))
        gq.append(dot(k[:, cut], grad_scores, 0, 0))
    grad_q = (jnp.concatenate(gq, axis=0).T * (depth**-0.5)).astype(BF16)
    grad_kv = jnp.concatenate(gk + gv, axis=1).astype(BF16)
    swapped = lane_pick(swaps + swaps, depth) == 1
    nothing = jnp.zeros((), BF16)
    grad_own = jnp.concatenate([jnp.where(swapped, nothing, grad_kv), grad_q], axis=1)
    grad_far = jnp.where(swapped, grad_kv, nothing)
    own = dot(grad_own, weight, 1, 1)
    other = dot(grad_far, weight[:, : 2 * width], 1, 1)

    @pl.when(step == 0)
    def first():
        own_out[...] = own if own_in is None else own_in[...] + own
        partner_out[...] = other if partner_in is None else partner_in[...] + other

    @pl.when(step > 0)
    def later():
        own_out[...] += own
        partner_out[...] += other

    grads = dot(tokens_t[...], grad_own)
    grads_kv = grads[:, : 2 * width] + dot(partner_t[...], grad_far)
    grads = jnp.concatenate([grads_kv, grads[:, 2 * width :]], axis=1).astype(BF16)
    chunks[...] = grads.reshape(chunks.shape)
    for spot in range(PARTS // 2):
        near_out[spot, 0] = chunks[info.part ^ (2 * spot)]
        far_out[spot, 0] = chunks[info.part ^ (2 * spot + 1)]
    bias_out[0] = jnp.broadcast_to(
        jnp.concatenate(
            [column_sum(grad_kv.astype(F32)), column_sum(grad_q.astype(F32))], axis=1
        ),
        bias_out.shape[1:],
    )


def fold_core_kernel(*refs):
    count = (len(refs) - 4) // 2
    mine, received, outs = refs[:count], refs[count : 2 * count], refs[2 * count :]
    for spot in range(4):
        parts = [a[spot, 0].astype(F32) + b[spot, 0].astype(F32) for a, b in zip(mine, received)]
        used = sum(part.shape[1] for part in parts)
        if used < outs[spot].shape[2]:
            parts.append(jnp.zeros((parts[0].shape[0], outs[spot].shape[2] - used), F32))
        value = jnp.concatenate(parts, axis=1) if len(parts) > 1 else parts[0]
        outs[spot][0] = value.astype(outs[spot].dtype)


def fold_chips_kernel(own, a, b, c, *outs):
    for q, out in enumerate(outs):
        value = own[q] + (a[q].astype(F32) + b[q].astype(F32)) + c[q].astype(F32)
        out[...] = value.astype(out.dtype)


def settle_down_kernel(info, near, far, out):
    for core, source in enumerate((near, far)):
        for spot in range(PARTS // 2):
            out[info[1] ^ (2 * spot + core)] = source[spot].astype(F32)


def settle_up_kernel(info, near, far, up_out, out_out, up_scratch, out_scratch):
    dim = up_out.shape[0]
    for core, source in enumerate((near, far)):
        for spot in range(PARTS // 2):
            place = info[1] ^ (2 * spot + core)
            value = source[spot].astype(F32)
            up_scratch[place] = value[:, :dim]
            out_scratch[place] = value[:, dim:]
    up_out[...] = up_scratch[...].reshape(-1, dim).T
    shards = out_out.shape[0]
    turned = out_scratch[...].reshape(-1, dim).T.reshape(shards, -1, dim)
    for q in range(shards):
        out_out[info[2] ^ q] = turned[q]


def settle_input_kernel(info, near, far, out):
    width = out.shape[3]
    for core, source in enumerate((near, far)):
        for spot in range(PARTS // 2):
            place = info[1] ^ (2 * spot + core)
            value = source[spot].astype(F32)
            for i in range(3):
                out[(i + 1) % 3, place] = value[:, i * width : (i + 1) * width]


def shape(dims, dtype):
    return jax.ShapeDtypeStruct(dims, dtype)


def whole(*dims):
    return pl.BlockSpec(dims, lambda *_: (0,) * len(dims))


SMEM = pl.BlockSpec(memory_space=pltpu.SMEM)


def attend(info, tokens, partner, near, far, bias, out_weight, vectors, heads, depth):
    rows, dim = tokens.shape
    spots, shards, piece, lanes = near.shape
    width = heads * depth
    weight_spec = pl.BlockSpec((spots, 1, piece, lanes), lambda s: (0, s, 0, 0))
    return pl.pallas_call(
        functools.partial(attend_kernel, heads, depth),
        grid=(shards,),
        in_specs=[
            SMEM,
            whole(rows, dim),
            whole(rows, dim),
            weight_spec,
            weight_spec,
            pl.BlockSpec((1, 8, lanes), lambda s: (s, 0, 0)),
            whole(shards, width, dim),
            whole(8, dim),
        ],
        out_specs=[
            pl.BlockSpec((1, rows, lanes), lambda s: (s, 0, 0)),
            pl.BlockSpec((1, rows, width), lambda s: (s, 0, 0)),
            pl.BlockSpec((1, 8, rows), lambda s: (s, 0, 0)),
            whole(rows, dim),
            whole(rows, dim),
        ],
        out_shape=[
            shape((shards, rows, lanes), BF16),
            shape((shards, rows, width), BF16),
            shape((shards, 8, rows), F32),
            shape((rows, dim), F32),
            shape((rows, dim), BF16),
        ],
        scratch_shapes=[pltpu.VMEM((PARTS, piece, lanes), BF16), pltpu.VMEM((rows, dim), F32)],
        compiler_params=PARAMS,
        cost_estimate=pl.CostEstimate(
            flops=12 * rows * dim * dim + 16 * rows * rows * dim,
            bytes_accessed=24 * rows * dim,
            transcendentals=shards * heads * rows * rows,
        ),
        name="attend",
    )(info, tokens, partner, near, far, bias, out_weight, vectors)


def cost(flops, moved, slow=0):
    return pl.CostEstimate(flops=flops, bytes_accessed=moved, transcendentals=slow)


def halves(weight):
    spots, shards, piece, dim = weight.shape
    return [
        pl.BlockSpec((1, shards, piece, dim), lambda s: (jnp.minimum(s, spots - 1), 0, 0, 0)),
        pl.BlockSpec((1, shards, piece, dim), lambda s: (jnp.maximum(s - spots, 0), 0, 0, 0)),
    ]


def feed_up(normed, near, far, bias):
    rows, dim = normed.shape
    spots, shards, piece, _ = near.shape
    tile = shards * piece
    steps = 2 * spots
    columns = pl.BlockSpec((rows, tile), lambda s: (0, s))
    return pl.pallas_call(
        feed_up_kernel,
        grid=(steps,),
        in_specs=[
            whole(rows, dim),
            *halves(near),
            pl.BlockSpec((1, 1, tile), lambda s: (s, 0, 0)),
        ],
        out_specs=[columns, columns],
        out_shape=[shape((rows, steps * tile), BF16), shape((rows, steps * tile), F32)],
        compiler_params=PARAMS,
        cost_estimate=cost(4 * rows * dim * tile * steps, 30 * rows * dim, rows * tile * steps),
        name="feed_up",
    )(normed, near, far, bias)


def feed_down(info, hidden, near, far, rows_one, cotangent, vectors):
    rows, dim = rows_one.shape
    spots, shards, piece, _ = near.shape
    tile = shards * piece
    steps = 2 * spots
    return pl.pallas_call(
        feed_down_kernel,
        grid=(steps,),
        in_specs=[
            SMEM,
            pl.BlockSpec((rows, tile), lambda s: (0, s)),
            *halves(near),
            whole(rows, dim),
            whole(rows, dim),
            whole(8, dim),
        ],
        out_specs=[whole(rows, dim)] * 3 + [whole(8, dim)],
        out_shape=[
            shape((rows, dim), BF16),
            shape((rows, dim), F32),
            shape((rows, dim), BF16),
            shape((8, dim), F32),
        ],
        scratch_shapes=[pltpu.VMEM((rows, dim), F32)],
        compiler_params=PARAMS,
        cost_estimate=cost(4 * rows * dim * tile * steps, 30 * rows * dim),
        name="feed_down",
    )(info, hidden, near, far, rows_one, cotangent, vectors)


def down_back(half, grad_branch, weight, hidden, slope):
    rows, dim = grad_branch.shape
    spots, shards, piece, _ = weight.shape
    tile = shards * piece
    weight_spec = pl.BlockSpec((1, shards, piece, dim), lambda s: (s, 0, 0, 0))
    columns = pl.BlockSpec((rows, tile), lambda s: (0, s + half * spots))
    return pl.pallas_call(
        down_back_kernel,
        grid=(spots,),
        in_specs=[whole(rows, dim), weight_spec, columns, columns],
        out_specs=[
            pl.BlockSpec((rows, tile), lambda s: (0, s)),
            weight_spec,
            pl.BlockSpec((1, 8, tile), lambda s: (s, 0, 0)),
        ],
        out_shape=[
            shape((rows, spots * tile), BF16),
            shape(weight.shape, BF16),
            shape((spots, 8, tile), F32),
        ],
        compiler_params=PARAMS,
        cost_estimate=cost(4 * rows * dim * tile * spots, 30 * rows * dim),
        name="down_back",
    )(grad_branch, weight, hidden, slope)


def up_back(last, normed, grad_pre, weight, *extra):
    rows, dim = normed.shape
    spots, shards, piece, _ = weight.shape
    tile = shards * piece
    weight_spec = pl.BlockSpec((1, shards, piece, dim), lambda s: (s, 0, 0, 0))
    in_specs = [whole(rows, dim), pl.BlockSpec((rows, tile), lambda s: (0, s)), weight_spec]
    out_specs = [weight_spec]
    out_shape = [shape(weight.shape, BF16)]
    scratch = []
    if last:
        width = extra[4].shape[2]
        in_specs += [SMEM] + [whole(rows, dim)] * 3 + [whole(shards, rows, width), whole(8, dim)]
        out_specs += [whole(rows, dim)] * 2 + [whole(8, dim)]
        out_specs += [whole(spots, shards, piece, width)] * 2
        out_shape += [
            shape((rows, dim), F32),
            shape((rows, dim), BF16),
            shape((8, dim), F32),
            shape((spots, shards, piece, width), BF16),
            shape((spots, shards, piece, width), BF16),
        ]
        scratch = [pltpu.VMEM((rows, dim), F32), pltpu.VMEM((PARTS, piece, width), BF16)]
    else:
        out_specs.append(whole(rows, dim))
        out_shape.append(shape((rows, dim), F32))
    return pl.pallas_call(
        functools.partial(up_back_kernel, last),
        grid=(spots,),
        in_specs=in_specs,
        out_specs=out_specs,
        out_shape=out_shape,
        scratch_shapes=scratch,
        compiler_params=PARAMS,
        cost_estimate=cost(4 * rows * dim * tile * spots, 30 * rows * dim),
        name="up_back",
    )(normed, grad_pre, weight, *extra)


def attend_back(
    info,
    tokens,
    partner,
    grad_proj,
    near,
    far,
    out_weight,
    qkv,
    stats,
    heads,
    depth,
    first_shard,
    count,
    carried,
):
    rows, dim = tokens.shape
    spots, shards, piece, lanes = near.shape
    width = heads * depth
    weight_in = pl.BlockSpec((spots, 1, piece, lanes), lambda s: (0, s + first_shard, 0, 0))
    weight_out = pl.BlockSpec((spots, 1, piece, lanes), lambda s: (0, s, 0, 0))
    kernel = functools.partial(attend_back_kernel, heads, depth, first_shard)
    if not carried:
        bare = kernel

        def kernel(*refs):
            bare(*refs[:9], None, None, *refs[9:])

    return pl.pallas_call(
        kernel,
        grid=(count,),
        in_specs=[
            SMEM,
            whole(rows, dim),
            whole(rows, dim),
            whole(rows, dim),
            weight_in,
            weight_in,
            whole(shards, width, dim),
            pl.BlockSpec((1, rows, lanes), lambda s: (s + first_shard, 0, 0)),
            pl.BlockSpec((1, 8, rows), lambda s: (s + first_shard, 0, 0)),
        ]
        + [whole(rows, dim)] * len(carried),
        out_specs=[
            whole(rows, dim),
            whole(rows, dim),
            weight_out,
            weight_out,
            pl.BlockSpec((1, 8, lanes), lambda s: (s, 0, 0)),
        ],
        out_shape=[
            shape((rows, dim), F32),
            shape((rows, dim), F32),
            shape((spots, count, piece, lanes), BF16),
            shape((spots, count, piece, lanes), BF16),
            shape((count, 8, lanes), F32),
        ],
        scratch_shapes=[
            pltpu.VMEM((PARTS, piece, lanes), BF16),
            pltpu.VMEM((dim, rows), BF16),
            pltpu.VMEM((dim, rows), BF16),
            pltpu.VMEM((PARTS, piece, lanes), BF16),
        ],
        compiler_params=PARAMS,
        cost_estimate=cost(
            count * (6 * rows * dim * dim + 10 * rows * rows * dim),
            count * 8 * rows * dim,
            count * heads * rows * rows,
        ),
        name="attend_back",
    )(info, tokens, partner, grad_proj, near, far, out_weight, qkv, stats, *carried)


def fold_core(mine, received, lanes):
    spots, shards, piece = mine[0].shape[:3]
    specs = [
        pl.BlockSpec((spots, 1, piece, a.shape[3]), lambda s: (0, s, 0, 0))
        for a in mine + received
    ]
    return pl.pallas_call(
        fold_core_kernel,
        grid=(shards,),
        in_specs=specs,
        out_specs=[pl.BlockSpec((1, piece, lanes), lambda s: (s, 0, 0))] * spots,
        out_shape=[shape((shards, piece, lanes), F32)]
        + [shape((shards, piece, lanes), BF16)] * (spots - 1),
        compiler_params=PARAMS,
        cost_estimate=pl.CostEstimate(
            flops=spots * shards * piece * lanes,
            bytes_accessed=8 * spots * shards * piece * lanes,
            transcendentals=0,
        ),
        name="fold_core",
    )(*mine, *received)


def fold_chips(own, received, first_stays=True):
    shards, piece, lanes = own.shape
    cut = 256 if lanes % 256 == 0 else lanes
    spec = pl.BlockSpec((shards, piece, cut), lambda s: (0, 0, s))
    stays = F32 if first_stays else BF16
    return pl.pallas_call(
        fold_chips_kernel,
        grid=(lanes // cut,),
        in_specs=[spec] * 4,
        out_specs=[pl.BlockSpec((piece, cut), lambda s: (0, s))] * shards,
        out_shape=[shape((piece, lanes), stays)] + [shape((piece, lanes), BF16)] * (shards - 1),
        compiler_params=PARAMS,
        cost_estimate=cost(4 * shards * piece * lanes, 12 * shards * piece * lanes),
        name="fold_chips",
    )(own, *received)


class Mover:
    def __init__(self, batch_size, shards):
        self.batch_size, self.shards = batch_size, shards

    def batch(self, value, mask):
        return lax.ppermute(value, "batch", [(i, i ^ mask) for i in range(self.batch_size)])

    def head(self, value, mask):
        return lax.ppermute(value, "head", [(i, i ^ mask) for i in range(self.shards)])

    def chips(self, values):
        masks = (NEAR_X, NEAR_Y, NEAR_X | NEAR_Y)
        return [self.batch(value, mask) for value, mask in zip(values, masks)]

    def around(self, value):
        return self.chips([value] * 3)

    def along(self, values):
        return [self.head(value, q) for q, value in enumerate(values, 1)]

    def column(self, piece):
        return [piece] + self.along([piece] * (self.shards - 1))

    def plane(self, column):
        return [column] + self.around(column)

    def settle(self, total):
        total = total.astype(BF16)
        mask = PARTS
        while mask < self.batch_size:
            total = (total.astype(F32) + self.batch(total, mask).astype(F32)).astype(BF16)
            mask *= 2
        return total

    def total(self, value):
        mask = 1
        while mask < self.batch_size:
            value = value + self.batch(value, mask)
            mask *= 2
        mask = 1
        while mask < self.shards:
            value = value + self.head(value, mask)
            mask *= 2
        return value


def after(value, *events):
    return lax.optimization_barrier((value, *events))[0]


def all_after(values, *events):
    return lax.optimization_barrier((*values, *events))[: len(values)]


def exchange_bits(value, axes):
    for axis, bit in axes:
        value = jnp.where(bit == 1, jnp.flip(value, axis), value)
    return value


def stack8(*rows):
    rows = [row.reshape(1, -1) for row in rows]
    return jnp.concatenate(rows + [jnp.zeros((8 - len(rows), rows[0].shape[1]), F32)], axis=0)


def local(
    batch_size,
    shards,
    tokens,
    lengths,
    block_swap,
    input_weight,
    input_bias,
    out_weight,
    out_bias,
    gain_one,
    shift_one,
    up_weight,
    up_bias,
    down_weight,
    down_bias,
    gain_two,
    shift_two,
    cotangent,
):
    move = Mover(batch_size, shards)
    heads = block_swap.shape[0]
    rows, dim = tokens.shape
    width = input_weight.shape[2]
    depth = width // heads
    hidden_own = up_weight.shape[1]
    piece = dim // PARTS
    batch_at, head_at = lax.axis_index("batch"), lax.axis_index("head")
    part = batch_at % PARTS
    part_bits = [(part >> i) & 1 for i in range(3)]
    head_bits = [(head_at >> i) & 1 for i in range(2)]
    blocks = SEQ_LEN // rows
    length = lax.dynamic_index_in_dim(lengths, head_at // blocks, 0, keepdims=False)
    block_at = head_at % blocks
    own_live = jnp.clip(length - block_at * rows, 0, rows)
    partner_live = jnp.clip(length - (blocks - 1 - block_at) * rows, 0, rows)

    input_piece = lax.dynamic_slice_in_dim(input_weight, part * piece, piece, 1)
    input_piece = jnp.concatenate([input_piece[1], input_piece[2], input_piece[0]], axis=1)
    small = jnp.concatenate([input_bias.reshape(-1), block_swap.astype(F32)])
    small = jnp.stack(move.column(small))
    input_column = move.column(input_piece)
    input_plane = move.plane(jnp.stack(input_column))
    up_piece = lax.dynamic_slice_in_dim(up_weight, part * piece, piece, 1).T
    down_piece = lax.dynamic_slice_in_dim(down_weight, part * piece, piece, 0)
    up_column = move.column(after(up_piece, *input_column))
    partner = move.head(after(tokens, *up_column), 1)
    input_near = jnp.stack(all_after(input_plane, *up_column))
    input_far = move.batch(input_near, CORE)
    up_plane = move.plane(after(jnp.stack(up_column), input_near))
    down_column = move.column(after(down_piece, partner))

    info = jnp.concatenate(
        [
            small[:, 2 * width :].reshape(-1).astype(jnp.int32),
            jnp.stack([own_live, partner_live, part, head_at]).astype(jnp.int32),
        ]
    )
    short_info = jnp.stack([own_live, part, head_at]).astype(jnp.int32)
    bias = jnp.concatenate(
        [jnp.zeros((shards, width), F32), small[:, width : 2 * width], small[:, :width]], axis=1
    )
    bias = jnp.broadcast_to(bias[:, None], (shards, 8, 3 * width))
    bits = [(0, head_bits[1]), (1, head_bits[0])]
    bits += [(2, part_bits[2]), (3, part_bits[1]), (4, part_bits[0])]
    up_bias_rel = exchange_bits(up_bias.reshape(2, 2, 2, 2, 2, piece), bits)
    up_bias_rel = up_bias_rel.transpose(4, 2, 3, 0, 1, 5).reshape(PARTS, 1, shards * piece)
    out_parts = out_weight.reshape(shards, width, dim)

    vectors_one = stack8(out_bias, gain_one, shift_one)
    vectors_two = stack8(gain_one, shift_one, down_bias, gain_two, shift_two)
    vectors_back = stack8(gain_one)
    qkv, context, stats, rows_one, normed = attend(
        info,
        after(tokens, up_bias_rel, vectors_two, vectors_back),
        partner,
        input_near,
        input_far,
        bias,
        out_parts,
        vectors_one,
        heads,
        depth,
    )
    down_plane = move.plane(jnp.stack(all_after(down_column, normed)))
    up_near = jnp.stack(all_after(up_plane, normed))
    up_far = move.batch(up_near, CORE)
    hidden, slope = feed_up(normed, up_near, up_far, up_bias_rel)
    down_near = jnp.stack(all_after(down_plane, hidden))
    down_far = move.batch(down_near, CORE)
    mixed_out, grad_second, grad_branch, sums_two = feed_down(
        short_info,
        hidden,
        down_near,
        down_far,
        rows_one,
        cotangent,
        vectors_two,
    )

    pre_far, down_grads_far, up_bias_far = down_back(1, grad_branch, down_far, hidden, slope)
    down_received = move.batch(down_grads_far, CORE)
    pre_near, down_grads_near, up_bias_near = down_back(
        0, after(grad_branch, pre_far), down_near, hidden, slope
    )
    down_own, *down_send = fold_core([down_grads_near], [down_received], dim)
    down_chips = move.chips(down_send)
    up_grads_far, grad_normed = up_back(False, after(normed, *down_send), pre_far, up_far)
    up_received = move.batch(up_grads_far, CORE)
    up_grads_near, grad_first, grad_proj, sums_one, out_grads_near, out_grads_far = up_back(
        True,
        normed,
        pre_near,
        up_near,
        short_info,
        grad_normed,
        rows_one,
        grad_second,
        context,
        vectors_back,
    )
    out_received = move.batch(out_grads_far, CORE)
    lanes = -(-(dim + width) // 256) * 256
    up_own, *up_send = fold_core(
        [up_grads_near, out_grads_near], [up_received, out_received], lanes
    )
    up_chips = move.chips(up_send)

    def back(grad, first_shard, count, carried):
        return attend_back(
            info,
            tokens,
            partner,
            grad,
            input_near,
            input_far,
            out_parts,
            qkv,
            stats,
            heads,
            depth,
            first_shard,
            count,
            carried,
        )

    up_bias_grad = jnp.stack([up_bias_near[:, 0], up_bias_far[:, 0]])
    up_bias_grad = up_bias_grad.reshape(2, 2, 2, 2, 2, piece).transpose(3, 4, 1, 2, 0, 5)
    up_bias_grad = exchange_bits(up_bias_grad, bits).reshape(-1, dim)
    vectors_now = jnp.concatenate([sums_one[:3], sums_two[:3], up_bias_grad])
    late_grad, vectors_now = all_after((grad_proj, vectors_now), *up_send)
    own_rows, partner_rows, late_near, late_far, late_sums = back(
        late_grad, shards // 2, shards // 2, []
    )
    late_received = move.batch(late_far, CORE)
    down_sums = fold_chips(after(down_own, late_sums), down_chips)
    down_along = move.along(down_sums[1:])
    late_own, *late_send = fold_core([late_near], [late_received], 3 * width)
    late_chips = move.chips(late_send)
    own_rows, partner_rows, early_near, early_far, early_sums = back(
        after(grad_proj, *down_sums, *late_send), 0, shards // 2, [own_rows, partner_rows]
    )
    early_received = move.batch(early_far, CORE)
    from_partner = move.head(partner_rows.astype(BF16), 1)

    def sum_of(first, values):
        for value in values:
            first = first + value.astype(F32)
        return move.settle(first)

    up_sums = fold_chips(after(up_own, early_sums), up_chips)
    up_along = move.along(up_sums[1:])
    early_own, *early_send = fold_core(
        [early_near], [after(early_received, *up_sums)], 3 * width
    )
    early_chips = move.chips(early_send)
    down_total = sum_of(after(down_sums[0], early_own), down_along)
    down_done = move.plane(down_total)
    late_sums_chips = fold_chips(after(late_own, down_total), late_chips, False)
    late_along = [move.head(v, q) for q, v in enumerate(late_sums_chips, shards // 2)]
    up_total = sum_of(after(up_sums[0], *late_sums_chips), up_along)
    out_total = move.column(up_total[:, dim : dim + width])
    early_sums_chips = fold_chips(after(early_own, up_total), early_chips)
    early_along = move.along(early_sums_chips[1:])
    up_total = jnp.concatenate([up_total[:, :dim], *out_total], axis=1)
    up_done = move.plane(up_total)
    input_total = sum_of(early_sums_chips[0], early_along + late_along)
    input_done = move.plane(input_total)
    down_done = jnp.stack(down_done)
    up_done = jnp.stack(up_done)
    input_done = jnp.stack(input_done)
    down_done = (down_done, move.batch(down_done, CORE))
    up_done = (up_done, move.batch(up_done, CORE))
    input_done = (input_done, move.batch(input_done, CORE))
    grad_tokens = grad_first + own_rows + from_partner.astype(F32)
    bias_sums = jnp.concatenate([early_sums, late_sums])

    bias_sums = exchange_bits(bias_sums[:, 0].reshape(2, 2, 3, width), bits[:2])
    bias_sums = bias_sums.reshape(shards, 3, width).transpose(1, 0, 2).reshape(3, dim)
    vectors = move.total(jnp.concatenate([vectors_now, bias_sums[2:], bias_sums[1:2]]))
    grad_input_bias = lax.dynamic_slice_in_dim(vectors[10:12], head_at * width, width, 1)
    grad_up_bias = lax.dynamic_slice_in_dim(
        vectors[6:10].reshape(-1), head_at * hidden_own, hidden_own
    )

    grad_down = pl.pallas_call(
        settle_down_kernel,
        in_specs=[SMEM] + [whole(4, piece, dim)] * 2,
        out_shape=shape((PARTS, piece, dim), F32),
        compiler_params=PARAMS,
        name="settle_down",
    )(short_info, *down_done)
    grad_up, grad_out = pl.pallas_call(
        settle_up_kernel,
        in_specs=[SMEM] + [whole(4, piece, dim + shards * width)] * 2,
        out_shape=[shape((dim, hidden_own), F32), shape((shards, width, dim), F32)],
        scratch_shapes=[pltpu.VMEM((PARTS, piece, dim), F32)] * 2,
        compiler_params=PARAMS,
        name="settle_up",
    )(short_info, *up_done)
    grad_input_weight = pl.pallas_call(
        settle_input_kernel,
        in_specs=[SMEM] + [whole(4, piece, 3 * width)] * 2,
        out_shape=shape((3, PARTS, piece, width), F32),
        compiler_params=PARAMS,
        name="settle_input",
    )(short_info, *input_done)
    return (
        mixed_out,
        grad_tokens,
        grad_input_weight.reshape(3, dim, width),
        grad_input_bias,
        grad_out.reshape(dim, dim),
        vectors[0],
        vectors[1],
        vectors[2],
        grad_up,
        grad_up_bias,
        grad_down.reshape(hidden_own, dim),
        vectors[3],
        vectors[4],
        vectors[5],
    )


def solution(mesh):
    rows_spec = P(("batch", "head"), None)
    placed = (
        rows_spec,
        P("batch"),
        P("head"),
        P(None, None, "head"),
        P(None, "head"),
        P(),
        P(),
        P(),
        P(),
        P(None, "head"),
        P(),
        P("head", None),
        P(),
        P(),
        P(),
        rows_spec,
    )
    return jax.shard_map(
        functools.partial(local, mesh.shape["batch"], mesh.shape["head"]),
        mesh=mesh,
        in_specs=placed,
        out_specs=(
            rows_spec,
            rows_spec,
            P(None, None, "head"),
            P(None, "head"),
            P(),
            P(),
            P(),
            P(),
            P(None, "head"),
            P("head"),
            P("head", None),
            P(),
            P(),
            P(),
        ),
        check_vma=False,
    )
```

```python
import functools

import jax
import jax.numpy as jnp
from jax import lax
from jax.experimental import pallas as pl
from jax.experimental.pallas import tpu as pltpu
from jax.sharding import PartitionSpec as P

SEQ_LEN = 1024
EPSILON = 1e-05
F32 = jnp.float32
BF16 = jnp.bfloat16
VMEM_LIMIT = 56 * 1024 * 1024
PARAMS = pltpu.CompilerParams(vmem_limit_bytes=VMEM_LIMIT)
CORE = 1
PARTS = 8
SPOTS = 4


def dot(left_side, right_side, left_dim=1, right_dim=0):
    return lax.dot_general(
        left_side,
        right_side,
        (((left_dim,), (right_dim,)), ((), ())),
        preferred_element_type=F32,
    )


def unit_parts(values):
    centred = values - jnp.mean(values, axis=-1, keepdims=True)
    inverse = lax.rsqrt(jnp.mean(centred * centred, axis=-1, keepdims=True) + EPSILON)
    return centred * inverse, inverse


def norm_back(grad_rows, unit_rows, inverse, gain_row):
    scaled = grad_rows * gain_row
    return inverse * (
        scaled
        - jnp.mean(scaled, axis=-1, keepdims=True)
        - unit_rows * jnp.mean(scaled * unit_rows, axis=-1, keepdims=True)
    )


def column_sum(values):
    return jnp.sum(values, axis=0, keepdims=True)


def gelu_parts(inner):
    bell = jnp.exp(inner * inner * -0.5)
    t = 1.0 / (1.0 + jnp.abs(inner) * (0.3275911 * 0.5**0.5))
    poly = t * (
        0.254829592
        + t * (-0.284496736 + t * (1.421413741 + t * (-1.453152027 + t * 1.061405429)))
    )
    tail = 0.5 * poly * bell
    below = jnp.where(inner < 0.0, tail, 1.0 - tail)
    return inner * below, below + inner * bell * 0.3989422804014327


def lane_pick(values, depth):
    lane = lax.broadcasted_iota(jnp.int32, (1, len(values) * depth), 1)
    picked = jnp.full(lane.shape, values[0], jnp.int32)
    for j in range(1, len(values)):
        picked = jnp.where(lane >= j * depth, values[j], picked)
    return picked


def place_of(part, half, spot):
    seen = part ^ half
    core = seen & 1
    low, high = 2 + 2 * core, 4 - 2 * core
    return seen ^ (low * (spot & 1) + high * (spot >> 1))


class Info:
    def __init__(self, ref, heads, shards):
        self.ref, self.heads, self.base = ref, heads, heads * shards

    def swaps(self, shard):
        return [self.ref[shard * self.heads + j] for j in range(self.heads)]

    own_live = property(lambda self: self.ref[self.base])
    partner_live = property(lambda self: self.ref[self.base + 1])
    part = property(lambda self: self.ref[self.base + 2])
    head_at = property(lambda self: self.ref[self.base + 3])


def gathered(part, near, far, scratch):
    for spot in range(SPOTS):
        scratch[place_of(part, 0, spot)] = near[spot, 0]
        scratch[place_of(part, 1, spot)] = far[spot, 0]
    return scratch[...].reshape(-1, scratch.shape[2])


def attend_kernel(setting, info_ref, tokens, partner, bias, out_weight, vectors, *refs):
    heads, depth, first_shard, last = setting
    refs = list(refs)
    if first_shard == 0:
        weight = refs.pop(0)[...]
        total_in = None
    else:
        near, far, total_in = refs[:3]
        del refs[:3]
    qkv_out, context_out, stats_out = refs[:3]
    step = pl.program_id(0)
    shard = first_shard + step
    info = Info(info_ref, heads, out_weight.shape[0])
    if first_shard:
        weight = gathered(info.part, near, far, refs.pop())
    total = refs.pop()
    swaps = info.swaps(shard)
    rows, dim = tokens.shape
    width = heads * depth
    own = dot(tokens[...], weight) + bias[0, 0:1]
    other = dot(partner[...], weight[:, : 2 * width]) + bias[0, 0:1, : 2 * width]
    swapped = lane_pick(swaps + swaps, depth) == 1
    kv = jnp.where(swapped, other, own[:, : 2 * width]).astype(BF16)
    q = own[:, 2 * width :].astype(BF16) * (depth**-0.5)
    qkv_out[0, :, : 2 * width] = kv
    qkv_out[0, :, 2 * width :] = q
    key_index = lax.broadcasted_iota(jnp.int32, (rows, 1), 0)
    stats = []
    pieces = []
    for j in range(heads):
        cut = slice(j * depth, (j + 1) * depth)
        live = jnp.where(swaps[j] == 1, info.partner_live, info.own_live)
        open_keys = key_index < live
        anyone = jnp.where(live > 0, 1.0, 0.0).astype(F32)
        scores = dot(kv[:, cut], q[:, cut], 1, 1)
        largest = jnp.max(jnp.where(open_keys, scores, -1e30), axis=0, keepdims=True)
        largest = jnp.where(anyone > 0.5, largest, 0.0)
        weights = jnp.exp(jnp.where(open_keys, scores - largest, -10000.0))
        totals = column_sum(weights) + (1.0 - anyone)
        mixing = (weights * (1.0 / totals)).astype(BF16)
        stats.append(largest + jnp.log(totals))
        pieces.append(dot(kv[:, width + j * depth : width + (j + 1) * depth], mixing, 0, 0))
    context = jnp.concatenate(pieces, axis=0).T.astype(BF16)
    context_out[0] = context
    stats_out[0] = jnp.concatenate(stats + [jnp.zeros((8 - heads, rows), F32)], axis=0)
    projected = dot(context, out_weight[info.head_at ^ shard])

    @pl.when(step == 0)
    def first():
        total[...] = projected if total_in is None else total_in[...] + projected

    @pl.when(step > 0)
    def later():
        total[...] += projected

    if not last:
        return

    rows_out, normed_out = refs[3:]

    @at_end
    def finish():
        values = tokens[...].astype(F32) + (total[...] + vectors[0:1])
        rows_out[...] = values
        unit, _ = unit_parts(values)
        normed_out[...] = (unit * vectors[1:2] + vectors[2:3]).astype(BF16)


def tile_of(own, near, far, shard, half):
    mine = jnp.concatenate([ref[0] for ref in own], axis=0)
    other = jnp.where(half == 0, near[:, 0], far[:, 0]).reshape(mine.shape)
    return jnp.where(shard == 0, mine, other)


def add_up(total, partial):
    first = (pl.program_id(0) == 0) & (pl.program_id(1) == 0)

    @pl.when(first)
    def start():
        total[...] = partial

    @pl.when(jnp.logical_not(first))
    def later():
        total[...] += partial


def at_end(run):
    pl.when(pl.program_id(0) == pl.num_programs(0) - 1)(run)


def at_both_ends(run):
    here = (pl.program_id(0) == pl.num_programs(0) - 1) & (
        pl.program_id(1) == pl.num_programs(1) - 1
    )
    pl.when(here)(run)


def eight_rows(*rows):
    width = rows[0].shape[1]
    return jnp.concatenate([*rows, jnp.zeros((8 - len(rows), width), F32)], axis=0)


def feed_up_kernel(info, normed, a, b, c, d, near, far, bias, *outs):
    shard, half = pl.program_id(0), pl.program_id(1)
    tile = tile_of((a, b, c, d), near, far, shard, half)
    pre = dot(normed[...], tile, 1, 1) + bias[0, 0]
    hidden, slope = gelu_parts(pre)
    for side in range(2):

        @pl.when(half == side)
        def keep():
            outs[side][...] = hidden.astype(BF16)
            outs[side + 2][...] = slope


def feed_down_kernel(
    info,
    near_hidden,
    far_hidden,
    a,
    b,
    c,
    d,
    near,
    far,
    rows_in,
    cotangent,
    vectors,
    mixed_out,
    second_out,
    grad_out,
    sums_out,
    total,
):
    shard, half = pl.program_id(0), pl.program_id(1)
    tile = tile_of((a, b, c, d), near, far, shard, half)
    hidden = jnp.where(half == 0, near_hidden[...], far_hidden[...])
    add_up(total, dot(hidden, tile))

    @at_both_ends
    def finish():
        unit_one, _ = unit_parts(rows_in[...])
        first_norm = unit_one * vectors[0:1] + vectors[1:2]
        unit, inverse = unit_parts(first_norm + (total[...] + vectors[2:3]))
        present = lax.broadcasted_iota(jnp.int32, (rows_in.shape[0], 1), 0) < info[0]
        mask = jnp.where(present, 1.0, 0.0).astype(F32)
        mixed_out[...] = ((unit * vectors[3:4] + vectors[4:5]) * mask).astype(BF16)
        incoming = cotangent[...].astype(F32) * mask
        grad = norm_back(incoming, unit, inverse, vectors[3:4])
        second_out[...] = grad
        low = grad.astype(BF16)
        grad_out[...] = low
        sums_out[...] = eight_rows(
            column_sum(low.astype(F32)), column_sum(incoming * unit), column_sum(incoming)
        )


def grad_pre_kernel(
    info, grad_branch, a, b, c, d, near, far, near_slope, far_slope, near_out, far_out, bias_out
):
    half, shard = 1 - pl.program_id(0), pl.program_id(1)
    tile = tile_of((a, b, c, d), near, far, shard, half)
    slope = jnp.where(half == 0, near_slope[...], far_slope[...])
    grad_pre = (dot(grad_branch[...], tile, 1, 1) * slope).astype(BF16)
    bias_out[0, 0] = jnp.broadcast_to(column_sum(grad_pre.astype(F32)), bias_out.shape[2:])
    for side, out in enumerate((near_out, far_out)):

        @pl.when(half == side)
        def keep():
            out[...] = grad_pre


def row_grads_kernel(with_more, mine, theirs, my_rows, their_rows, *refs):
    if with_more:
        (more, more_received, keep_out, send_out) = refs
    else:
        (keep_out, send_out) = refs
    value = dot(mine[...], my_rows[...], 0, 0) + dot(theirs[...], their_rows[...], 0, 0)
    dim = value.shape[1]
    value = value.reshape(SPOTS, -1, dim)
    for spot in range(SPOTS):
        out = (keep_out, send_out)[spot & 1]
        out[spot >> 1, 0, :, :dim] = value[spot].astype(out.dtype)
        if with_more:
            extra = more[spot, 0].astype(F32) + more_received[spot, 0].astype(F32)
            pad = jnp.zeros((extra.shape[0], out.shape[3] - dim - extra.shape[1]), F32)
            extra = jnp.concatenate([extra, pad], axis=1)
            out[spot >> 1, 0, :, dim:] = extra.astype(out.dtype)


def up_back_kernel(
    info,
    near_pre,
    far_pre,
    a,
    b,
    c,
    d,
    near,
    far,
    rows_in,
    second_in,
    vectors,
    first_out,
    proj_out,
    sums_out,
    total,
):
    half, shard = pl.program_id(0), pl.program_id(1)
    tile = tile_of((a, b, c, d), near, far, shard, half)
    grad_pre = jnp.where(half == 0, near_pre[...], far_pre[...])
    add_up(total, dot(grad_pre, tile))

    @at_both_ends
    def finish():
        unit, inverse = unit_parts(rows_in[...])
        grad_normed = second_in[...] + total[...]
        grad = norm_back(grad_normed, unit, inverse, vectors[0:1])
        first_out[...] = grad
        low = grad.astype(BF16)
        proj_out[...] = low
        sums_out[...] = eight_rows(
            column_sum(low.astype(F32)), column_sum(grad_normed * unit), column_sum(grad_normed)
        )


def scatter_parts(part, value, chunks, near_out, far_out):
    chunks[...] = value.reshape(chunks.shape)
    for spot in range(SPOTS):
        near_out[spot, 0] = chunks[place_of(part, 0, spot)]
        far_out[spot, 0] = chunks[place_of(part, 1, spot)]


def out_back_kernel(info, grad_proj, context, near_out, far_out, turned, chunks):
    @pl.when(pl.program_id(0) == 0)
    def turn():
        turned[...] = grad_proj[...].T

    value = dot(turned[...], context[0]).astype(BF16)
    scatter_parts(info[1], value, chunks, near_out, far_out)


def attend_back_kernel(setting, info_ref, tokens_t, partner_t, grad_proj, out_weight, *refs):
    heads, depth, first_shard, carried = setting
    refs = list(refs)
    if first_shard == 0:
        weight = refs.pop(0)[...]
    else:
        near, far = refs[:2]
        del refs[:2]
    qkv_in, stats_in = refs[:2]
    del refs[:2]
    own_in = partner_in = None
    if carried:
        own_in, partner_in = refs[:2]
        del refs[:2]
    own_out, partner_out, near_out, far_out, bias_out, chunks = refs[:6]
    step = pl.program_id(0)
    shard = step + first_shard
    info = Info(info_ref, heads, out_weight.shape[0])
    if first_shard:
        weight = gathered(info.part, near, far, refs[6])
    swaps = info.swaps(shard)
    dim, rows = tokens_t.shape
    width = heads * depth
    grad = dot(grad_proj[...], out_weight[info.head_at ^ shard], 1, 1).astype(BF16)
    k, v, q = (qkv_in[0, :, i * width : (i + 1) * width] for i in range(3))
    stats = stats_in[0]
    key_index = lax.broadcasted_iota(jnp.int32, (rows, 1), 0)
    gq, gk, gv = [], [], []
    for j in range(heads):
        cut = slice(j * depth, (j + 1) * depth)
        live = jnp.where(swaps[j] == 1, info.partner_live, info.own_live)
        open_keys = key_index < live
        scores = dot(k[:, cut], q[:, cut], 1, 1)
        chances = jnp.exp(jnp.where(open_keys, scores - stats[j : j + 1, :], -10000.0))
        grad_mix = dot(v[:, cut], grad[:, cut], 1, 1)
        shared = column_sum(grad_mix * chances)
        grad_scores = (chances * (grad_mix - shared)).astype(BF16)
        gk.append(dot(grad_scores, q[:, cut]))
        gv.append(dot(chances.astype(BF16), grad[:, cut]))
        gq.append(dot(k[:, cut], grad_scores, 0, 0))
    grad_q = (jnp.concatenate(gq, axis=0).T * (depth**-0.5)).astype(BF16)
    grad_kv = jnp.concatenate(gk + gv, axis=1).astype(BF16)
    swapped = lane_pick(swaps + swaps, depth) == 1
    nothing = jnp.zeros((), BF16)
    grad_own = jnp.concatenate([jnp.where(swapped, nothing, grad_kv), grad_q], axis=1)
    grad_far = jnp.where(swapped, grad_kv, nothing)
    own = dot(grad_own, weight, 1, 1)
    other = dot(grad_far, weight[:, : 2 * width], 1, 1)

    @pl.when(step == 0)
    def first():
        own_out[...] = own if own_in is None else own_in[...] + own
        partner_out[...] = other if partner_in is None else partner_in[...] + other

    @pl.when(step > 0)
    def later():
        own_out[...] += own
        partner_out[...] += other

    grads = dot(tokens_t[...], grad_own)
    grads_kv = grads[:, : 2 * width] + dot(partner_t[...], grad_far)
    grads = jnp.concatenate([grads_kv, grads[:, 2 * width :]], axis=1).astype(BF16)
    scatter_parts(info.part, grads, chunks, near_out.at[:], far_out.at[:])
    bias_out[0] = jnp.broadcast_to(
        jnp.concatenate(
            [column_sum(grad_kv.astype(F32)), column_sum(grad_q.astype(F32))], axis=1
        ),
        bias_out.shape[1:],
    )


def settle_down_kernel(info, near, far, out):
    for half, source in enumerate((near, far)):
        for spot in range(SPOTS):
            out[place_of(info[1], half, spot)] = source[spot].astype(F32)


def settle_up_kernel(info, near, far, up_out, out_out, up_scratch, out_scratch):
    dim = up_out.shape[0]
    for half, source in enumerate((near, far)):
        for spot in range(SPOTS):
            place = place_of(info[1], half, spot)
            value = source[spot].astype(F32)
            up_scratch[place] = value[:, :dim]
            out_scratch[place] = value[:, dim:]
    up_out[...] = up_scratch[...].reshape(-1, dim).T
    shards = out_out.shape[0]
    turned = out_scratch[...].reshape(-1, dim).T.reshape(shards, -1, dim)
    for q in range(shards):
        out_out[info[2] ^ q] = turned[q]


def settle_input_kernel(info, near, far, out):
    width = out.shape[3]
    for half, source in enumerate((near, far)):
        for spot in range(SPOTS):
            value = source[spot].astype(F32)
            for i in range(3):
                place = place_of(info[1], half, spot)
                out[(i + 1) % 3, place] = value[:, i * width : (i + 1) * width]


def shape(dims, dtype):
    return jax.ShapeDtypeStruct(dims, dtype)


def whole(*dims):
    return pl.BlockSpec(dims, lambda *_: (0,) * len(dims))


def cost(flops, moved, slow=0):
    return pl.CostEstimate(flops=flops, bytes_accessed=moved, transcendentals=slow)


SMEM = pl.BlockSpec(memory_space=pltpu.SMEM)


def gathered_specs(near, first_shard):
    spots, _, piece, lanes = near.shape
    return [pl.BlockSpec((spots, 1, piece, lanes), lambda s: (0, s + first_shard - 1, 0, 0))] * 2


def attend(setting, count, info, tokens, partner, bias, out_weight, vectors, weights, carried):
    heads, depth, first_shard, last = setting
    rows, dim = tokens.shape
    shards, width, _ = out_weight.shape
    lanes = 3 * width
    scratch = []
    if first_shard == 0:
        weight_specs = [whole(dim, lanes)]
    else:
        weight_specs = gathered_specs(weights[0], first_shard)
        scratch = [pltpu.VMEM((PARTS, dim // PARTS, lanes), BF16)]
    out_specs = [
        pl.BlockSpec((1, rows, lanes), lambda s: (s, 0, 0)),
        pl.BlockSpec((1, rows, width), lambda s: (s, 0, 0)),
        pl.BlockSpec((1, 8, rows), lambda s: (s, 0, 0)),
    ]
    out_shape = [
        shape((count, rows, lanes), BF16),
        shape((count, rows, width), BF16),
        shape((count, 8, rows), F32),
    ]
    if last:
        out_specs += [whole(rows, dim)] * 2
        out_shape += [shape((rows, dim), F32), shape((rows, dim), BF16)]
        scratch = [pltpu.VMEM((rows, dim), F32)] + scratch
    else:
        out_specs.append(whole(rows, dim))
        out_shape.append(shape((rows, dim), F32))
    return pl.pallas_call(
        functools.partial(attend_kernel, setting),
        grid=(count,),
        in_specs=[
            SMEM,
            whole(rows, dim),
            whole(rows, dim),
            pl.BlockSpec((1, 8, lanes), lambda s: (s + first_shard, 0, 0)),
            whole(shards, width, dim),
            whole(8, dim),
        ]
        + weight_specs
        + [whole(rows, dim)] * len(carried),
        out_specs=out_specs,
        out_shape=out_shape,
        scratch_shapes=scratch,
        compiler_params=PARAMS,
        cost_estimate=cost(
            count * (3 * rows * dim * dim + 4 * rows * rows * dim),
            count * 6 * rows * dim,
            count * heads * rows * rows,
        ),
        name="attend",
    )(info, tokens, partner, bias, out_weight, vectors, *weights, *carried)


def feed_specs(own, near, half_first):
    spots, _, piece, lanes = near.shape

    def at(spot, half, info):
        return (place_of(info[1], half, spot), 0, 0)

    def other(shard):
        return (0, jnp.maximum(shard - 1, 0), 0, 0)

    if half_first is None:
        own_specs = [
            pl.BlockSpec((1, piece, lanes), lambda q, h, info, spot=spot: at(spot, h, info))
            for spot in range(spots)
        ]
        near_spec = pl.BlockSpec((spots, 1, piece, lanes), lambda q, h, info: other(q))
    else:
        own_specs = [
            pl.BlockSpec(
                (1, piece, lanes),
                lambda h, q, info, spot=spot: at(spot, h ^ half_first, info),
            )
            for spot in range(spots)
        ]
        near_spec = pl.BlockSpec((spots, 1, piece, lanes), lambda h, q, info: other(q))
    return own_specs + [near_spec] * 2


def feed_call(kernel, grid, in_specs, out_specs, out_shape, scratch, flops, moved, slow, name):
    return pl.pallas_call(
        kernel,
        grid_spec=pltpu.PrefetchScalarGridSpec(
            num_scalar_prefetch=1,
            grid=grid,
            in_specs=in_specs,
            out_specs=out_specs,
            scratch_shapes=scratch,
        ),
        out_shape=out_shape,
        compiler_params=PARAMS,
        cost_estimate=cost(flops, moved, slow),
        name=name,
    )


def feed_up(info, normed, weight, bias):
    own, near, far = weight
    rows, dim = normed.shape
    shards = near.shape[1] + 1
    tile = SPOTS * near.shape[2]
    columns = pl.BlockSpec((rows, tile), lambda q, h, info: (0, q))
    return feed_call(
        feed_up_kernel,
        (shards, 2),
        [
            whole(rows, dim),
            *feed_specs(own, near, None),
            pl.BlockSpec((1, 1, 1, tile), lambda q, h, info: (q, h, 0, 0)),
        ],
        [columns] * 4,
        [shape((rows, shards * tile), BF16)] * 2 + [shape((rows, shards * tile), F32)] * 2,
        [],
        4 * rows * dim * tile * shards,
        30 * rows * dim,
        2 * rows * tile * shards,
        "feed_up",
    )(info, normed, own, own, own, own, near, far, bias)


def feed_down(info, hidden, weight, rows_one, cotangent, vectors):
    own, near, far = weight
    rows, dim = rows_one.shape
    shards = near.shape[1] + 1
    tile = SPOTS * near.shape[2]
    columns = pl.BlockSpec((rows, tile), lambda q, h, info: (0, q))
    return feed_call(
        feed_down_kernel,
        (shards, 2),
        [
            columns,
            columns,
            *feed_specs(own, near, None),
            whole(rows, dim),
            whole(rows, dim),
            whole(8, dim),
        ],
        [whole(rows, dim)] * 3 + [whole(8, dim)],
        [
            shape((rows, dim), BF16),
            shape((rows, dim), F32),
            shape((rows, dim), BF16),
            shape((8, dim), F32),
        ],
        [pltpu.VMEM((rows, dim), F32)],
        4 * rows * dim * tile * shards,
        20 * rows * dim,
        0,
        "feed_down",
    )(info, *hidden, own, own, own, own, near, far, rows_one, cotangent, vectors)


def grad_pre_of(info, grad_branch, weight, slopes):
    own, near, far = weight
    rows, dim = grad_branch.shape
    shards = near.shape[1] + 1
    tile = SPOTS * near.shape[2]
    near_columns = pl.BlockSpec((rows, tile), lambda h, q, info: (0, q * h))
    far_columns = pl.BlockSpec(
        (rows, tile), lambda h, q, info: (0, q * (1 - h) + (shards - 1) * h)
    )
    return feed_call(
        grad_pre_kernel,
        (2, shards),
        [whole(rows, dim), *feed_specs(own, near, 1), near_columns, far_columns],
        [
            near_columns,
            far_columns,
            pl.BlockSpec((1, 1, 8, tile), lambda h, q, info: (q, 1 - h, 0, 0)),
        ],
        [shape((rows, shards * tile), BF16)] * 2 + [shape((shards, 2, 8, tile), F32)],
        [],
        4 * rows * dim * tile * shards,
        30 * rows * dim,
        0,
        "grad_pre",
    )(info, grad_branch, own, own, own, own, near, far, *slopes)


def up_back(info, pres, weight, rows_one, grad_second, vectors):
    own, near, far = weight
    rows, dim = rows_one.shape
    shards = near.shape[1] + 1
    tile = SPOTS * near.shape[2]
    near_columns = pl.BlockSpec(
        (rows, tile), lambda h, q, info: (0, q * (1 - h) + (shards - 1) * h)
    )
    far_columns = pl.BlockSpec((rows, tile), lambda h, q, info: (0, q * h))
    return feed_call(
        up_back_kernel,
        (2, shards),
        [
            near_columns,
            far_columns,
            *feed_specs(own, near, 0),
            whole(rows, dim),
            whole(rows, dim),
            whole(8, dim),
        ],
        [whole(rows, dim)] * 2 + [whole(8, dim)],
        [shape((rows, dim), F32), shape((rows, dim), BF16), shape((8, dim), F32)],
        [pltpu.VMEM((rows, dim), F32)],
        4 * rows * dim * tile * shards,
        24 * rows * dim,
        0,
        "up_back",
    )(info, *pres, own, own, own, own, near, far, rows_one, grad_second, vectors)


def row_grads(shards, mine, theirs, my_rows, their_rows, more, lanes, name):
    rows, dim = my_rows.shape
    tile = mine.shape[1] // shards
    piece = tile // SPOTS
    columns = pl.BlockSpec((rows, tile), lambda q: (0, q))
    out = pl.BlockSpec((2, 1, piece, lanes), lambda q: (0, q, 0, 0))
    more_specs = [
        pl.BlockSpec((SPOTS, 1, piece, a.shape[3]), lambda q: (0, q, 0, 0)) for a in more
    ]
    return pl.pallas_call(
        functools.partial(row_grads_kernel, bool(more)),
        grid=(shards,),
        in_specs=[columns, columns, whole(rows, dim), whole(rows, dim)] + more_specs,
        out_specs=[out, out],
        out_shape=[shape((2, shards, piece, lanes), F32), shape((2, shards, piece, lanes), BF16)],
        compiler_params=PARAMS,
        cost_estimate=cost(4 * rows * dim * tile * shards, 20 * rows * dim),
        name=name,
    )(mine, theirs, my_rows, their_rows, *more)


def out_back(info, grad_proj, context):
    rows, dim = grad_proj.shape
    shards, _, width = context.shape
    piece = dim // PARTS
    spec = pl.BlockSpec((SPOTS, 1, piece, width), lambda q: (0, q, 0, 0))
    return pl.pallas_call(
        out_back_kernel,
        grid=(shards,),
        in_specs=[SMEM, whole(rows, dim), pl.BlockSpec((1, rows, width), lambda q: (q, 0, 0))],
        out_specs=[spec, spec],
        out_shape=[shape((SPOTS, shards, piece, width), BF16)] * 2,
        scratch_shapes=[pltpu.VMEM((dim, rows), BF16), pltpu.VMEM((PARTS, piece, width), BF16)],
        compiler_params=PARAMS,
        cost_estimate=cost(2 * rows * dim * dim, 6 * rows * dim),
        name="out_back",
    )(info, grad_proj, context)


def attend_back(
    setting, count, info, tokens_t, partner_t, grad_proj, out_weight, weights, qkv, stats, carried
):
    heads, depth, first_shard, _ = setting
    offset = max(first_shard - 1, 0) if qkv.shape[0] > 1 else 0
    dim, rows = tokens_t.shape
    shards, width, _ = out_weight.shape
    lanes = 3 * width
    piece = dim // PARTS
    scratch = [pltpu.VMEM((PARTS, piece, lanes), BF16)]
    if first_shard == 0:
        weight_specs = [whole(dim, lanes)]
    else:
        weight_specs = gathered_specs(weights[0], first_shard)
        scratch = scratch * 2
    parts_out = pl.BlockSpec((SPOTS, 1, piece, lanes), lambda s: (0, s, 0, 0))
    return pl.pallas_call(
        functools.partial(attend_back_kernel, setting),
        grid=(count,),
        in_specs=[
            SMEM,
            whole(dim, rows),
            whole(dim, rows),
            whole(rows, dim),
            whole(shards, width, dim),
        ]
        + weight_specs
        + [
            pl.BlockSpec((1, rows, lanes), lambda s: (s + offset, 0, 0)),
            pl.BlockSpec((1, 8, rows), lambda s: (s + offset, 0, 0)),
        ]
        + [whole(rows, dim)] * len(carried),
        out_specs=[
            whole(rows, dim),
            whole(rows, dim),
            parts_out,
            parts_out,
            pl.BlockSpec((1, 8, lanes), lambda s: (s, 0, 0)),
        ],
        out_shape=[
            shape((rows, dim), F32),
            shape((rows, dim), F32),
            shape((SPOTS, count, piece, lanes), BF16),
            shape((SPOTS, count, piece, lanes), BF16),
            shape((count, 8, lanes), F32),
        ],
        scratch_shapes=scratch,
        compiler_params=PARAMS,
        cost_estimate=cost(
            count * (6 * rows * dim * dim + 10 * rows * rows * dim),
            count * 8 * rows * dim,
            count * heads * rows * rows,
        ),
        name="attend_back",
    )(info, tokens_t, partner_t, grad_proj, out_weight, *weights, qkv, stats, *carried)


class Mover:
    def __init__(self, batch_size, shards):
        self.batch_size, self.shards = batch_size, shards

    def batch(self, value, mask_of):
        perm = [(i, i ^ mask_of(i)) for i in range(self.batch_size)]
        return lax.ppermute(value, "batch", perm)

    def core(self, value):
        return self.batch(value, lambda i: CORE)

    def low(self, value):
        return self.batch(value, lambda i: 4 if i & 1 else 2)

    def high(self, value):
        return self.batch(value, lambda i: 2 if i & 1 else 4)

    def head(self, value, mask):
        return lax.ppermute(value, "head", [(i, i ^ mask) for i in range(self.shards)])

    def along(self, values, first=1):
        return [self.head(value, q) for q, value in enumerate(values, first)]

    def column(self, piece):
        return self.along([piece] * (self.shards - 1))

    def settle(self, total):
        total = total.astype(BF16)
        mask = PARTS
        while mask < self.batch_size:
            other = self.batch(total, lambda i, mask=mask: mask)
            total = (total.astype(F32) + other.astype(F32)).astype(BF16)
            mask *= 2
        return total

    def hops(self):
        steps, mask = [], 1
        while mask < self.batch_size:
            steps.append(lambda value, mask=mask: self.batch(value, lambda i: mask))
            mask *= 2
        mask = 1
        while mask < self.shards:
            steps.append(lambda value, mask=mask: self.head(value, mask))
            mask *= 2
        return steps


def after(value, *events):
    return lax.optimization_barrier((value, *events))[0]


def all_after(values, *events):
    return lax.optimization_barrier((*values, *events))[: len(values)]


def pair_of(first, second):
    return jnp.stack([first, second])


def four_of(pair, received):
    return jnp.concatenate([pair, received])


def exchange_bits(value, axes):
    for axis, bit in axes:
        value = jnp.where(bit == 1, jnp.flip(value, axis), value)
    return value


def stack8(*rows):
    rows = [row.reshape(1, -1) for row in rows]
    return jnp.concatenate(rows + [jnp.zeros((8 - len(rows), rows[0].shape[1]), F32)], axis=0)


def local(
    batch_size,
    shards,
    tokens,
    lengths,
    block_swap,
    input_weight,
    input_bias,
    out_weight,
    out_bias,
    gain_one,
    shift_one,
    up_weight,
    up_bias,
    down_weight,
    down_bias,
    gain_two,
    shift_two,
    cotangent,
):
    move = Mover(batch_size, shards)
    heads = block_swap.shape[0]
    rows, dim = tokens.shape
    width = input_weight.shape[2]
    depth = width // heads
    hidden_own = up_weight.shape[1]
    piece = dim // PARTS
    batch_at, head_at = lax.axis_index("batch"), lax.axis_index("head")
    part = batch_at % PARTS
    part_bits = [(part >> i) & 1 for i in range(3)]
    head_bits = [(head_at >> i) & 1 for i in range(2)]
    blocks = SEQ_LEN // rows
    length = lax.dynamic_index_in_dim(lengths, head_at // blocks, 0, keepdims=False)
    block_at = head_at % blocks
    own_live = jnp.clip(length - block_at * rows, 0, rows)
    partner_live = jnp.clip(length - (blocks - 1 - block_at) * rows, 0, rows)

    input_piece = lax.dynamic_slice_in_dim(input_weight, part * piece, piece, 1)
    input_piece = jnp.concatenate([input_piece[1], input_piece[2], input_piece[0]], axis=1)
    input_column = move.column(input_piece)
    small = jnp.concatenate([input_bias.reshape(-1), block_swap.astype(F32)])
    small = jnp.stack([small] + move.column(small))
    partner = move.head(after(tokens, *input_column), 1)
    input_column = jnp.stack(input_column)
    input_pair = pair_of(input_column, move.low(input_column))
    input_high, partner = all_after((move.high(input_pair), partner))
    input_near = four_of(input_pair, input_high)
    input_far = move.core(input_near)
    input_own = jnp.concatenate([input_weight[1], input_weight[2], input_weight[0]], axis=1)
    up_own = up_weight.T.reshape(PARTS, piece, dim)
    up_piece = lax.dynamic_index_in_dim(up_own, part, 0, keepdims=False)
    down_own = down_weight.reshape(PARTS, piece, dim)
    down_piece = lax.dynamic_index_in_dim(down_own, part, 0, keepdims=False)
    up_far = move.head(after(up_piece, partner), 2)

    info = jnp.concatenate(
        [
            small[:, 2 * width :].reshape(-1).astype(jnp.int32),
            jnp.stack([own_live, partner_live, part, head_at]).astype(jnp.int32),
        ]
    )
    short_info = jnp.stack([own_live, part, head_at]).astype(jnp.int32)
    bias = jnp.concatenate(
        [jnp.zeros((shards, width), F32), small[:, width : 2 * width], small[:, :width]], axis=1
    )
    bias = jnp.broadcast_to(bias[:, None], (shards, 8, 3 * width))
    head_flips = [(0, head_bits[1]), (1, head_bits[0])]
    part_flips = [(2, part_bits[2]), (3, part_bits[1]), (4, part_bits[0])]
    up_bias_rel = exchange_bits(up_bias.reshape(2, 2, 2, 2, 2, piece), head_flips + part_flips)
    turned = up_bias_rel.swapaxes(2, 3)
    odd = part_bits[0] == 1
    near_bias = jnp.where(odd, turned, up_bias_rel)[:, :, :, :, 0]
    far_bias = jnp.where(odd, up_bias_rel, turned)[:, :, :, :, 1]
    up_bias_rel = jnp.stack([near_bias, far_bias], axis=2)
    up_bias_rel = up_bias_rel.reshape(shards, 2, 1, SPOTS * piece)
    out_parts = out_weight.reshape(shards, width, dim)
    vectors_one = stack8(out_bias, gain_one, shift_one)
    vectors_two = stack8(gain_one, shift_one, down_bias, gain_two, shift_two)
    vectors_back = stack8(gain_one)
    tokens_t, partner_t = tokens.T, partner.T

    def attend_shards(tokens, first_shard, count, last, weights, carried):
        return attend(
            (heads, depth, first_shard, last),
            count,
            info,
            tokens,
            partner,
            bias,
            out_parts,
            vectors_one,
            weights,
            carried,
        )

    tokens_now = after(tokens, up_bias_rel, vectors_two, vectors_back)
    qkv_0, context_0, stats_0, total = attend_shards(
        tokens_now, 0, 1, False, [input_own], []
    )
    up_ends = pair_of(up_piece, after(up_far, total))
    up_others = move.head(up_ends, 1)
    down_far = move.head(after(down_piece, total), 2)
    total, up_ends = all_after((total, up_ends))
    others = [input_near, input_far]
    qkv_1, context_1, stats_1, total = attend_shards(tokens, 1, 2, False, others, [total])
    up_others, down_far = all_after((up_others, down_far), total)
    up_column = jnp.stack([up_others[0], up_ends[1], up_others[1]])
    up_low = move.low(up_column)
    down_ends = pair_of(down_piece, down_far)
    down_others = move.head(down_ends, 1)
    total, up_column, down_ends = all_after((total, up_column, down_ends))
    qkv_3, context_3, stats_3, rows_one, normed = attend_shards(
        tokens, 3, 1, True, others, [total]
    )
    context = jnp.concatenate([context_0, context_1, context_3])
    up_low, down_others = all_after((up_low, down_others), normed)
    up_pair = pair_of(up_column, up_low)
    up_high = move.high(up_pair)
    down_column = jnp.stack([down_others[0], down_ends[1], down_others[1]])
    down_low = move.low(down_column)
    up_near = four_of(up_pair, up_high)
    up_all = (up_own, up_near, move.core(up_near))
    down_pair = pair_of(down_column, after(down_low, up_near))
    down_high = move.high(down_pair)
    normed, down_pair = all_after((normed, down_pair))
    normed_received = move.core(normed)
    hidden_near, hidden_far, *slopes = feed_up(short_info, normed, up_all, up_bias_rel)
    hidden_received = move.core(hidden_far)
    down_near = four_of(down_pair, after(down_high, hidden_near))
    down_all = (down_own, down_near, move.core(down_near))
    mixed_out, grad_second, grad_branch, sums_two = feed_down(
        short_info, (hidden_near, hidden_far), down_all, rows_one, cotangent, vectors_two
    )

    branch_received = move.core(grad_branch)
    pre_near, pre_far, up_bias_sums = grad_pre_of(short_info, grad_branch, down_all, slopes)
    pre_received = move.core(pre_far)
    down_keep, down_send = row_grads(
        shards,
        hidden_near,
        hidden_received,
        after(grad_branch, pre_near),
        branch_received,
        [],
        dim,
        "down_grads",
    )
    down_low = move.low(down_send)
    grad_first, grad_proj, sums_one = up_back(
        short_info, (pre_near, pre_far), up_all, rows_one, after(grad_second, down_send), vectors_back
    )
    out_near, out_far = out_back(short_info, grad_proj, context)
    out_received = move.core(out_far)
    lanes = -(-(dim + width) // 256) * 256
    up_keep, up_send = row_grads(
        shards, pre_near, pre_received, normed, normed_received, [out_near, out_received], lanes,
        "up_grads",
    )
    up_low = move.low(up_send)

    def core_sum(mine, received):
        both = mine.astype(F32) + received.astype(F32)
        return both[0::2], both[1::2].astype(BF16)

    def fold_low(keep, received):
        return keep[0] + received[0].astype(F32), (keep[1] + received[1].astype(F32)).astype(BF16)

    def fold_high(own, received):
        total = own + received.astype(F32)
        return total[0::2], total[1::2].astype(BF16)

    def fold_near(own, received):
        return own[0] + received[0].astype(F32), (own[1] + received[1].astype(F32)).astype(BF16)

    def fold_last(own, received):
        return move.settle(own + received.astype(F32))

    def back(grad, first_shard, count, weights, qkv, stats, carried):
        return attend_back(
            (heads, depth, first_shard, bool(carried)),
            count,
            info,
            tokens_t,
            partner_t,
            grad,
            out_parts,
            weights,
            qkv,
            stats,
            carried,
        )

    up_bias_grad = up_bias_sums[:, :, 0].reshape(2, 2, 2, 2, 2, piece)
    turned = up_bias_grad.swapaxes(3, 4)
    near_bias = jnp.where(odd, turned, up_bias_grad)[:, :, 0]
    far_bias = jnp.where(odd, up_bias_grad, turned)[:, :, 1]
    up_bias_grad = jnp.stack([near_bias, far_bias], axis=4)
    up_bias_grad = exchange_bits(up_bias_grad, head_flips + part_flips).reshape(-1, dim)
    vectors_now = jnp.concatenate([sums_one[:3], sums_two[:3], up_bias_grad])

    late_grad, vectors_now = all_after((grad_proj, vectors_now), up_send)
    own_rows, partner_rows, near_3, far_3, bias_3 = back(
        late_grad, 3, 1, others, qkv_3, stats_3, []
    )
    down_mine, down_next = fold_low(down_keep, after(down_low, bias_3))
    down_high = move.high(down_next)

    own_rows, partner_rows, near_2, far_2, bias_2 = back(
        after(grad_proj, down_next, bias_3), 2, 1, others, qkv_1, stats_1,
        [own_rows, partner_rows],
    )
    late_core = move.core(jnp.concatenate([far_2, far_3], axis=1))
    down_mine, down_next = fold_high(down_mine, after(down_high, bias_2))
    down_near = move.head(down_next, 1)

    own_rows, partner_rows, near_1, far_1, bias_1 = back(
        after(grad_proj, down_next, bias_2), 1, 1, others, qkv_1, stats_1,
        [own_rows, partner_rows],
    )
    up_mine, up_next = fold_low(up_keep, after(up_low, bias_1))
    up_high = move.high(up_next)
    late_keep, late_next = core_sum(
        jnp.concatenate([near_2, near_3], axis=1), after(late_core, up_next)
    )
    late_low = move.low(late_next)
    down_mine, down_next = fold_near(down_mine, after(down_near, late_next))
    down_last = move.head(down_next, 2)

    own_rows, partner_rows, near_0, far_0, bias_0 = back(
        after(grad_proj, up_next, late_next, down_next), 0, 1, [input_own], qkv_0, stats_0,
        [own_rows, partner_rows],
    )
    early_core = move.core(jnp.concatenate([far_0, far_1], axis=1))
    bias_sums = jnp.concatenate([bias_0, bias_1, bias_2, bias_3])
    bias_sums = exchange_bits(bias_sums[:, 0].reshape(2, 2, 3, width), head_flips)
    bias_sums = bias_sums.reshape(shards, 3, width).transpose(1, 0, 2).reshape(3, dim)
    vectors = jnp.concatenate([vectors_now, bias_sums[2:], bias_sums[1:2]])
    hops = move.hops()

    def hop(value, sent, event):
        value = value + after(sent, event)
        return value, hops.pop(0)(value) if hops else None

    vectors_sent = hops.pop(0)(vectors)
    up_mine, up_next = fold_high(up_mine, after(up_high, bias_0))
    up_near = move.head(up_next, 1)
    late_mine, late_next = fold_low(late_keep, after(late_low, up_next))
    late_high = move.high(late_next)
    down_total = fold_last(down_mine, after(down_last, late_next))
    down_low = move.low(down_total)
    early_keep, early_next = core_sum(
        jnp.concatenate([near_0, near_1], axis=1), after(early_core, down_total)
    )
    early_low = move.low(early_next)
    vectors, vectors_sent = hop(vectors, vectors_sent, early_next)
    from_partner = move.head(after(partner_rows.astype(BF16), early_next), 1)
    up_mine, up_next = fold_near(up_mine, after(up_near, vectors))
    up_last = move.head(up_next, 2)
    early_mine, early_next = fold_low(early_keep, after(early_low, up_next))
    early_high = move.high(early_next)
    down_pair = pair_of(down_total, after(down_low, early_next))
    down_high = move.high(down_pair)
    vectors, vectors_sent = hop(vectors, vectors_sent, down_pair)
    late_mine = late_mine + after(late_high, vectors).astype(F32)
    early_mine = early_mine + after(early_high, vectors).astype(F32)
    input_next = jnp.stack([early_mine[1], late_mine[1]]).astype(BF16)
    input_near = move.head(input_next, 1)
    up_total = fold_last(up_mine, after(up_last, input_next))
    out_total = up_total[:, dim : dim + width]
    out_near = move.head(out_total, 1)
    vectors, vectors_sent = hop(vectors, vectors_sent, up_total)
    down_done = four_of(down_pair, after(down_high, vectors))
    down_far = move.core(down_done)
    input_mine, input_next = fold_near(
        jnp.stack([early_mine[0], late_mine[0]]), after(input_near, down_done)
    )
    input_last = move.head(input_next, 2)
    out_total = pair_of(out_total, after(out_near, input_next))
    out_last = move.head(out_total, 2)
    vectors, vectors_sent = hop(vectors, vectors_sent, out_total)
    input_total = fold_last(input_mine, after(input_last, vectors))
    input_low = move.low(input_total)
    out_last, from_partner = all_after((out_last, from_partner), input_total)
    out_total = four_of(out_total, out_last)
    up_total = jnp.concatenate([up_total[:, :dim], *out_total], axis=1)
    up_low = move.low(up_total)
    while vectors_sent is not None:
        vectors, vectors_sent = hop(vectors, vectors_sent, up_total)
    input_pair = pair_of(input_total, after(input_low, vectors))
    input_high = move.high(input_pair)
    up_pair = pair_of(up_total, after(up_low, input_pair))
    up_high = move.high(up_pair)
    down_done = (down_done, after(down_far, up_pair))
    input_done = four_of(input_pair, after(input_high, up_pair))
    input_done = (input_done, move.core(input_done))
    up_done = four_of(up_pair, after(up_high, input_done[0]))
    up_done = (up_done, move.core(up_done))
    grad_tokens = grad_first + own_rows + from_partner.astype(F32)

    grad_input_bias = lax.dynamic_slice_in_dim(vectors[10:12], head_at * width, width, 1)
    grad_up_bias = lax.dynamic_slice_in_dim(
        vectors[6:10].reshape(-1), head_at * hidden_own, hidden_own
    )

    grad_down = pl.pallas_call(
        settle_down_kernel,
        in_specs=[SMEM] + [whole(4, piece, dim)] * 2,
        out_shape=shape((PARTS, piece, dim), F32),
        compiler_params=PARAMS,
        name="settle_down",
    )(short_info, *down_done)
    grad_up, grad_out = pl.pallas_call(
        settle_up_kernel,
        in_specs=[SMEM] + [whole(4, piece, dim + shards * width)] * 2,
        out_shape=[shape((dim, hidden_own), F32), shape((shards, width, dim), F32)],
        scratch_shapes=[pltpu.VMEM((PARTS, piece, dim), F32)] * 2,
        compiler_params=PARAMS,
        name="settle_up",
    )(short_info, *up_done)
    grad_input_weight = pl.pallas_call(
        settle_input_kernel,
        in_specs=[SMEM] + [whole(4, piece, 3 * width)] * 2,
        out_shape=shape((3, PARTS, piece, width), F32),
        compiler_params=PARAMS,
        name="settle_input",
    )(short_info, *input_done)
    return (
        mixed_out,
        grad_tokens,
        grad_input_weight.reshape(3, dim, width),
        grad_input_bias,
        grad_out.reshape(dim, dim),
        vectors[0],
        vectors[1],
        vectors[2],
        grad_up,
        grad_up_bias,
        grad_down.reshape(hidden_own, dim),
        vectors[3],
        vectors[4],
        vectors[5],
    )


def solution(mesh):
    rows_spec = P(("batch", "head"), None)
    placed = (
        rows_spec,
        P("batch"),
        P("head"),
        P(None, None, "head"),
        P(None, "head"),
        P(),
        P(),
        P(),
        P(),
        P(None, "head"),
        P(),
        P("head", None),
        P(),
        P(),
        P(),
        rows_spec,
    )
    return jax.shard_map(
        functools.partial(local, mesh.shape["batch"], mesh.shape["head"]),
        mesh=mesh,
        in_specs=placed,
        out_specs=(
            rows_spec,
            rows_spec,
            P(None, None, "head"),
            P(None, "head"),
            P(),
            P(),
            P(),
            P(),
            P(None, "head"),
            P("head"),
            P("head", None),
            P(),
            P(),
            P(),
        ),
        check_vma=False,
    )
```

```python
import functools

import jax
import jax.numpy as jnp
from jax import lax
from jax.experimental import pallas as pl
from jax.experimental.pallas import tpu as pltpu
from jax.sharding import PartitionSpec as P

SEQ_LEN = 1024
EPSILON = 1e-05
F32 = jnp.float32
BF16 = jnp.bfloat16
VMEM_LIMIT = 56 * 1024 * 1024
PARAMS = pltpu.CompilerParams(vmem_limit_bytes=VMEM_LIMIT)
CORE = 1
PARTS = 8
SPOTS = 4


def dot(left_side, right_side, left_dim=1, right_dim=0):
    return lax.dot_general(
        left_side,
        right_side,
        (((left_dim,), (right_dim,)), ((), ())),
        preferred_element_type=F32,
    )


def unit_parts(values):
    centred = values - jnp.mean(values, axis=-1, keepdims=True)
    inverse = lax.rsqrt(jnp.mean(centred * centred, axis=-1, keepdims=True) + EPSILON)
    return centred * inverse, inverse


def norm_back(grad_rows, unit_rows, inverse, gain_row):
    scaled = grad_rows * gain_row
    return inverse * (
        scaled
        - jnp.mean(scaled, axis=-1, keepdims=True)
        - unit_rows * jnp.mean(scaled * unit_rows, axis=-1, keepdims=True)
    )


def column_sum(values):
    return jnp.sum(values, axis=0, keepdims=True)


def gelu_parts(inner):
    below = 0.5 + 0.5 * lax.erf(inner * 0.7071067811865476)
    bell = jnp.exp(inner * inner * -0.5) * 0.3989422804014327
    return inner * below, below + inner * bell


def row_chunks(rows, step):
    return [slice(i, i + step) for i in range(0, rows, step)]


def eight_sum(values):
    return sum(values[cut] for cut in row_chunks(values.shape[0], 8))


def lane_pick(values, depth):
    lane = lax.broadcasted_iota(jnp.int32, (1, len(values) * depth), 1)
    picked = jnp.full(lane.shape, values[0], jnp.int32)
    for j in range(1, len(values)):
        picked = jnp.where(lane >= j * depth, values[j], picked)
    return picked


def place_of(part, half, spot):
    seen = part ^ half
    core = seen & 1
    low, high = 2 + 2 * core, 4 - 2 * core
    return seen ^ (low * (spot & 1) + high * (spot >> 1))


class Info:
    def __init__(self, ref, heads, shards):
        self.ref, self.heads, self.base = ref, heads, heads * shards

    def swaps(self, shard):
        return [self.ref[shard * self.heads + j] for j in range(self.heads)]

    own_live = property(lambda self: self.ref[self.base])
    partner_live = property(lambda self: self.ref[self.base + 1])
    part = property(lambda self: self.ref[self.base + 2])
    head_at = property(lambda self: self.ref[self.base + 3])


def gathered(part, near, far, scratch):
    for spot in range(SPOTS):
        scratch[place_of(part, 0, spot)] = near[spot, 0]
        scratch[place_of(part, 1, spot)] = far[spot, 0]
    return scratch[...].reshape(-1, scratch.shape[2])


def attend_kernel(setting, info_ref, tokens, partner, bias, out_weight, vectors, *refs):
    heads, depth, first_shard, last = setting
    refs = list(refs)
    if first_shard == 0:
        turned = refs.pop(0)
        total_in = None
    else:
        near, far, total_in = refs[:3]
        del refs[:3]
    earlier = []
    if last:
        earlier = refs[:2]
        del refs[:2]
    qkv_out, context_out, stats_out = refs[:3]
    step = pl.program_id(0)
    shard = first_shard + step
    info = Info(info_ref, heads, out_weight.shape[0])
    if first_shard:
        weight = gathered(info.part, near, far, refs.pop())
    total = refs.pop()
    swaps = info.swaps(shard)
    rows, dim = tokens.shape
    width = heads * depth
    x, xp = tokens[...], partner[...]
    if first_shard:
        own = dot(x, weight)
        other = dot(xp, weight[:, : 2 * width])
    else:
        kv_rows = jnp.concatenate([turned[1], turned[2]], axis=0)
        own = jnp.concatenate([dot(x, kv_rows, 1, 1), dot(x, turned[0], 1, 1)], axis=1)
        other = dot(xp, kv_rows, 1, 1)
    swapped = lane_pick(swaps + swaps, depth) == 1
    bias_row = bias[0, 0:1]
    kv, q = [], []
    for cut in row_chunks(rows, 32):
        mine = own[cut] + bias_row
        theirs = other[cut] + bias_row[:, : 2 * width]
        kv.append(jnp.where(swapped, theirs, mine[:, : 2 * width]).astype(BF16))
        q.append(mine[:, 2 * width :].astype(BF16) * (depth**-0.5))
    kv, q = jnp.concatenate(kv, axis=0), jnp.concatenate(q, axis=0)
    qkv_out[0, :, : 2 * width] = kv
    qkv_out[0, :, 2 * width :] = q
    stats = []
    pieces = []
    for j in range(heads):
        head = slice(j * depth, (j + 1) * depth)
        live = jnp.where(swaps[j] == 1, info.partner_live, info.own_live)
        anyone = jnp.where(live > 0, 1.0, 0.0).astype(F32)
        scores = dot(kv[:, head], q[:, head], 1, 1)
        masked, most = [], None
        for cut in row_chunks(rows, 32):
            index = cut.start + lax.broadcasted_iota(jnp.int32, (32, 1), 0)
            part = jnp.where(index < live, scores[cut], -1e30)
            masked.append(part)
            for tile in row_chunks(32, 8):
                most = part[tile] if most is None else jnp.maximum(most, part[tile])
        largest = jnp.max(most, axis=0, keepdims=True)
        largest = jnp.where(anyone > 0.5, largest, 0.0)
        total_rows = None
        for part in masked:
            weights = eight_sum(jnp.exp(part - largest))
            total_rows = weights if total_rows is None else total_rows + weights
        stat = largest + jnp.log(column_sum(total_rows) + (1.0 - anyone))
        mixing = [jnp.exp(part - stat).astype(BF16) for part in masked]
        stats.append(stat)
        values = kv[:, width + j * depth : width + (j + 1) * depth]
        pieces.append(dot(values, jnp.concatenate(mixing, axis=0), 0, 0))
    context = jnp.concatenate(pieces, axis=0).T.astype(BF16)
    stats_out[0] = jnp.concatenate(stats + [jnp.zeros((8 - heads, rows), F32)], axis=0)
    projected = dot(context, out_weight[info.head_at ^ shard])
    if not last:
        context_out[0] = context

        @pl.when(step == 0)
        def first():
            total[...] = projected if total_in is None else total_in[...] + projected

        @pl.when(step > 0)
        def later():
            total[...] += projected

        return

    context_out[...] = jnp.concatenate(
        [ref[q] for ref in earlier for q in range(ref.shape[0])] + [context], axis=1
    )
    rows_out, normed_out = refs[3:]
    for cut in row_chunks(rows, 16):
        values = x[cut].astype(F32) + ((total_in[cut] + projected[cut]) + vectors[0:1])
        rows_out[cut] = values
        unit, _ = unit_parts(values)
        normed_out[cut] = (unit * vectors[1:2] + vectors[2:3]).astype(BF16)


def tiles_of(part, own, near, far, run):
    @pl.when(pl.program_id(0) == 0)
    def mine():
        run(
            *(
                jnp.concatenate([own[place_of(part, half, spot)] for spot in range(SPOTS)], axis=0)
                for half in range(2)
            )
        )

    @pl.when(pl.program_id(0) > 0)
    def other():
        run(*(ref[:, 0].reshape(-1, ref.shape[3]) for ref in (near, far)))


def add_up(total, *partials):
    @pl.when(pl.program_id(0) == 0)
    def start():
        total[...] = sum(partials[1:], partials[0])

    @pl.when(pl.program_id(0) > 0)
    def later():
        total[...] = sum(partials, total[...])


def at_end(run):
    pl.when(pl.program_id(0) == pl.num_programs(0) - 1)(run)


def eight_rows(*rows):
    width = rows[0].shape[1]
    return jnp.concatenate([*rows, jnp.zeros((8 - len(rows), width), F32)], axis=0)


def feed_up_kernel(info, normed, own, near, far, bias, *outs):
    def run(*tiles):
        for half, tile in enumerate(tiles):
            pre = dot(normed[...], tile, 1, 1)
            for cut in row_chunks(pre.shape[0], 32):
                hidden, slope = gelu_parts(pre[cut] + bias[0, half])
                outs[half][cut] = hidden.astype(BF16)
                outs[half + 2][cut] = slope

    tiles_of(info[1], own, near, far, run)


def feed_down_kernel(
    info,
    near_hidden,
    far_hidden,
    own,
    near,
    far,
    rows_in,
    cotangent,
    vectors,
    mixed_out,
    second_out,
    grad_out,
    sums_out,
    total,
):
    def run(near_tile, far_tile):
        add_up(total, dot(near_hidden[...], near_tile), dot(far_hidden[...], far_tile))

    tiles_of(info[1], own, near, far, run)

    @at_end
    def finish():
        sums = [jnp.zeros((8, rows_in.shape[1]), F32)] * 3
        for cut in row_chunks(rows_in.shape[0], 16):
            unit_one, _ = unit_parts(rows_in[cut])
            first_norm = unit_one * vectors[0:1] + vectors[1:2]
            unit, inverse = unit_parts(first_norm + (total[cut] + vectors[2:3]))
            index = cut.start + lax.broadcasted_iota(jnp.int32, (16, 1), 0)
            mask = jnp.where(index < info[0], 1.0, 0.0).astype(F32)
            mixed_out[cut] = ((unit * vectors[3:4] + vectors[4:5]) * mask).astype(BF16)
            incoming = cotangent[cut].astype(F32) * mask
            grad = norm_back(incoming, unit, inverse, vectors[3:4])
            second_out[cut] = grad
            low = grad.astype(BF16)
            grad_out[cut] = low
            more = (low.astype(F32), incoming * unit, incoming)
            sums = [a + eight_sum(b) for a, b in zip(sums, more)]
        sums_out[...] = eight_rows(*(column_sum(a) for a in sums))


def feed_back_kernel(
    info,
    grad_branch,
    down_own,
    down_near,
    down_far,
    up_own,
    up_near,
    up_far,
    near_slope,
    far_slope,
    rows_in,
    second_in,
    vectors,
    near_out,
    far_out,
    bias_out,
    first_out,
    proj_out,
    sums_out,
    total,
):
    def run_down(*tiles):
        for half, tile in enumerate(tiles):
            out, slope = (near_out, far_out)[half], (near_slope, far_slope)[half]
            grad = dot(grad_branch[...], tile, 1, 1)
            sums = jnp.zeros((8, grad.shape[1]), F32)
            for cut in row_chunks(grad.shape[0], 32):
                low = (grad[cut] * slope[cut]).astype(BF16)
                out[cut] = low
                sums = sums + eight_sum(low.astype(F32))
            bias_out[0, half] = sums

    def run_up(near_tile, far_tile):
        add_up(total, dot(near_out[...], near_tile), dot(far_out[...], far_tile))

    tiles_of(info[1], down_own, down_near, down_far, run_down)
    tiles_of(info[1], up_own, up_near, up_far, run_up)

    @at_end
    def finish():
        sums = [jnp.zeros((8, rows_in.shape[1]), F32)] * 3
        for cut in row_chunks(rows_in.shape[0], 16):
            unit, inverse = unit_parts(rows_in[cut])
            grad_normed = second_in[cut] + total[cut]
            grad = norm_back(grad_normed, unit, inverse, vectors[0:1])
            first_out[cut] = grad
            low = grad.astype(BF16)
            proj_out[cut] = low
            more = (low.astype(F32), grad_normed * unit, grad_normed)
            sums = [a + eight_sum(b) for a, b in zip(sums, more)]
        sums_out[...] = eight_rows(*(column_sum(a) for a in sums))


def row_grads_kernel(mine, theirs, my_rows, their_rows, keep_out, send_out):
    value = dot(mine[...], my_rows[...], 0, 0) + dot(theirs[...], their_rows[...], 0, 0)
    value = value.reshape(SPOTS, -1, value.shape[1])
    for spot in range(SPOTS):
        out = (keep_out, send_out)[spot & 1]
        out[spot >> 1, 0] = value[spot].astype(out.dtype)


def out_grads_kernel(info, mine, theirs, my_context, their_context, keep_out, send_out, turned):
    value = 0.0
    for i, (grad, context) in enumerate(((mine, my_context), (theirs, their_context))):
        turned[i] = grad[...].T.reshape(turned.shape[1:])
        rows = [turned[i, place_of(info[1], 0, spot)] for spot in range(SPOTS)]
        value = value + dot(jnp.concatenate(rows, axis=0), context[...])
    value = value.reshape(SPOTS, -1, value.shape[1])
    for spot in range(SPOTS):
        out = (keep_out, send_out)[spot & 1]
        out[spot >> 1] = value[spot].astype(out.dtype)


def scatter_parts(part, value, chunks, near_out, far_out):
    chunks[...] = value.reshape(chunks.shape)
    for spot in range(SPOTS):
        near_out[spot, 0] = chunks[place_of(part, 0, spot)]
        far_out[spot, 0] = chunks[place_of(part, 1, spot)]


def attend_back_kernel(setting, info_ref, tokens_t, partner_t, grad_proj, out_weight, *refs):
    heads, depth, first_shard, carried, shards = setting
    refs = list(refs)
    if first_shard == 0:
        turned = refs.pop(0)
    else:
        near, far = refs[:2]
        del refs[:2]
    qkv_in, stats_in = refs[:2]
    del refs[:2]
    if carried:
        own_in, partner_in = refs[:2]
        del refs[:2]
    own_out, partner_out, near_out, far_out, bias_out, chunks = refs[:6]
    shard = first_shard
    info = Info(info_ref, heads, shards)
    if first_shard:
        weight = gathered(info.part, near, far, refs[6])
    swaps = info.swaps(shard)
    dim, rows = tokens_t.shape
    width = heads * depth
    grad = dot(grad_proj[...], out_weight[0], 1, 1).astype(BF16)
    k, v, q = (qkv_in[0, :, i * width : (i + 1) * width] for i in range(3))
    stats = stats_in[0]
    gq, gk, gv = [], [], []
    for j in range(heads):
        head = slice(j * depth, (j + 1) * depth)
        stat = stats[j : j + 1, :]
        live = jnp.where(swaps[j] == 1, info.partner_live, info.own_live)
        scores = dot(k[:, head], q[:, head], 1, 1)
        grad_mix = dot(v[:, head], grad[:, head], 1, 1)
        chances, shared = [], jnp.zeros((8, rows), F32)
        for cut in row_chunks(rows, 32):
            index = cut.start + lax.broadcasted_iota(jnp.int32, (32, 1), 0)
            part = jnp.exp(jnp.where(index < live, scores[cut] - stat, -10000.0))
            chances.append(part)
            shared = shared + eight_sum(part * grad_mix[cut])
        shared = column_sum(shared)
        mixing = jnp.concatenate([part.astype(BF16) for part in chances], axis=0)
        grad_scores = jnp.concatenate(
            [
                (part * (grad_mix[cut] - shared)).astype(BF16)
                for part, cut in zip(chances, row_chunks(rows, 32))
            ],
            axis=0,
        )
        gk.append(dot(grad_scores, q[:, head]))
        gv.append(dot(mixing, grad[:, head]))
        gq.append(dot(k[:, head], grad_scores, 0, 0))
    grad_q = (jnp.concatenate(gq, axis=0).T * (depth**-0.5)).astype(BF16)
    grad_kv = jnp.concatenate(gk + gv, axis=1).astype(BF16)
    swapped = lane_pick(swaps + swaps, depth) == 1
    nothing = jnp.zeros((), BF16)
    grad_own = jnp.concatenate([jnp.where(swapped, nothing, grad_kv), grad_q], axis=1)
    grad_far = jnp.where(swapped, grad_kv, nothing)
    if first_shard:
        own = dot(grad_own, weight, 1, 1)
        other = dot(grad_far, weight[:, : 2 * width], 1, 1)
    else:
        kv_rows = jnp.concatenate([turned[1], turned[2]], axis=0)
        own = dot(grad_own, jnp.concatenate([kv_rows, turned[0]], axis=0))
        other = dot(grad_far, kv_rows)
    if carried:
        own, other = own_in[...] + own, partner_in[...] + other
    own_out[...] = own
    partner_out[...] = other.astype(partner_out.dtype)
    grads = dot(tokens_t[...], grad_own)
    grads_kv = grads[:, : 2 * width] + dot(partner_t[...], grad_far)
    grads = jnp.concatenate([grads_kv, grads[:, 2 * width :]], axis=1).astype(BF16)
    chunks[...] = grads.reshape(chunks.shape)
    for spot in range(SPOTS):
        near_out[spot, 0] = chunks[place_of(info.part, 0, spot)]
        far_out[spot, 0] = chunks[place_of(info.part, 1, spot)]
    bias_out[0] = jnp.broadcast_to(
        jnp.concatenate(
            [column_sum(grad_kv.astype(F32)), column_sum(grad_q.astype(F32))], axis=1
        ),
        bias_out.shape[1:],
    )


def settle_down_kernel(info, near, far, out):
    for half, source in enumerate((near, far)):
        for spot in range(SPOTS):
            out[place_of(info[1], half, spot)] = source[spot].astype(F32)


def settle_up_kernel(info, near, far, up_out, out_out, up_scratch, out_scratch):
    dim = up_out.shape[0]
    for half, source in enumerate((near, far)):
        for spot in range(SPOTS):
            place = place_of(info[1], half, spot)
            value = source[spot].astype(F32)
            up_scratch[place] = value[:, :dim]
            out_scratch[place] = value[:, dim:]
    up_out[...] = up_scratch[...].reshape(-1, dim).T
    shards = out_out.shape[0]
    turned = out_scratch[...].reshape(-1, dim).T.reshape(shards, -1, dim)
    for q in range(shards):
        out_out[info[2] ^ q] = turned[q]


def settle_input_kernel(info, near, far, out, scratch):
    width = out.shape[1]
    for half, source in enumerate((near, far)):
        for spot in range(SPOTS):
            scratch[place_of(info[1], half, spot)] = source[spot].astype(F32)
    turned = scratch[...].reshape(-1, scratch.shape[2]).T
    for i in range(3):
        out[(i + 1) % 3] = turned[i * width : (i + 1) * width]


def shape(dims, dtype):
    return jax.ShapeDtypeStruct(dims, dtype)


def whole(*dims):
    return pl.BlockSpec(dims, lambda *_: (0,) * len(dims))


def cost(flops, moved, slow=0):
    return pl.CostEstimate(flops=flops, bytes_accessed=moved, transcendentals=slow)


SMEM = pl.BlockSpec(memory_space=pltpu.SMEM)


def gathered_specs(near, first_shard):
    spots, _, piece, lanes = near.shape
    return [pl.BlockSpec((spots, 1, piece, lanes), lambda s: (0, s + first_shard - 1, 0, 0))] * 2


def attend(setting, count, info, tokens, partner, bias, out_weight, vectors, weights, carried):
    heads, depth, first_shard, last = setting
    rows, dim = tokens.shape
    shards, width, _ = out_weight.shape
    lanes = 3 * width
    scratch = []
    if first_shard == 0:
        weight_specs = [whole(3, width, dim)]
    else:
        weight_specs = gathered_specs(weights[0], first_shard)
        scratch = [pltpu.VMEM((PARTS, dim // PARTS, lanes), BF16)]
    out_specs = [
        pl.BlockSpec((1, rows, lanes), lambda s: (s, 0, 0)),
        whole(rows, dim) if last else pl.BlockSpec((1, rows, width), lambda s: (s, 0, 0)),
        pl.BlockSpec((1, 8, rows), lambda s: (s, 0, 0)),
    ]
    out_shape = [
        shape((count, rows, lanes), BF16),
        shape((rows, dim) if last else (count, rows, width), BF16),
        shape((count, 8, rows), F32),
    ]
    if last:
        out_specs += [whole(rows, dim)] * 2
        out_shape += [shape((rows, dim), F32), shape((rows, dim), BF16)]
        scratch = [pltpu.VMEM((8, 128), F32)] + scratch
    else:
        out_specs.append(whole(rows, dim))
        out_shape.append(shape((rows, dim), F32))
    return pl.pallas_call(
        functools.partial(attend_kernel, setting),
        grid=(count,),
        in_specs=[
            SMEM,
            whole(rows, dim),
            whole(rows, dim),
            pl.BlockSpec((1, 8, lanes), lambda s: (s + first_shard, 0, 0)),
            whole(shards, width, dim),
            whole(8, dim),
        ]
        + weight_specs
        + [whole(*value.shape) for value in carried],
        out_specs=out_specs,
        out_shape=out_shape,
        scratch_shapes=scratch,
        compiler_params=PARAMS,
        cost_estimate=cost(
            count * (3 * rows * dim * dim + 4 * rows * rows * dim),
            count * 6 * rows * dim,
            count * heads * rows * rows,
        ),
        name="attend",
    )(info, tokens, partner, bias, out_weight, vectors, *weights, *carried)


def feed_specs(near):
    spots, _, piece, lanes = near.shape
    other = pl.BlockSpec(
        (spots, 1, piece, lanes), lambda q: (0, jnp.maximum(q - 1, 0), 0, 0)
    )
    return [whole(PARTS, piece, lanes), other, other]


def feed_up(info, normed, weight, bias):
    rows, dim = normed.shape
    near = weight[1]
    shards = near.shape[1] + 1
    tile = SPOTS * near.shape[2]
    columns = pl.BlockSpec((rows, tile), lambda q: (0, q))
    return pl.pallas_call(
        feed_up_kernel,
        grid=(shards,),
        in_specs=[
            SMEM,
            whole(rows, dim),
            *feed_specs(near),
            pl.BlockSpec((1, 2, 1, tile), lambda q: (q, 0, 0, 0)),
        ],
        out_specs=[columns] * 4,
        out_shape=[shape((rows, shards * tile), BF16)] * 2
        + [shape((rows, shards * tile), F32)] * 2,
        compiler_params=PARAMS,
        cost_estimate=cost(4 * rows * dim * tile * shards, 30 * rows * dim, rows * dim * 8),
        name="feed_up",
    )(info, normed, *weight, bias)


def feed_down(info, hidden, weight, rows_one, cotangent, vectors):
    rows, dim = rows_one.shape
    near = weight[1]
    shards = near.shape[1] + 1
    tile = SPOTS * near.shape[2]
    columns = pl.BlockSpec((rows, tile), lambda q: (0, q))
    return pl.pallas_call(
        feed_down_kernel,
        grid=(shards,),
        in_specs=[
            SMEM,
            columns,
            columns,
            *feed_specs(near),
            whole(rows, dim),
            whole(rows, dim),
            whole(8, dim),
        ],
        out_specs=[whole(rows, dim)] * 3 + [whole(8, dim)],
        out_shape=[
            shape((rows, dim), BF16),
            shape((rows, dim), F32),
            shape((rows, dim), BF16),
            shape((8, dim), F32),
        ],
        scratch_shapes=[pltpu.VMEM((rows, dim), F32)],
        compiler_params=PARAMS,
        cost_estimate=cost(4 * rows * dim * tile * shards, 20 * rows * dim),
        name="feed_down",
    )(info, *hidden, *weight, rows_one, cotangent, vectors)


def feed_back(info, grad_branch, down, up, slopes, rows_one, grad_second, vectors):
    rows, dim = rows_one.shape
    near = up[1]
    shards = near.shape[1] + 1
    tile = SPOTS * near.shape[2]
    columns = pl.BlockSpec((rows, tile), lambda q: (0, q))
    return pl.pallas_call(
        feed_back_kernel,
        grid=(shards,),
        in_specs=[
            SMEM,
            whole(rows, dim),
            *feed_specs(near),
            *feed_specs(near),
            columns,
            columns,
            whole(rows, dim),
            whole(rows, dim),
            whole(8, dim),
        ],
        out_specs=[
            columns,
            columns,
            pl.BlockSpec((1, 2, 8, tile), lambda q: (q, 0, 0, 0)),
            whole(rows, dim),
            whole(rows, dim),
            whole(8, dim),
        ],
        out_shape=[
            shape((rows, shards * tile), BF16),
            shape((rows, shards * tile), BF16),
            shape((shards, 2, 8, tile), F32),
            shape((rows, dim), F32),
            shape((rows, dim), BF16),
            shape((8, dim), F32),
        ],
        scratch_shapes=[pltpu.VMEM((rows, dim), F32)],
        compiler_params=PARAMS,
        cost_estimate=cost(8 * rows * dim * tile * shards, 40 * rows * dim),
        name="feed_back",
    )(info, grad_branch, *down, *up, *slopes, rows_one, grad_second, vectors)


def row_grads(shards, mine, theirs, my_rows, their_rows, name):
    rows, dim = my_rows.shape
    tile = mine.shape[1] // shards
    piece = tile // SPOTS
    columns = pl.BlockSpec((rows, tile), lambda q: (0, q))
    out = pl.BlockSpec((2, 1, piece, dim), lambda q: (0, q, 0, 0))
    return pl.pallas_call(
        row_grads_kernel,
        grid=(shards,),
        in_specs=[columns, columns, whole(rows, dim), whole(rows, dim)],
        out_specs=[out, out],
        out_shape=[shape((2, shards, piece, dim), F32), shape((2, shards, piece, dim), BF16)],
        compiler_params=PARAMS,
        cost_estimate=cost(4 * rows * dim * tile * shards, 20 * rows * dim),
        name=name,
    )(mine, theirs, my_rows, their_rows)


def out_grads(info, mine, theirs, my_context, their_context):
    rows, dim = mine.shape
    piece = dim // PARTS
    return pl.pallas_call(
        out_grads_kernel,
        in_specs=[SMEM] + [whole(rows, dim)] * 4,
        out_specs=[whole(2, piece, dim)] * 2,
        out_shape=[shape((2, piece, dim), F32), shape((2, piece, dim), BF16)],
        scratch_shapes=[pltpu.VMEM((2, PARTS, piece, rows), BF16)],
        compiler_params=PARAMS,
        cost_estimate=cost(2 * rows * dim * dim, 10 * rows * dim),
        name="out_grads",
    )(info, mine, theirs, my_context, their_context)


def attend_back(
    setting, info, tokens_t, partner_t, grad_proj, out_weight, weights, qkv, stats, carried
):
    heads, depth, shard, last, shards = setting
    offset = max(shard - 1, 0) if qkv.shape[0] > 1 else 0
    dim, rows = tokens_t.shape
    width = heads * depth
    lanes = 3 * width
    piece = dim // PARTS
    head_spot = heads * shards + 3
    scratch = [pltpu.VMEM((PARTS, piece, lanes), BF16)]
    if shard == 0:
        weight_specs = [whole(3, width, dim)]
    else:
        weight_specs = [
            pl.BlockSpec((SPOTS, 1, piece, lanes), lambda s, info: (0, shard - 1, 0, 0))
        ] * 2
        scratch = scratch * 2
    kernel = functools.partial(attend_back_kernel, (heads, depth, shard, bool(carried), shards))
    parts_out = whole(SPOTS, 1, piece, lanes)
    return pl.pallas_call(
        kernel,
        grid_spec=pltpu.PrefetchScalarGridSpec(
            num_scalar_prefetch=1,
            grid=(1,),
            in_specs=[
                whole(dim, rows),
                whole(dim, rows),
                whole(rows, dim),
                pl.BlockSpec((1, width, dim), lambda s, info: (info[head_spot] ^ shard, 0, 0)),
            ]
            + weight_specs
            + [
                pl.BlockSpec((1, rows, lanes), lambda s, info: (offset, 0, 0)),
                pl.BlockSpec((1, 8, rows), lambda s, info: (offset, 0, 0)),
            ]
            + [whole(rows, dim)] * len(carried),
            out_specs=[
                whole(rows, dim),
                whole(rows, dim),
                parts_out,
                parts_out,
                whole(1, 8, lanes),
            ],
            scratch_shapes=scratch,
        ),
        out_shape=[
            shape((rows, dim), F32),
            shape((rows, dim), BF16 if last else F32),
            shape((SPOTS, 1, piece, lanes), BF16),
            shape((SPOTS, 1, piece, lanes), BF16),
            shape((1, 8, lanes), F32),
        ],
        compiler_params=PARAMS,
        cost_estimate=cost(
            6 * rows * dim * dim + 10 * rows * rows * dim, 8 * rows * dim, heads * rows * rows
        ),
        name="attend_back",
    )(info, tokens_t, partner_t, grad_proj, out_weight, *weights, qkv, stats, *carried)


class Mover:
    def __init__(self, batch_size, shards):
        self.batch_size, self.shards = batch_size, shards

    def batch(self, value, mask_of):
        perm = [(i, i ^ mask_of(i)) for i in range(self.batch_size)]
        return lax.ppermute(value, "batch", perm)

    def core(self, value):
        return self.batch(value, lambda i: CORE)

    def low(self, value):
        return self.batch(value, lambda i: 4 if i & 1 else 2)

    def high(self, value):
        return self.batch(value, lambda i: 2 if i & 1 else 4)

    def head(self, value, mask):
        return lax.ppermute(value, "head", [(i, i ^ mask) for i in range(self.shards)])

    def along(self, values, first=1):
        return [self.head(value, q) for q, value in enumerate(values, first)]

    def column(self, piece):
        return self.along([piece] * (self.shards - 1))

    def settle(self, total):
        total = total.astype(BF16)
        mask = PARTS
        while mask < self.batch_size:
            other = self.batch(total, lambda i, mask=mask: mask)
            total = (total.astype(F32) + other.astype(F32)).astype(BF16)
            mask *= 2
        return total

    def hops(self):
        steps, mask = [], 1
        while mask < self.batch_size:
            steps.append(lambda value, mask=mask: self.batch(value, lambda i: mask))
            mask *= 2
        mask = 1
        while mask < self.shards:
            steps.append(lambda value, mask=mask: self.head(value, mask))
            mask *= 2
        return steps


def after(value, *events):
    return lax.optimization_barrier((value, *events))[0]


def all_after(values, *events):
    return lax.optimization_barrier((*values, *events))[: len(values)]


def pair_of(first, second):
    return jnp.stack([first, second])


def four_of(pair, received):
    return jnp.concatenate([pair, received])


def exchange_bits(value, axes):
    for axis, bit in axes:
        value = jnp.where(bit == 1, jnp.flip(value, axis), value)
    return value


def shards_swapped(value, shards, mask):
    width = value.shape[1] // shards
    blocks = [value[:, (q ^ mask) * width : ((q ^ mask) + 1) * width] for q in range(shards)]
    return jnp.concatenate(blocks, axis=1)


def stack8(*rows):
    rows = [row.reshape(1, -1) for row in rows]
    return jnp.concatenate(rows + [jnp.zeros((8 - len(rows), rows[0].shape[1]), F32)], axis=0)


def local(
    batch_size,
    shards,
    tokens,
    lengths,
    block_swap,
    input_weight,
    input_bias,
    out_weight,
    out_bias,
    gain_one,
    shift_one,
    up_weight,
    up_bias,
    down_weight,
    down_bias,
    gain_two,
    shift_two,
    cotangent,
):
    move = Mover(batch_size, shards)
    heads = block_swap.shape[0]
    rows, dim = tokens.shape
    width = input_weight.shape[2]
    depth = width // heads
    hidden_own = up_weight.shape[1]
    piece = dim // PARTS
    batch_at, head_at = lax.axis_index("batch"), lax.axis_index("head")
    part = batch_at % PARTS
    part_bits = [(part >> i) & 1 for i in range(3)]
    head_bits = [(head_at >> i) & 1 for i in range(2)]
    blocks = SEQ_LEN // rows
    length = lax.dynamic_index_in_dim(lengths, head_at // blocks, 0, keepdims=False)
    block_at = head_at % blocks
    own_live = jnp.clip(length - block_at * rows, 0, rows)
    partner_live = jnp.clip(length - (blocks - 1 - block_at) * rows, 0, rows)

    input_piece = lax.dynamic_slice_in_dim(input_weight, part * piece, piece, 1)
    input_piece = jnp.concatenate([input_piece[1], input_piece[2], input_piece[0]], axis=1)
    input_column = move.column(input_piece)
    small = jnp.concatenate([input_bias.reshape(-1), block_swap.astype(F32)])
    small = jnp.stack([small] + move.column(small))
    partner = move.head(after(tokens, *input_column), 1)
    input_column = jnp.stack(input_column)
    input_pair = pair_of(input_column, move.low(input_column))
    input_high = move.high(input_pair)
    input_own = input_weight.transpose(0, 2, 1)
    up_own = after(up_weight, input_pair).T.reshape(PARTS, piece, dim)
    up_piece = lax.dynamic_index_in_dim(up_own, part, 0, keepdims=False)
    down_own = down_weight.reshape(PARTS, piece, dim)
    down_piece = lax.dynamic_index_in_dim(down_own, part, 0, keepdims=False)
    info = jnp.concatenate(
        [
            small[:, 2 * width :].reshape(-1).astype(jnp.int32),
            jnp.stack([own_live, partner_live, part, head_at]).astype(jnp.int32),
        ]
    )
    short_info = jnp.stack([own_live, part, head_at]).astype(jnp.int32)
    bias = jnp.concatenate(
        [jnp.zeros((shards, width), F32), small[:, width : 2 * width], small[:, :width]], axis=1
    )
    bias = jnp.broadcast_to(bias[:, None], (shards, 8, 3 * width))
    head_flips = [(0, head_bits[1]), (1, head_bits[0])]
    part_flips = [(2, part_bits[2]), (3, part_bits[1]), (4, part_bits[0])]
    up_bias_rel = exchange_bits(up_bias.reshape(2, 2, 2, 2, 2, piece), head_flips + part_flips)
    turned = up_bias_rel.swapaxes(2, 3)
    odd = part_bits[0] == 1
    near_bias = jnp.where(odd, turned, up_bias_rel)[:, :, :, :, 0]
    far_bias = jnp.where(odd, up_bias_rel, turned)[:, :, :, :, 1]
    up_bias_rel = jnp.stack([near_bias, far_bias], axis=2)
    up_bias_rel = up_bias_rel.reshape(shards, 2, 1, SPOTS * piece)
    out_parts = out_weight.reshape(shards, width, dim)
    vectors_one = stack8(out_bias, gain_one, shift_one)
    vectors_two = stack8(gain_one, shift_one, down_bias, gain_two, shift_two)
    vectors_back = stack8(gain_one)
    input_high, partner = all_after(
        (input_high, partner), info, bias, up_bias_rel, vectors_one, vectors_two, up_piece
    )
    input_near = four_of(input_pair, input_high)
    input_far = move.core(input_near)
    up_far = move.head(after(up_piece, input_high), 2)

    def attend_shards(first_shard, count, last, weights, carried):
        return attend(
            (heads, depth, first_shard, last),
            count,
            info,
            tokens,
            partner,
            bias,
            out_parts,
            vectors_one,
            weights,
            carried,
        )

    qkv_0, context_0, stats_0, total = attend_shards(0, 1, False, [input_own], [])
    up_ends = pair_of(up_piece, after(up_far, total))
    up_others = move.head(up_ends, 1)
    down_far = move.head(after(down_piece, total), 2)
    total, up_ends = all_after((total, up_ends))
    others = [input_near, input_far]
    qkv_1, context_1, stats_1, total = attend_shards(1, 2, False, others, [total])
    up_others, down_far = all_after((up_others, down_far), total)
    up_column = jnp.stack([up_others[0], up_ends[1], up_others[1]])
    up_low = move.low(up_column)
    down_ends = pair_of(down_piece, down_far)
    down_others = move.head(down_ends, 1)
    total, up_column, down_ends = all_after((total, up_column, down_ends))
    qkv_3, context, stats_3, rows_one, normed = attend_shards(
        3, 1, True, others, [total, context_0, context_1]
    )
    up_low, down_others = all_after((up_low, down_others), normed)
    up_pair = pair_of(up_column, up_low)
    up_high = move.high(up_pair)
    down_column = jnp.stack([down_others[0], down_ends[1], down_others[1]])
    down_low = move.low(down_column)
    up_high, down_low = all_after((up_high, down_low))
    up_near = four_of(up_pair, up_high)
    up_all = (up_own, up_near, move.core(up_near))
    down_pair = pair_of(down_column, down_low)
    down_high = move.high(down_pair)
    normed, down_pair = all_after((normed, down_pair))
    normed_received = move.core(normed)
    tokens_t, partner_t = (value.T for value in all_after((tokens, partner), normed))
    normed, tokens_t, partner_t = all_after((normed, tokens_t, partner_t))
    hidden_near, hidden_far, *slopes = feed_up(short_info, normed, up_all, up_bias_rel)
    hidden_received = move.core(hidden_far)
    down_near = four_of(down_pair, after(down_high, hidden_near))
    down_all = (down_own, down_near, move.core(down_near))
    mixed_out, grad_second, grad_branch, sums_two = feed_down(
        short_info, (hidden_near, hidden_far), down_all, rows_one, cotangent, vectors_two
    )

    branch_received = move.core(grad_branch)
    context_received = move.core(context)
    down_keep, down_send = row_grads(
        shards, hidden_near, hidden_received, grad_branch, branch_received, "down_grads"
    )
    down_low = move.low(down_send)
    pre_near, pre_far, up_bias_sums, grad_first, grad_proj, sums_one = feed_back(
        short_info,
        after(grad_branch, down_send),
        down_all,
        up_all,
        slopes,
        rows_one,
        grad_second,
        vectors_back,
    )
    pre_received = move.core(pre_far)
    proj_received = move.core(grad_proj)

    def core_sum(mine, received):
        both = mine.astype(F32) + received.astype(F32)
        return both[0::2], both[1::2].astype(BF16)

    def fold_low(keep, received):
        return keep[0] + received[0].astype(F32), (keep[1] + received[1].astype(F32)).astype(BF16)

    def fold_high(own, received):
        total = own + received.astype(F32)
        return total[0::2], total[1::2].astype(BF16)

    def fold_near(own, received):
        return own[0] + received[0].astype(F32), (own[1] + received[1].astype(F32)).astype(BF16)

    def fold_last(own, received):
        return move.settle(own + received.astype(F32))

    def back(grad, shard, weights, qkv, stats, carried):
        return attend_back(
            (heads, depth, shard, shard == 0, shards),
            info,
            tokens_t,
            partner_t,
            grad,
            out_parts,
            weights,
            qkv,
            stats,
            carried,
        )

    up_bias_grad = jnp.sum(up_bias_sums, axis=2).reshape(2, 2, 2, 2, 2, piece)
    turned = up_bias_grad.swapaxes(3, 4)
    near_bias = jnp.where(odd, turned, up_bias_grad)[:, :, 0]
    far_bias = jnp.where(odd, up_bias_grad, turned)[:, :, 1]
    up_bias_grad = jnp.stack([near_bias, far_bias], axis=4)
    up_bias_grad = exchange_bits(up_bias_grad, head_flips + part_flips).reshape(-1, dim)
    vectors_now = jnp.concatenate([sums_one[:3], sums_two[:3], up_bias_grad])

    own_rows, partner_rows, near_3, far_3, bias_3 = back(
        grad_proj, 3, others, qkv_3, stats_3, []
    )
    up_keep, up_send = row_grads(
        shards, pre_near, pre_received, after(normed, bias_3), normed_received, "up_grads"
    )
    up_low = move.low(up_send)
    down_mine, down_next = fold_low(down_keep, after(down_low, bias_3))
    down_high = move.high(down_next)
    out_keep, out_send = out_grads(
        short_info, after(grad_proj, up_send), proj_received, context, context_received
    )
    out_low = move.low(out_send)

    late_grad, vectors_now = all_after((grad_proj, vectors_now), up_send, out_send, down_next)
    own_rows, partner_rows, near_2, far_2, bias_2 = back(
        late_grad, 2, others, qkv_1, stats_1, [own_rows, partner_rows]
    )
    late_core = move.core(jnp.concatenate([far_2, far_3], axis=1))
    down_mine, down_next = fold_high(down_mine, after(down_high, bias_2))
    down_near = move.head(down_next, 1)
    out_mine = out_keep[0] + after(out_low, bias_2)[0].astype(F32)
    out_next = (out_keep[1] + after(out_low, bias_2)[1].astype(F32)).astype(BF16)
    out_high = move.high(out_next)

    own_rows, partner_rows, near_1, far_1, bias_1 = back(
        after(grad_proj, down_next, bias_2, out_next), 1, others, qkv_1, stats_1,
        [own_rows, partner_rows],
    )
    up_mine, up_next = fold_low(up_keep, after(up_low, bias_1))
    up_high = move.high(up_next)
    late_keep, late_next = core_sum(
        jnp.concatenate([near_2, near_3], axis=1), after(late_core, up_next)
    )
    late_low = move.low(late_next)
    down_mine, down_next = fold_near(down_mine, after(down_near, late_next))
    down_last = move.head(down_next, 2)
    out_next = (out_mine + after(out_high, down_next).astype(F32)).astype(BF16)
    out_near = move.head(out_next, 1)

    own_rows, partner_rows, near_0, far_0, bias_0 = back(
        after(grad_proj, up_next, late_next, down_next, out_next), 0, [input_own], qkv_0, stats_0,
        [own_rows, partner_rows],
    )
    early_core = move.core(jnp.concatenate([far_0, far_1], axis=1))
    bias_sums = jnp.concatenate([bias_0, bias_1, bias_2, bias_3])
    bias_sums = exchange_bits(bias_sums[:, 0].reshape(2, 2, 3, width), head_flips)
    bias_sums = bias_sums.reshape(shards, 3, width).transpose(1, 0, 2).reshape(3, dim)
    vectors = jnp.concatenate([vectors_now, bias_sums[2:], bias_sums[1:2]])
    hops = move.hops()

    def hop(value, sent, event):
        value = value + after(sent, event)
        return value, hops.pop(0)(value) if hops else None

    vectors_sent = hops.pop(0)(vectors)
    up_mine, up_next = fold_high(up_mine, after(up_high, bias_0))
    up_near = move.head(up_next, 1)
    late_mine, late_next = fold_low(late_keep, after(late_low, up_next))
    late_high = move.high(late_next)
    down_total = fold_last(down_mine, after(down_last, late_next))
    down_low = move.low(down_total)
    early_keep, early_next = core_sum(
        jnp.concatenate([near_0, near_1], axis=1), after(early_core, down_total)
    )
    early_low = move.low(early_next)
    vectors, vectors_sent = hop(vectors, vectors_sent, early_next)
    from_partner = move.head(after(partner_rows, early_next), 1)
    up_mine, up_next = fold_near(up_mine, after(up_near, vectors))
    up_last = move.head(up_next, 2)
    out_near = shards_swapped(after(out_near, up_next), shards, 1)
    out_next = (out_next.astype(F32) + out_near.astype(F32)).astype(BF16)
    out_last = move.head(out_next, 2)
    early_mine, early_next = fold_low(early_keep, after(early_low, out_next))
    early_high = move.high(early_next)
    down_pair = pair_of(down_total, after(down_low, early_next))
    down_high = move.high(down_pair)
    vectors, vectors_sent = hop(vectors, vectors_sent, down_pair)
    late_mine = late_mine + after(late_high, vectors).astype(F32)
    early_mine = early_mine + after(early_high, vectors).astype(F32)
    input_next = jnp.stack([early_mine[1], late_mine[1]]).astype(BF16)
    input_near = move.head(input_next, 1)
    up_total = fold_last(up_mine, after(up_last, input_next))
    vectors, vectors_sent = hop(vectors, vectors_sent, up_total)
    down_done = four_of(down_pair, after(down_high, vectors))
    down_far = move.core(down_done)
    input_mine, input_next = fold_near(
        jnp.stack([early_mine[0], late_mine[0]]), after(input_near, down_done)
    )
    input_last = move.head(input_next, 2)
    vectors, vectors_sent = hop(vectors, vectors_sent, input_next)
    input_total = fold_last(input_mine, after(input_last, vectors))
    input_low = move.low(input_total)
    out_last, from_partner = all_after((out_last, from_partner), input_total)
    out_last = shards_swapped(out_last, shards, 2)
    out_total = move.settle(out_next.astype(F32) + out_last.astype(F32))
    up_total = jnp.concatenate([up_total, out_total], axis=1)
    up_low = move.low(up_total)
    while vectors_sent is not None:
        vectors, vectors_sent = hop(vectors, vectors_sent, up_total)
    input_pair = pair_of(input_total, after(input_low, vectors))
    input_high = move.high(input_pair)
    up_pair = pair_of(up_total, after(up_low, input_pair))
    up_high = move.high(up_pair)
    down_done = (down_done, after(down_far, up_pair))
    input_done = four_of(input_pair, after(input_high, up_pair))
    input_done = (input_done, move.core(input_done))
    up_done = four_of(up_pair, after(up_high, input_done[0]))
    up_done = (up_done, move.core(up_done))
    grad_tokens = grad_first + own_rows + from_partner.astype(F32)

    grad_input_bias = lax.dynamic_slice_in_dim(vectors[10:12], head_at * width, width, 1)
    grad_up_bias = lax.dynamic_slice_in_dim(
        vectors[6:10].reshape(-1), head_at * hidden_own, hidden_own
    )

    grad_down = pl.pallas_call(
        settle_down_kernel,
        in_specs=[SMEM] + [whole(4, piece, dim)] * 2,
        out_shape=shape((PARTS, piece, dim), F32),
        compiler_params=PARAMS,
        name="settle_down",
    )(short_info, *down_done)
    grad_up, grad_out = pl.pallas_call(
        settle_up_kernel,
        in_specs=[SMEM] + [whole(4, piece, dim + shards * width)] * 2,
        out_shape=[shape((dim, hidden_own), F32), shape((shards, width, dim), F32)],
        scratch_shapes=[pltpu.VMEM((PARTS, piece, dim), F32)] * 2,
        compiler_params=PARAMS,
        name="settle_up",
    )(short_info, *up_done)
    grad_input_weight = pl.pallas_call(
        settle_input_kernel,
        in_specs=[SMEM] + [whole(4, piece, 3 * width)] * 2,
        out_shape=shape((3, width, dim), F32),
        scratch_shapes=[pltpu.VMEM((PARTS, piece, 3 * width), F32)],
        compiler_params=PARAMS,
        name="settle_input",
    )(short_info, *input_done)
    return (
        mixed_out,
        grad_tokens,
        grad_input_weight.transpose(0, 2, 1),
        grad_input_bias,
        grad_out.reshape(dim, dim),
        vectors[0],
        vectors[1],
        vectors[2],
        grad_up,
        grad_up_bias,
        grad_down.reshape(hidden_own, dim),
        vectors[3],
        vectors[4],
        vectors[5],
    )


def solution(mesh):
    rows_spec = P(("batch", "head"), None)
    placed = (
        rows_spec,
        P("batch"),
        P("head"),
        P(None, None, "head"),
        P(None, "head"),
        P(),
        P(),
        P(),
        P(),
        P(None, "head"),
        P(),
        P("head", None),
        P(),
        P(),
        P(),
        rows_spec,
    )
    return jax.shard_map(
        functools.partial(local, mesh.shape["batch"], mesh.shape["head"]),
        mesh=mesh,
        in_specs=placed,
        out_specs=(
            rows_spec,
            rows_spec,
            P(None, None, "head"),
            P(None, "head"),
            P(),
            P(),
            P(),
            P(),
            P(None, "head"),
            P("head"),
            P("head", None),
            P(),
            P(),
            P(),
        ),
        check_vma=False,
    )
```

```python
import functools

import jax
import jax.numpy as jnp
from jax import lax
from jax.experimental import pallas as pl
from jax.experimental.pallas import tpu as pltpu
from jax.sharding import PartitionSpec as P

SEQ_LEN = 1024
EPSILON = 1e-05
F32 = jnp.float32
BF16 = jnp.bfloat16
VMEM_LIMIT = 44 * 1024 * 1024
PARAMS = pltpu.CompilerParams(vmem_limit_bytes=VMEM_LIMIT)
CORE = 1
PARTS = 8
SPOTS = 4


def dot(left_side, right_side, left_dim=1, right_dim=0):
    return lax.dot_general(
        left_side,
        right_side,
        (((left_dim,), (right_dim,)), ((), ())),
        preferred_element_type=F32,
    )


def unit_parts(values):
    centred = values - jnp.mean(values, axis=-1, keepdims=True)
    inverse = lax.rsqrt(jnp.mean(centred * centred, axis=-1, keepdims=True) + EPSILON)
    return centred * inverse, inverse


def norm_back(grad_rows, unit_rows, inverse, gain_row):
    scaled = grad_rows * gain_row
    return inverse * (
        scaled
        - jnp.mean(scaled, axis=-1, keepdims=True)
        - unit_rows * jnp.mean(scaled * unit_rows, axis=-1, keepdims=True)
    )


def column_sum(values):
    return jnp.sum(values, axis=0, keepdims=True)


def gelu_parts(inner):
    below = 0.5 + 0.5 * lax.erf(inner * 0.7071067811865476)
    bell = jnp.exp(inner * inner * -0.5) * 0.3989422804014327
    return inner * below, below + inner * bell


def row_chunks(rows, step):
    return [slice(i, i + step) for i in range(0, rows, step)]


def eight_sum(values):
    return sum(values[cut] for cut in row_chunks(values.shape[0], 8))


def lane_pick(values, depth):
    lane = lax.broadcasted_iota(jnp.int32, (1, len(values) * depth), 1)
    picked = jnp.full(lane.shape, values[0], jnp.int32)
    for j in range(1, len(values)):
        picked = jnp.where(lane >= j * depth, values[j], picked)
    return picked


def place_of(part, half, spot):
    seen = part ^ half
    core = seen & 1
    low, high = 2 + 2 * core, 4 - 2 * core
    return seen ^ (low * (spot & 1) + high * (spot >> 1))


class Info:
    def __init__(self, ref, heads, shards):
        self.ref, self.heads, self.base = ref, heads, heads * shards

    def swaps(self, shard):
        return [self.ref[shard * self.heads + j] for j in range(self.heads)]

    own_live = property(lambda self: self.ref[self.base])
    partner_live = property(lambda self: self.ref[self.base + 1])
    part = property(lambda self: self.ref[self.base + 2])
    head_at = property(lambda self: self.ref[self.base + 3])


def gathered(part, near, far, scratch):
    for spot in range(SPOTS):
        scratch[place_of(part, 0, spot)] = near[spot, 0]
        scratch[place_of(part, 1, spot)] = far[spot, 0]
    return scratch[...].reshape(-1, scratch.shape[2])


def attend_kernel(setting, info_ref, tokens, partner, bias, out_weight, vectors, *refs):
    heads, depth, first_shard, last = setting
    refs = list(refs)
    if first_shard == 0:
        turned = refs.pop(0)
        total_in = None
    else:
        near, far, total_in = refs[:3]
        del refs[:3]
    earlier = []
    if last:
        earlier = refs[:2]
        del refs[:2]
    if first_shard:
        del refs[:2]
    qkv_out, context_out, stats_out = refs[:3]
    step = pl.program_id(0)
    shard = first_shard + step
    info = Info(info_ref, heads, out_weight.shape[0])
    if first_shard:
        weight = gathered(info.part, near, far, refs.pop())
    total = refs.pop()
    swaps = info.swaps(shard)
    rows, dim = tokens.shape
    width = heads * depth
    x, xp = tokens[...], partner[...]
    if first_shard:
        own = dot(x, weight)
        other = dot(xp, weight[:, : 2 * width])
    else:
        kv_rows = jnp.concatenate([turned[1], turned[2]], axis=0)
        own = jnp.concatenate([dot(x, kv_rows, 1, 1), dot(x, turned[0], 1, 1)], axis=1)
        other = dot(xp, kv_rows, 1, 1)
    swapped = lane_pick(swaps + swaps, depth) == 1
    bias_row = bias[0, 0:1]
    kv, q = [], []
    for cut in row_chunks(rows, 32):
        mine = own[cut] + bias_row
        theirs = other[cut] + bias_row[:, : 2 * width]
        kv.append(jnp.where(swapped, theirs, mine[:, : 2 * width]).astype(BF16))
        q.append(mine[:, 2 * width :].astype(BF16) * (depth**-0.5))
    kv, q = jnp.concatenate(kv, axis=0), jnp.concatenate(q, axis=0)
    qkv_out[0, :, : 2 * width] = kv
    qkv_out[0, :, 2 * width :] = q
    stats = []
    pieces = []
    for j in range(heads):
        head = slice(j * depth, (j + 1) * depth)
        live = jnp.where(swaps[j] == 1, info.partner_live, info.own_live)
        anyone = jnp.where(live > 0, 1.0, 0.0).astype(F32)
        scores = dot(kv[:, head], q[:, head], 1, 1)
        masked, most = [], None
        for cut in row_chunks(rows, 32):
            index = cut.start + lax.broadcasted_iota(jnp.int32, (32, 1), 0)
            part = jnp.where(index < live, scores[cut], -1e30)
            masked.append(part)
            for tile in row_chunks(32, 8):
                most = part[tile] if most is None else jnp.maximum(most, part[tile])
        largest = jnp.max(most, axis=0, keepdims=True)
        largest = jnp.where(anyone > 0.5, largest, 0.0)
        total_rows = None
        for part in masked:
            weights = eight_sum(jnp.exp(part - largest))
            total_rows = weights if total_rows is None else total_rows + weights
        stat = largest + jnp.log(column_sum(total_rows) + (1.0 - anyone))
        mixing = [jnp.exp(part - stat).astype(BF16) for part in masked]
        stats.append(stat)
        values = kv[:, width + j * depth : width + (j + 1) * depth]
        pieces.append(dot(values, jnp.concatenate(mixing, axis=0), 0, 0))
    context = jnp.concatenate(pieces, axis=0).T.astype(BF16)
    stats_out[0] = jnp.concatenate(stats + [jnp.zeros((8 - heads, rows), F32)], axis=0)
    projected = dot(context, out_weight[info.head_at ^ shard])
    if not last:
        context_out[0] = context

        @pl.when(step == 0)
        def first():
            total[...] = projected if total_in is None else total_in[...] + projected

        @pl.when(step > 0)
        def later():
            total[...] += projected

        return

    context_out[...] = jnp.concatenate(
        [ref[q] for ref in earlier for q in range(ref.shape[0])] + [context], axis=1
    )
    rows_out, normed_out, tokens_out, partner_out = refs[3:]
    tokens_out[...] = x.T
    partner_out[...] = xp.T
    for cut in row_chunks(rows, 16):
        values = x[cut].astype(F32) + ((total_in[cut] + projected[cut]) + vectors[0:1])
        rows_out[cut] = values
        unit, _ = unit_parts(values)
        normed_out[cut] = (unit * vectors[1:2] + vectors[2:3]).astype(BF16)


def tiles_of(part, own, near, far, run):
    @pl.when(pl.program_id(0) == 0)
    def mine():
        run(
            *(
                jnp.concatenate([own[place_of(part, half, spot)] for spot in range(SPOTS)], axis=0)
                for half in range(2)
            )
        )

    @pl.when(pl.program_id(0) > 0)
    def other():
        run(*(ref[:, 0].reshape(-1, ref.shape[3]) for ref in (near, far)))


def add_up(total, *partials):
    @pl.when(pl.program_id(0) == 0)
    def start():
        total[...] = sum(partials[1:], partials[0])

    @pl.when(pl.program_id(0) > 0)
    def later():
        total[...] = sum(partials, total[...])


def at_end(run):
    pl.when(pl.program_id(0) == pl.num_programs(0) - 1)(run)


def eight_rows(*rows):
    width = rows[0].shape[1]
    return jnp.concatenate([*rows, jnp.zeros((8 - len(rows), width), F32)], axis=0)


def feed_up_kernel(info, normed, own, near, far, bias, *outs):
    shard = info[2] ^ pl.program_id(0)

    def run(*tiles):
        for half, tile in enumerate(tiles):
            places = [place_of(info[1], half, spot) for spot in range(SPOTS)]
            bias_row = jnp.concatenate([bias[shard, place] for place in places], axis=1)
            pre = dot(normed[...], tile, 1, 1)
            for cut in row_chunks(pre.shape[0], 32):
                hidden, slope = gelu_parts(pre[cut] + bias_row)
                outs[half][cut] = hidden.astype(BF16)
                outs[half + 2][cut] = slope

    tiles_of(info[1], own, near, far, run)


def feed_down_kernel(
    info,
    near_hidden,
    far_hidden,
    own,
    near,
    far,
    rows_in,
    cotangent,
    vectors,
    mixed_out,
    second_out,
    grad_out,
    sums_out,
    total,
):
    def run(near_tile, far_tile):
        add_up(total, dot(near_hidden[...], near_tile), dot(far_hidden[...], far_tile))

    tiles_of(info[1], own, near, far, run)

    @at_end
    def finish():
        sums = [jnp.zeros((8, rows_in.shape[1]), F32)] * 3
        for cut in row_chunks(rows_in.shape[0], 16):
            unit_one, _ = unit_parts(rows_in[cut])
            first_norm = unit_one * vectors[0:1] + vectors[1:2]
            unit, inverse = unit_parts(first_norm + (total[cut] + vectors[2:3]))
            index = cut.start + lax.broadcasted_iota(jnp.int32, (16, 1), 0)
            mask = jnp.where(index < info[0], 1.0, 0.0).astype(F32)
            mixed_out[cut] = ((unit * vectors[3:4] + vectors[4:5]) * mask).astype(BF16)
            incoming = cotangent[cut].astype(F32) * mask
            grad = norm_back(incoming, unit, inverse, vectors[3:4])
            second_out[cut] = grad
            low = grad.astype(BF16)
            grad_out[cut] = low
            more = (low.astype(F32), incoming * unit, incoming)
            sums = [a + eight_sum(b) for a, b in zip(sums, more)]
        sums_out[...] = eight_rows(*(column_sum(a) for a in sums))


def feed_back_kernel(
    info,
    grad_branch,
    down_own,
    down_near,
    down_far,
    up_own,
    up_near,
    up_far,
    near_slope,
    far_slope,
    rows_in,
    second_in,
    vectors,
    near_out,
    far_out,
    bias_out,
    first_out,
    proj_out,
    sums_out,
    total,
):
    def run_down(*tiles):
        for half, tile in enumerate(tiles):
            out, slope = (near_out, far_out)[half], (near_slope, far_slope)[half]
            grad = dot(grad_branch[...], tile, 1, 1)
            sums = jnp.zeros((8, grad.shape[1]), F32)
            for cut in row_chunks(grad.shape[0], 32):
                low = (grad[cut] * slope[cut]).astype(BF16)
                out[cut] = low
                sums = sums + eight_sum(low.astype(F32))
            sums = jnp.broadcast_to(column_sum(sums), sums.shape)
            width = bias_out.shape[3]
            for spot in range(SPOTS):
                row = sums[:, spot * width : (spot + 1) * width]
                bias_out[0, place_of(info[1], half, spot)] = row

    def run_up(near_tile, far_tile):
        add_up(total, dot(near_out[...], near_tile), dot(far_out[...], far_tile))

    tiles_of(info[1], down_own, down_near, down_far, run_down)
    tiles_of(info[1], up_own, up_near, up_far, run_up)

    @at_end
    def finish():
        sums = [jnp.zeros((8, rows_in.shape[1]), F32)] * 3
        for cut in row_chunks(rows_in.shape[0], 16):
            unit, inverse = unit_parts(rows_in[cut])
            grad_normed = second_in[cut] + total[cut]
            grad = norm_back(grad_normed, unit, inverse, vectors[0:1])
            first_out[cut] = grad
            low = grad.astype(BF16)
            proj_out[cut] = low
            more = (low.astype(F32), grad_normed * unit, grad_normed)
            sums = [a + eight_sum(b) for a, b in zip(sums, more)]
        sums_out[...] = eight_rows(*(column_sum(a) for a in sums))


def row_grads_kernel(mine, theirs, my_rows, their_rows, keep_out, send_out):
    value = dot(mine[...], my_rows[...], 0, 0) + dot(theirs[...], their_rows[...], 0, 0)
    value = value.reshape(SPOTS, -1, value.shape[1])
    for spot in range(SPOTS):
        out = (keep_out, send_out)[spot & 1]
        out[spot >> 1, 0] = value[spot].astype(out.dtype)


def out_grads_kernel(info, mine, theirs, my_context, their_context, keep_out, send_out, turned):
    value = 0.0
    for i, (grad, context) in enumerate(((mine, my_context), (theirs, their_context))):
        turned[i] = grad[...].T.reshape(turned.shape[1:])
        rows = [turned[i, place_of(info[1], 0, spot)] for spot in range(SPOTS)]
        value = value + dot(jnp.concatenate(rows, axis=0), context[...])
    value = value.reshape(SPOTS, -1, value.shape[1])
    for spot in range(SPOTS):
        out = (keep_out, send_out)[spot & 1]
        out[spot >> 1] = value[spot].astype(out.dtype)


def scatter_parts(part, value, chunks, near_out, far_out):
    chunks[...] = value.reshape(chunks.shape)
    for spot in range(SPOTS):
        near_out[spot, 0] = chunks[place_of(part, 0, spot)]
        far_out[spot, 0] = chunks[place_of(part, 1, spot)]


def attend_back_kernel(setting, info_ref, tokens_t, partner_t, grad_proj, out_weight, *refs):
    heads, depth, first_shard, carried, shards = setting
    refs = list(refs)
    if first_shard == 0:
        turned = refs.pop(0)
    near, far, qkv_in, stats_in = refs[:4]
    del refs[:4]
    if carried:
        own_in, partner_in = refs[:2]
        del refs[:2]
    own_out, partner_out, near_out, far_out, bias_out, total, weight_scratch, chunks = refs
    step = pl.program_id(0)
    shard = first_shard + step
    info = Info(info_ref, heads, shards)
    if first_shard:
        gathered(info.part, near, far, weight_scratch)
    else:
        width = turned.shape[1]

        @pl.when(shard == 0)
        def own_weight():
            rows_kv = jnp.concatenate([turned[1], turned[2], turned[0]], axis=0)
            weight_scratch[...] = rows_kv.T.reshape(weight_scratch.shape)

        @pl.when(shard > 0)
        def other_weight():
            gathered(info.part, near, far, weight_scratch)

    weight = weight_scratch[...].reshape(-1, weight_scratch.shape[2])
    swaps = info.swaps(shard)
    dim, rows = tokens_t.shape
    width = heads * depth
    grad = dot(grad_proj[...], out_weight[0], 1, 1).astype(BF16)
    k, v, q = (qkv_in[0, :, i * width : (i + 1) * width] for i in range(3))
    stats = stats_in[0]
    gq, gk, gv = [], [], []
    for j in range(heads):
        head = slice(j * depth, (j + 1) * depth)
        stat = stats[j : j + 1, :]
        live = jnp.where(swaps[j] == 1, info.partner_live, info.own_live)
        scores = dot(k[:, head], q[:, head], 1, 1)
        grad_mix = dot(v[:, head], grad[:, head], 1, 1)
        chances, shared = [], jnp.zeros((8, rows), F32)
        for cut in row_chunks(rows, 32):
            index = cut.start + lax.broadcasted_iota(jnp.int32, (32, 1), 0)
            part = jnp.exp(jnp.where(index < live, scores[cut] - stat, -10000.0))
            chances.append(part)
            shared = shared + eight_sum(part * grad_mix[cut])
        shared = column_sum(shared)
        mixing = jnp.concatenate([part.astype(BF16) for part in chances], axis=0)
        grad_scores = jnp.concatenate(
            [
                (part * (grad_mix[cut] - shared)).astype(BF16)
                for part, cut in zip(chances, row_chunks(rows, 32))
            ],
            axis=0,
        )
        gk.append(dot(grad_scores, q[:, head]))
        gv.append(dot(mixing, grad[:, head]))
        gq.append(dot(k[:, head], grad_scores, 0, 0))
    grad_q = (jnp.concatenate(gq, axis=0).T * (depth**-0.5)).astype(BF16)
    grad_kv = jnp.concatenate(gk + gv, axis=1).astype(BF16)
    swapped = lane_pick(swaps + swaps, depth) == 1
    nothing = jnp.zeros((), BF16)
    grad_own = jnp.concatenate([jnp.where(swapped, nothing, grad_kv), grad_q], axis=1)
    grad_far = jnp.where(swapped, grad_kv, nothing)
    own = dot(grad_own, weight, 1, 1)
    other = dot(grad_far, weight[:, : 2 * width], 1, 1)

    @pl.when(step == 0)
    def first():
        own_out[...] = own_in[...] + own if carried else own
        total[...] = partner_in[...] + other if carried else other

    @pl.when(step > 0)
    def later():
        own_out[...] += own
        total[...] += other

    @at_end
    def finish():
        partner_out[...] = total[...].astype(partner_out.dtype)

    grads = dot(tokens_t[...], grad_own)
    grads_kv = grads[:, : 2 * width] + dot(partner_t[...], grad_far)
    grads = jnp.concatenate([grads_kv, grads[:, 2 * width :]], axis=1).astype(BF16)
    chunks[...] = grads.reshape(chunks.shape)
    for spot in range(SPOTS):
        near_out[spot, 0] = chunks[place_of(info.part, 0, spot)]
        far_out[spot, 0] = chunks[place_of(info.part, 1, spot)]
    bias_out[0] = jnp.broadcast_to(
        jnp.concatenate(
            [column_sum(grad_kv.astype(F32)), column_sum(grad_q.astype(F32))], axis=1
        ),
        bias_out.shape[1:],
    )


def settle_down_kernel(info, near, far, out):
    for half, source in enumerate((near, far)):
        for spot in range(SPOTS):
            out[place_of(info[1], half, spot)] = source[spot].astype(F32)


def settle_up_kernel(info, near, far, up_out, out_out, up_scratch, out_scratch):
    dim = up_out.shape[0]
    for half, source in enumerate((near, far)):
        for spot in range(SPOTS):
            place = place_of(info[1], half, spot)
            value = source[spot].astype(F32)
            up_scratch[place] = value[:, :dim]
            out_scratch[place] = value[:, dim:]
    up_out[...] = up_scratch[...].reshape(-1, dim).T
    shards = out_out.shape[0]
    turned = out_scratch[...].reshape(-1, dim).T.reshape(shards, -1, dim)
    for q in range(shards):
        out_out[info[2] ^ q] = turned[q]


def settle_input_kernel(info, near, far, out, scratch):
    width = out.shape[1]
    for half, source in enumerate((near, far)):
        for spot in range(SPOTS):
            scratch[place_of(info[1], half, spot)] = source[spot].astype(F32)
    turned = scratch[...].reshape(-1, scratch.shape[2]).T
    for i in range(3):
        out[(i + 1) % 3] = turned[i * width : (i + 1) * width]


def shape(dims, dtype):
    return jax.ShapeDtypeStruct(dims, dtype)


def whole(*dims):
    return pl.BlockSpec(dims, lambda *_: (0,) * len(dims))


def cost(flops, moved, slow=0):
    return pl.CostEstimate(flops=flops, bytes_accessed=moved, transcendentals=slow)


SMEM = pl.BlockSpec(memory_space=pltpu.SMEM)


def gathered_specs(near, first_shard):
    spots, _, piece, lanes = near.shape
    return [pl.BlockSpec((spots, 1, piece, lanes), lambda s: (0, s + first_shard - 1, 0, 0))] * 2


def attend(
    setting, count, info, tokens, partner, bias, out_weight, vectors, weights, carried, so_far
):
    heads, depth, first_shard, last = setting
    rows, dim = tokens.shape
    shards, width, _ = out_weight.shape
    lanes = 3 * width
    scratch = []
    if first_shard == 0:
        weight_specs = [whole(3, width, dim)]
    else:
        weight_specs = gathered_specs(weights[0], first_shard)
        scratch = [pltpu.VMEM((PARTS, dim // PARTS, lanes), BF16)]
    out_specs = [
        pl.BlockSpec((1, rows, lanes), lambda s: (s + first_shard, 0, 0)),
        whole(rows, dim) if last else pl.BlockSpec((1, rows, width), lambda s: (s, 0, 0)),
        pl.BlockSpec((1, 8, rows), lambda s: (s + first_shard, 0, 0)),
    ]
    out_shape = [
        shape((shards, rows, lanes), BF16),
        shape((rows, dim) if last else (count, rows, width), BF16),
        shape((shards, 8, rows), F32),
    ]
    fixed = 6 + len(weights) + len(carried)
    if last:
        out_specs += [whole(rows, dim)] * 2 + [whole(dim, rows)] * 2
        out_shape += [shape((rows, dim), F32), shape((rows, dim), BF16)]
        out_shape += [shape((dim, rows), BF16)] * 2
        scratch = [pltpu.VMEM((8, 128), F32)] + scratch
    else:
        out_specs.append(whole(rows, dim))
        out_shape.append(shape((rows, dim), F32))
    return pl.pallas_call(
        functools.partial(attend_kernel, setting),
        grid=(count,),
        in_specs=[
            SMEM,
            whole(rows, dim),
            whole(rows, dim),
            pl.BlockSpec((1, 8, lanes), lambda s: (s + first_shard, 0, 0)),
            whole(shards, width, dim),
            whole(8, dim),
        ]
        + weight_specs
        + [whole(*value.shape) for value in carried]
        + [pl.BlockSpec(memory_space=pl.ANY)] * len(so_far),
        out_specs=out_specs,
        out_shape=out_shape,
        scratch_shapes=scratch,
        input_output_aliases={fixed + i: (0, 2)[i] for i in range(len(so_far))},
        compiler_params=PARAMS,
        cost_estimate=cost(
            count * (3 * rows * dim * dim + 4 * rows * rows * dim),
            count * 6 * rows * dim,
            count * heads * rows * rows,
        ),
        name="attend",
    )(info, tokens, partner, bias, out_weight, vectors, *weights, *carried, *so_far)


def feed_specs(near):
    spots, _, piece, lanes = near.shape
    other = pl.BlockSpec(
        (spots, 1, piece, lanes), lambda q: (0, jnp.maximum(q - 1, 0), 0, 0)
    )
    return [whole(PARTS, piece, lanes), other, other]


def feed_up(info, normed, weight, bias):
    rows, dim = normed.shape
    near = weight[1]
    shards = near.shape[1] + 1
    tile = SPOTS * near.shape[2]
    columns = pl.BlockSpec((rows, tile), lambda q: (0, q))
    return pl.pallas_call(
        feed_up_kernel,
        grid=(shards,),
        in_specs=[
            SMEM,
            whole(rows, dim),
            *feed_specs(near),
            whole(*bias.shape),
        ],
        out_specs=[columns] * 4,
        out_shape=[shape((rows, shards * tile), BF16)] * 2
        + [shape((rows, shards * tile), F32)] * 2,
        compiler_params=PARAMS,
        cost_estimate=cost(4 * rows * dim * tile * shards, 30 * rows * dim, rows * dim * 8),
        name="feed_up",
    )(info, normed, *weight, bias)


def feed_down(info, hidden, weight, rows_one, cotangent, vectors):
    rows, dim = rows_one.shape
    near = weight[1]
    shards = near.shape[1] + 1
    tile = SPOTS * near.shape[2]
    columns = pl.BlockSpec((rows, tile), lambda q: (0, q))
    return pl.pallas_call(
        feed_down_kernel,
        grid=(shards,),
        in_specs=[
            SMEM,
            columns,
            columns,
            *feed_specs(near),
            whole(rows, dim),
            whole(rows, dim),
            whole(8, dim),
        ],
        out_specs=[whole(rows, dim)] * 3 + [whole(8, dim)],
        out_shape=[
            shape((rows, dim), BF16),
            shape((rows, dim), F32),
            shape((rows, dim), BF16),
            shape((8, dim), F32),
        ],
        scratch_shapes=[pltpu.VMEM((rows, dim), F32)],
        compiler_params=PARAMS,
        cost_estimate=cost(4 * rows * dim * tile * shards, 20 * rows * dim),
        name="feed_down",
    )(info, *hidden, *weight, rows_one, cotangent, vectors)


def feed_back(info, grad_branch, down, up, slopes, rows_one, grad_second, vectors):
    rows, dim = rows_one.shape
    near = up[1]
    shards = near.shape[1] + 1
    tile = SPOTS * near.shape[2]
    columns = pl.BlockSpec((rows, tile), lambda q: (0, q))
    return pl.pallas_call(
        feed_back_kernel,
        grid=(shards,),
        in_specs=[
            SMEM,
            whole(rows, dim),
            *feed_specs(near),
            *feed_specs(near),
            columns,
            columns,
            whole(rows, dim),
            whole(rows, dim),
            whole(8, dim),
        ],
        out_specs=[
            columns,
            columns,
            pl.BlockSpec((1, PARTS, 8, near.shape[2]), lambda q: (q, 0, 0, 0)),
            whole(rows, dim),
            whole(rows, dim),
            whole(8, dim),
        ],
        out_shape=[
            shape((rows, shards * tile), BF16),
            shape((rows, shards * tile), BF16),
            shape((shards, PARTS, 8, near.shape[2]), F32),
            shape((rows, dim), F32),
            shape((rows, dim), BF16),
            shape((8, dim), F32),
        ],
        scratch_shapes=[pltpu.VMEM((rows, dim), F32)],
        compiler_params=PARAMS,
        cost_estimate=cost(8 * rows * dim * tile * shards, 40 * rows * dim),
        name="feed_back",
    )(info, grad_branch, *down, *up, *slopes, rows_one, grad_second, vectors)


def row_grads(shards, mine, theirs, my_rows, their_rows, name):
    rows, dim = my_rows.shape
    tile = mine.shape[1] // shards
    piece = tile // SPOTS
    columns = pl.BlockSpec((rows, tile), lambda q: (0, q))
    out = pl.BlockSpec((2, 1, piece, dim), lambda q: (0, q, 0, 0))
    return pl.pallas_call(
        row_grads_kernel,
        grid=(shards,),
        in_specs=[columns, columns, whole(rows, dim), whole(rows, dim)],
        out_specs=[out, out],
        out_shape=[shape((2, shards, piece, dim), F32), shape((2, shards, piece, dim), BF16)],
        compiler_params=PARAMS,
        cost_estimate=cost(4 * rows * dim * tile * shards, 20 * rows * dim),
        name=name,
    )(mine, theirs, my_rows, their_rows)


def out_grads(info, mine, theirs, my_context, their_context):
    rows, dim = mine.shape
    piece = dim // PARTS
    return pl.pallas_call(
        out_grads_kernel,
        in_specs=[SMEM] + [whole(rows, dim)] * 4,
        out_specs=[whole(2, piece, dim)] * 2,
        out_shape=[shape((2, piece, dim), F32), shape((2, piece, dim), BF16)],
        scratch_shapes=[pltpu.VMEM((2, PARTS, piece, rows), BF16)],
        compiler_params=PARAMS,
        cost_estimate=cost(2 * rows * dim * dim, 10 * rows * dim),
        name="out_grads",
    )(info, mine, theirs, my_context, their_context)


def attend_back(
    setting, info, tokens_t, partner_t, grad_proj, out_weight, own, near, far, qkvs, stats, carried
):
    heads, depth, first_shard, count, shards = setting
    dim, rows = tokens_t.shape
    width = heads * depth
    lanes = 3 * width
    piece = dim // PARTS
    head_spot = heads * shards + 3
    own_specs = [] if first_shard else [whole(3, width, dim)]
    kernel = functools.partial(
        attend_back_kernel, (heads, depth, first_shard, bool(carried), shards)
    )

    def other(s, info):
        return (0, jnp.maximum(s + first_shard - 1, 0), 0, 0)

    parts_out = pl.BlockSpec((SPOTS, 1, piece, lanes), lambda s, info: (0, s, 0, 0))
    return pl.pallas_call(
        kernel,
        grid_spec=pltpu.PrefetchScalarGridSpec(
            num_scalar_prefetch=1,
            grid=(count,),
            in_specs=[
                whole(dim, rows),
                whole(dim, rows),
                whole(rows, dim),
                pl.BlockSpec(
                    (1, width, dim), lambda s, info: (info[head_spot] ^ (s + first_shard), 0, 0)
                ),
            ]
            + own_specs
            + [pl.BlockSpec((SPOTS, 1, piece, lanes), other)] * 2
            + [
                pl.BlockSpec((1, rows, lanes), lambda s, info: (s + first_shard, 0, 0)),
                pl.BlockSpec((1, 8, rows), lambda s, info: (s + first_shard, 0, 0)),
            ]
            + [whole(rows, dim)] * len(carried),
            out_specs=[
                whole(rows, dim),
                whole(rows, dim),
                parts_out,
                parts_out,
                pl.BlockSpec((1, 8, lanes), lambda s, info: (s, 0, 0)),
            ],
            scratch_shapes=[
                pltpu.VMEM((rows, dim), F32),
                pltpu.VMEM((PARTS, piece, lanes), BF16),
                pltpu.VMEM((PARTS, piece, lanes), BF16),
            ],
        ),
        out_shape=[
            shape((rows, dim), F32),
            shape((rows, dim), F32 if first_shard else BF16),
            shape((SPOTS, count, piece, lanes), BF16),
            shape((SPOTS, count, piece, lanes), BF16),
            shape((count, 8, lanes), F32),
        ],
        compiler_params=PARAMS,
        cost_estimate=cost(
            count * (6 * rows * dim * dim + 10 * rows * rows * dim),
            count * 8 * rows * dim,
            count * heads * rows * rows,
        ),
        name="attend_back",
    )(info, tokens_t, partner_t, grad_proj, out_weight, *own, near, far, qkvs, stats, *carried)


class Mover:
    def __init__(self, batch_size, shards):
        self.batch_size, self.shards = batch_size, shards

    def batch(self, value, mask_of):
        perm = [(i, i ^ mask_of(i)) for i in range(self.batch_size)]
        return lax.ppermute(value, "batch", perm)

    def core(self, value):
        return self.batch(value, lambda i: CORE)

    def low(self, value):
        return self.batch(value, lambda i: 4 if i & 1 else 2)

    def high(self, value):
        return self.batch(value, lambda i: 2 if i & 1 else 4)

    def head(self, value, mask):
        return lax.ppermute(value, "head", [(i, i ^ mask) for i in range(self.shards)])

    def along(self, values, first=1):
        return [self.head(value, q) for q, value in enumerate(values, first)]

    def column(self, piece):
        return self.along([piece] * (self.shards - 1))

    def settle(self, total):
        total = total.astype(BF16)
        mask = PARTS
        while mask < self.batch_size:
            other = self.batch(total, lambda i, mask=mask: mask)
            total = (total.astype(F32) + other.astype(F32)).astype(BF16)
            mask *= 2
        return total

    def shards_in_order(self, value, mask):
        first = value.shape[0] - 2 * self.shards
        rows = [first + base + (q ^ mask) for base in (0, self.shards) for q in range(self.shards)]
        return jnp.concatenate([value[:first]] + [value[row : row + 1] for row in rows])

    def hops(self):
        steps, mask = [], 1
        while mask < self.batch_size:
            steps.append(lambda value, mask=mask: self.batch(value, lambda i: mask))
            mask *= 2
        mask = 1
        while mask < self.shards:
            steps.append(lambda value, mask=mask: self.shards_in_order(self.head(value, mask), mask))
            mask *= 2
        return steps


def after(value, *events):
    return lax.optimization_barrier((value, *events))[0]


def all_after(values, *events):
    return lax.optimization_barrier((*values, *events))[: len(values)]


def pair_of(first, second):
    return jnp.stack([first, second])


def four_of(pair, received):
    return jnp.concatenate([pair, received])


def shards_swapped(value, shards, mask):
    width = value.shape[1] // shards
    blocks = [value[:, (q ^ mask) * width : ((q ^ mask) + 1) * width] for q in range(shards)]
    return jnp.concatenate(blocks, axis=1)


def stack8(*rows):
    rows = [row.reshape(1, -1) for row in rows]
    return jnp.concatenate(rows + [jnp.zeros((8 - len(rows), rows[0].shape[1]), F32)], axis=0)


def local(
    batch_size,
    shards,
    tokens,
    lengths,
    block_swap,
    input_weight,
    input_bias,
    out_weight,
    out_bias,
    gain_one,
    shift_one,
    up_weight,
    up_bias,
    down_weight,
    down_bias,
    gain_two,
    shift_two,
    cotangent,
):
    move = Mover(batch_size, shards)
    heads = block_swap.shape[0]
    rows, dim = tokens.shape
    width = input_weight.shape[2]
    depth = width // heads
    hidden_own = up_weight.shape[1]
    piece = dim // PARTS
    batch_at, head_at = lax.axis_index("batch"), lax.axis_index("head")
    part = batch_at % PARTS
    blocks = SEQ_LEN // rows
    length = lax.dynamic_index_in_dim(lengths, head_at // blocks, 0, keepdims=False)
    block_at = head_at % blocks
    own_live = jnp.clip(length - block_at * rows, 0, rows)
    partner_live = jnp.clip(length - (blocks - 1 - block_at) * rows, 0, rows)

    input_piece = lax.dynamic_slice_in_dim(input_weight, part * piece, piece, 1)
    input_piece = jnp.concatenate([input_piece[1], input_piece[2], input_piece[0]], axis=1)
    input_column = move.column(input_piece)
    small = jnp.concatenate([input_bias.reshape(-1), block_swap.astype(F32)])
    small = jnp.stack([small] + move.column(small))
    partner = move.head(after(tokens, *input_column), 1)
    input_column = jnp.stack(input_column)
    input_low = move.low(input_column)
    input_own = input_weight.transpose(0, 2, 1)
    up_own = up_weight.T.reshape(PARTS, piece, dim)
    up_piece = lax.dynamic_index_in_dim(up_own, part, 0, keepdims=False)
    up_far = move.head(after(up_piece, input_column), 2)
    down_own = down_weight.reshape(PARTS, piece, dim)
    down_piece = lax.dynamic_index_in_dim(down_own, part, 0, keepdims=False)

    info = jnp.concatenate(
        [
            small[:, 2 * width :].reshape(-1).astype(jnp.int32),
            jnp.stack([own_live, partner_live, part, head_at]).astype(jnp.int32),
        ]
    )
    short_info = jnp.stack([own_live, part, head_at]).astype(jnp.int32)
    bias = jnp.concatenate(
        [jnp.zeros((shards, width), F32), small[:, width : 2 * width], small[:, :width]], axis=1
    )
    bias = jnp.broadcast_to(bias[:, None], (shards, 8, 3 * width))
    up_bias_parts = up_bias.reshape(shards, PARTS, 1, piece)
    out_parts = out_weight.reshape(shards, width, dim)
    vectors_one = stack8(out_bias, gain_one, shift_one)
    vectors_two = stack8(gain_one, shift_one, down_bias, gain_two, shift_two)
    vectors_back = stack8(gain_one)
    input_low, up_far = all_after((input_low, up_far), info, bias, vectors_one, vectors_two)
    input_pair = pair_of(input_column, input_low)
    input_high = move.high(input_pair)
    up_ends = pair_of(up_piece, up_far)
    up_others = move.head(up_ends, 1)
    input_high, partner, up_others = all_after((input_high, partner, up_others))
    input_near = four_of(input_pair, input_high)
    input_far = move.core(input_near)
    up_column = jnp.stack([up_others[0], up_ends[1], up_others[1]])
    up_low = move.low(up_column)
    down_far = move.head(after(down_piece, up_others), 2)

    def attend_shards(first_shard, count, last, weights, carried, so_far):
        return attend(
            (heads, depth, first_shard, last),
            count,
            info,
            tokens,
            partner,
            bias,
            out_parts,
            vectors_one,
            weights,
            carried,
            so_far,
        )

    now = after(input_own, up_column)
    qkv, context_0, stats, total = attend_shards(0, 1, False, [now], [], [])
    others = [input_near, input_far]
    up_low, down_far = all_after((up_low, down_far), total)
    up_pair = pair_of(up_column, up_low)
    up_high = move.high(up_pair)
    down_ends = pair_of(down_piece, down_far)
    down_others = move.head(down_ends, 1)
    total, up_pair, down_ends = all_after((total, up_pair, down_ends))
    qkv, context_1, stats, total = attend_shards(1, 2, False, others, [total], [qkv, stats])
    up_high, down_others = all_after((up_high, down_others), total)
    up_near = four_of(up_pair, up_high)
    up_all = (up_own, up_near, move.core(up_near))
    down_column = jnp.stack([down_others[0], down_ends[1], down_others[1]])
    down_low = move.low(down_column)
    total, up_near, down_column = all_after((total, up_near, down_column))
    qkv, context, stats, rows_one, normed, tokens_t, partner_t = attend_shards(
        3, 1, True, others, [total, context_0, context_1], [qkv, stats]
    )
    normed_received = move.core(normed)
    context_received = move.core(context)
    down_pair = pair_of(down_column, after(down_low, normed))
    down_high = move.high(down_pair)
    normed, down_pair = all_after((normed, down_pair))
    hidden_near, hidden_far, *slopes = feed_up(short_info, normed, up_all, up_bias_parts)
    hidden_received = move.core(hidden_far)
    down_near = four_of(down_pair, after(down_high, hidden_near))
    down_all = (down_own, down_near, move.core(down_near))
    mixed_out, grad_second, grad_branch, sums_two = feed_down(
        short_info, (hidden_near, hidden_far), down_all, rows_one, cotangent, vectors_two
    )

    branch_received = move.core(grad_branch)
    pre_near, pre_far, up_bias_sums, grad_first, grad_proj, sums_one = feed_back(
        short_info, grad_branch, down_all, up_all, slopes, rows_one, grad_second, vectors_back
    )
    pre_received = move.core(pre_far)
    proj_received = move.core(grad_proj)
    down_keep, down_send = row_grads(
        shards,
        hidden_near,
        hidden_received,
        after(grad_branch, grad_proj),
        branch_received,
        "down_grads",
    )
    down_low = move.low(down_send)
    up_keep, up_send = row_grads(
        shards, pre_near, pre_received, after(normed, down_send), normed_received, "up_grads"
    )
    up_low = move.low(up_send)

    def core_sum(mine, received):
        both = mine.astype(F32) + received.astype(F32)
        return both[0::2], both[1::2].astype(BF16)

    def fold_low(keep, received):
        return keep[0] + received[0].astype(F32), (keep[1] + received[1].astype(F32)).astype(BF16)

    def fold_high(own, received):
        total = own + received.astype(F32)
        return total[0::2], total[1::2].astype(BF16)

    def fold_near(own, received):
        return own[0] + received[0].astype(F32), (own[1] + received[1].astype(F32)).astype(BF16)

    def fold_last(own, received):
        return move.settle(own + received.astype(F32))

    def back(grad, first_shard, carried):
        return attend_back(
            (heads, depth, first_shard, shards // 2, shards),
            info,
            tokens_t,
            partner_t,
            grad,
            out_parts,
            [] if first_shard else [input_own],
            *others,
            qkv,
            stats,
            carried,
        )

    own_rows, partner_rows, late_near, late_far, late_bias = back(
        after(grad_proj, up_send), shards // 2, []
    )
    late_core = move.core(late_far)
    down_mine, down_next = fold_low(down_keep, after(down_low, late_bias))
    down_high = move.high(down_next)
    out_keep, out_send = out_grads(
        short_info, after(grad_proj, down_next), proj_received, context, context_received
    )
    out_low = move.low(out_send)
    late_keep, late_next = core_sum(late_near, after(late_core, out_send))
    late_low = move.low(late_next)
    own_rows, partner_rows, early_near, early_far, early_bias = back(
        after(grad_proj, down_next, out_send, late_next), 0, [own_rows, partner_rows]
    )

    from_partner = move.head(partner_rows, 1)
    early_core = move.core(early_far)
    vectors = jnp.concatenate(
        [
            sums_one[:3],
            sums_two[:3],
            up_bias_sums[:, :, 0].reshape(shards, dim),
            jnp.pad(jnp.concatenate([early_bias, late_bias])[:, 0], ((0, 0), (0, dim - 3 * width))),
        ]
    )
    hops = move.hops()

    def hop(value, sent, event):
        value = value + after(sent, event)
        return value, hops.pop(0)(value) if hops else None

    up_mine, up_next = fold_low(up_keep, after(up_low, early_bias))
    up_high = move.high(up_next)
    down_mine, down_next = fold_high(down_mine, after(down_high, up_next))
    down_near = move.head(down_next, 1)
    late_mine, late_next = fold_low(late_keep, after(late_low, down_next))
    late_high = move.high(late_next)
    early_keep, early_next = core_sum(early_near, after(early_core, late_next))
    early_low = move.low(early_next)
    out_mine = out_keep[0] + after(out_low, early_next)[0].astype(F32)
    out_next = (out_keep[1] + after(out_low, early_next)[1].astype(F32)).astype(BF16)
    out_high = move.high(out_next)
    vectors_sent = hops.pop(0)(after(vectors, out_next))
    down_mine, down_next = fold_near(down_mine, after(down_near, out_next))
    down_last = move.head(down_next, 2)
    up_mine, up_next = fold_high(up_mine, after(up_high, down_next))
    up_near = move.head(up_next, 1)
    vectors, vectors_sent = hop(vectors, vectors_sent, up_next)
    late_mine = late_mine + after(late_high, vectors).astype(F32)
    early_mine, early_next = fold_low(early_keep, after(early_low, late_mine))
    early_high = move.high(early_next)
    out_next = (out_mine + after(out_high, early_next).astype(F32)).astype(BF16)
    out_near = move.head(out_next, 1)
    down_total = fold_last(down_mine, after(down_last, out_next))
    down_low = move.low(down_total)
    vectors, vectors_sent = hop(vectors, vectors_sent, down_total)
    up_mine, up_next = fold_near(up_mine, after(up_near, vectors))
    up_last = move.head(up_next, 2)
    early_mine = early_mine + after(early_high, up_next).astype(F32)
    input_next = jnp.stack([early_mine[1], late_mine[1]]).astype(BF16)
    input_near = move.head(input_next, 1)
    out_near = shards_swapped(after(out_near, input_next), shards, 1)
    out_next = (out_next.astype(F32) + out_near.astype(F32)).astype(BF16)
    out_last = move.head(out_next, 2)
    down_pair = pair_of(down_total, after(down_low, out_next))
    down_high = move.high(down_pair)
    vectors, vectors_sent = hop(vectors, vectors_sent, down_pair)
    grad_tokens = grad_first + own_rows + after(from_partner, vectors).astype(F32)
    up_total = fold_last(up_mine, after(up_last, grad_tokens))
    input_mine, input_next = fold_near(
        jnp.stack([early_mine[0], late_mine[0]]), after(input_near, up_total)
    )
    input_last = move.head(input_next, 2)
    out_last = shards_swapped(after(out_last, input_next), shards, 2)
    out_total = move.settle(out_next.astype(F32) + out_last.astype(F32))
    up_total = jnp.concatenate([up_total, out_total], axis=1)
    up_low = move.low(up_total)
    down_near = four_of(down_pair, after(down_high, up_total))
    down_done = (down_near, move.core(down_near))
    vectors, vectors_sent = hop(vectors, vectors_sent, down_near)
    input_total = fold_last(input_mine, after(input_last, vectors))
    input_low = move.low(input_total)
    up_pair = pair_of(up_total, after(up_low, input_total))
    up_high = move.high(up_pair)
    while vectors_sent is not None:
        vectors, vectors_sent = hop(vectors, vectors_sent, up_pair)
    input_pair = pair_of(input_total, after(input_low, up_pair, vectors))
    input_high = move.high(input_pair)
    grad_down = pl.pallas_call(
        settle_down_kernel,
        in_specs=[SMEM] + [whole(4, piece, dim)] * 2,
        out_shape=shape((PARTS, piece, dim), F32),
        compiler_params=PARAMS,
        name="settle_down",
    )(short_info, after(down_done[0], input_pair), down_done[1])
    up_done = four_of(up_pair, after(up_high, grad_down))
    up_done = (up_done, move.core(up_done))
    input_done = four_of(input_pair, after(input_high, up_done[0]))
    input_done = (input_done, move.core(input_done))
    grad_input_bias = jnp.stack([vectors[10, 2 * width : 3 * width], vectors[10, width : 2 * width]])
    grad_up_bias = vectors[6]
    grad_up, grad_out = pl.pallas_call(
        settle_up_kernel,
        in_specs=[SMEM] + [whole(4, piece, dim + shards * width)] * 2,
        out_shape=[shape((dim, hidden_own), F32), shape((shards, width, dim), F32)],
        scratch_shapes=[pltpu.VMEM((PARTS, piece, dim), F32)] * 2,
        compiler_params=PARAMS,
        name="settle_up",
    )(short_info, *up_done)
    grad_input_weight = pl.pallas_call(
        settle_input_kernel,
        in_specs=[SMEM] + [whole(4, piece, 3 * width)] * 2,
        out_shape=shape((3, width, dim), F32),
        scratch_shapes=[pltpu.VMEM((PARTS, piece, 3 * width), F32)],
        compiler_params=PARAMS,
        name="settle_input",
    )(short_info, *input_done)
    return (
        mixed_out,
        grad_tokens,
        grad_input_weight.transpose(0, 2, 1),
        grad_input_bias,
        grad_out.reshape(dim, dim),
        vectors[0],
        vectors[1],
        vectors[2],
        grad_up,
        grad_up_bias,
        grad_down.reshape(hidden_own, dim),
        vectors[3],
        vectors[4],
        vectors[5],
    )


def solution(mesh):
    rows_spec = P(("batch", "head"), None)
    placed = (
        rows_spec,
        P("batch"),
        P("head"),
        P(None, None, "head"),
        P(None, "head"),
        P(),
        P(),
        P(),
        P(),
        P(None, "head"),
        P(),
        P("head", None),
        P(),
        P(),
        P(),
        rows_spec,
    )
    return jax.shard_map(
        functools.partial(local, mesh.shape["batch"], mesh.shape["head"]),
        mesh=mesh,
        in_specs=placed,
        out_specs=(
            rows_spec,
            rows_spec,
            P(None, None, "head"),
            P(None, "head"),
            P(),
            P(),
            P(),
            P(),
            P(None, "head"),
            P("head"),
            P("head", None),
            P(),
            P(),
            P(),
        ),
        check_vma=False,
    )
```

```python
import functools

import jax
import jax.numpy as jnp
from jax import lax
from jax.experimental import pallas as pl
from jax.experimental.pallas import tpu as pltpu
from jax.sharding import PartitionSpec as P

SEQ_LEN = 1024
EPSILON = 1e-05
F32 = jnp.float32
BF16 = jnp.bfloat16
VMEM_LIMIT = 44 * 1024 * 1024
PARAMS = pltpu.CompilerParams(vmem_limit_bytes=VMEM_LIMIT)
CORE = 1
PARTS = 8
SPOTS = 4


def dot(left_side, right_side, left_dim=1, right_dim=0):
    return lax.dot_general(
        left_side,
        right_side,
        (((left_dim,), (right_dim,)), ((), ())),
        preferred_element_type=F32,
    )


def unit_parts(values):
    centred = values - jnp.mean(values, axis=-1, keepdims=True)
    inverse = lax.rsqrt(jnp.mean(centred * centred, axis=-1, keepdims=True) + EPSILON)
    return centred * inverse, inverse


def norm_back(grad_rows, unit_rows, inverse, gain_row):
    scaled = grad_rows * gain_row
    return inverse * (
        scaled
        - jnp.mean(scaled, axis=-1, keepdims=True)
        - unit_rows * jnp.mean(scaled * unit_rows, axis=-1, keepdims=True)
    )


def column_sum(values):
    return jnp.sum(values, axis=0, keepdims=True)


def gelu_parts(inner):
    below = 0.5 + 0.5 * lax.erf(inner * 0.7071067811865476)
    bell = jnp.exp(inner * inner * -0.5) * 0.3989422804014327
    return inner * below, below + inner * bell


def row_chunks(rows, step):
    return [slice(i, i + step) for i in range(0, rows, step)]


def eight_sum(values):
    return sum(values[cut] for cut in row_chunks(values.shape[0], 8))


def lane_pick(values, depth):
    lane = lax.broadcasted_iota(jnp.int32, (1, len(values) * depth), 1)
    picked = jnp.full(lane.shape, values[0], jnp.int32)
    for j in range(1, len(values)):
        picked = jnp.where(lane >= j * depth, values[j], picked)
    return picked


def place_of(part, half, spot):
    seen = part ^ half
    core = seen & 1
    low, high = 2 + 2 * core, 4 - 2 * core
    return seen ^ (low * (spot & 1) + high * (spot >> 1))


class Info:
    def __init__(self, ref, heads, shards):
        self.ref, self.heads, self.base = ref, heads, heads * shards

    def swaps(self, shard):
        return [self.ref[shard * self.heads + j] for j in range(self.heads)]

    own_live = property(lambda self: self.ref[self.base])
    partner_live = property(lambda self: self.ref[self.base + 1])
    part = property(lambda self: self.ref[self.base + 2])
    head_at = property(lambda self: self.ref[self.base + 3])


def gathered(part, near, far, scratch):
    for spot in range(SPOTS):
        scratch[place_of(part, 0, spot)] = near[spot, 0]
        scratch[place_of(part, 1, spot)] = far[spot, 0]
    return scratch[...].reshape(-1, scratch.shape[2])


def attend_kernel(setting, info_ref, tokens, partner, bias, out_weight, vectors, *refs):
    heads, depth, first_shard, last = setting
    refs = list(refs)
    if first_shard == 0:
        turned = refs.pop(0)
        total_in = None
    else:
        near, far, total_in = refs[:3]
        del refs[:3]
    earlier = []
    if last:
        earlier = refs[:2]
        del refs[:2]
    if first_shard:
        del refs[:2]
    qkv_out, context_out, stats_out = refs[:3]
    step = pl.program_id(0)
    shard = first_shard + step
    info = Info(info_ref, heads, out_weight.shape[0])
    if first_shard:
        weight = gathered(info.part, near, far, refs.pop())
    total = refs.pop()
    swaps = info.swaps(shard)
    rows, dim = tokens.shape
    width = heads * depth
    x, xp = tokens[...], partner[...]
    if first_shard:
        own = dot(x, weight)
        other = dot(xp, weight[:, : 2 * width])
    else:
        kv_rows = jnp.concatenate([turned[1], turned[2]], axis=0)
        own = jnp.concatenate([dot(x, kv_rows, 1, 1), dot(x, turned[0], 1, 1)], axis=1)
        other = dot(xp, kv_rows, 1, 1)
    swapped = lane_pick(swaps + swaps, depth) == 1
    bias_row = bias[0, 0:1]
    kv, q = [], []
    for cut in row_chunks(rows, 32):
        mine = own[cut] + bias_row
        theirs = other[cut] + bias_row[:, : 2 * width]
        kv.append(jnp.where(swapped, theirs, mine[:, : 2 * width]).astype(BF16))
        q.append(mine[:, 2 * width :].astype(BF16) * (depth**-0.5))
    kv, q = jnp.concatenate(kv, axis=0), jnp.concatenate(q, axis=0)
    qkv_out[0, :, : 2 * width] = kv
    qkv_out[0, :, 2 * width :] = q
    stats = []
    pieces = []
    for j in range(heads):
        head = slice(j * depth, (j + 1) * depth)
        live = jnp.where(swaps[j] == 1, info.partner_live, info.own_live)
        anyone = jnp.where(live > 0, 1.0, 0.0).astype(F32)
        scores = dot(kv[:, head], q[:, head], 1, 1)
        masked, most = [], None
        for cut in row_chunks(rows, 32):
            index = cut.start + lax.broadcasted_iota(jnp.int32, (32, 1), 0)
            part = jnp.where(index < live, scores[cut], -1e30)
            masked.append(part)
            for tile in row_chunks(32, 8):
                most = part[tile] if most is None else jnp.maximum(most, part[tile])
        largest = jnp.max(most, axis=0, keepdims=True)
        largest = jnp.where(anyone > 0.5, largest, 0.0)
        total_rows = None
        for part in masked:
            weights = eight_sum(jnp.exp(part - largest))
            total_rows = weights if total_rows is None else total_rows + weights
        stat = largest + jnp.log(column_sum(total_rows) + (1.0 - anyone))
        mixing = [jnp.exp(part - stat).astype(BF16) for part in masked]
        stats.append(stat)
        values = kv[:, width + j * depth : width + (j + 1) * depth]
        pieces.append(dot(values, jnp.concatenate(mixing, axis=0), 0, 0))
    context = jnp.concatenate(pieces, axis=0).T.astype(BF16)
    stats_out[0] = jnp.concatenate(stats + [jnp.zeros((8 - heads, rows), F32)], axis=0)
    projected = dot(context, out_weight[info.head_at ^ shard])
    if not last:
        context_out[0] = context

        @pl.when(step == 0)
        def first():
            total[...] = projected if total_in is None else total_in[...] + projected

        @pl.when(step > 0)
        def later():
            total[...] += projected

        return

    context_out[...] = jnp.concatenate(
        [ref[q] for ref in earlier for q in range(ref.shape[0])] + [context], axis=1
    )
    rows_out, normed_out, tokens_out, partner_out = refs[3:]
    tokens_out[...] = x.T
    partner_out[...] = xp.T
    for cut in row_chunks(rows, 16):
        values = x[cut].astype(F32) + ((total_in[cut] + projected[cut]) + vectors[0:1])
        rows_out[cut] = values
        unit, _ = unit_parts(values)
        normed_out[cut] = (unit * vectors[1:2] + vectors[2:3]).astype(BF16)


def tiles_of(part, own, near, far, run):
    @pl.when(pl.program_id(0) == 0)
    def mine():
        run(
            *(
                jnp.concatenate([own[place_of(part, half, spot)] for spot in range(SPOTS)], axis=0)
                for half in range(2)
            )
        )

    @pl.when(pl.program_id(0) > 0)
    def other():
        run(*(ref[:, 0].reshape(-1, ref.shape[3]) for ref in (near, far)))


def add_up(total, *partials):
    @pl.when(pl.program_id(0) == 0)
    def start():
        total[...] = sum(partials[1:], partials[0])

    @pl.when(pl.program_id(0) > 0)
    def later():
        total[...] = sum(partials, total[...])


def at_end(run):
    pl.when(pl.program_id(0) == pl.num_programs(0) - 1)(run)


def eight_rows(*rows):
    width = rows[0].shape[1]
    return jnp.concatenate([*rows, jnp.zeros((8 - len(rows), width), F32)], axis=0)


def feed_up_kernel(info, normed, own, near, far, bias, *outs):
    shard = info[2] ^ pl.program_id(0)

    def run(*tiles):
        for half, tile in enumerate(tiles):
            places = [place_of(info[1], half, spot) for spot in range(SPOTS)]
            bias_row = jnp.concatenate([bias[shard, place] for place in places], axis=1)
            pre = dot(normed[...], tile, 1, 1)
            for cut in row_chunks(pre.shape[0], 32):
                hidden, slope = gelu_parts(pre[cut] + bias_row)
                outs[half][cut] = hidden.astype(BF16)
                outs[half + 2][cut] = slope

    tiles_of(info[1], own, near, far, run)


def feed_down_kernel(
    info,
    near_hidden,
    far_hidden,
    own,
    near,
    far,
    rows_in,
    cotangent,
    vectors,
    mixed_out,
    second_out,
    grad_out,
    sums_out,
    total,
):
    def run(near_tile, far_tile):
        add_up(total, dot(near_hidden[...], near_tile), dot(far_hidden[...], far_tile))

    tiles_of(info[1], own, near, far, run)

    @at_end
    def finish():
        sums = [jnp.zeros((8, rows_in.shape[1]), F32)] * 3
        for cut in row_chunks(rows_in.shape[0], 16):
            unit_one, _ = unit_parts(rows_in[cut])
            first_norm = unit_one * vectors[0:1] + vectors[1:2]
            unit, inverse = unit_parts(first_norm + (total[cut] + vectors[2:3]))
            index = cut.start + lax.broadcasted_iota(jnp.int32, (16, 1), 0)
            mask = jnp.where(index < info[0], 1.0, 0.0).astype(F32)
            mixed_out[cut] = ((unit * vectors[3:4] + vectors[4:5]) * mask).astype(BF16)
            incoming = cotangent[cut].astype(F32) * mask
            grad = norm_back(incoming, unit, inverse, vectors[3:4])
            second_out[cut] = grad
            low = grad.astype(BF16)
            grad_out[cut] = low
            more = (low.astype(F32), incoming * unit, incoming)
            sums = [a + eight_sum(b) for a, b in zip(sums, more)]
        sums_out[...] = eight_rows(*(column_sum(a) for a in sums))


def feed_back_kernel(
    info,
    grad_branch,
    down_own,
    down_near,
    down_far,
    up_own,
    up_near,
    up_far,
    near_slope,
    far_slope,
    rows_in,
    second_in,
    vectors,
    near_out,
    far_out,
    bias_out,
    first_out,
    proj_out,
    sums_out,
    total,
):
    def run_down(*tiles):
        for half, tile in enumerate(tiles):
            out, slope = (near_out, far_out)[half], (near_slope, far_slope)[half]
            grad = dot(grad_branch[...], tile, 1, 1)
            sums = jnp.zeros((8, grad.shape[1]), F32)
            for cut in row_chunks(grad.shape[0], 32):
                low = (grad[cut] * slope[cut]).astype(BF16)
                out[cut] = low
                sums = sums + eight_sum(low.astype(F32))
            sums = jnp.broadcast_to(column_sum(sums), sums.shape)
            width = bias_out.shape[3]
            for spot in range(SPOTS):
                row = sums[:, spot * width : (spot + 1) * width]
                bias_out[0, place_of(info[1], half, spot)] = row

    def run_up(near_tile, far_tile):
        add_up(total, dot(near_out[...], near_tile), dot(far_out[...], far_tile))

    tiles_of(info[1], down_own, down_near, down_far, run_down)
    tiles_of(info[1], up_own, up_near, up_far, run_up)

    @at_end
    def finish():
        sums = [jnp.zeros((8, rows_in.shape[1]), F32)] * 3
        for cut in row_chunks(rows_in.shape[0], 16):
            unit, inverse = unit_parts(rows_in[cut])
            grad_normed = second_in[cut] + total[cut]
            grad = norm_back(grad_normed, unit, inverse, vectors[0:1])
            first_out[cut] = grad
            low = grad.astype(BF16)
            proj_out[cut] = low
            more = (low.astype(F32), grad_normed * unit, grad_normed)
            sums = [a + eight_sum(b) for a, b in zip(sums, more)]
        sums_out[...] = eight_rows(*(column_sum(a) for a in sums))


def row_grads_kernel(mine, theirs, my_rows, their_rows, keep_out, send_out):
    value = dot(mine[...], my_rows[...], 0, 0) + dot(theirs[...], their_rows[...], 0, 0)
    value = value.reshape(SPOTS, -1, value.shape[1])
    for spot in range(SPOTS):
        out = (keep_out, send_out)[spot & 1]
        out[spot >> 1, 0] = value[spot].astype(out.dtype)


def out_grads_kernel(info, mine, theirs, my_context, their_context, keep_out, send_out, turned):
    value = 0.0
    for i, (grad, context) in enumerate(((mine, my_context), (theirs, their_context))):
        turned[i] = grad[...].T.reshape(turned.shape[1:])
        rows = [turned[i, place_of(info[1], 0, spot)] for spot in range(SPOTS)]
        value = value + dot(jnp.concatenate(rows, axis=0), context[...])
    value = value.reshape(SPOTS, -1, value.shape[1])
    for spot in range(SPOTS):
        out = (keep_out, send_out)[spot & 1]
        out[spot >> 1] = value[spot].astype(out.dtype)


def scatter_parts(part, value, chunks, near_out, far_out):
    chunks[...] = value.reshape(chunks.shape)
    for spot in range(SPOTS):
        near_out[spot, 0] = chunks[place_of(part, 0, spot)]
        far_out[spot, 0] = chunks[place_of(part, 1, spot)]


def attend_back_kernel(setting, info_ref, tokens_t, partner_t, grad_proj, out_weight, *refs):
    heads, depth, first_shard, carried, so_far, shards = setting
    refs = list(refs)
    if first_shard == 0:
        turned = refs.pop(0)
    near, far, qkv_in, stats_in = refs[:4]
    del refs[:4]
    if carried:
        own_in, partner_in = refs[:2]
        del refs[:2]
    del refs[:so_far]
    own_out, partner_out, near_out, far_out, bias_out, total, weight_scratch, chunks = refs
    step = pl.program_id(0)
    shard = first_shard + step
    info = Info(info_ref, heads, shards)
    if first_shard:
        gathered(info.part, near, far, weight_scratch)
    else:
        width = turned.shape[1]

        @pl.when(shard == 0)
        def own_weight():
            rows_kv = jnp.concatenate([turned[1], turned[2], turned[0]], axis=0)
            weight_scratch[...] = rows_kv.T.reshape(weight_scratch.shape)

        @pl.when(shard > 0)
        def other_weight():
            gathered(info.part, near, far, weight_scratch)

    weight = weight_scratch[...].reshape(-1, weight_scratch.shape[2])
    swaps = info.swaps(shard)
    dim, rows = tokens_t.shape
    width = heads * depth
    grad = dot(grad_proj[...], out_weight[0], 1, 1).astype(BF16)
    k, v, q = (qkv_in[0, :, i * width : (i + 1) * width] for i in range(3))
    stats = stats_in[0]
    gq, gk, gv = [], [], []
    for j in range(heads):
        head = slice(j * depth, (j + 1) * depth)
        stat = stats[j : j + 1, :]
        live = jnp.where(swaps[j] == 1, info.partner_live, info.own_live)
        scores = dot(k[:, head], q[:, head], 1, 1)
        grad_mix = dot(v[:, head], grad[:, head], 1, 1)
        chances, shared = [], jnp.zeros((8, rows), F32)
        for cut in row_chunks(rows, 32):
            index = cut.start + lax.broadcasted_iota(jnp.int32, (32, 1), 0)
            part = jnp.exp(jnp.where(index < live, scores[cut] - stat, -10000.0))
            chances.append(part)
            shared = shared + eight_sum(part * grad_mix[cut])
        shared = column_sum(shared)
        mixing = jnp.concatenate([part.astype(BF16) for part in chances], axis=0)
        grad_scores = jnp.concatenate(
            [
                (part * (grad_mix[cut] - shared)).astype(BF16)
                for part, cut in zip(chances, row_chunks(rows, 32))
            ],
            axis=0,
        )
        gk.append(dot(grad_scores, q[:, head]))
        gv.append(dot(mixing, grad[:, head]))
        gq.append(dot(k[:, head], grad_scores, 0, 0))
    grad_q = (jnp.concatenate(gq, axis=0).T * (depth**-0.5)).astype(BF16)
    grad_kv = jnp.concatenate(gk + gv, axis=1).astype(BF16)
    swapped = lane_pick(swaps + swaps, depth) == 1
    nothing = jnp.zeros((), BF16)
    grad_own = jnp.concatenate([jnp.where(swapped, nothing, grad_kv), grad_q], axis=1)
    grad_far = jnp.where(swapped, grad_kv, nothing)
    own = dot(grad_own, weight, 1, 1)
    other = dot(grad_far, weight[:, : 2 * width], 1, 1)

    @pl.when(step == 0)
    def first():
        own_out[...] = own_in[...] + own if carried else own
        total[...] = partner_in[...] + other if carried else other

    @pl.when(step > 0)
    def later():
        own_out[...] += own
        total[...] += other

    @at_end
    def finish():
        partner_out[...] = total[...].astype(partner_out.dtype)

    grads = dot(tokens_t[...], grad_own)
    grads_kv = grads[:, : 2 * width] + dot(partner_t[...], grad_far)
    grads = jnp.concatenate([grads_kv, grads[:, 2 * width :]], axis=1).astype(BF16)
    chunks[...] = grads.reshape(chunks.shape)
    for spot in range(SPOTS):
        near_out[spot, 0] = chunks[place_of(info.part, 0, spot)]
        far_out[spot, 0] = chunks[place_of(info.part, 1, spot)]
    bias_out[0] = jnp.broadcast_to(
        jnp.concatenate(
            [column_sum(grad_kv.astype(F32)), column_sum(grad_q.astype(F32))], axis=1
        ),
        bias_out.shape[1:],
    )


def settle_down_kernel(info, near, far, out):
    for half, source in enumerate((near, far)):
        for spot in range(SPOTS):
            out[place_of(info[1], half, spot)] = source[spot].astype(F32)


def settle_up_kernel(info, near, far, up_out, out_out, up_scratch, out_scratch):
    dim = up_out.shape[0]
    for half, source in enumerate((near, far)):
        for spot in range(SPOTS):
            place = place_of(info[1], half, spot)
            value = source[spot].astype(F32)
            up_scratch[place] = value[:, :dim]
            out_scratch[place] = value[:, dim:]
    up_out[...] = up_scratch[...].reshape(-1, dim).T
    shards = out_out.shape[0]
    turned = out_scratch[...].reshape(-1, dim).T.reshape(shards, -1, dim)
    for q in range(shards):
        out_out[info[2] ^ q] = turned[q]


def settle_input_kernel(info, near, far, out, scratch):
    width = out.shape[1]
    for half, source in enumerate((near, far)):
        for spot in range(SPOTS):
            scratch[place_of(info[1], half, spot)] = source[spot].astype(F32)
    turned = scratch[...].reshape(-1, scratch.shape[2]).T
    for i in range(3):
        out[(i + 1) % 3] = turned[i * width : (i + 1) * width]


def shape(dims, dtype):
    return jax.ShapeDtypeStruct(dims, dtype)


def whole(*dims):
    return pl.BlockSpec(dims, lambda *_: (0,) * len(dims))


def cost(flops, moved, slow=0):
    return pl.CostEstimate(flops=flops, bytes_accessed=moved, transcendentals=slow)


SMEM = pl.BlockSpec(memory_space=pltpu.SMEM)


def gathered_specs(near, first_shard):
    spots, _, piece, lanes = near.shape
    return [pl.BlockSpec((spots, 1, piece, lanes), lambda s: (0, s + first_shard - 1, 0, 0))] * 2


def attend(
    setting, count, info, tokens, partner, bias, out_weight, vectors, weights, carried, so_far
):
    heads, depth, first_shard, last = setting
    rows, dim = tokens.shape
    shards, width, _ = out_weight.shape
    lanes = 3 * width
    scratch = []
    if first_shard == 0:
        weight_specs = [whole(3, width, dim)]
    else:
        weight_specs = gathered_specs(weights[0], first_shard)
        scratch = [pltpu.VMEM((PARTS, dim // PARTS, lanes), BF16)]
    out_specs = [
        pl.BlockSpec((1, rows, lanes), lambda s: (s + first_shard, 0, 0)),
        whole(rows, dim) if last else pl.BlockSpec((1, rows, width), lambda s: (s, 0, 0)),
        pl.BlockSpec((1, 8, rows), lambda s: (s + first_shard, 0, 0)),
    ]
    out_shape = [
        shape((shards, rows, lanes), BF16),
        shape((rows, dim) if last else (count, rows, width), BF16),
        shape((shards, 8, rows), F32),
    ]
    fixed = 6 + len(weights) + len(carried)
    if last:
        out_specs += [whole(rows, dim)] * 2 + [whole(dim, rows)] * 2
        out_shape += [shape((rows, dim), F32), shape((rows, dim), BF16)]
        out_shape += [shape((dim, rows), BF16)] * 2
        scratch = [pltpu.VMEM((8, 128), F32)] + scratch
    else:
        out_specs.append(whole(rows, dim))
        out_shape.append(shape((rows, dim), F32))
    return pl.pallas_call(
        functools.partial(attend_kernel, setting),
        grid=(count,),
        in_specs=[
            SMEM,
            whole(rows, dim),
            whole(rows, dim),
            pl.BlockSpec((1, 8, lanes), lambda s: (s + first_shard, 0, 0)),
            whole(shards, width, dim),
            whole(8, dim),
        ]
        + weight_specs
        + [whole(*value.shape) for value in carried]
        + [pl.BlockSpec(memory_space=pl.ANY)] * len(so_far),
        out_specs=out_specs,
        out_shape=out_shape,
        scratch_shapes=scratch,
        input_output_aliases={fixed + i: (0, 2)[i] for i in range(len(so_far))},
        compiler_params=PARAMS,
        cost_estimate=cost(
            count * (3 * rows * dim * dim + 4 * rows * rows * dim),
            count * 6 * rows * dim,
            count * heads * rows * rows,
        ),
        name="attend",
    )(info, tokens, partner, bias, out_weight, vectors, *weights, *carried, *so_far)


def feed_specs(near):
    spots, _, piece, lanes = near.shape
    other = pl.BlockSpec(
        (spots, 1, piece, lanes), lambda q: (0, jnp.maximum(q - 1, 0), 0, 0)
    )
    return [whole(PARTS, piece, lanes), other, other]


def feed_up(info, normed, weight, bias):
    rows, dim = normed.shape
    near = weight[1]
    shards = near.shape[1] + 1
    tile = SPOTS * near.shape[2]
    columns = pl.BlockSpec((rows, tile), lambda q: (0, q))
    return pl.pallas_call(
        feed_up_kernel,
        grid=(shards,),
        in_specs=[
            SMEM,
            whole(rows, dim),
            *feed_specs(near),
            whole(*bias.shape),
        ],
        out_specs=[columns] * 4,
        out_shape=[shape((rows, shards * tile), BF16)] * 2
        + [shape((rows, shards * tile), F32)] * 2,
        compiler_params=PARAMS,
        cost_estimate=cost(4 * rows * dim * tile * shards, 30 * rows * dim, rows * dim * 8),
        name="feed_up",
    )(info, normed, *weight, bias)


def feed_down(info, hidden, weight, rows_one, cotangent, vectors):
    rows, dim = rows_one.shape
    near = weight[1]
    shards = near.shape[1] + 1
    tile = SPOTS * near.shape[2]
    columns = pl.BlockSpec((rows, tile), lambda q: (0, q))
    return pl.pallas_call(
        feed_down_kernel,
        grid=(shards,),
        in_specs=[
            SMEM,
            columns,
            columns,
            *feed_specs(near),
            whole(rows, dim),
            whole(rows, dim),
            whole(8, dim),
        ],
        out_specs=[whole(rows, dim)] * 3 + [whole(8, dim)],
        out_shape=[
            shape((rows, dim), BF16),
            shape((rows, dim), F32),
            shape((rows, dim), BF16),
            shape((8, dim), F32),
        ],
        scratch_shapes=[pltpu.VMEM((rows, dim), F32)],
        compiler_params=PARAMS,
        cost_estimate=cost(4 * rows * dim * tile * shards, 20 * rows * dim),
        name="feed_down",
    )(info, *hidden, *weight, rows_one, cotangent, vectors)


def feed_back(info, grad_branch, down, up, slopes, rows_one, grad_second, vectors):
    rows, dim = rows_one.shape
    near = up[1]
    shards = near.shape[1] + 1
    tile = SPOTS * near.shape[2]
    columns = pl.BlockSpec((rows, tile), lambda q: (0, q))
    return pl.pallas_call(
        feed_back_kernel,
        grid=(shards,),
        in_specs=[
            SMEM,
            whole(rows, dim),
            *feed_specs(near),
            *feed_specs(near),
            columns,
            columns,
            whole(rows, dim),
            whole(rows, dim),
            whole(8, dim),
        ],
        out_specs=[
            columns,
            columns,
            pl.BlockSpec((1, PARTS, 8, near.shape[2]), lambda q: (q, 0, 0, 0)),
            whole(rows, dim),
            whole(rows, dim),
            whole(8, dim),
        ],
        out_shape=[
            shape((rows, shards * tile), BF16),
            shape((rows, shards * tile), BF16),
            shape((shards, PARTS, 8, near.shape[2]), F32),
            shape((rows, dim), F32),
            shape((rows, dim), BF16),
            shape((8, dim), F32),
        ],
        scratch_shapes=[pltpu.VMEM((rows, dim), F32)],
        compiler_params=PARAMS,
        cost_estimate=cost(8 * rows * dim * tile * shards, 40 * rows * dim),
        name="feed_back",
    )(info, grad_branch, *down, *up, *slopes, rows_one, grad_second, vectors)


def row_grads(shards, mine, theirs, my_rows, their_rows, name):
    rows, dim = my_rows.shape
    tile = mine.shape[1] // shards
    piece = tile // SPOTS
    columns = pl.BlockSpec((rows, tile), lambda q: (0, q))
    out = pl.BlockSpec((2, 1, piece, dim), lambda q: (0, q, 0, 0))
    return pl.pallas_call(
        row_grads_kernel,
        grid=(shards,),
        in_specs=[columns, columns, whole(rows, dim), whole(rows, dim)],
        out_specs=[out, out],
        out_shape=[shape((2, shards, piece, dim), F32), shape((2, shards, piece, dim), BF16)],
        compiler_params=PARAMS,
        cost_estimate=cost(4 * rows * dim * tile * shards, 20 * rows * dim),
        name=name,
    )(mine, theirs, my_rows, their_rows)


def out_grads(info, mine, theirs, my_context, their_context):
    rows, dim = mine.shape
    piece = dim // PARTS
    return pl.pallas_call(
        out_grads_kernel,
        in_specs=[SMEM] + [whole(rows, dim)] * 4,
        out_specs=[whole(2, piece, dim)] * 2,
        out_shape=[shape((2, piece, dim), F32), shape((2, piece, dim), BF16)],
        scratch_shapes=[pltpu.VMEM((2, PARTS, piece, rows), BF16)],
        compiler_params=PARAMS,
        cost_estimate=cost(2 * rows * dim * dim, 10 * rows * dim),
        name="out_grads",
    )(info, mine, theirs, my_context, their_context)


def attend_back(
    setting,
    info,
    tokens_t,
    partner_t,
    grad_proj,
    out_weight,
    own,
    near,
    far,
    qkvs,
    stats,
    carried,
    so_far,
):
    heads, depth, first_shard, count, shards = setting
    half = shards // 2
    slot = first_shard % half
    fixed = 9 + len(own) + len(carried)
    dim, rows = tokens_t.shape
    width = heads * depth
    lanes = 3 * width
    piece = dim // PARTS
    head_spot = heads * shards + 3
    own_specs = [] if first_shard else [whole(3, width, dim)]
    kernel = functools.partial(
        attend_back_kernel, (heads, depth, first_shard, bool(carried), len(so_far), shards)
    )

    def other(s, info):
        return (0, jnp.maximum(s + first_shard - 1, 0), 0, 0)

    parts_out = pl.BlockSpec((SPOTS, 1, piece, lanes), lambda s, info: (0, s + slot, 0, 0))
    return pl.pallas_call(
        kernel,
        grid_spec=pltpu.PrefetchScalarGridSpec(
            num_scalar_prefetch=1,
            grid=(count,),
            in_specs=[
                whole(dim, rows),
                whole(dim, rows),
                whole(rows, dim),
                pl.BlockSpec(
                    (1, width, dim), lambda s, info: (info[head_spot] ^ (s + first_shard), 0, 0)
                ),
            ]
            + own_specs
            + [pl.BlockSpec((SPOTS, 1, piece, lanes), other)] * 2
            + [
                pl.BlockSpec((1, rows, lanes), lambda s, info: (s + first_shard, 0, 0)),
                pl.BlockSpec((1, 8, rows), lambda s, info: (s + first_shard, 0, 0)),
            ]
            + [whole(rows, dim)] * len(carried)
            + [pl.BlockSpec(memory_space=pl.ANY)] * len(so_far),
            out_specs=[
                whole(rows, dim),
                whole(rows, dim),
                parts_out,
                parts_out,
                pl.BlockSpec((1, 8, lanes), lambda s, info: (s + slot, 0, 0)),
            ],
            scratch_shapes=[
                pltpu.VMEM((rows, dim), F32),
                pltpu.VMEM((PARTS, piece, lanes), BF16),
                pltpu.VMEM((PARTS, piece, lanes), BF16),
            ],
        ),
        out_shape=[
            shape((rows, dim), F32),
            shape((rows, dim), F32 if first_shard else BF16),
            shape((SPOTS, half, piece, lanes), BF16),
            shape((SPOTS, half, piece, lanes), BF16),
            shape((half, 8, lanes), F32),
        ],
        input_output_aliases={fixed + i: 2 + i for i in range(len(so_far))},
        compiler_params=PARAMS,
        cost_estimate=cost(
            count * (6 * rows * dim * dim + 10 * rows * rows * dim),
            count * 8 * rows * dim,
            count * heads * rows * rows,
        ),
        name="attend_back",
    )(
        info,
        tokens_t,
        partner_t,
        grad_proj,
        out_weight,
        *own,
        near,
        far,
        qkvs,
        stats,
        *carried,
        *so_far,
    )


class Mover:
    def __init__(self, batch_size, shards):
        self.batch_size, self.shards = batch_size, shards

    def batch(self, value, mask_of):
        perm = [(i, i ^ mask_of(i)) for i in range(self.batch_size)]
        return lax.ppermute(value, "batch", perm)

    def core(self, value):
        return self.batch(value, lambda i: CORE)

    def low(self, value):
        return self.batch(value, lambda i: 4 if i & 1 else 2)

    def high(self, value):
        return self.batch(value, lambda i: 2 if i & 1 else 4)

    def head(self, value, mask):
        return lax.ppermute(value, "head", [(i, i ^ mask) for i in range(self.shards)])

    def along(self, values, first=1):
        return [self.head(value, q) for q, value in enumerate(values, first)]

    def column(self, piece):
        return self.along([piece] * (self.shards - 1))

    def settle(self, total):
        total = total.astype(BF16)
        mask = PARTS
        while mask < self.batch_size:
            other = self.batch(total, lambda i, mask=mask: mask)
            total = (total.astype(F32) + other.astype(F32)).astype(BF16)
            mask *= 2
        return total

    def shards_in_order(self, value, mask):
        first = value.shape[0] - 2 * self.shards
        rows = [first + base + (q ^ mask) for base in (0, self.shards) for q in range(self.shards)]
        return jnp.concatenate([value[:first]] + [value[row : row + 1] for row in rows])

    def hops(self):
        steps, mask = [], 1
        while mask < self.batch_size:
            steps.append(lambda value, mask=mask: self.batch(value, lambda i: mask))
            mask *= 2
        mask = 1
        while mask < self.shards:
            steps.append(lambda value, mask=mask: self.shards_in_order(self.head(value, mask), mask))
            mask *= 2
        return steps


def after(value, *events):
    return lax.optimization_barrier((value, *events))[0]


def all_after(values, *events):
    return lax.optimization_barrier((*values, *events))[: len(values)]


def pair_of(first, second):
    return jnp.stack([first, second])


def four_of(pair, received):
    return jnp.concatenate([pair, received])


def shards_swapped(value, shards, mask):
    width = value.shape[1] // shards
    blocks = [value[:, (q ^ mask) * width : ((q ^ mask) + 1) * width] for q in range(shards)]
    return jnp.concatenate(blocks, axis=1)


def stack8(*rows):
    rows = [row.reshape(1, -1) for row in rows]
    return jnp.concatenate(rows + [jnp.zeros((8 - len(rows), rows[0].shape[1]), F32)], axis=0)


def local(
    batch_size,
    shards,
    tokens,
    lengths,
    block_swap,
    input_weight,
    input_bias,
    out_weight,
    out_bias,
    gain_one,
    shift_one,
    up_weight,
    up_bias,
    down_weight,
    down_bias,
    gain_two,
    shift_two,
    cotangent,
):
    move = Mover(batch_size, shards)
    heads = block_swap.shape[0]
    rows, dim = tokens.shape
    width = input_weight.shape[2]
    depth = width // heads
    hidden_own = up_weight.shape[1]
    piece = dim // PARTS
    batch_at, head_at = lax.axis_index("batch"), lax.axis_index("head")
    part = batch_at % PARTS
    blocks = SEQ_LEN // rows
    length = lax.dynamic_index_in_dim(lengths, head_at // blocks, 0, keepdims=False)
    block_at = head_at % blocks
    own_live = jnp.clip(length - block_at * rows, 0, rows)
    partner_live = jnp.clip(length - (blocks - 1 - block_at) * rows, 0, rows)

    input_piece = lax.dynamic_slice_in_dim(input_weight, part * piece, piece, 1)
    input_piece = jnp.concatenate([input_piece[1], input_piece[2], input_piece[0]], axis=1)
    input_column = move.column(input_piece)
    small = jnp.concatenate([input_bias.reshape(-1), block_swap.astype(F32)])
    small_ends = pair_of(small, move.head(small, 2))
    small_others = move.head(after(small_ends, *input_column), 1)
    partner = move.head(after(tokens, *input_column), 1)
    input_column = jnp.stack(input_column)
    input_low = move.low(input_column)
    input_own = input_weight.transpose(0, 2, 1)
    up_own = up_weight.T.reshape(PARTS, piece, dim)
    up_piece = lax.dynamic_index_in_dim(up_own, part, 0, keepdims=False)
    up_far = move.head(after(up_piece, input_column), 2)
    down_own = down_weight.reshape(PARTS, piece, dim)
    down_piece = lax.dynamic_index_in_dim(down_own, part, 0, keepdims=False)

    small = jnp.stack([small_ends[0], small_others[0], small_ends[1], small_others[1]])
    info = jnp.concatenate(
        [
            small[:, 2 * width :].reshape(-1).astype(jnp.int32),
            jnp.stack([own_live, partner_live, part, head_at]).astype(jnp.int32),
        ]
    )
    short_info = jnp.stack([own_live, part, head_at]).astype(jnp.int32)
    bias = jnp.concatenate(
        [jnp.zeros((shards, width), F32), small[:, width : 2 * width], small[:, :width]], axis=1
    )
    bias = jnp.broadcast_to(bias[:, None], (shards, 8, 3 * width))
    up_bias_parts = up_bias.reshape(shards, PARTS, 1, piece)
    out_parts = out_weight.reshape(shards, width, dim)
    vectors_one = stack8(out_bias, gain_one, shift_one)
    vectors_two = stack8(gain_one, shift_one, down_bias, gain_two, shift_two)
    vectors_back = stack8(gain_one)
    input_low, up_far = all_after((input_low, up_far), info, bias, vectors_one, vectors_two)
    input_pair = pair_of(input_column, input_low)
    input_high = move.high(input_pair)
    up_ends = pair_of(up_piece, up_far)
    up_others = move.head(up_ends, 1)
    input_high, partner, up_others = all_after((input_high, partner, up_others))
    input_near = four_of(input_pair, input_high)
    input_far = move.core(input_near)
    up_column = jnp.stack([up_others[0], up_ends[1], up_others[1]])
    up_low = move.low(up_column)
    down_far = move.head(after(down_piece, up_others), 2)

    def attend_shards(first_shard, count, last, weights, carried, so_far):
        return attend(
            (heads, depth, first_shard, last),
            count,
            info,
            tokens,
            partner,
            bias,
            out_parts,
            vectors_one,
            weights,
            carried,
            so_far,
        )

    now = after(input_own, up_column)
    qkv, context_0, stats, total = attend_shards(0, 1, False, [now], [], [])
    others = [input_near, input_far]
    up_low, down_far = all_after((up_low, down_far), total)
    up_pair = pair_of(up_column, up_low)
    up_high = move.high(up_pair)
    down_ends = pair_of(down_piece, down_far)
    down_others = move.head(down_ends, 1)
    total, up_pair, down_ends = all_after((total, up_pair, down_ends))
    qkv, context_1, stats, total = attend_shards(1, 2, False, others, [total], [qkv, stats])
    up_high, down_others = all_after((up_high, down_others), total)
    up_near = four_of(up_pair, up_high)
    up_all = (up_own, up_near, move.core(up_near))
    down_column = jnp.stack([down_others[0], down_ends[1], down_others[1]])
    down_low = move.low(down_column)
    total, up_near, down_column = all_after((total, up_near, down_column))
    qkv, context, stats, rows_one, normed, tokens_t, partner_t = attend_shards(
        3, 1, True, others, [total, context_0, context_1], [qkv, stats]
    )
    normed_received = move.core(normed)
    context_received = move.core(context)
    down_pair = pair_of(down_column, after(down_low, normed))
    down_high = move.high(down_pair)
    normed, down_pair = all_after((normed, down_pair))
    hidden_near, hidden_far, *slopes = feed_up(short_info, normed, up_all, up_bias_parts)
    hidden_received = move.core(hidden_far)
    down_near = four_of(down_pair, after(down_high, hidden_near))
    down_all = (down_own, down_near, move.core(down_near))
    mixed_out, grad_second, grad_branch, sums_two = feed_down(
        short_info, (hidden_near, hidden_far), down_all, rows_one, cotangent, vectors_two
    )

    branch_received = move.core(grad_branch)
    pre_near, pre_far, up_bias_sums, grad_first, grad_proj, sums_one = feed_back(
        short_info, grad_branch, down_all, up_all, slopes, rows_one, grad_second, vectors_back
    )
    branch_received, pre_near, pre_far, up_bias_sums, grad_proj, sums_one = all_after(
        (branch_received, pre_near, pre_far, up_bias_sums, grad_proj, sums_one)
    )
    pre_received = move.core(pre_far)
    proj_received = move.core(grad_proj)
    down_keep, down_send = row_grads(
        shards,
        hidden_near,
        hidden_received,
        after(grad_branch, grad_proj),
        branch_received,
        "down_grads",
    )
    down_low = move.low(down_send)
    up_keep, up_send = row_grads(
        shards, pre_near, pre_received, after(normed, down_send), normed_received, "up_grads"
    )
    out_keep, out_send = out_grads(
        short_info, after(grad_proj, up_send), proj_received, context, context_received
    )

    def core_sum(mine, received):
        both = mine.astype(F32) + received.astype(F32)
        return both[0::2], both[1::2].astype(BF16)

    def fold_low(keep, received):
        return keep[0] + received[0].astype(F32), (keep[1] + received[1].astype(F32)).astype(BF16)

    def fold_high(own, received):
        total = own + received.astype(F32)
        return total[0::2], total[1::2].astype(BF16)

    def fold_near(own, received):
        return own[0] + received[0].astype(F32), (own[1] + received[1].astype(F32)).astype(BF16)

    def fold_last(own, received):
        return move.settle(own + received.astype(F32))

    def back(grad, first_shard, count, carried, so_far):
        return attend_back(
            (heads, depth, first_shard, count, shards),
            info,
            tokens_t,
            partner_t,
            grad,
            out_parts,
            [] if first_shard else [input_own],
            *others,
            qkv,
            stats,
            carried,
            so_far,
        )

    down_mine, down_next = fold_low(down_keep, after(down_low, out_send))
    down_high = move.high(down_next)
    up_low = move.low(after(up_send, down_next))
    out_low = move.low(after(out_send, down_next))
    own_rows, partner_rows, late_near, late_far, late_bias = back(
        after(grad_proj, down_next), 2, 2, [], []
    )

    down_high, up_low, out_low, own_rows, partner_rows, late_near, late_far, late_bias = all_after(
        (down_high, up_low, out_low, own_rows, partner_rows, late_near, late_far, late_bias)
    )
    up_mine, up_next = fold_low(up_keep, up_low)
    up_high = move.high(up_next)
    late_core = move.core(late_far)
    down_mine, down_next = fold_high(down_mine, after(down_high, up_next))
    down_near = move.head(down_next, 1)
    out_mine = out_keep[0] + out_low[0].astype(F32)
    out_next = (out_keep[1] + out_low[1].astype(F32)).astype(BF16)
    out_high = move.high(out_next)
    own_rows, partner_rows, *early = back(
        after(grad_proj, down_next, up_next, out_next), 1, 1, [own_rows, partner_rows], []
    )

    up_high, down_near, late_core, out_high, own_rows, partner_rows, *early = all_after(
        (up_high, down_near, late_core, out_high, own_rows, partner_rows, *early)
    )
    up_mine, up_next = fold_high(up_mine, up_high)
    up_near = move.head(up_next, 1)
    late_keep, late_next = core_sum(late_near, late_core)
    late_low = move.low(late_next)
    down_mine, down_next = fold_near(down_mine, down_near)
    down_last = move.head(down_next, 2)
    out_next = (out_mine + out_high.astype(F32)).astype(BF16)
    out_near = move.head(out_next, 1)
    own_rows, partner_rows, early_near, early_far, early_bias = back(
        after(grad_proj, up_next, down_next, late_next, out_next),
        0,
        1,
        [own_rows, partner_rows],
        early,
    )

    up_near, down_last, late_low, out_near, own_rows, partner_rows = all_after(
        (up_near, down_last, late_low, out_near, own_rows, partner_rows), early_bias
    )
    early_near, early_far, early_bias = all_after((early_near, early_far, early_bias), up_near)

    from_partner = move.head(partner_rows, 1)
    early_core = move.core(early_far)
    vectors = jnp.concatenate(
        [
            sums_one[:3],
            sums_two[:3],
            up_bias_sums[:, :, 0].reshape(shards, dim),
            jnp.pad(jnp.concatenate([early_bias, late_bias])[:, 0], ((0, 0), (0, dim - 3 * width))),
        ]
    )
    hops = move.hops()

    def hop(value, sent, event):
        value = value + after(sent, event)
        return value, hops.pop(0)(value) if hops else None

    up_mine, up_next = fold_near(up_mine, up_near)
    up_last = move.head(up_next, 2)
    late_mine, late_next = fold_low(late_keep, after(late_low, up_next))
    late_high = move.high(late_next)
    early_keep, early_next = core_sum(early_near, after(early_core, late_next))
    early_low = move.low(early_next)
    down_total = fold_last(down_mine, after(down_last, early_next))
    down_low = move.low(down_total)
    out_near = shards_swapped(after(out_near, down_total), shards, 1)
    out_next = (out_next.astype(F32) + out_near.astype(F32)).astype(BF16)
    out_last = move.head(out_next, 2)
    vectors_sent = hops.pop(0)(after(vectors, out_next))
    down_pair = pair_of(down_total, after(down_low, out_next))
    down_high = move.high(down_pair)
    late_mine = late_mine + after(late_high, down_pair).astype(F32)
    early_mine, early_next = fold_low(early_keep, after(early_low, late_mine))
    early_high = move.high(early_next)
    vectors, vectors_sent = hop(vectors, vectors_sent, early_next)
    up_total = fold_last(up_mine, after(up_last, vectors))
    out_last = shards_swapped(after(out_last, vectors), shards, 2)
    out_total = move.settle(out_next.astype(F32) + out_last.astype(F32))
    up_total = jnp.concatenate([up_total, out_total], axis=1)
    up_low = move.low(up_total)
    early_mine = early_mine + after(early_high, up_total).astype(F32)
    input_next = jnp.stack([early_mine[1], late_mine[1]]).astype(BF16)
    input_near = move.head(input_next, 1)
    down_near = four_of(down_pair, after(down_high, input_next))
    down_far = move.core(down_near)
    vectors, vectors_sent = hop(vectors, vectors_sent, down_near)
    up_pair = pair_of(up_total, after(up_low, vectors))
    up_high = move.high(up_pair)
    input_mine, input_next = fold_near(
        jnp.stack([early_mine[0], late_mine[0]]), after(input_near, up_pair)
    )
    input_last = move.head(input_next, 2)
    vectors, vectors_sent = hop(vectors, vectors_sent, input_next)
    grad_tokens = grad_first + own_rows + after(from_partner, vectors).astype(F32)
    input_total = fold_last(input_mine, after(input_last, grad_tokens))
    input_low = move.low(input_total)
    up_near = four_of(up_pair, after(up_high, input_total))
    up_far = move.core(up_near)
    vectors, vectors_sent = hop(vectors, vectors_sent, up_near)
    input_pair = pair_of(input_total, after(input_low, vectors))
    input_high = move.high(input_pair)
    while vectors_sent is not None:
        vectors, vectors_sent = hop(vectors, vectors_sent, input_pair)
    grad_down = pl.pallas_call(
        settle_down_kernel,
        in_specs=[SMEM] + [whole(4, piece, dim)] * 2,
        out_shape=shape((PARTS, piece, dim), F32),
        compiler_params=PARAMS,
        name="settle_down",
    )(short_info, after(down_near, input_pair), down_far)
    input_near = four_of(input_pair, after(input_high, grad_down))
    input_done = (input_near, move.core(input_near))
    up_done = (after(up_near, input_near), up_far)
    grad_input_bias = jnp.stack([vectors[10, 2 * width : 3 * width], vectors[10, width : 2 * width]])
    grad_up_bias = vectors[6]
    grad_up, grad_out = pl.pallas_call(
        settle_up_kernel,
        in_specs=[SMEM] + [whole(4, piece, dim + shards * width)] * 2,
        out_shape=[shape((dim, hidden_own), F32), shape((shards, width, dim), F32)],
        scratch_shapes=[pltpu.VMEM((PARTS, piece, dim), F32)] * 2,
        compiler_params=PARAMS,
        name="settle_up",
    )(short_info, *up_done)
    grad_input_weight = pl.pallas_call(
        settle_input_kernel,
        in_specs=[SMEM] + [whole(4, piece, 3 * width)] * 2,
        out_shape=shape((3, width, dim), F32),
        scratch_shapes=[pltpu.VMEM((PARTS, piece, 3 * width), F32)],
        compiler_params=PARAMS,
        name="settle_input",
    )(short_info, *input_done)
    return (
        mixed_out,
        grad_tokens,
        grad_input_weight.transpose(0, 2, 1),
        grad_input_bias,
        grad_out.reshape(dim, dim),
        vectors[0],
        vectors[1],
        vectors[2],
        grad_up,
        grad_up_bias,
        grad_down.reshape(hidden_own, dim),
        vectors[3],
        vectors[4],
        vectors[5],
    )


def solution(mesh):
    rows_spec = P(("batch", "head"), None)
    placed = (
        rows_spec,
        P("batch"),
        P("head"),
        P(None, None, "head"),
        P(None, "head"),
        P(),
        P(),
        P(),
        P(),
        P(None, "head"),
        P(),
        P("head", None),
        P(),
        P(),
        P(),
        rows_spec,
    )
    return jax.shard_map(
        functools.partial(local, mesh.shape["batch"], mesh.shape["head"]),
        mesh=mesh,
        in_specs=placed,
        out_specs=(
            rows_spec,
            rows_spec,
            P(None, None, "head"),
            P(None, "head"),
            P(),
            P(),
            P(),
            P(),
            P(None, "head"),
            P("head"),
            P("head", None),
            P(),
            P(),
            P(),
        ),
        check_vma=False,
    )
```

```python
import functools

import jax
import jax.numpy as jnp
from jax import lax
from jax.experimental import pallas as pl
from jax.experimental.pallas import tpu as pltpu
from jax.sharding import PartitionSpec as P

SEQ_LEN = 1024
EPSILON = 1e-05
F32 = jnp.float32
BF16 = jnp.bfloat16
VMEM_LIMIT = 24 * 1024 * 1024
PARAMS = pltpu.CompilerParams(vmem_limit_bytes=VMEM_LIMIT)
CORE = 1
PARTS = 8
SPOTS = 4


def dot(left_side, right_side, left_dim=1, right_dim=0):
    return lax.dot_general(
        left_side,
        right_side,
        (((left_dim,), (right_dim,)), ((), ())),
        preferred_element_type=F32,
    )


def unit_parts(values):
    centred = values - jnp.mean(values, axis=-1, keepdims=True)
    inverse = lax.rsqrt(jnp.mean(centred * centred, axis=-1, keepdims=True) + EPSILON)
    return centred * inverse, inverse


def norm_back(grad_rows, unit_rows, inverse, gain_row):
    scaled = grad_rows * gain_row
    return inverse * (
        scaled
        - jnp.mean(scaled, axis=-1, keepdims=True)
        - unit_rows * jnp.mean(scaled * unit_rows, axis=-1, keepdims=True)
    )


def column_sum(values):
    return jnp.sum(values, axis=0, keepdims=True)


def gelu_parts(inner):
    below = 0.5 + 0.5 * lax.erf(inner * 0.7071067811865476)
    bell = jnp.exp(inner * inner * -0.5) * 0.3989422804014327
    return inner * below, below + inner * bell


def row_chunks(rows, step):
    return [slice(i, i + step) for i in range(0, rows, step)]


def eight_sum(values):
    return sum(values[cut] for cut in row_chunks(values.shape[0], 8))


def lane_pick(values, depth):
    lane = lax.broadcasted_iota(jnp.int32, (1, len(values) * depth), 1)
    picked = jnp.full(lane.shape, values[0], jnp.int32)
    for j in range(1, len(values)):
        picked = jnp.where(lane >= j * depth, values[j], picked)
    return picked


def place_of(part, half, spot):
    seen = part ^ half
    core = seen & 1
    low, high = 2 + 2 * core, 4 - 2 * core
    return seen ^ (low * (spot & 1) + high * (spot >> 1))


class Info:
    def __init__(self, ref, heads, shards):
        self.ref, self.heads, self.base = ref, heads, heads * shards

    def swaps(self, shard):
        return [self.ref[shard * self.heads + j] for j in range(self.heads)]

    own_live = property(lambda self: self.ref[self.base])
    partner_live = property(lambda self: self.ref[self.base + 1])
    part = property(lambda self: self.ref[self.base + 2])
    head_at = property(lambda self: self.ref[self.base + 3])


def gathered(part, near, far, scratch):
    for spot in range(SPOTS):
        scratch[place_of(part, 0, spot)] = near[spot, 0]
        scratch[place_of(part, 1, spot)] = far[spot, 0]
    return scratch[...].reshape(-1, scratch.shape[2])


def attend_kernel(setting, info_ref, tokens, partner, bias, out_weight, vectors, *refs):
    heads, depth, first_shard, last = setting
    refs = list(refs)
    if first_shard == 0:
        turned = refs.pop(0)
        total_in = None
    else:
        near, far, total_in = refs[:3]
        del refs[:3]
    earlier = []
    if last:
        earlier = refs[:2]
        del refs[:2]
    if first_shard:
        del refs[:2]
    qkv_out, context_out, stats_out = refs[:3]
    step = pl.program_id(0)
    shard = first_shard + step
    info = Info(info_ref, heads, out_weight.shape[0])
    if first_shard:
        weight = gathered(info.part, near, far, refs.pop())
    total = refs.pop()
    swaps = info.swaps(shard)
    rows, dim = tokens.shape
    width = heads * depth
    x, xp = tokens[...], partner[...]
    if first_shard:
        own = dot(x, weight)
        other = dot(xp, weight[:, : 2 * width])
    else:
        kv_rows = jnp.concatenate([turned[1], turned[2]], axis=0)
        own = jnp.concatenate([dot(x, kv_rows, 1, 1), dot(x, turned[0], 1, 1)], axis=1)
        other = dot(xp, kv_rows, 1, 1)
    swapped = lane_pick(swaps + swaps, depth) == 1
    bias_row = bias[0, 0:1]
    kv, q = [], []
    for cut in row_chunks(rows, 32):
        mine = own[cut] + bias_row
        theirs = other[cut] + bias_row[:, : 2 * width]
        kv.append(jnp.where(swapped, theirs, mine[:, : 2 * width]).astype(BF16))
        q.append(mine[:, 2 * width :].astype(BF16) * (depth**-0.5))
    kv, q = jnp.concatenate(kv, axis=0), jnp.concatenate(q, axis=0)
    qkv_out[0, :, : 2 * width] = kv
    qkv_out[0, :, 2 * width :] = q
    stats = []
    pieces = []
    for j in range(heads):
        head = slice(j * depth, (j + 1) * depth)
        live = jnp.where(swaps[j] == 1, info.partner_live, info.own_live)
        anyone = jnp.where(live > 0, 1.0, 0.0).astype(F32)
        scores = dot(kv[:, head], q[:, head], 1, 1)
        masked, most = [], None
        for cut in row_chunks(rows, 32):
            index = cut.start + lax.broadcasted_iota(jnp.int32, (32, 1), 0)
            part = jnp.where(index < live, scores[cut], -1e30)
            masked.append(part)
            for tile in row_chunks(32, 8):
                most = part[tile] if most is None else jnp.maximum(most, part[tile])
        largest = jnp.max(most, axis=0, keepdims=True)
        largest = jnp.where(anyone > 0.5, largest, 0.0)
        total_rows = None
        for part in masked:
            weights = eight_sum(jnp.exp(part - largest))
            total_rows = weights if total_rows is None else total_rows + weights
        stat = largest + jnp.log(column_sum(total_rows) + (1.0 - anyone))
        mixing = [jnp.exp(part - stat).astype(BF16) for part in masked]
        stats.append(stat)
        values = kv[:, width + j * depth : width + (j + 1) * depth]
        pieces.append(dot(values, jnp.concatenate(mixing, axis=0), 0, 0))
    context = jnp.concatenate(pieces, axis=0).T.astype(BF16)
    stats_out[0] = jnp.concatenate(stats + [jnp.zeros((8 - heads, rows), F32)], axis=0)
    projected = dot(context, out_weight[info.head_at ^ shard])
    if not last:
        context_out[0] = context

        @pl.when(step == 0)
        def first():
            total[...] = projected if total_in is None else total_in[...] + projected

        @pl.when(step > 0)
        def later():
            total[...] += projected

        return

    context_out[...] = jnp.concatenate(
        [ref[q] for ref in earlier for q in range(ref.shape[0])] + [context], axis=1
    )
    rows_out, normed_out = refs[3:]
    for cut in row_chunks(rows, 16):
        values = x[cut].astype(F32) + ((total_in[cut] + projected[cut]) + vectors[0:1])
        rows_out[cut] = values
        unit, _ = unit_parts(values)
        normed_out[cut] = (unit * vectors[1:2] + vectors[2:3]).astype(BF16)


def tiles_of(part, own, near, far, run):
    @pl.when(pl.program_id(0) == 0)
    def mine():
        run(
            *(
                jnp.concatenate([own[place_of(part, half, spot)] for spot in range(SPOTS)], axis=0)
                for half in range(2)
            )
        )

    @pl.when(pl.program_id(0) > 0)
    def other():
        run(*(ref[:, 0].reshape(-1, ref.shape[3]) for ref in (near, far)))


def add_up(total, *partials):
    @pl.when(pl.program_id(0) == 0)
    def start():
        total[...] = sum(partials[1:], partials[0])

    @pl.when(pl.program_id(0) > 0)
    def later():
        total[...] = sum(partials, total[...])


def at_end(run):
    pl.when(pl.program_id(0) == pl.num_programs(0) - 1)(run)


def eight_rows(*rows):
    width = rows[0].shape[1]
    return jnp.concatenate([*rows, jnp.zeros((8 - len(rows), width), F32)], axis=0)


def feed_up_kernel(info, normed, own, near, far, bias, *outs):
    shard = info[2] ^ pl.program_id(0)

    def run(*tiles):
        for half, tile in enumerate(tiles):
            places = [place_of(info[1], half, spot) for spot in range(SPOTS)]
            bias_row = jnp.concatenate([bias[shard, place] for place in places], axis=1)
            pre = dot(normed[...], tile, 1, 1)
            for cut in row_chunks(pre.shape[0], 32):
                hidden, slope = gelu_parts(pre[cut] + bias_row)
                outs[half][cut] = hidden.astype(BF16)
                outs[half + 2][cut] = slope

    tiles_of(info[1], own, near, far, run)


def feed_down_kernel(
    info,
    near_hidden,
    far_hidden,
    own,
    near,
    far,
    rows_in,
    cotangent,
    vectors,
    mixed_out,
    second_out,
    grad_out,
    sums_out,
    total,
):
    def run(near_tile, far_tile):
        add_up(total, dot(near_hidden[...], near_tile), dot(far_hidden[...], far_tile))

    tiles_of(info[1], own, near, far, run)

    @at_end
    def finish():
        sums = [jnp.zeros((8, rows_in.shape[1]), F32)] * 3
        for cut in row_chunks(rows_in.shape[0], 16):
            unit_one, _ = unit_parts(rows_in[cut])
            first_norm = unit_one * vectors[0:1] + vectors[1:2]
            unit, inverse = unit_parts(first_norm + (total[cut] + vectors[2:3]))
            index = cut.start + lax.broadcasted_iota(jnp.int32, (16, 1), 0)
            mask = jnp.where(index < info[0], 1.0, 0.0).astype(F32)
            mixed_out[cut] = ((unit * vectors[3:4] + vectors[4:5]) * mask).astype(BF16)
            incoming = cotangent[cut].astype(F32) * mask
            grad = norm_back(incoming, unit, inverse, vectors[3:4])
            second_out[cut] = grad
            low = grad.astype(BF16)
            grad_out[cut] = low
            more = (low.astype(F32), incoming * unit, incoming)
            sums = [a + eight_sum(b) for a, b in zip(sums, more)]
        sums_out[...] = eight_rows(*(column_sum(a) for a in sums))


def grad_pre_kernel(
    info, grad_branch, own, near, far, near_slope, far_slope, near_out, far_out, bias_out
):
    def run(*tiles):
        for half, tile in enumerate(tiles):
            out, slope = (near_out, far_out)[half], (near_slope, far_slope)[half]
            grad = dot(grad_branch[...], tile, 1, 1)
            sums = jnp.zeros((8, grad.shape[1]), F32)
            for cut in row_chunks(grad.shape[0], 32):
                low = (grad[cut] * slope[cut]).astype(BF16)
                out[cut] = low
                sums = sums + eight_sum(low.astype(F32))
            sums = jnp.broadcast_to(column_sum(sums), sums.shape)
            width = bias_out.shape[3]
            for spot in range(SPOTS):
                row = sums[:, spot * width : (spot + 1) * width]
                bias_out[0, place_of(info[1], half, spot)] = row

    tiles_of(info[1], own, near, far, run)


def up_back_kernel(
    info,
    near_pre,
    far_pre,
    own,
    near,
    far,
    rows_in,
    second_in,
    vectors,
    first_out,
    proj_out,
    sums_out,
    total,
):
    def run(near_tile, far_tile):
        add_up(total, dot(near_pre[...], near_tile), dot(far_pre[...], far_tile))

    tiles_of(info[1], own, near, far, run)

    @at_end
    def finish():
        sums = [jnp.zeros((8, rows_in.shape[1]), F32)] * 3
        for cut in row_chunks(rows_in.shape[0], 16):
            unit, inverse = unit_parts(rows_in[cut])
            grad_normed = second_in[cut] + total[cut]
            grad = norm_back(grad_normed, unit, inverse, vectors[0:1])
            first_out[cut] = grad
            low = grad.astype(BF16)
            proj_out[cut] = low
            more = (low.astype(F32), grad_normed * unit, grad_normed)
            sums = [a + eight_sum(b) for a, b in zip(sums, more)]
        sums_out[...] = eight_rows(*(column_sum(a) for a in sums))


def turn_kernel(tokens, partner, tokens_out, partner_out):
    tokens_out[...] = tokens[...].T
    partner_out[...] = partner[...].T


def row_grads_kernel(mine, theirs, my_rows, their_rows, *outs):
    value = dot(mine[...], my_rows[...], 0, 0) + dot(theirs[...], their_rows[...], 0, 0)
    value = value.reshape(SPOTS, -1, value.shape[1])
    for spot, out in enumerate(outs):
        out[0] = value[spot].astype(out.dtype)


def out_grads_kernel(info, mine, theirs, my_context, their_context, keep_out, send_out, turned):
    value = 0.0
    for i, (grad, context) in enumerate(((mine, my_context), (theirs, their_context))):
        turned[i] = grad[...].T.reshape(turned.shape[1:])
        rows = [turned[i, place_of(info[1], 0, spot)] for spot in range(SPOTS)]
        value = value + dot(jnp.concatenate(rows, axis=0), context[...])
    value = value.reshape(SPOTS, -1, value.shape[1])
    for spot in range(SPOTS):
        out = (keep_out, send_out)[spot & 1]
        out[spot >> 1] = value[spot].astype(out.dtype)


def scatter_parts(part, value, chunks, near_out, far_out):
    chunks[...] = value.reshape(chunks.shape)
    for spot in range(SPOTS):
        near_out[spot, 0] = chunks[place_of(part, 0, spot)]
        far_out[spot, 0] = chunks[place_of(part, 1, spot)]


def attend_back_kernel(setting, info_ref, tokens_t, partner_t, grad_proj, out_weight, *refs):
    heads, depth, first_shard, carried, so_far, shards = setting
    refs = list(refs)
    if first_shard == 0:
        turned = refs.pop(0)
    near, far, qkv_in, stats_in = refs[:4]
    del refs[:4]
    if carried:
        own_in, partner_in = refs[:2]
        del refs[:2]
    del refs[:so_far]
    own_out, partner_out, near_out, far_out, bias_out, total, weight_scratch, chunks = refs
    step = pl.program_id(0)
    shard = first_shard + step
    info = Info(info_ref, heads, shards)
    if first_shard:
        gathered(info.part, near, far, weight_scratch)
    else:
        width = turned.shape[1]

        @pl.when(shard == 0)
        def own_weight():
            rows_kv = jnp.concatenate([turned[1], turned[2], turned[0]], axis=0)
            weight_scratch[...] = rows_kv.T.reshape(weight_scratch.shape)

        @pl.when(shard > 0)
        def other_weight():
            gathered(info.part, near, far, weight_scratch)

    weight = weight_scratch[...].reshape(-1, weight_scratch.shape[2])
    swaps = info.swaps(shard)
    dim, rows = tokens_t.shape
    width = heads * depth
    grad = dot(grad_proj[...], out_weight[0], 1, 1).astype(BF16)
    k, v, q = (qkv_in[0, :, i * width : (i + 1) * width] for i in range(3))
    stats = stats_in[0]
    gq, gk, gv = [], [], []
    for j in range(heads):
        head = slice(j * depth, (j + 1) * depth)
        stat = stats[j : j + 1, :]
        live = jnp.where(swaps[j] == 1, info.partner_live, info.own_live)
        scores = dot(k[:, head], q[:, head], 1, 1)
        grad_mix = dot(v[:, head], grad[:, head], 1, 1)
        chances, shared = [], jnp.zeros((8, rows), F32)
        for cut in row_chunks(rows, 32):
            index = cut.start + lax.broadcasted_iota(jnp.int32, (32, 1), 0)
            part = jnp.exp(jnp.where(index < live, scores[cut] - stat, -10000.0))
            chances.append(part)
            shared = shared + eight_sum(part * grad_mix[cut])
        shared = column_sum(shared)
        mixing = jnp.concatenate([part.astype(BF16) for part in chances], axis=0)
        grad_scores = jnp.concatenate(
            [
                (part * (grad_mix[cut] - shared)).astype(BF16)
                for part, cut in zip(chances, row_chunks(rows, 32))
            ],
            axis=0,
        )
        gk.append(dot(grad_scores, q[:, head]))
        gv.append(dot(mixing, grad[:, head]))
        gq.append(dot(k[:, head], grad_scores, 0, 0))
    grad_q = (jnp.concatenate(gq, axis=0).T * (depth**-0.5)).astype(BF16)
    grad_kv = jnp.concatenate(gk + gv, axis=1).astype(BF16)
    swapped = lane_pick(swaps + swaps, depth) == 1
    nothing = jnp.zeros((), BF16)
    grad_own = jnp.concatenate([jnp.where(swapped, nothing, grad_kv), grad_q], axis=1)
    grad_far = jnp.where(swapped, grad_kv, nothing)
    own = dot(grad_own, weight, 1, 1)
    other = dot(grad_far, weight[:, : 2 * width], 1, 1)

    @pl.when(step == 0)
    def first():
        own_out[...] = own_in[...] + own if carried else own
        total[...] = partner_in[...] + other if carried else other

    @pl.when(step > 0)
    def later():
        own_out[...] += own
        total[...] += other

    @at_end
    def finish():
        partner_out[...] = total[...].astype(partner_out.dtype)

    grads = dot(tokens_t[...], grad_own)
    grads_kv = grads[:, : 2 * width] + dot(partner_t[...], grad_far)
    grads = jnp.concatenate([grads_kv, grads[:, 2 * width :]], axis=1).astype(BF16)
    chunks[...] = grads.reshape(chunks.shape)
    for spot in range(SPOTS):
        near_out[spot, 0] = chunks[place_of(info.part, 0, spot)]
        far_out[spot, 0] = chunks[place_of(info.part, 1, spot)]
    bias_out[0] = jnp.broadcast_to(
        jnp.concatenate(
            [column_sum(grad_kv.astype(F32)), column_sum(grad_q.astype(F32))], axis=1
        ),
        bias_out.shape[1:],
    )


def settle_down_kernel(info, near, far, out):
    for half, source in enumerate((near, far)):
        for spot in range(SPOTS):
            out[place_of(info[1], half, spot)] = source[spot].astype(F32)


def settle_up_kernel(info, near, far, up_out, out_out, up_scratch, out_scratch):
    dim = up_out.shape[0]
    for half, source in enumerate((near, far)):
        for spot in range(SPOTS):
            place = place_of(info[1], half, spot)
            value = source[spot].astype(F32)
            up_scratch[place] = value[:, :dim]
            out_scratch[place] = value[:, dim:]
    up_out[...] = up_scratch[...].reshape(-1, dim).T
    shards = out_out.shape[0]
    turned = out_scratch[...].reshape(-1, dim).T.reshape(shards, -1, dim)
    for q in range(shards):
        out_out[info[2] ^ q] = turned[q]


def settle_input_kernel(info, near, far, out, scratch):
    width = out.shape[1]
    for half, source in enumerate((near, far)):
        for spot in range(SPOTS):
            scratch[place_of(info[1], half, spot)] = source[spot].astype(F32)
    turned = scratch[...].reshape(-1, scratch.shape[2]).T
    for i in range(3):
        out[(i + 1) % 3] = turned[i * width : (i + 1) * width]


def shape(dims, dtype):
    return jax.ShapeDtypeStruct(dims, dtype)


def whole(*dims):
    return pl.BlockSpec(dims, lambda *_: (0,) * len(dims))


def cost(flops, moved, slow=0):
    return pl.CostEstimate(flops=flops, bytes_accessed=moved, transcendentals=slow)


SMEM = pl.BlockSpec(memory_space=pltpu.SMEM)


def gathered_specs(near, first_shard):
    spots, _, piece, lanes = near.shape
    return [pl.BlockSpec((spots, 1, piece, lanes), lambda s: (0, s + first_shard - 1, 0, 0))] * 2


def attend(
    setting, count, info, tokens, partner, bias, out_weight, vectors, weights, carried, so_far
):
    heads, depth, first_shard, last = setting
    rows, dim = tokens.shape
    shards, width, _ = out_weight.shape
    lanes = 3 * width
    scratch = []
    if first_shard == 0:
        weight_specs = [whole(3, width, dim)]
    else:
        weight_specs = gathered_specs(weights[0], first_shard)
        scratch = [pltpu.VMEM((PARTS, dim // PARTS, lanes), BF16)]
    out_specs = [
        pl.BlockSpec((1, rows, lanes), lambda s: (s + first_shard, 0, 0)),
        whole(rows, dim) if last else pl.BlockSpec((1, rows, width), lambda s: (s, 0, 0)),
        pl.BlockSpec((1, 8, rows), lambda s: (s + first_shard, 0, 0)),
    ]
    out_shape = [
        shape((shards, rows, lanes), BF16),
        shape((rows, dim) if last else (count, rows, width), BF16),
        shape((shards, 8, rows), F32),
    ]
    fixed = 6 + len(weights) + len(carried)
    if last:
        out_specs += [whole(rows, dim)] * 2
        out_shape += [shape((rows, dim), F32), shape((rows, dim), BF16)]
        scratch = [pltpu.VMEM((8, 128), F32)] + scratch
    else:
        out_specs.append(whole(rows, dim))
        out_shape.append(shape((rows, dim), F32))
    return pl.pallas_call(
        functools.partial(attend_kernel, setting),
        grid=(count,),
        in_specs=[
            SMEM,
            whole(rows, dim),
            whole(rows, dim),
            pl.BlockSpec((1, 8, lanes), lambda s: (s + first_shard, 0, 0)),
            whole(shards, width, dim),
            whole(8, dim),
        ]
        + weight_specs
        + [whole(*value.shape) for value in carried]
        + [pl.BlockSpec(memory_space=pl.ANY)] * len(so_far),
        out_specs=out_specs,
        out_shape=out_shape,
        scratch_shapes=scratch,
        input_output_aliases={fixed + i: (0, 2)[i] for i in range(len(so_far))},
        compiler_params=PARAMS,
        cost_estimate=cost(
            count * (3 * rows * dim * dim + 4 * rows * rows * dim),
            count * 6 * rows * dim,
            count * heads * rows * rows,
        ),
        name="attend",
    )(info, tokens, partner, bias, out_weight, vectors, *weights, *carried, *so_far)


def feed_specs(near):
    spots, _, piece, lanes = near.shape
    other = pl.BlockSpec(
        (spots, 1, piece, lanes), lambda q: (0, jnp.maximum(q - 1, 0), 0, 0)
    )
    return [whole(PARTS, piece, lanes), other, other]


def feed_up(info, normed, weight, bias):
    rows, dim = normed.shape
    near = weight[1]
    shards = near.shape[1] + 1
    tile = SPOTS * near.shape[2]
    columns = pl.BlockSpec((rows, tile), lambda q: (0, q))
    return pl.pallas_call(
        feed_up_kernel,
        grid=(shards,),
        in_specs=[
            SMEM,
            whole(rows, dim),
            *feed_specs(near),
            whole(*bias.shape),
        ],
        out_specs=[columns] * 4,
        out_shape=[shape((rows, shards * tile), BF16)] * 2
        + [shape((rows, shards * tile), F32)] * 2,
        compiler_params=PARAMS,
        cost_estimate=cost(4 * rows * dim * tile * shards, 30 * rows * dim, rows * dim * 8),
        name="feed_up",
    )(info, normed, *weight, bias)


def feed_down(info, hidden, weight, rows_one, cotangent, vectors):
    rows, dim = rows_one.shape
    near = weight[1]
    shards = near.shape[1] + 1
    tile = SPOTS * near.shape[2]
    columns = pl.BlockSpec((rows, tile), lambda q: (0, q))
    return pl.pallas_call(
        feed_down_kernel,
        grid=(shards,),
        in_specs=[
            SMEM,
            columns,
            columns,
            *feed_specs(near),
            whole(rows, dim),
            whole(rows, dim),
            whole(8, dim),
        ],
        out_specs=[whole(rows, dim)] * 3 + [whole(8, dim)],
        out_shape=[
            shape((rows, dim), BF16),
            shape((rows, dim), F32),
            shape((rows, dim), BF16),
            shape((8, dim), F32),
        ],
        scratch_shapes=[pltpu.VMEM((rows, dim), F32)],
        compiler_params=PARAMS,
        cost_estimate=cost(4 * rows * dim * tile * shards, 20 * rows * dim),
        name="feed_down",
    )(info, *hidden, *weight, rows_one, cotangent, vectors)


def grad_pre_of(info, grad_branch, weight, slopes):
    rows, dim = grad_branch.shape
    near = weight[1]
    shards = near.shape[1] + 1
    tile = SPOTS * near.shape[2]
    columns = pl.BlockSpec((rows, tile), lambda q: (0, q))
    return pl.pallas_call(
        grad_pre_kernel,
        grid=(shards,),
        in_specs=[SMEM, whole(rows, dim), *feed_specs(near), columns, columns],
        out_specs=[
            columns,
            columns,
            pl.BlockSpec((1, PARTS, 8, near.shape[2]), lambda q: (q, 0, 0, 0)),
        ],
        out_shape=[
            shape((rows, shards * tile), BF16),
            shape((rows, shards * tile), BF16),
            shape((shards, PARTS, 8, near.shape[2]), F32),
        ],
        compiler_params=PARAMS,
        cost_estimate=cost(4 * rows * dim * tile * shards, 30 * rows * dim),
        name="grad_pre",
    )(info, grad_branch, *weight, *slopes)


def up_back(info, pres, weight, rows_one, grad_second, vectors):
    rows, dim = rows_one.shape
    near = weight[1]
    shards = near.shape[1] + 1
    tile = SPOTS * near.shape[2]
    columns = pl.BlockSpec((rows, tile), lambda q: (0, q))
    return pl.pallas_call(
        up_back_kernel,
        grid=(shards,),
        in_specs=[
            SMEM,
            columns,
            columns,
            *feed_specs(near),
            whole(rows, dim),
            whole(rows, dim),
            whole(8, dim),
        ],
        out_specs=[whole(rows, dim), whole(rows, dim), whole(8, dim)],
        out_shape=[shape((rows, dim), F32), shape((rows, dim), BF16), shape((8, dim), F32)],
        scratch_shapes=[pltpu.VMEM((rows, dim), F32)],
        compiler_params=PARAMS,
        cost_estimate=cost(4 * rows * dim * tile * shards, 24 * rows * dim),
        name="up_back",
    )(info, *pres, *weight, rows_one, grad_second, vectors)


def turn(tokens, partner):
    rows, dim = tokens.shape
    return pl.pallas_call(
        turn_kernel,
        out_shape=[shape((dim, rows), BF16)] * 2,
        compiler_params=PARAMS,
        cost_estimate=cost(rows * dim, 8 * rows * dim),
        name="turn",
    )(tokens, partner)


def row_grads(shards, mine, theirs, my_rows, their_rows, name):
    rows, dim = my_rows.shape
    tile = mine.shape[1] // shards
    piece = tile // SPOTS
    columns = pl.BlockSpec((rows, tile), lambda q: (0, q))
    out = pl.BlockSpec((1, piece, dim), lambda q: (q, 0, 0))
    return pl.pallas_call(
        row_grads_kernel,
        grid=(shards,),
        in_specs=[columns, columns, whole(rows, dim), whole(rows, dim)],
        out_specs=[out] * SPOTS,
        out_shape=[shape((shards, piece, dim), (F32, BF16)[spot & 1]) for spot in range(SPOTS)],
        compiler_params=PARAMS,
        cost_estimate=cost(4 * rows * dim * tile * shards, 20 * rows * dim),
        name=name,
    )(mine, theirs, my_rows, their_rows)


def out_grads(info, mine, theirs, my_context, their_context):
    rows, dim = mine.shape
    piece = dim // PARTS
    return pl.pallas_call(
        out_grads_kernel,
        in_specs=[SMEM] + [whole(rows, dim)] * 4,
        out_specs=[whole(2, piece, dim)] * 2,
        out_shape=[shape((2, piece, dim), F32), shape((2, piece, dim), BF16)],
        scratch_shapes=[pltpu.VMEM((2, PARTS, piece, rows), BF16)],
        compiler_params=PARAMS,
        cost_estimate=cost(2 * rows * dim * dim, 10 * rows * dim),
        name="out_grads",
    )(info, mine, theirs, my_context, their_context)


def attend_back(
    setting,
    info,
    tokens_t,
    partner_t,
    grad_proj,
    out_weight,
    own,
    near,
    far,
    qkvs,
    stats,
    carried,
    so_far,
):
    heads, depth, first_shard, count, shards = setting
    half = shards // 2
    slot = first_shard % half
    fixed = 9 + len(own) + len(carried)
    dim, rows = tokens_t.shape
    width = heads * depth
    lanes = 3 * width
    piece = dim // PARTS
    head_spot = heads * shards + 3
    own_specs = [] if first_shard else [whole(3, width, dim)]
    kernel = functools.partial(
        attend_back_kernel, (heads, depth, first_shard, bool(carried), len(so_far), shards)
    )

    def other(s, info):
        return (0, jnp.maximum(s + first_shard - 1, 0), 0, 0)

    parts_out = pl.BlockSpec((SPOTS, 1, piece, lanes), lambda s, info: (0, s + slot, 0, 0))
    return pl.pallas_call(
        kernel,
        grid_spec=pltpu.PrefetchScalarGridSpec(
            num_scalar_prefetch=1,
            grid=(count,),
            in_specs=[
                whole(dim, rows),
                whole(dim, rows),
                whole(rows, dim),
                pl.BlockSpec(
                    (1, width, dim), lambda s, info: (info[head_spot] ^ (s + first_shard), 0, 0)
                ),
            ]
            + own_specs
            + [pl.BlockSpec((SPOTS, 1, piece, lanes), other)] * 2
            + [
                pl.BlockSpec((1, rows, lanes), lambda s, info: (s + first_shard, 0, 0)),
                pl.BlockSpec((1, 8, rows), lambda s, info: (s + first_shard, 0, 0)),
            ]
            + [whole(rows, dim)] * len(carried)
            + [pl.BlockSpec(memory_space=pl.ANY)] * len(so_far),
            out_specs=[
                whole(rows, dim),
                whole(rows, dim),
                parts_out,
                parts_out,
                pl.BlockSpec((1, 8, lanes), lambda s, info: (s + slot, 0, 0)),
            ],
            scratch_shapes=[
                pltpu.VMEM((rows, dim), F32),
                pltpu.VMEM((PARTS, piece, lanes), BF16),
                pltpu.VMEM((PARTS, piece, lanes), BF16),
            ],
        ),
        out_shape=[
            shape((rows, dim), F32),
            shape((rows, dim), F32 if first_shard else BF16),
            shape((SPOTS, half, piece, lanes), BF16),
            shape((SPOTS, half, piece, lanes), BF16),
            shape((half, 8, lanes), F32),
        ],
        input_output_aliases={fixed + i: 2 + i for i in range(len(so_far))},
        compiler_params=PARAMS,
        cost_estimate=cost(
            count * (6 * rows * dim * dim + 10 * rows * rows * dim),
            count * 8 * rows * dim,
            count * heads * rows * rows,
        ),
        name="attend_back",
    )(
        info,
        tokens_t,
        partner_t,
        grad_proj,
        out_weight,
        *own,
        near,
        far,
        qkvs,
        stats,
        *carried,
        *so_far,
    )


class Mover:
    def __init__(self, batch_size, shards):
        self.batch_size, self.shards = batch_size, shards

    def batch(self, value, mask_of):
        perm = [(i, i ^ mask_of(i)) for i in range(self.batch_size)]
        return lax.ppermute(value, "batch", perm)

    def core(self, value):
        return self.batch(value, lambda i: CORE)

    def low(self, value):
        return self.batch(value, lambda i: 4 if i & 1 else 2)

    def high(self, value):
        return self.batch(value, lambda i: 2 if i & 1 else 4)

    def head(self, value, mask):
        return lax.ppermute(value, "head", [(i, i ^ mask) for i in range(self.shards)])

    def along(self, values, first=1):
        return [self.head(value, q) for q, value in enumerate(values, first)]

    def column(self, piece):
        return self.along([piece] * (self.shards - 1))

    def settle(self, total):
        total = total.astype(BF16)
        mask = PARTS
        while mask < self.batch_size:
            other = self.batch(total, lambda i, mask=mask: mask)
            total = (total.astype(F32) + other.astype(F32)).astype(BF16)
            mask *= 2
        return total

    def shards_in_order(self, value, mask):
        first = value.shape[0] - 2 * self.shards
        rows = [first + base + (q ^ mask) for base in (0, self.shards) for q in range(self.shards)]
        return jnp.concatenate([value[:first]] + [value[row : row + 1] for row in rows])

    def hops(self):
        steps, mask = [], 1
        while mask < self.batch_size:
            steps.append(lambda value, mask=mask: self.batch(value, lambda i: mask))
            mask *= 2
        mask = 1
        while mask < self.shards:
            steps.append(lambda value, mask=mask: self.shards_in_order(self.head(value, mask), mask))
            mask *= 2
        return steps


def after(value, *events):
    return lax.optimization_barrier((value, *events))[0]


def all_after(values, *events):
    return lax.optimization_barrier((*values, *events))[: len(values)]


def pair_of(first, second):
    return jnp.stack([first, second])


def four_of(pair, received):
    return jnp.concatenate([pair, received])


def shards_swapped(value, shards, mask):
    width = value.shape[1] // shards
    blocks = [value[:, (q ^ mask) * width : ((q ^ mask) + 1) * width] for q in range(shards)]
    return jnp.concatenate(blocks, axis=1)


def stack8(*rows):
    rows = [row.reshape(1, -1) for row in rows]
    return jnp.concatenate(rows + [jnp.zeros((8 - len(rows), rows[0].shape[1]), F32)], axis=0)


def local(
    batch_size,
    shards,
    tokens,
    lengths,
    block_swap,
    input_weight,
    input_bias,
    out_weight,
    out_bias,
    gain_one,
    shift_one,
    up_weight,
    up_bias,
    down_weight,
    down_bias,
    gain_two,
    shift_two,
    cotangent,
):
    move = Mover(batch_size, shards)
    heads = block_swap.shape[0]
    rows, dim = tokens.shape
    width = input_weight.shape[2]
    depth = width // heads
    hidden_own = up_weight.shape[1]
    piece = dim // PARTS
    batch_at, head_at = lax.axis_index("batch"), lax.axis_index("head")
    part = batch_at % PARTS
    blocks = SEQ_LEN // rows
    length = lax.dynamic_index_in_dim(lengths, head_at // blocks, 0, keepdims=False)
    block_at = head_at % blocks
    own_live = jnp.clip(length - block_at * rows, 0, rows)
    partner_live = jnp.clip(length - (blocks - 1 - block_at) * rows, 0, rows)

    input_piece = lax.dynamic_slice_in_dim(input_weight, part * piece, piece, 1)
    input_piece = jnp.concatenate([input_piece[1], input_piece[2], input_piece[0]], axis=1)
    input_column = move.column(input_piece)
    small = jnp.concatenate([input_bias.reshape(-1), block_swap.astype(F32)])
    small_far = move.head(small, 2)
    up_own = up_weight.T.reshape(PARTS, piece, dim)
    up_piece = lax.dynamic_index_in_dim(up_own, part, 0, keepdims=False)
    up_far = move.head(up_piece, 2)
    input_own = input_weight.transpose(0, 2, 1)
    down_own = down_weight.reshape(PARTS, piece, dim)
    down_piece = lax.dynamic_index_in_dim(down_own, part, 0, keepdims=False)
    short_info = jnp.stack([own_live, part, head_at]).astype(jnp.int32)
    up_bias_parts = up_bias.reshape(shards, PARTS, 1, piece)
    out_parts = out_weight.reshape(shards, width, dim)
    vectors_one = stack8(out_bias, gain_one, shift_one)
    vectors_two = stack8(gain_one, shift_one, down_bias, gain_two, shift_two)
    vectors_back = stack8(gain_one)
    *input_column, small_far, up_far, tokens_sent = all_after(
        (*input_column, small_far, up_far, tokens), vectors_one, vectors_two, down_piece
    )
    input_column = jnp.stack(input_column)
    input_low = move.low(input_column)
    up_ends = pair_of(up_piece, up_far)
    up_others = move.head(up_ends, 1)
    small_ends = pair_of(small, small_far)
    small_others = move.head(small_ends, 1)
    partner = move.head(tokens_sent, 1)
    input_pair = pair_of(input_column, input_low)
    input_high = move.high(input_pair)
    small = jnp.stack([small_ends[0], small_others[0], small_ends[1], small_others[1]])
    info = jnp.concatenate(
        [
            small[:, 2 * width :].reshape(-1).astype(jnp.int32),
            jnp.stack([own_live, partner_live, part, head_at]).astype(jnp.int32),
        ]
    )
    bias = jnp.concatenate(
        [jnp.zeros((shards, width), F32), small[:, width : 2 * width], small[:, :width]], axis=1
    )
    bias = jnp.broadcast_to(bias[:, None], (shards, 8, 3 * width))
    input_high, up_others = all_after((input_high, up_others), info, bias)
    up_column = jnp.stack([up_others[0], up_ends[1], up_others[1]])
    up_low = move.low(up_column)
    input_near = four_of(input_pair, input_high)
    input_far = move.core(input_near)
    up_pair = pair_of(up_column, up_low)
    up_high = move.high(up_pair)
    down_piece, partner, up_pair = all_after((down_piece, partner, up_pair))
    down_far = move.head(down_piece, 2)

    def attend_shards(first_shard, count, last, weights, carried, so_far):
        return attend(
            (heads, depth, first_shard, last),
            count,
            info,
            tokens,
            partner,
            bias,
            out_parts,
            vectors_one,
            weights,
            carried,
            so_far,
        )

    qkv, context_0, stats, total = attend_shards(0, 1, False, [input_own], [], [])
    input_far, down_far, total, qkv, stats = all_after((input_far, down_far, total, qkv, stats))
    others = [input_near, input_far]
    down_ends = pair_of(down_piece, down_far)
    down_others = move.head(down_ends, 1)
    total, down_ends = all_after((total, down_ends))
    qkv, context_1, stats, total = attend_shards(1, 2, False, others, [total], [qkv, stats])
    up_high, down_others, total, qkv, stats = all_after((up_high, down_others, total, qkv, stats))
    up_near = four_of(up_pair, up_high)
    up_far = move.core(up_near)
    down_column = jnp.stack([down_others[0], down_ends[1], down_others[1]])
    down_low = move.low(down_column)
    total, up_near, down_column = all_after((total, up_near, down_column))
    qkv, context, stats, rows_one, normed = attend_shards(
        3, 1, True, others, [total, context_0, context_1], [qkv, stats]
    )
    up_far, down_low, normed, context = all_after((up_far, down_low, normed, context))
    up_all = (up_own, up_near, up_far)
    down_pair = pair_of(down_column, down_low)
    down_high = move.high(down_pair)
    normed, down_pair = all_after((normed, down_pair))
    hidden_near, hidden_far, *slopes = feed_up(short_info, normed, up_all, up_bias_parts)
    down_high, hidden_near, hidden_far = all_after((down_high, hidden_near, hidden_far))
    down_near = four_of(down_pair, down_high)
    down_far = move.core(down_near)
    down_all = (down_own, down_near, down_far)
    hidden_received = move.core(hidden_far)
    normed_received = move.core(after(normed, hidden_near))
    context_received = move.core(after(context, hidden_near))
    mixed_out, grad_second, grad_branch, sums_two = feed_down(
        short_info, (hidden_near, hidden_far), down_all, rows_one, cotangent, vectors_two
    )

    branch_received = move.core(grad_branch)
    tokens_t, partner_t = turn(after(tokens, grad_branch), partner)
    branch_received, tokens_t, partner_t = all_after((branch_received, tokens_t, partner_t))
    down_mine, down_one, down_two, down_three = row_grads(
        shards,
        hidden_near,
        hidden_received,
        after(grad_branch, tokens_t),
        branch_received,
        "down_grads",
    )
    down_three = move.low(down_three)
    pre_near, pre_far, up_bias_sums = grad_pre_of(
        short_info, after(grad_branch, down_two), down_all, slopes
    )
    down_three, pre_near, pre_far, up_bias_sums = all_after(
        (down_three, pre_near, pre_far, up_bias_sums)
    )
    pre_received = move.core(pre_far)
    down_two = (down_two + down_three.astype(F32)).astype(BF16)
    down_high = move.high(down_two)
    grad_first, grad_proj, sums_one = up_back(
        short_info, (pre_near, pre_far), up_all, rows_one, after(grad_second, down_two), vectors_back
    )
    pre_received, down_high, grad_proj, grad_first, sums_one = all_after(
        (pre_received, down_high, grad_proj, grad_first, sums_one)
    )
    proj_received = move.core(grad_proj)
    down_one = move.low(after(down_one, down_high))

    def core_sum(mine, received):
        mine, received = (a.reshape(2, 2, *a.shape[1:]) for a in (mine, received))
        keep = mine[:, 0].astype(F32) + received[:, 0].astype(F32)
        return keep, (mine[:, 1].astype(F32) + received[:, 1].astype(F32)).astype(BF16)

    def fold_low(keep, received):
        return keep[0] + received[0].astype(F32), (keep[1] + received[1].astype(F32)).astype(BF16)

    def fold_high(own, received):
        total = own + received.astype(F32)
        return total[0::2], total[1::2].astype(BF16)

    def fold_near(own, received):
        return own[0] + received[0].astype(F32), (own[1] + received[1].astype(F32)).astype(BF16)

    def fold_last(own, received):
        return move.settle(own + received.astype(F32))

    up_mine, up_one, up_two, up_three = row_grads(
        shards, pre_near, pre_received, normed, normed_received, "up_grads"
    )
    proj_received, up_one, up_three = all_after((proj_received, up_one, up_three))
    up_three = move.low(up_three)
    out_keep, out_send = out_grads(
        short_info, after(grad_proj, up_one), proj_received, context, context_received
    )
    down_one, out_keep, out_send = all_after((down_one, out_keep, out_send))
    up_one = move.low(after(up_one, down_one))
    out_low = move.low(out_send)
    down_mine = down_mine + (down_one.astype(F32) + down_high.astype(F32))
    down_mine, down_next = down_mine[0::2], down_mine[1::2].astype(BF16)
    down_near = move.head(down_next, 1)

    def back(grad, first_shard, count, carried, so_far):
        return attend_back(
            (heads, depth, first_shard, count, shards),
            info,
            tokens_t,
            partner_t,
            grad,
            out_parts,
            [] if first_shard else [input_own],
            *others,
            qkv,
            stats,
            carried,
            so_far,
        )

    own_rows, partner_rows, late_near, late_far, late_bias = back(
        after(grad_proj, out_send, down_next), 2, 2, [], []
    )

    (
        down_near,
        up_one,
        up_three,
        out_low,
        own_rows,
        partner_rows,
        late_near,
        late_far,
        late_bias,
    ) = all_after(
        (
            down_near,
            up_one,
            up_three,
            out_low,
            own_rows,
            partner_rows,
            late_near,
            late_far,
            late_bias,
        )
    )
    up_next = (up_two + up_three.astype(F32)).astype(BF16)
    up_mine = up_mine + up_one.astype(F32)
    up_high = move.high(up_next)
    late_core = move.core(late_far)
    down_mine, down_next = fold_near(down_mine, after(down_near, up_next))
    down_last = move.head(down_next, 2)
    out_mine = out_keep[0] + out_low[0].astype(F32)
    out_next = (out_keep[1] + out_low[1].astype(F32)).astype(BF16)
    out_high = move.high(out_next)
    own_rows, partner_rows, *early = back(
        after(grad_proj, down_next, up_next, out_next), 1, 1, [own_rows, partner_rows], []
    )

    up_high, down_last, late_core, out_high, own_rows, partner_rows, *early = all_after(
        (up_high, down_last, late_core, out_high, own_rows, partner_rows, *early)
    )
    up_mine, up_next = fold_high(up_mine, up_high)
    up_near = move.head(up_next, 1)
    late_keep, late_next = core_sum(late_near, late_core)
    late_low = move.low(late_next)
    down_total = fold_last(down_mine, down_last)
    down_low = move.low(down_total)
    out_next = (out_mine + out_high.astype(F32)).astype(BF16)
    out_near = move.head(out_next, 1)
    own_rows, partner_rows, early_near, early_far, early_bias = back(
        after(grad_proj, up_next, down_total, late_next, out_next),
        0,
        1,
        [own_rows, partner_rows],
        early,
    )

    up_near, down_low, late_low, out_near, own_rows, partner_rows = all_after(
        (up_near, down_low, late_low, out_near, own_rows, partner_rows), early_bias
    )
    early_near, early_far, early_bias = all_after((early_near, early_far, early_bias), up_near)

    from_partner = move.head(partner_rows, 1)
    early_core = move.core(early_far)
    vectors = jnp.concatenate(
        [
            sums_one[:3],
            sums_two[:3],
            up_bias_sums[:, :, 0].reshape(shards, dim),
            jnp.pad(jnp.concatenate([early_bias, late_bias])[:, 0], ((0, 0), (0, dim - 3 * width))),
        ]
    )
    hops = move.hops()

    def hop(value, sent, event):
        value = value + after(sent, event)
        return value, hops.pop(0)(value) if hops else None

    up_mine, up_next = fold_near(up_mine, up_near)
    up_last = move.head(up_next, 2)
    late_mine, late_next = fold_low(late_keep, after(late_low, up_next))
    late_high = move.high(late_next)
    early_keep, early_next = core_sum(early_near, after(early_core, late_next))
    early_low = move.low(early_next)
    down_pair = pair_of(down_total, after(down_low, early_next))
    down_high = move.high(down_pair)
    out_near = shards_swapped(out_near, shards, 1)
    out_next = (out_next.astype(F32) + out_near.astype(F32)).astype(BF16)
    out_last = move.head(out_next, 2)
    vectors_sent = hops.pop(0)(after(vectors, out_next))
    late_mine = late_mine + after(late_high, out_next).astype(F32)
    early_mine, early_next = fold_low(early_keep, after(early_low, late_mine))
    early_high = move.high(early_next)
    vectors, vectors_sent = hop(vectors, vectors_sent, early_next)
    up_total = fold_last(up_mine, after(up_last, vectors))
    out_last = shards_swapped(after(out_last, vectors), shards, 2)
    out_total = move.settle(out_next.astype(F32) + out_last.astype(F32))
    up_total = jnp.concatenate([up_total, out_total], axis=1)
    up_low = move.low(up_total)
    early_mine = early_mine + after(early_high, up_total).astype(F32)
    input_next = jnp.stack([early_mine[1], late_mine[1]]).astype(BF16)
    input_near = move.head(input_next, 1)
    down_near = four_of(down_pair, after(down_high, input_next))
    down_far = move.core(down_near)
    vectors, vectors_sent = hop(vectors, vectors_sent, down_near)
    up_pair = pair_of(up_total, after(up_low, vectors))
    up_high = move.high(up_pair)
    input_mine, input_next = fold_near(
        jnp.stack([early_mine[0], late_mine[0]]), after(input_near, up_pair)
    )
    input_last = move.head(input_next, 2)
    vectors, vectors_sent = hop(vectors, vectors_sent, input_next)
    grad_tokens = grad_first + own_rows + after(from_partner, vectors).astype(F32)
    input_total = fold_last(input_mine, after(input_last, grad_tokens))
    input_low = move.low(input_total)
    up_near = four_of(up_pair, after(up_high, input_total))
    up_far = move.core(up_near)
    vectors, vectors_sent = hop(vectors, vectors_sent, up_near)
    input_pair = pair_of(input_total, after(input_low, vectors))
    input_high = move.high(input_pair)
    while vectors_sent is not None:
        vectors, vectors_sent = hop(vectors, vectors_sent, input_pair)
    grad_down = pl.pallas_call(
        settle_down_kernel,
        in_specs=[SMEM] + [whole(4, piece, dim)] * 2,
        out_shape=shape((PARTS, piece, dim), F32),
        compiler_params=PARAMS,
        name="settle_down",
    )(short_info, after(down_near, input_pair), down_far)
    input_near = four_of(input_pair, after(input_high, grad_down))
    input_done = (input_near, move.core(input_near))
    up_done = (after(up_near, input_near), up_far)
    grad_input_bias = jnp.stack([vectors[10, 2 * width : 3 * width], vectors[10, width : 2 * width]])
    grad_up_bias = vectors[6]
    grad_up, grad_out = pl.pallas_call(
        settle_up_kernel,
        in_specs=[SMEM] + [whole(4, piece, dim + shards * width)] * 2,
        out_shape=[shape((dim, hidden_own), F32), shape((shards, width, dim), F32)],
        scratch_shapes=[pltpu.VMEM((PARTS, piece, dim), F32)] * 2,
        compiler_params=PARAMS,
        name="settle_up",
    )(short_info, *up_done)
    grad_input_weight = pl.pallas_call(
        settle_input_kernel,
        in_specs=[SMEM] + [whole(4, piece, 3 * width)] * 2,
        out_shape=shape((3, width, dim), F32),
        scratch_shapes=[pltpu.VMEM((PARTS, piece, 3 * width), F32)],
        compiler_params=PARAMS,
        name="settle_input",
    )(short_info, *input_done)
    return (
        mixed_out,
        grad_tokens,
        grad_input_weight.transpose(0, 2, 1),
        grad_input_bias,
        grad_out.reshape(dim, dim),
        vectors[0],
        vectors[1],
        vectors[2],
        grad_up,
        grad_up_bias,
        grad_down.reshape(hidden_own, dim),
        vectors[3],
        vectors[4],
        vectors[5],
    )


def solution(mesh):
    rows_spec = P(("batch", "head"), None)
    placed = (
        rows_spec,
        P("batch"),
        P("head"),
        P(None, None, "head"),
        P(None, "head"),
        P(),
        P(),
        P(),
        P(),
        P(None, "head"),
        P(),
        P("head", None),
        P(),
        P(),
        P(),
        rows_spec,
    )
    return jax.shard_map(
        functools.partial(local, mesh.shape["batch"], mesh.shape["head"]),
        mesh=mesh,
        in_specs=placed,
        out_specs=(
            rows_spec,
            rows_spec,
            P(None, None, "head"),
            P(None, "head"),
            P(),
            P(),
            P(),
            P(),
            P(None, "head"),
            P("head"),
            P("head", None),
            P(),
            P(),
            P(),
        ),
        check_vma=False,
    )
```

```python
import functools

import jax
import jax.numpy as jnp
from jax import lax
from jax.experimental import pallas as pl
from jax.experimental.pallas import tpu as pltpu
from jax.sharding import PartitionSpec as P

SEQ_LEN = 1024
EPSILON = 1e-05
F32 = jnp.float32
BF16 = jnp.bfloat16
VMEM_LIMIT = 24 * 1024 * 1024
PARAMS = pltpu.CompilerParams(vmem_limit_bytes=VMEM_LIMIT)
LARGE = pltpu.CompilerParams(vmem_limit_bytes=44 * 1024 * 1024)
CORE = 1
PARTS = 8
SPOTS = 4


def dot(left_side, right_side, left_dim=1, right_dim=0):
    return lax.dot_general(
        left_side,
        right_side,
        (((left_dim,), (right_dim,)), ((), ())),
        preferred_element_type=F32,
    )


def unit_parts(values):
    centred = values - jnp.mean(values, axis=-1, keepdims=True)
    inverse = lax.rsqrt(jnp.mean(centred * centred, axis=-1, keepdims=True) + EPSILON)
    return centred * inverse, inverse


def norm_back(grad_rows, unit_rows, inverse, gain_row):
    scaled = grad_rows * gain_row
    return inverse * (
        scaled
        - jnp.mean(scaled, axis=-1, keepdims=True)
        - unit_rows * jnp.mean(scaled * unit_rows, axis=-1, keepdims=True)
    )


def column_sum(values):
    return jnp.sum(values, axis=0, keepdims=True)


def gelu_parts(inner):
    below = 0.5 + 0.5 * lax.erf(inner * 0.7071067811865476)
    bell = jnp.exp(inner * inner * -0.5) * 0.3989422804014327
    return inner * below, below + inner * bell


def row_chunks(rows, step):
    return [slice(i, i + step) for i in range(0, rows, step)]


def eight_sum(values):
    return sum(values[cut] for cut in row_chunks(values.shape[0], 8))


def lane_pick(values, depth):
    lane = lax.broadcasted_iota(jnp.int32, (1, len(values) * depth), 1)
    picked = jnp.full(lane.shape, values[0], jnp.int32)
    for j in range(1, len(values)):
        picked = jnp.where(lane >= j * depth, values[j], picked)
    return picked


def place_of(part, half, spot):
    seen = part ^ half
    core = seen & 1
    low, high = 2 + 2 * core, 4 - 2 * core
    return seen ^ (low * (spot & 1) + high * (spot >> 1))


class Info:
    def __init__(self, ref, heads, shards):
        self.ref, self.heads, self.base = ref, heads, heads * shards

    def swaps(self, shard):
        return [self.ref[shard * self.heads + j] for j in range(self.heads)]

    own_live = property(lambda self: self.ref[self.base])
    partner_live = property(lambda self: self.ref[self.base + 1])
    part = property(lambda self: self.ref[self.base + 2])
    head_at = property(lambda self: self.ref[self.base + 3])


def gathered(part, near, far, scratch):
    for spot in range(SPOTS):
        scratch[place_of(part, 0, spot)] = near[spot, 0]
        scratch[place_of(part, 1, spot)] = far[spot, 0]
    return scratch[...].reshape(-1, scratch.shape[2])


def attend_kernel(setting, info_ref, tokens, partner, bias, out_weight, vectors, *refs):
    heads, depth, first_shard, last = setting
    refs = list(refs)
    if first_shard == 0:
        turned = refs.pop(0)
        total_in = None
    else:
        near, far, total_in = refs[:3]
        del refs[:3]
    earlier = []
    if last:
        earlier = refs[:2]
        del refs[:2]
    if first_shard:
        del refs[:2]
    qkv_out, context_out, stats_out = refs[:3]
    step = pl.program_id(0)
    shard = first_shard + step
    info = Info(info_ref, heads, out_weight.shape[0])
    if first_shard:
        weight = gathered(info.part, near, far, refs.pop())
    total = refs.pop()
    swaps = info.swaps(shard)
    rows, dim = tokens.shape
    width = heads * depth
    x, xp = tokens[...], partner[...]
    if first_shard:
        own = dot(x, weight)
        other = dot(xp, weight[:, : 2 * width])
    else:
        kv_rows = jnp.concatenate([turned[1], turned[2]], axis=0)
        own = jnp.concatenate([dot(x, kv_rows, 1, 1), dot(x, turned[0], 1, 1)], axis=1)
        other = dot(xp, kv_rows, 1, 1)
    swapped = lane_pick(swaps + swaps, depth) == 1
    bias_row = bias[0, 0:1]
    kv, q = [], []
    for cut in row_chunks(rows, 32):
        mine = own[cut] + bias_row
        theirs = other[cut] + bias_row[:, : 2 * width]
        kv.append(jnp.where(swapped, theirs, mine[:, : 2 * width]).astype(BF16))
        q.append(mine[:, 2 * width :].astype(BF16) * (depth**-0.5))
    kv, q = jnp.concatenate(kv, axis=0), jnp.concatenate(q, axis=0)
    qkv_out[0, :, : 2 * width] = kv
    qkv_out[0, :, 2 * width :] = q
    stats = []
    pieces = []
    for j in range(heads):
        head = slice(j * depth, (j + 1) * depth)
        live = jnp.where(swaps[j] == 1, info.partner_live, info.own_live)
        anyone = jnp.where(live > 0, 1.0, 0.0).astype(F32)
        scores = dot(kv[:, head], q[:, head], 1, 1)
        masked, most = [], None
        for cut in row_chunks(rows, 32):
            index = cut.start + lax.broadcasted_iota(jnp.int32, (32, 1), 0)
            part = jnp.where(index < live, scores[cut], -1e30)
            masked.append(part)
            for tile in row_chunks(32, 8):
                most = part[tile] if most is None else jnp.maximum(most, part[tile])
        largest = jnp.max(most, axis=0, keepdims=True)
        largest = jnp.where(anyone > 0.5, largest, 0.0)
        total_rows = None
        for part in masked:
            weights = eight_sum(jnp.exp(part - largest))
            total_rows = weights if total_rows is None else total_rows + weights
        stat = largest + jnp.log(column_sum(total_rows) + (1.0 - anyone))
        mixing = [jnp.exp(part - stat).astype(BF16) for part in masked]
        stats.append(stat)
        values = kv[:, width + j * depth : width + (j + 1) * depth]
        pieces.append(dot(values, jnp.concatenate(mixing, axis=0), 0, 0))
    context = jnp.concatenate(pieces, axis=0).T.astype(BF16)
    stats_out[0] = jnp.concatenate(stats + [jnp.zeros((8 - heads, rows), F32)], axis=0)
    projected = dot(context, out_weight[info.head_at ^ shard])
    if not last:
        context_out[0] = context

        @pl.when(step == 0)
        def first():
            total[...] = projected if total_in is None else total_in[...] + projected

        @pl.when(step > 0)
        def later():
            total[...] += projected

        return

    context_out[...] = jnp.concatenate(
        [ref[q] for ref in earlier for q in range(ref.shape[0])] + [context], axis=1
    )
    rows_out, normed_out = refs[3:]
    for cut in row_chunks(rows, 16):
        values = x[cut].astype(F32) + ((total_in[cut] + projected[cut]) + vectors[0:1])
        rows_out[cut] = values
        unit, _ = unit_parts(values)
        normed_out[cut] = (unit * vectors[1:2] + vectors[2:3]).astype(BF16)


def tiles_of(part, own, near, far, run):
    @pl.when(pl.program_id(0) == 0)
    def mine():
        run(
            *(
                jnp.concatenate([own[place_of(part, half, spot)] for spot in range(SPOTS)], axis=0)
                for half in range(2)
            )
        )

    @pl.when(pl.program_id(0) > 0)
    def other():
        run(*(ref[:, 0].reshape(-1, ref.shape[3]) for ref in (near, far)))


def add_up(total, *partials):
    @pl.when(pl.program_id(0) == 0)
    def start():
        total[...] = sum(partials[1:], partials[0])

    @pl.when(pl.program_id(0) > 0)
    def later():
        total[...] = sum(partials, total[...])


def at_end(run):
    pl.when(pl.program_id(0) == pl.num_programs(0) - 1)(run)


def eight_rows(*rows):
    width = rows[0].shape[1]
    return jnp.concatenate([*rows, jnp.zeros((8 - len(rows), width), F32)], axis=0)


def feed_up_kernel(info, normed, own, near, far, bias, *outs):
    shard = info[2] ^ pl.program_id(0)

    def run(*tiles):
        for half, tile in enumerate(tiles):
            places = [place_of(info[1], half, spot) for spot in range(SPOTS)]
            bias_row = jnp.concatenate([bias[shard, place] for place in places], axis=1)
            pre = dot(normed[...], tile, 1, 1)
            for cut in row_chunks(pre.shape[0], 32):
                hidden, slope = gelu_parts(pre[cut] + bias_row)
                outs[half][cut] = hidden.astype(BF16)
                outs[half + 2][cut] = slope

    tiles_of(info[1], own, near, far, run)


def feed_down_kernel(
    info,
    near_hidden,
    far_hidden,
    own,
    near,
    far,
    rows_in,
    cotangent,
    vectors,
    mixed_out,
    second_out,
    grad_out,
    sums_out,
    total,
):
    def run(near_tile, far_tile):
        add_up(total, dot(near_hidden[...], near_tile), dot(far_hidden[...], far_tile))

    tiles_of(info[1], own, near, far, run)

    @at_end
    def finish():
        sums = [jnp.zeros((8, rows_in.shape[1]), F32)] * 3
        for cut in row_chunks(rows_in.shape[0], 16):
            unit_one, _ = unit_parts(rows_in[cut])
            first_norm = unit_one * vectors[0:1] + vectors[1:2]
            unit, inverse = unit_parts(first_norm + (total[cut] + vectors[2:3]))
            index = cut.start + lax.broadcasted_iota(jnp.int32, (16, 1), 0)
            mask = jnp.where(index < info[0], 1.0, 0.0).astype(F32)
            mixed_out[cut] = ((unit * vectors[3:4] + vectors[4:5]) * mask).astype(BF16)
            incoming = cotangent[cut].astype(F32) * mask
            grad = norm_back(incoming, unit, inverse, vectors[3:4])
            second_out[cut] = grad
            low = grad.astype(BF16)
            grad_out[cut] = low
            more = (low.astype(F32), incoming * unit, incoming)
            sums = [a + eight_sum(b) for a, b in zip(sums, more)]
        sums_out[...] = eight_rows(*(column_sum(a) for a in sums))


def grad_pre_kernel(
    info, grad_branch, own, near, far, near_slope, far_slope, near_out, far_out, bias_out
):
    def run(*tiles):
        for half, tile in enumerate(tiles):
            out, slope = (near_out, far_out)[half], (near_slope, far_slope)[half]
            grad = dot(grad_branch[...], tile, 1, 1)
            sums = jnp.zeros((8, grad.shape[1]), F32)
            for cut in row_chunks(grad.shape[0], 32):
                low = (grad[cut] * slope[cut]).astype(BF16)
                out[cut] = low
                sums = sums + eight_sum(low.astype(F32))
            sums = jnp.broadcast_to(column_sum(sums), sums.shape)
            width = bias_out.shape[3]
            for spot in range(SPOTS):
                row = sums[:, spot * width : (spot + 1) * width]
                bias_out[info[2] ^ pl.program_id(0), place_of(info[1], half, spot)] = row

    tiles_of(info[1], own, near, far, run)


def up_back_kernel(
    info,
    near_pre,
    far_pre,
    own,
    near,
    far,
    rows_in,
    second_in,
    vectors,
    first_out,
    proj_out,
    sums_out,
    total,
):
    def run(near_tile, far_tile):
        add_up(total, dot(near_pre[...], near_tile), dot(far_pre[...], far_tile))

    tiles_of(info[1], own, near, far, run)

    @at_end
    def finish():
        sums = [jnp.zeros((8, rows_in.shape[1]), F32)] * 3
        for cut in row_chunks(rows_in.shape[0], 16):
            unit, inverse = unit_parts(rows_in[cut])
            grad_normed = second_in[cut] + total[cut]
            grad = norm_back(grad_normed, unit, inverse, vectors[0:1])
            first_out[cut] = grad
            low = grad.astype(BF16)
            proj_out[cut] = low
            more = (low.astype(F32), grad_normed * unit, grad_normed)
            sums = [a + eight_sum(b) for a, b in zip(sums, more)]
        sums_out[...] = eight_rows(*(column_sum(a) for a in sums))


def turn_kernel(tokens, partner, tokens_out, partner_out):
    tokens_out[...] = tokens[...].T
    partner_out[...] = partner[...].T


def row_grads_kernel(mine, theirs, my_rows, their_rows, *outs):
    value = dot(mine[...], my_rows[...], 0, 0) + dot(theirs[...], their_rows[...], 0, 0)
    value = value.reshape(SPOTS, -1, value.shape[1])
    for spot, out in enumerate(outs):
        out[0] = value[spot].astype(out.dtype)


def out_grads_kernel(info, mine, theirs, my_context, their_context, keep_out, send_out, turned):
    value = 0.0
    for i, (grad, context) in enumerate(((mine, my_context), (theirs, their_context))):
        turned[i] = grad[...].T.reshape(turned.shape[1:])
        rows = [turned[i, place_of(info[1], 0, spot)] for spot in range(SPOTS)]
        value = value + dot(jnp.concatenate(rows, axis=0), context[...])
    value = value.reshape(SPOTS, -1, value.shape[1])
    for spot in range(SPOTS):
        out = (keep_out, send_out)[spot & 1]
        out[spot >> 1] = value[spot].astype(out.dtype)


def scatter_parts(part, value, chunks, near_out, far_out):
    chunks[...] = value.reshape(chunks.shape)
    for spot in range(SPOTS):
        near_out[spot, 0] = chunks[place_of(part, 0, spot)]
        far_out[spot, 0] = chunks[place_of(part, 1, spot)]


def attend_back_kernel(setting, info_ref, tokens_t, partner_t, grad_proj, out_weight, *refs):
    heads, depth, first_shard, carried, so_far, shards = setting
    refs = list(refs)
    if first_shard == 0:
        turned = refs.pop(0)
    near, far, qkv_in, stats_in = refs[:4]
    del refs[:4]
    if carried:
        own_in, partner_in = refs[:2]
        del refs[:2]
    del refs[:so_far]
    own_out, partner_out, near_out, far_out, bias_out, total, weight_scratch, chunks = refs
    step = pl.program_id(0)
    shard = first_shard + step
    info = Info(info_ref, heads, shards)
    if first_shard:
        gathered(info.part, near, far, weight_scratch)
    else:
        width = turned.shape[1]

        @pl.when(shard == 0)
        def own_weight():
            rows_kv = jnp.concatenate([turned[1], turned[2], turned[0]], axis=0)
            weight_scratch[...] = rows_kv.T.reshape(weight_scratch.shape)

        @pl.when(shard > 0)
        def other_weight():
            gathered(info.part, near, far, weight_scratch)

    weight = weight_scratch[...].reshape(-1, weight_scratch.shape[2])
    swaps = info.swaps(shard)
    dim, rows = tokens_t.shape
    width = heads * depth
    grad = dot(grad_proj[...], out_weight[0], 1, 1).astype(BF16)
    k, v, q = (qkv_in[0, :, i * width : (i + 1) * width] for i in range(3))
    stats = stats_in[0]
    gq, gk, gv = [], [], []
    for j in range(heads):
        head = slice(j * depth, (j + 1) * depth)
        stat = stats[j : j + 1, :]
        live = jnp.where(swaps[j] == 1, info.partner_live, info.own_live)
        scores = dot(k[:, head], q[:, head], 1, 1)
        grad_mix = dot(v[:, head], grad[:, head], 1, 1)
        chances, shared = [], jnp.zeros((8, rows), F32)
        for cut in row_chunks(rows, 32):
            index = cut.start + lax.broadcasted_iota(jnp.int32, (32, 1), 0)
            part = jnp.exp(jnp.where(index < live, scores[cut] - stat, -10000.0))
            chances.append(part)
            shared = shared + eight_sum(part * grad_mix[cut])
        shared = column_sum(shared)
        mixing = jnp.concatenate([part.astype(BF16) for part in chances], axis=0)
        grad_scores = jnp.concatenate(
            [
                (part * (grad_mix[cut] - shared)).astype(BF16)
                for part, cut in zip(chances, row_chunks(rows, 32))
            ],
            axis=0,
        )
        gk.append(dot(grad_scores, q[:, head]))
        gv.append(dot(mixing, grad[:, head]))
        gq.append(dot(k[:, head], grad_scores, 0, 0))
    grad_q = (jnp.concatenate(gq, axis=0).T * (depth**-0.5)).astype(BF16)
    grad_kv = jnp.concatenate(gk + gv, axis=1).astype(BF16)
    swapped = lane_pick(swaps + swaps, depth) == 1
    nothing = jnp.zeros((), BF16)
    grad_own = jnp.concatenate([jnp.where(swapped, nothing, grad_kv), grad_q], axis=1)
    grad_far = jnp.where(swapped, grad_kv, nothing)
    own = dot(grad_own, weight, 1, 1)
    other = dot(grad_far, weight[:, : 2 * width], 1, 1)

    @pl.when(step == 0)
    def first():
        own_out[...] = own_in[...] + own if carried else own
        total[...] = partner_in[...] + other if carried else other

    @pl.when(step > 0)
    def later():
        own_out[...] += own
        total[...] += other

    @at_end
    def finish():
        partner_out[...] = total[...].astype(partner_out.dtype)

    grads = dot(tokens_t[...], grad_own)
    grads_kv = grads[:, : 2 * width] + dot(partner_t[...], grad_far)
    grads = jnp.concatenate([grads_kv, grads[:, 2 * width :]], axis=1).astype(BF16)
    chunks[...] = grads.reshape(chunks.shape)
    for spot in range(SPOTS):
        near_out[spot, 0] = chunks[place_of(info.part, 0, spot)]
        far_out[spot, 0] = chunks[place_of(info.part, 1, spot)]
    bias_out[0] = jnp.broadcast_to(
        jnp.concatenate(
            [column_sum(grad_kv.astype(F32)), column_sum(grad_q.astype(F32))], axis=1
        ),
        bias_out.shape[1:],
    )


def settle_down_kernel(info, near, far, out):
    for half, source in enumerate((near, far)):
        for spot in range(SPOTS):
            out[place_of(info[1], half, spot)] = source[spot].astype(F32)


def settle_up_kernel(info, near, far, up_out, out_out, up_scratch, out_scratch):
    dim = up_out.shape[0]
    for half, source in enumerate((near, far)):
        for spot in range(SPOTS):
            place = place_of(info[1], half, spot)
            value = source[spot].astype(F32)
            up_scratch[place] = value[:, :dim]
            out_scratch[place] = value[:, dim:]
    up_out[...] = up_scratch[...].reshape(-1, dim).T
    shards = out_out.shape[0]
    turned = out_scratch[...].reshape(-1, dim).T.reshape(shards, -1, dim)
    for q in range(shards):
        out_out[info[2] ^ q] = turned[q]


def settle_input_kernel(info, near, far, out, scratch):
    width = out.shape[1]
    for half, source in enumerate((near, far)):
        for spot in range(SPOTS):
            scratch[place_of(info[1], half, spot)] = source[spot].astype(F32)
    turned = scratch[...].reshape(-1, scratch.shape[2]).T
    for i in range(3):
        out[(i + 1) % 3] = turned[i * width : (i + 1) * width]


def shape(dims, dtype):
    return jax.ShapeDtypeStruct(dims, dtype)


def whole(*dims):
    return pl.BlockSpec(dims, lambda *_: (0,) * len(dims))


def cost(flops, moved, slow=0):
    return pl.CostEstimate(flops=flops, bytes_accessed=moved, transcendentals=slow)


SMEM = pl.BlockSpec(memory_space=pltpu.SMEM)


def gathered_specs(near, first_shard):
    spots, _, piece, lanes = near.shape
    return [pl.BlockSpec((spots, 1, piece, lanes), lambda s: (0, s + first_shard - 1, 0, 0))] * 2


def attend(
    setting, count, info, tokens, partner, bias, out_weight, vectors, weights, carried, so_far
):
    heads, depth, first_shard, last = setting
    rows, dim = tokens.shape
    shards, width, _ = out_weight.shape
    lanes = 3 * width
    scratch = []
    if first_shard == 0:
        weight_specs = [whole(3, width, dim)]
    else:
        weight_specs = gathered_specs(weights[0], first_shard)
        scratch = [pltpu.VMEM((PARTS, dim // PARTS, lanes), BF16)]
    out_specs = [
        pl.BlockSpec((1, rows, lanes), lambda s: (s + first_shard, 0, 0)),
        whole(rows, dim) if last else pl.BlockSpec((1, rows, width), lambda s: (s, 0, 0)),
        pl.BlockSpec((1, 8, rows), lambda s: (s + first_shard, 0, 0)),
    ]
    out_shape = [
        shape((shards, rows, lanes), BF16),
        shape((rows, dim) if last else (count, rows, width), BF16),
        shape((shards, 8, rows), F32),
    ]
    fixed = 6 + len(weights) + len(carried)
    if last:
        out_specs += [whole(rows, dim)] * 2
        out_shape += [shape((rows, dim), F32), shape((rows, dim), BF16)]
        scratch = [pltpu.VMEM((8, 128), F32)] + scratch
    else:
        out_specs.append(whole(rows, dim))
        out_shape.append(shape((rows, dim), F32))
    return pl.pallas_call(
        functools.partial(attend_kernel, setting),
        grid=(count,),
        in_specs=[
            SMEM,
            whole(rows, dim),
            whole(rows, dim),
            pl.BlockSpec((1, 8, lanes), lambda s: (s + first_shard, 0, 0)),
            whole(shards, width, dim),
            whole(8, dim),
        ]
        + weight_specs
        + [whole(*value.shape) for value in carried]
        + [pl.BlockSpec(memory_space=pl.ANY)] * len(so_far),
        out_specs=out_specs,
        out_shape=out_shape,
        scratch_shapes=scratch,
        input_output_aliases={fixed + i: (0, 2)[i] for i in range(len(so_far))},
        compiler_params=PARAMS,
        cost_estimate=cost(
            count * (3 * rows * dim * dim + 4 * rows * rows * dim),
            count * 6 * rows * dim,
            count * heads * rows * rows,
        ),
        name="attend",
    )(info, tokens, partner, bias, out_weight, vectors, *weights, *carried, *so_far)


def feed_specs(near):
    spots, _, piece, lanes = near.shape
    other = pl.BlockSpec(
        (spots, 1, piece, lanes), lambda q: (0, jnp.maximum(q - 1, 0), 0, 0)
    )
    return [whole(PARTS, piece, lanes), other, other]


def feed_up(info, normed, weight, bias):
    rows, dim = normed.shape
    near = weight[1]
    shards = near.shape[1] + 1
    tile = SPOTS * near.shape[2]
    columns = pl.BlockSpec((rows, tile), lambda q: (0, q))
    return pl.pallas_call(
        feed_up_kernel,
        grid=(shards,),
        in_specs=[
            SMEM,
            whole(rows, dim),
            *feed_specs(near),
            whole(*bias.shape),
        ],
        out_specs=[columns] * 4,
        out_shape=[shape((rows, shards * tile), BF16)] * 2
        + [shape((rows, shards * tile), F32)] * 2,
        compiler_params=PARAMS,
        cost_estimate=cost(4 * rows * dim * tile * shards, 30 * rows * dim, rows * dim * 8),
        name="feed_up",
    )(info, normed, *weight, bias)


def feed_down(info, hidden, weight, rows_one, cotangent, vectors):
    rows, dim = rows_one.shape
    near = weight[1]
    shards = near.shape[1] + 1
    tile = SPOTS * near.shape[2]
    columns = pl.BlockSpec((rows, tile), lambda q: (0, q))
    return pl.pallas_call(
        feed_down_kernel,
        grid=(shards,),
        in_specs=[
            SMEM,
            columns,
            columns,
            *feed_specs(near),
            whole(rows, dim),
            whole(rows, dim),
            whole(8, dim),
        ],
        out_specs=[whole(rows, dim)] * 3 + [whole(8, dim)],
        out_shape=[
            shape((rows, dim), BF16),
            shape((rows, dim), F32),
            shape((rows, dim), BF16),
            shape((8, dim), F32),
        ],
        scratch_shapes=[pltpu.VMEM((rows, dim), F32)],
        compiler_params=LARGE,
        cost_estimate=cost(4 * rows * dim * tile * shards, 20 * rows * dim),
        name="feed_down",
    )(info, *hidden, *weight, rows_one, cotangent, vectors)


def grad_pre_of(info, grad_branch, weight, slopes):
    rows, dim = grad_branch.shape
    near = weight[1]
    shards = near.shape[1] + 1
    tile = SPOTS * near.shape[2]
    columns = pl.BlockSpec((rows, tile), lambda q: (0, q))
    return pl.pallas_call(
        grad_pre_kernel,
        grid=(shards,),
        in_specs=[SMEM, whole(rows, dim), *feed_specs(near), columns, columns],
        out_specs=[columns, columns, whole(shards, PARTS, 8, near.shape[2])],
        out_shape=[
            shape((rows, shards * tile), BF16),
            shape((rows, shards * tile), BF16),
            shape((shards, PARTS, 8, near.shape[2]), F32),
        ],
        compiler_params=PARAMS,
        cost_estimate=cost(4 * rows * dim * tile * shards, 30 * rows * dim),
        name="grad_pre",
    )(info, grad_branch, *weight, *slopes)


def up_back(info, pres, weight, rows_one, grad_second, vectors):
    rows, dim = rows_one.shape
    near = weight[1]
    shards = near.shape[1] + 1
    tile = SPOTS * near.shape[2]
    columns = pl.BlockSpec((rows, tile), lambda q: (0, q))
    return pl.pallas_call(
        up_back_kernel,
        grid=(shards,),
        in_specs=[
            SMEM,
            columns,
            columns,
            *feed_specs(near),
            whole(rows, dim),
            whole(rows, dim),
            whole(8, dim),
        ],
        out_specs=[whole(rows, dim), whole(rows, dim), whole(8, dim)],
        out_shape=[shape((rows, dim), F32), shape((rows, dim), BF16), shape((8, dim), F32)],
        scratch_shapes=[pltpu.VMEM((rows, dim), F32)],
        compiler_params=PARAMS,
        cost_estimate=cost(4 * rows * dim * tile * shards, 24 * rows * dim),
        name="up_back",
    )(info, *pres, *weight, rows_one, grad_second, vectors)


def turn(tokens, partner):
    rows, dim = tokens.shape
    return pl.pallas_call(
        turn_kernel,
        out_shape=[shape((dim, rows), BF16)] * 2,
        compiler_params=PARAMS,
        cost_estimate=cost(rows * dim, 8 * rows * dim),
        name="turn",
    )(tokens, partner)


def row_grads(shards, mine, theirs, my_rows, their_rows, name):
    rows, dim = my_rows.shape
    tile = mine.shape[1] // shards
    piece = tile // SPOTS
    columns = pl.BlockSpec((rows, tile), lambda q: (0, q))
    out = pl.BlockSpec((1, piece, dim), lambda q: (q, 0, 0))
    return pl.pallas_call(
        row_grads_kernel,
        grid=(shards,),
        in_specs=[columns, columns, whole(rows, dim), whole(rows, dim)],
        out_specs=[out] * SPOTS,
        out_shape=[shape((shards, piece, dim), (F32, BF16)[spot & 1]) for spot in range(SPOTS)],
        compiler_params=PARAMS,
        cost_estimate=cost(4 * rows * dim * tile * shards, 20 * rows * dim),
        name=name,
    )(mine, theirs, my_rows, their_rows)


def out_grads(info, mine, theirs, my_context, their_context):
    rows, dim = mine.shape
    piece = dim // PARTS
    return pl.pallas_call(
        out_grads_kernel,
        in_specs=[SMEM] + [whole(rows, dim)] * 4,
        out_specs=[whole(2, piece, dim)] * 2,
        out_shape=[shape((2, piece, dim), F32), shape((2, piece, dim), BF16)],
        scratch_shapes=[pltpu.VMEM((2, PARTS, piece, rows), BF16)],
        compiler_params=PARAMS,
        cost_estimate=cost(2 * rows * dim * dim, 10 * rows * dim),
        name="out_grads",
    )(info, mine, theirs, my_context, their_context)


def attend_back(
    setting,
    info,
    tokens_t,
    partner_t,
    grad_proj,
    out_weight,
    own,
    near,
    far,
    qkvs,
    stats,
    carried,
    so_far,
):
    heads, depth, first_shard, count, shards = setting
    half = shards // 2
    slot = first_shard % half
    fixed = 9 + len(own) + len(carried)
    dim, rows = tokens_t.shape
    width = heads * depth
    lanes = 3 * width
    piece = dim // PARTS
    head_spot = heads * shards + 3
    own_specs = [] if first_shard else [whole(3, width, dim)]
    kernel = functools.partial(
        attend_back_kernel, (heads, depth, first_shard, bool(carried), len(so_far), shards)
    )

    def other(s, info):
        return (0, jnp.maximum(s + first_shard - 1, 0), 0, 0)

    parts_out = pl.BlockSpec((SPOTS, 1, piece, lanes), lambda s, info: (0, s + slot, 0, 0))
    return pl.pallas_call(
        kernel,
        grid_spec=pltpu.PrefetchScalarGridSpec(
            num_scalar_prefetch=1,
            grid=(count,),
            in_specs=[
                whole(dim, rows),
                whole(dim, rows),
                whole(rows, dim),
                pl.BlockSpec(
                    (1, width, dim), lambda s, info: (info[head_spot] ^ (s + first_shard), 0, 0)
                ),
            ]
            + own_specs
            + [pl.BlockSpec((SPOTS, 1, piece, lanes), other)] * 2
            + [
                pl.BlockSpec((1, rows, lanes), lambda s, info: (s + first_shard, 0, 0)),
                pl.BlockSpec((1, 8, rows), lambda s, info: (s + first_shard, 0, 0)),
            ]
            + [whole(rows, dim)] * len(carried)
            + [pl.BlockSpec(memory_space=pl.ANY)] * len(so_far),
            out_specs=[
                whole(rows, dim),
                whole(rows, dim),
                parts_out,
                parts_out,
                pl.BlockSpec(
                    (1, 8, lanes), lambda s, info: (info[head_spot] ^ (s + first_shard), 0, 0)
                ),
            ],
            scratch_shapes=[
                pltpu.VMEM((rows, dim), F32),
                pltpu.VMEM((PARTS, piece, lanes), BF16),
                pltpu.VMEM((PARTS, piece, lanes), BF16),
            ],
        ),
        out_shape=[
            shape((rows, dim), F32),
            shape((rows, dim), F32 if first_shard else BF16),
            shape((SPOTS, half, piece, lanes), BF16),
            shape((SPOTS, half, piece, lanes), BF16),
            shape((shards, 8, lanes), F32),
        ],
        input_output_aliases={
            fixed + i: 5 - len(so_far) + i for i in range(len(so_far))
        },
        compiler_params=PARAMS,
        cost_estimate=cost(
            count * (6 * rows * dim * dim + 10 * rows * rows * dim),
            count * 8 * rows * dim,
            count * heads * rows * rows,
        ),
        name="attend_back",
    )(
        info,
        tokens_t,
        partner_t,
        grad_proj,
        out_weight,
        *own,
        near,
        far,
        qkvs,
        stats,
        *carried,
        *so_far,
    )


class Mover:
    def __init__(self, batch_size, shards):
        self.batch_size, self.shards = batch_size, shards

    def batch(self, value, mask_of):
        perm = [(i, i ^ mask_of(i)) for i in range(self.batch_size)]
        return lax.ppermute(value, "batch", perm)

    def core(self, value):
        return self.batch(value, lambda i: CORE)

    def low(self, value):
        return self.batch(value, lambda i: 4 if i & 1 else 2)

    def high(self, value):
        return self.batch(value, lambda i: 2 if i & 1 else 4)

    def head(self, value, mask):
        return lax.ppermute(value, "head", [(i, i ^ mask) for i in range(self.shards)])

    def along(self, values, first=1):
        return [self.head(value, q) for q, value in enumerate(values, first)]

    def column(self, piece):
        return self.along([piece] * (self.shards - 1))

    def settle(self, total):
        total = total.astype(BF16)
        mask = PARTS
        while mask < self.batch_size:
            other = self.batch(total, lambda i, mask=mask: mask)
            total = (total.astype(F32) + other.astype(F32)).astype(BF16)
            mask *= 2
        return total

    def hops(self):
        steps, mask = [], 1
        while mask < self.batch_size:
            steps.append(lambda value, mask=mask: self.batch(value, lambda i: mask))
            mask *= 2
        mask = 1
        while mask < self.shards:
            steps.append(lambda value, mask=mask: self.head(value, mask))
            mask *= 2
        return steps


def after(value, *events):
    return lax.optimization_barrier((value, *events))[0]


def all_after(values, *events):
    return lax.optimization_barrier((*values, *events))[: len(values)]


def pair_of(first, second):
    return jnp.stack([first, second])


def four_of(pair, received):
    return jnp.concatenate([pair, received])


def shards_swapped(value, shards, mask):
    width = value.shape[1] // shards
    blocks = [value[:, (q ^ mask) * width : ((q ^ mask) + 1) * width] for q in range(shards)]
    return jnp.concatenate(blocks, axis=1)


def stack8(*rows):
    rows = [row.reshape(1, -1) for row in rows]
    return jnp.concatenate(rows + [jnp.zeros((8 - len(rows), rows[0].shape[1]), F32)], axis=0)


def local(
    batch_size,
    shards,
    tokens,
    lengths,
    block_swap,
    input_weight,
    input_bias,
    out_weight,
    out_bias,
    gain_one,
    shift_one,
    up_weight,
    up_bias,
    down_weight,
    down_bias,
    gain_two,
    shift_two,
    cotangent,
):
    move = Mover(batch_size, shards)
    heads = block_swap.shape[0]
    rows, dim = tokens.shape
    width = input_weight.shape[2]
    depth = width // heads
    hidden_own = up_weight.shape[1]
    piece = dim // PARTS
    batch_at, head_at = lax.axis_index("batch"), lax.axis_index("head")
    part = batch_at % PARTS
    blocks = SEQ_LEN // rows
    length = lax.dynamic_index_in_dim(lengths, head_at // blocks, 0, keepdims=False)
    block_at = head_at % blocks
    own_live = jnp.clip(length - block_at * rows, 0, rows)
    partner_live = jnp.clip(length - (blocks - 1 - block_at) * rows, 0, rows)

    input_piece = lax.dynamic_slice_in_dim(input_weight, part * piece, piece, 1)
    input_piece = jnp.concatenate([input_piece[1], input_piece[2], input_piece[0]], axis=1)
    small = jnp.concatenate([jnp.zeros((width,), F32), input_bias[1], input_bias[0]])
    high = lax.reduce_precision(small, 8, 7)
    middle = lax.reduce_precision(small - high, 8, 7)
    swaps = jnp.pad(block_swap.astype(F32), (0, 3 * width - heads))
    small = jnp.stack([high, middle, small - high - middle, swaps])
    small = jnp.pad(small, ((0, 12), (0, 0))).astype(BF16)
    input_column = move.column(jnp.concatenate([input_piece, small]))
    up_own = up_weight.T.reshape(PARTS, piece, dim)
    up_piece = lax.dynamic_index_in_dim(up_own, part, 0, keepdims=False)
    up_far = move.head(up_piece, 2)
    input_own = input_weight.transpose(0, 2, 1)
    down_own = down_weight.reshape(PARTS, piece, dim)
    down_piece = lax.dynamic_index_in_dim(down_own, part, 0, keepdims=False)
    short_info = jnp.stack([own_live, part, head_at]).astype(jnp.int32)
    up_bias_parts = up_bias.reshape(shards, PARTS, 1, piece)
    out_parts = out_weight.reshape(shards, width, dim)
    vectors_one = stack8(out_bias, gain_one, shift_one)
    vectors_two = stack8(gain_one, shift_one, down_bias, gain_two, shift_two)
    vectors_back = stack8(gain_one)
    *input_column, up_far, tokens_sent = all_after(
        (*input_column, up_far, tokens), vectors_one, vectors_two, down_piece
    )
    small = jnp.stack([small] + [value[piece:] for value in input_column]).astype(F32)
    input_column = jnp.stack([value[:piece] for value in input_column])
    input_low = move.low(input_column)
    up_ends = pair_of(up_piece, up_far)
    up_others = move.head(up_ends, 1)
    partner = move.head(tokens_sent, 1)
    input_pair = pair_of(input_column, input_low)
    input_high = move.high(input_pair)
    info = jnp.concatenate(
        [
            small[:, 3, :heads].reshape(-1).astype(jnp.int32),
            jnp.stack([own_live, partner_live, part, head_at]).astype(jnp.int32),
        ]
    )
    bias = (small[:, 0] + small[:, 1]) + small[:, 2]
    bias = jnp.broadcast_to(bias[:, None], (shards, 8, 3 * width))
    input_high, up_others = all_after((input_high, up_others), info, bias)
    up_column = jnp.stack([up_others[0], up_ends[1], up_others[1]])
    up_low = move.low(up_column)
    input_near = four_of(input_pair, input_high)
    input_far = move.core(input_near)
    up_pair = pair_of(up_column, up_low)
    up_high = move.high(up_pair)
    down_piece, partner, up_pair = all_after((down_piece, partner, up_pair))
    down_far = move.head(down_piece, 2)

    def attend_shards(first_shard, count, last, weights, carried, so_far):
        return attend(
            (heads, depth, first_shard, last),
            count,
            info,
            tokens,
            partner,
            bias,
            out_parts,
            vectors_one,
            weights,
            carried,
            so_far,
        )

    qkv, context_0, stats, total = attend_shards(0, 1, False, [input_own], [], [])
    input_far, down_far, total, qkv, stats = all_after((input_far, down_far, total, qkv, stats))
    others = [input_near, input_far]
    down_ends = pair_of(down_piece, down_far)
    down_others = move.head(down_ends, 1)
    total, down_ends = all_after((total, down_ends))
    qkv, context_1, stats, total = attend_shards(1, 2, False, others, [total], [qkv, stats])
    up_high, down_others, total, qkv, stats = all_after((up_high, down_others, total, qkv, stats))
    up_near = four_of(up_pair, up_high)
    up_far = move.core(up_near)
    down_column = jnp.stack([down_others[0], down_ends[1], down_others[1]])
    down_low = move.low(down_column)
    total, up_near, down_column = all_after((total, up_near, down_column))
    qkv, context, stats, rows_one, normed = attend_shards(
        3, 1, True, others, [total, context_0, context_1], [qkv, stats]
    )
    up_far, down_low, normed, context = all_after((up_far, down_low, normed, context))
    up_all = (up_own, up_near, up_far)
    down_pair = pair_of(down_column, down_low)
    down_high = move.high(down_pair)
    normed, down_pair = all_after((normed, down_pair))
    hidden_near, hidden_far, *slopes = feed_up(short_info, normed, up_all, up_bias_parts)
    down_high, hidden_near, hidden_far = all_after((down_high, hidden_near, hidden_far))
    down_near = four_of(down_pair, down_high)
    down_far = move.core(down_near)
    down_all = (down_own, down_near, down_far)
    hidden_received = move.core(hidden_far)
    normed_received = move.core(after(normed, hidden_near))
    context_received = move.core(after(context, hidden_near))
    mixed_out, grad_second, grad_branch, sums_two = feed_down(
        short_info, (hidden_near, hidden_far), down_all, rows_one, cotangent, vectors_two
    )

    branch_received = move.core(grad_branch)
    tokens_t, partner_t = turn(after(tokens, grad_branch), partner)
    branch_received, tokens_t, partner_t = all_after((branch_received, tokens_t, partner_t))
    down_mine, down_one, down_two, down_three = row_grads(
        shards,
        hidden_near,
        hidden_received,
        after(grad_branch, tokens_t),
        branch_received,
        "down_grads",
    )
    down_three = move.low(down_three)
    pre_near, pre_far, up_bias_sums = grad_pre_of(
        short_info, after(grad_branch, down_two), down_all, slopes
    )
    down_three, pre_near, pre_far, up_bias_sums = all_after(
        (down_three, pre_near, pre_far, up_bias_sums)
    )
    pre_received = move.core(pre_far)
    down_two = (down_two + down_three.astype(F32)).astype(BF16)
    down_high = move.high(down_two)
    grad_first, grad_proj, sums_one = up_back(
        short_info, (pre_near, pre_far), up_all, rows_one, after(grad_second, down_two), vectors_back
    )
    pre_received, down_high, grad_proj, grad_first, sums_one = all_after(
        (pre_received, down_high, grad_proj, grad_first, sums_one)
    )
    proj_received = move.core(grad_proj)
    down_one = move.low(after(down_one, down_high))

    def core_sum(mine, received):
        mine, received = (a.reshape(2, 2, *a.shape[1:]) for a in (mine, received))
        keep = mine[:, 0].astype(F32) + received[:, 0].astype(F32)
        return keep, (mine[:, 1].astype(F32) + received[:, 1].astype(F32)).astype(BF16)

    def fold_low(keep, received):
        return keep[0] + received[0].astype(F32), (keep[1] + received[1].astype(F32)).astype(BF16)

    def fold_high(own, received):
        total = own + received.astype(F32)
        return total[0::2], total[1::2].astype(BF16)

    def fold_near(own, received):
        return own[0] + received[0].astype(F32), (own[1] + received[1].astype(F32)).astype(BF16)

    def fold_last(own, received):
        return move.settle(own + received.astype(F32))

    up_mine, up_one, up_two, up_three = row_grads(
        shards, pre_near, pre_received, normed, normed_received, "up_grads"
    )
    proj_received, up_one, up_three = all_after((proj_received, up_one, up_three))
    up_three = move.low(up_three)
    out_keep, out_send = out_grads(
        short_info, after(grad_proj, up_one), proj_received, context, context_received
    )
    down_one, out_keep, out_send = all_after((down_one, out_keep, out_send))
    up_one = move.low(after(up_one, down_one))
    out_low = move.low(out_send)
    down_mine = down_mine + (down_one.astype(F32) + down_high.astype(F32))
    down_mine, down_next = down_mine[0::2], down_mine[1::2].astype(BF16)
    down_near = move.head(down_next, 1)

    def back(grad, first_shard, count, carried, so_far):
        return attend_back(
            (heads, depth, first_shard, count, shards),
            info,
            tokens_t,
            partner_t,
            grad,
            out_parts,
            [] if first_shard else [input_own],
            *others,
            qkv,
            stats,
            carried,
            so_far,
        )

    own_rows, partner_rows, late_near, late_far, late_bias = back(
        after(grad_proj, out_send, down_next), 2, 2, [], []
    )

    (
        down_near,
        up_one,
        up_three,
        out_low,
        own_rows,
        partner_rows,
        late_near,
        late_far,
        late_bias,
    ) = all_after(
        (
            down_near,
            up_one,
            up_three,
            out_low,
            own_rows,
            partner_rows,
            late_near,
            late_far,
            late_bias,
        )
    )
    up_next = (up_two + up_three.astype(F32)).astype(BF16)
    up_mine = up_mine + up_one.astype(F32)
    up_high = move.high(up_next)
    late_core = move.core(late_far)
    down_mine, down_next = fold_near(down_mine, after(down_near, up_next))
    down_last = move.head(down_next, 2)
    out_mine = out_keep[0] + out_low[0].astype(F32)
    out_next = (out_keep[1] + out_low[1].astype(F32)).astype(BF16)
    out_high = move.high(out_next)
    own_rows, partner_rows, *early = back(
        after(grad_proj, down_next, up_next, out_next), 1, 1, [own_rows, partner_rows], [late_bias]
    )

    up_high, down_last, late_core, out_high, own_rows, partner_rows, *early = all_after(
        (up_high, down_last, late_core, out_high, own_rows, partner_rows, *early)
    )
    up_mine, up_next = fold_high(up_mine, up_high)
    up_near = move.head(up_next, 1)
    late_keep, late_next = core_sum(late_near, late_core)
    late_low = move.low(late_next)
    down_total = fold_last(down_mine, down_last)
    down_low = move.low(down_total)
    out_next = (out_mine + out_high.astype(F32)).astype(BF16)
    out_near = move.head(out_next, 1)
    own_rows, partner_rows, early_near, early_far, early_bias = back(
        after(grad_proj, up_next, down_total, late_next, out_next),
        0,
        1,
        [own_rows, partner_rows],
        early,
    )

    up_near, down_low, late_low, out_near, own_rows, partner_rows = all_after(
        (up_near, down_low, late_low, out_near, own_rows, partner_rows), early_bias
    )
    early_near, early_far, early_bias = all_after((early_near, early_far, early_bias), up_near)

    from_partner = move.head(partner_rows, 1)
    early_core = move.core(early_far)
    vectors = jnp.concatenate(
        [
            sums_one[:3],
            sums_two[:3],
            up_bias_sums[:, :, 0].reshape(shards, dim),
            jnp.pad(early_bias[:, 0], ((0, 0), (0, dim - 3 * width))),
        ]
    )
    hops = move.hops()

    def hop(value, sent, event):
        value = value + after(sent, event)
        return value, hops.pop(0)(value) if hops else None

    up_mine, up_next = fold_near(up_mine, up_near)
    up_last = move.head(up_next, 2)
    late_mine, late_next = fold_low(late_keep, after(late_low, up_next))
    late_high = move.high(late_next)
    early_keep, early_next = core_sum(early_near, after(early_core, late_next))
    early_low = move.low(early_next)
    down_pair = pair_of(down_total, after(down_low, early_next))
    down_high = move.high(down_pair)
    out_near = shards_swapped(out_near, shards, 1)
    out_next = (out_next.astype(F32) + out_near.astype(F32)).astype(BF16)
    out_last = move.head(out_next, 2)
    vectors_sent = hops.pop(0)(after(vectors, out_next))
    late_mine = late_mine + after(late_high, out_next).astype(F32)
    early_mine, early_next = fold_low(early_keep, after(early_low, late_mine))
    early_high = move.high(early_next)
    vectors, vectors_sent = hop(vectors, vectors_sent, early_next)
    up_total = fold_last(up_mine, after(up_last, vectors))
    out_last = shards_swapped(after(out_last, vectors), shards, 2)
    out_total = move.settle(out_next.astype(F32) + out_last.astype(F32))
    up_total = jnp.concatenate([up_total, out_total], axis=1)
    up_low = move.low(up_total)
    early_mine = early_mine + after(early_high, up_total).astype(F32)
    input_next = jnp.stack([early_mine[1], late_mine[1]]).astype(BF16)
    input_near = move.head(input_next, 1)
    down_near = four_of(down_pair, after(down_high, input_next))
    down_far = move.core(down_near)
    vectors, vectors_sent = hop(vectors, vectors_sent, down_near)
    up_pair = pair_of(up_total, after(up_low, vectors))
    up_high = move.high(up_pair)
    input_mine, input_next = fold_near(
        jnp.stack([early_mine[0], late_mine[0]]), after(input_near, up_pair)
    )
    input_last = move.head(input_next, 2)
    vectors, vectors_sent = hop(vectors, vectors_sent, input_next)
    grad_tokens = grad_first + own_rows + after(from_partner, vectors).astype(F32)
    input_total = fold_last(input_mine, after(input_last, grad_tokens))
    input_low = move.low(input_total)
    up_near = four_of(up_pair, after(up_high, input_total))
    up_far = move.core(up_near)
    vectors, vectors_sent = hop(vectors, vectors_sent, up_near)
    input_pair = pair_of(input_total, after(input_low, vectors))
    input_high = move.high(input_pair)
    while vectors_sent is not None:
        vectors, vectors_sent = hop(vectors, vectors_sent, input_pair)
    grad_down = pl.pallas_call(
        settle_down_kernel,
        in_specs=[SMEM] + [whole(4, piece, dim)] * 2,
        out_shape=shape((PARTS, piece, dim), F32),
        compiler_params=PARAMS,
        name="settle_down",
    )(short_info, after(down_near, input_pair), down_far)
    grad_up, grad_out = pl.pallas_call(
        settle_up_kernel,
        in_specs=[SMEM] + [whole(4, piece, dim + shards * width)] * 2,
        out_shape=[shape((dim, hidden_own), F32), shape((shards, width, dim), F32)],
        scratch_shapes=[pltpu.VMEM((PARTS, piece, dim), F32)] * 2,
        compiler_params=PARAMS,
        name="settle_up",
    )(short_info, after(up_near, grad_down), up_far)
    input_near = four_of(input_pair, after(input_high, grad_up))
    input_done = (input_near, move.core(input_near))
    grad_input_bias = lax.dynamic_index_in_dim(vectors[10:], head_at, 0, keepdims=False)
    grad_input_bias = jnp.stack(
        [grad_input_bias[2 * width : 3 * width], grad_input_bias[width : 2 * width]]
    )
    grad_up_bias = lax.dynamic_index_in_dim(vectors[6:10], head_at, 0, keepdims=False)
    grad_input_weight = pl.pallas_call(
        settle_input_kernel,
        in_specs=[SMEM] + [whole(4, piece, 3 * width)] * 2,
        out_shape=shape((3, width, dim), F32),
        scratch_shapes=[pltpu.VMEM((PARTS, piece, 3 * width), F32)],
        compiler_params=PARAMS,
        name="settle_input",
    )(short_info, *input_done)
    return (
        mixed_out,
        grad_tokens,
        grad_input_weight.transpose(0, 2, 1),
        grad_input_bias,
        grad_out.reshape(dim, dim),
        vectors[0],
        vectors[1],
        vectors[2],
        grad_up,
        grad_up_bias,
        grad_down.reshape(hidden_own, dim),
        vectors[3],
        vectors[4],
        vectors[5],
    )


def solution(mesh):
    rows_spec = P(("batch", "head"), None)
    placed = (
        rows_spec,
        P("batch"),
        P("head"),
        P(None, None, "head"),
        P(None, "head"),
        P(),
        P(),
        P(),
        P(),
        P(None, "head"),
        P(),
        P("head", None),
        P(),
        P(),
        P(),
        rows_spec,
    )
    return jax.shard_map(
        functools.partial(local, mesh.shape["batch"], mesh.shape["head"]),
        mesh=mesh,
        in_specs=placed,
        out_specs=(
            rows_spec,
            rows_spec,
            P(None, None, "head"),
            P(None, "head"),
            P(),
            P(),
            P(),
            P(),
            P(None, "head"),
            P("head"),
            P("head", None),
            P(),
            P(),
            P(),
        ),
        check_vma=False,
    )
```

```python
import functools

import jax
import jax.numpy as jnp
from jax import lax
from jax.experimental import pallas as pl
from jax.experimental.pallas import tpu as pltpu
from jax.sharding import PartitionSpec as P

SEQ_LEN = 1024
EPSILON = 1e-05
F32 = jnp.float32
BF16 = jnp.bfloat16
VMEM_LIMIT = 24 * 1024 * 1024
PARAMS = pltpu.CompilerParams(vmem_limit_bytes=VMEM_LIMIT)
CORE = 1
PARTS = 8
SPOTS = 4


def dot(left_side, right_side, left_dim=1, right_dim=0):
    return lax.dot_general(
        left_side,
        right_side,
        (((left_dim,), (right_dim,)), ((), ())),
        preferred_element_type=F32,
    )


def unit_parts(values):
    centred = values - jnp.mean(values, axis=-1, keepdims=True)
    inverse = lax.rsqrt(jnp.mean(centred * centred, axis=-1, keepdims=True) + EPSILON)
    return centred * inverse, inverse


def norm_back(grad_rows, unit_rows, inverse, gain_row):
    scaled = grad_rows * gain_row
    return inverse * (
        scaled
        - jnp.mean(scaled, axis=-1, keepdims=True)
        - unit_rows * jnp.mean(scaled * unit_rows, axis=-1, keepdims=True)
    )


def column_sum(values):
    return jnp.sum(values, axis=0, keepdims=True)


def gelu_parts(inner):
    below = 0.5 + 0.5 * lax.erf(inner * 0.7071067811865476)
    bell = jnp.exp(inner * inner * -0.5) * 0.3989422804014327
    return inner * below, below + inner * bell


def row_chunks(rows, step):
    return [slice(i, i + step) for i in range(0, rows, step)]


def eight_sum(values):
    return sum(values[cut] for cut in row_chunks(values.shape[0], 8))


def lane_pick(values, depth):
    lane = lax.broadcasted_iota(jnp.int32, (1, len(values) * depth), 1)
    picked = jnp.full(lane.shape, values[0], jnp.int32)
    for j in range(1, len(values)):
        picked = jnp.where(lane >= j * depth, values[j], picked)
    return picked


def place_of(part, half, spot):
    seen = part ^ half
    core = seen & 1
    low, high = 2 + 2 * core, 4 - 2 * core
    return seen ^ (low * (spot & 1) + high * (spot >> 1))


class Info:
    def __init__(self, ref, heads, shards):
        self.ref, self.heads, self.base = ref, heads, heads * shards

    def swaps(self, shard):
        return [self.ref[shard * self.heads + j] for j in range(self.heads)]

    own_live = property(lambda self: self.ref[self.base])
    partner_live = property(lambda self: self.ref[self.base + 1])
    part = property(lambda self: self.ref[self.base + 2])
    head_at = property(lambda self: self.ref[self.base + 3])


def gathered(part, near, far, scratch):
    for spot in range(SPOTS):
        scratch[place_of(part, 0, spot)] = near[spot, 0]
        scratch[place_of(part, 1, spot)] = far[spot, 0]
    return scratch[...].reshape(-1, scratch.shape[2])


def attend_kernel(setting, info_ref, tokens, partner, bias, out_weight, vectors, *refs):
    heads, depth, first_shard, last = setting
    refs = list(refs)
    if first_shard == 0:
        turned = refs.pop(0)
        total_in = None
    else:
        near, far, total_in = refs[:3]
        del refs[:3]
    earlier = []
    if last:
        earlier = refs[:2]
        del refs[:2]
    if first_shard:
        del refs[:2]
    qkv_out, context_out, stats_out = refs[:3]
    step = pl.program_id(0)
    shard = first_shard + step
    info = Info(info_ref, heads, out_weight.shape[0])
    if first_shard:
        weight = gathered(info.part, near, far, refs.pop())
    total = refs.pop()
    swaps = info.swaps(shard)
    rows, dim = tokens.shape
    width = heads * depth
    x, xp = tokens[...], partner[...]
    if first_shard:
        own = dot(x, weight)
        other = dot(xp, weight[:, : 2 * width])
    else:
        kv_rows = jnp.concatenate([turned[1], turned[2]], axis=0)
        own = jnp.concatenate([dot(x, kv_rows, 1, 1), dot(x, turned[0], 1, 1)], axis=1)
        other = dot(xp, kv_rows, 1, 1)
    swapped = lane_pick(swaps + swaps, depth) == 1
    bias_row = bias[0, 0:1]
    kv, q = [], []
    for cut in row_chunks(rows, 32):
        mine = own[cut] + bias_row
        theirs = other[cut] + bias_row[:, : 2 * width]
        kv.append(jnp.where(swapped, theirs, mine[:, : 2 * width]).astype(BF16))
        q.append(mine[:, 2 * width :].astype(BF16) * (depth**-0.5))
    kv, q = jnp.concatenate(kv, axis=0), jnp.concatenate(q, axis=0)
    qkv_out[0, :, : 2 * width] = kv
    qkv_out[0, :, 2 * width :] = q
    stats = []
    pieces = []
    for j in range(heads):
        head = slice(j * depth, (j + 1) * depth)
        live = jnp.where(swaps[j] == 1, info.partner_live, info.own_live)
        anyone = jnp.where(live > 0, 1.0, 0.0).astype(F32)
        scores = dot(kv[:, head], q[:, head], 1, 1)
        masked, most = [], None
        for cut in row_chunks(rows, 32):
            index = cut.start + lax.broadcasted_iota(jnp.int32, (32, 1), 0)
            part = jnp.where(index < live, scores[cut], -1e30)
            masked.append(part)
            for tile in row_chunks(32, 8):
                most = part[tile] if most is None else jnp.maximum(most, part[tile])
        largest = jnp.max(most, axis=0, keepdims=True)
        largest = jnp.where(anyone > 0.5, largest, 0.0)
        total_rows = None
        for part in masked:
            weights = eight_sum(jnp.exp(part - largest))
            total_rows = weights if total_rows is None else total_rows + weights
        stat = largest + jnp.log(column_sum(total_rows) + (1.0 - anyone))
        mixing = [jnp.exp(part - stat).astype(BF16) for part in masked]
        stats.append(stat)
        values = kv[:, width + j * depth : width + (j + 1) * depth]
        pieces.append(dot(values, jnp.concatenate(mixing, axis=0), 0, 0))
    context = jnp.concatenate(pieces, axis=0).T.astype(BF16)
    stats_out[0] = jnp.concatenate(stats + [jnp.zeros((8 - heads, rows), F32)], axis=0)
    projected = dot(context, out_weight[info.head_at ^ shard])
    if not last:
        context_out[0] = context

        @pl.when(step == 0)
        def first():
            total[...] = projected if total_in is None else total_in[...] + projected

        @pl.when(step > 0)
        def later():
            total[...] += projected

        return

    context_out[...] = jnp.concatenate(
        [ref[q] for ref in earlier for q in range(ref.shape[0])] + [context], axis=1
    )
    rows_out, normed_out = refs[3:]
    for cut in row_chunks(rows, 16):
        values = x[cut].astype(F32) + ((total_in[cut] + projected[cut]) + vectors[0:1])
        rows_out[cut] = values
        unit, _ = unit_parts(values)
        normed_out[cut] = (unit * vectors[1:2] + vectors[2:3]).astype(BF16)


def tiles_of(part, own, near, far, run):
    @pl.when(pl.program_id(0) == 0)
    def mine():
        run(
            *(
                jnp.concatenate([own[place_of(part, half, spot)] for spot in range(SPOTS)], axis=0)
                for half in range(2)
            )
        )

    @pl.when(pl.program_id(0) > 0)
    def other():
        run(*(ref[:, 0].reshape(-1, ref.shape[3]) for ref in (near, far)))


def add_up(total, *partials):
    @pl.when(pl.program_id(0) == 0)
    def start():
        total[...] = sum(partials[1:], partials[0])

    @pl.when(pl.program_id(0) > 0)
    def later():
        total[...] = sum(partials, total[...])


def at_end(run):
    pl.when(pl.program_id(0) == pl.num_programs(0) - 1)(run)


def eight_rows(*rows):
    width = rows[0].shape[1]
    return jnp.concatenate([*rows, jnp.zeros((8 - len(rows), width), F32)], axis=0)


def feed_up_kernel(info, normed, own, near, far, bias, *outs):
    shard = info[2] ^ pl.program_id(0)

    def run(*tiles):
        for half, tile in enumerate(tiles):
            places = [place_of(info[1], half, spot) for spot in range(SPOTS)]
            bias_row = jnp.concatenate([bias[shard, place] for place in places], axis=1)
            pre = dot(normed[...], tile, 1, 1)
            for cut in row_chunks(pre.shape[0], 32):
                hidden, slope = gelu_parts(pre[cut] + bias_row)
                outs[half][cut] = hidden.astype(BF16)
                outs[half + 2][cut] = slope

    tiles_of(info[1], own, near, far, run)


def feed_down_kernel(
    info,
    near_hidden,
    far_hidden,
    own,
    near,
    far,
    rows_in,
    cotangent,
    vectors,
    mixed_out,
    second_out,
    grad_out,
    sums_out,
    total,
):
    def run(near_tile, far_tile):
        add_up(total, dot(near_hidden[...], near_tile), dot(far_hidden[...], far_tile))

    tiles_of(info[1], own, near, far, run)

    @at_end
    def finish():
        sums = [jnp.zeros((8, rows_in.shape[1]), F32)] * 3
        for cut in row_chunks(rows_in.shape[0], 16):
            unit_one, _ = unit_parts(rows_in[cut])
            first_norm = unit_one * vectors[0:1] + vectors[1:2]
            unit, inverse = unit_parts(first_norm + (total[cut] + vectors[2:3]))
            index = cut.start + lax.broadcasted_iota(jnp.int32, (16, 1), 0)
            mask = jnp.where(index < info[0], 1.0, 0.0).astype(F32)
            mixed_out[cut] = ((unit * vectors[3:4] + vectors[4:5]) * mask).astype(BF16)
            incoming = cotangent[cut].astype(F32) * mask
            grad = norm_back(incoming, unit, inverse, vectors[3:4])
            second_out[cut] = grad
            low = grad.astype(BF16)
            grad_out[cut] = low
            more = (low.astype(F32), incoming * unit, incoming)
            sums = [a + eight_sum(b) for a, b in zip(sums, more)]
        sums_out[...] = eight_rows(*(column_sum(a) for a in sums))


def grad_pre_kernel(
    info, grad_branch, own, near, far, near_slope, far_slope, near_out, far_out, bias_out
):
    def run(*tiles):
        for half, tile in enumerate(tiles):
            out, slope = (near_out, far_out)[half], (near_slope, far_slope)[half]
            grad = dot(grad_branch[...], tile, 1, 1)
            sums = jnp.zeros((8, grad.shape[1]), F32)
            for cut in row_chunks(grad.shape[0], 32):
                low = (grad[cut] * slope[cut]).astype(BF16)
                out[cut] = low
                sums = sums + eight_sum(low.astype(F32))
            sums = jnp.broadcast_to(column_sum(sums), sums.shape)
            width = bias_out.shape[3]
            for spot in range(SPOTS):
                row = sums[:, spot * width : (spot + 1) * width]
                bias_out[info[2] ^ pl.program_id(0), place_of(info[1], half, spot)] = row

    tiles_of(info[1], own, near, far, run)


def up_back_kernel(
    info,
    near_pre,
    far_pre,
    own,
    near,
    far,
    rows_in,
    second_in,
    vectors,
    first_out,
    proj_out,
    sums_out,
    total,
):
    def run(near_tile, far_tile):
        add_up(total, dot(near_pre[...], near_tile), dot(far_pre[...], far_tile))

    tiles_of(info[1], own, near, far, run)

    @at_end
    def finish():
        sums = [jnp.zeros((8, rows_in.shape[1]), F32)] * 3
        for cut in row_chunks(rows_in.shape[0], 16):
            unit, inverse = unit_parts(rows_in[cut])
            grad_normed = second_in[cut] + total[cut]
            grad = norm_back(grad_normed, unit, inverse, vectors[0:1])
            first_out[cut] = grad
            low = grad.astype(BF16)
            proj_out[cut] = low
            more = (low.astype(F32), grad_normed * unit, grad_normed)
            sums = [a + eight_sum(b) for a, b in zip(sums, more)]
        sums_out[...] = eight_rows(*(column_sum(a) for a in sums))


def turn_kernel(tokens, partner, tokens_out, partner_out):
    tokens_out[...] = tokens[...].T
    partner_out[...] = partner[...].T


def row_grads_kernel(mine, theirs, my_rows, their_rows, *outs):
    value = dot(mine[...], my_rows[...], 0, 0) + dot(theirs[...], their_rows[...], 0, 0)
    value = value.reshape(SPOTS, -1, value.shape[1])
    for spot, out in enumerate(outs):
        out[0] = value[spot].astype(out.dtype)


def out_grads_kernel(info, mine, theirs, my_context, their_context, keep_out, send_out, turned):
    value = 0.0
    for i, (grad, context) in enumerate(((mine, my_context), (theirs, their_context))):
        turned[i] = grad[...].T.reshape(turned.shape[1:])
        rows = [turned[i, place_of(info[1], 0, spot)] for spot in range(SPOTS)]
        value = value + dot(jnp.concatenate(rows, axis=0), context[...])
    value = value.reshape(SPOTS, -1, value.shape[1])
    for spot in range(SPOTS):
        out = (keep_out, send_out)[spot & 1]
        out[spot >> 1] = value[spot].astype(out.dtype)


def scatter_parts(part, value, chunks, near_out, far_out):
    chunks[...] = value.reshape(chunks.shape)
    for spot in range(SPOTS):
        near_out[spot, 0] = chunks[place_of(part, 0, spot)]
        far_out[spot, 0] = chunks[place_of(part, 1, spot)]


def attend_back_kernel(setting, info_ref, tokens_t, partner_t, grad_proj, out_weight, *refs):
    heads, depth, first_shard, carried, so_far, shards = setting
    refs = list(refs)
    if first_shard == 0:
        turned = refs.pop(0)
    near, far, qkv_in, stats_in = refs[:4]
    del refs[:4]
    if carried:
        own_in, partner_in = refs[:2]
        del refs[:2]
    del refs[:so_far]
    own_out, partner_out, near_out, far_out, bias_out, total, weight_scratch, chunks = refs
    step = pl.program_id(0)
    shard = first_shard + step
    info = Info(info_ref, heads, shards)
    if first_shard:
        gathered(info.part, near, far, weight_scratch)
    else:
        width = turned.shape[1]

        @pl.when(shard == 0)
        def own_weight():
            rows_kv = jnp.concatenate([turned[1], turned[2], turned[0]], axis=0)
            weight_scratch[...] = rows_kv.T.reshape(weight_scratch.shape)

        @pl.when(shard > 0)
        def other_weight():
            gathered(info.part, near, far, weight_scratch)

    weight = weight_scratch[...].reshape(-1, weight_scratch.shape[2])
    swaps = info.swaps(shard)
    dim, rows = tokens_t.shape
    width = heads * depth
    grad = dot(grad_proj[...], out_weight[0], 1, 1).astype(BF16)
    k, v, q = (qkv_in[0, :, i * width : (i + 1) * width] for i in range(3))
    stats = stats_in[0]
    gq, gk, gv = [], [], []
    for j in range(heads):
        head = slice(j * depth, (j + 1) * depth)
        stat = stats[j : j + 1, :]
        live = jnp.where(swaps[j] == 1, info.partner_live, info.own_live)
        scores = dot(k[:, head], q[:, head], 1, 1)
        grad_mix = dot(v[:, head], grad[:, head], 1, 1)
        chances, shared = [], jnp.zeros((8, rows), F32)
        for cut in row_chunks(rows, 32):
            index = cut.start + lax.broadcasted_iota(jnp.int32, (32, 1), 0)
            part = jnp.exp(jnp.where(index < live, scores[cut] - stat, -10000.0))
            chances.append(part)
            shared = shared + eight_sum(part * grad_mix[cut])
        shared = column_sum(shared)
        mixing = jnp.concatenate([part.astype(BF16) for part in chances], axis=0)
        grad_scores = jnp.concatenate(
            [
                (part * (grad_mix[cut] - shared)).astype(BF16)
                for part, cut in zip(chances, row_chunks(rows, 32))
            ],
            axis=0,
        )
        gk.append(dot(grad_scores, q[:, head]))
        gv.append(dot(mixing, grad[:, head]))
        gq.append(dot(k[:, head], grad_scores, 0, 0))
    grad_q = (jnp.concatenate(gq, axis=0).T * (depth**-0.5)).astype(BF16)
    grad_kv = jnp.concatenate(gk + gv, axis=1).astype(BF16)
    swapped = lane_pick(swaps + swaps, depth) == 1
    nothing = jnp.zeros((), BF16)
    grad_own = jnp.concatenate([jnp.where(swapped, nothing, grad_kv), grad_q], axis=1)
    grad_far = jnp.where(swapped, grad_kv, nothing)
    own = dot(grad_own, weight, 1, 1)
    other = dot(grad_far, weight[:, : 2 * width], 1, 1)

    @pl.when(step == 0)
    def first():
        own_out[...] = own_in[...] + own if carried else own
        total[...] = partner_in[...] + other if carried else other

    @pl.when(step > 0)
    def later():
        own_out[...] += own
        total[...] += other

    @at_end
    def finish():
        partner_out[...] = total[...].astype(partner_out.dtype)

    grads = dot(tokens_t[...], grad_own)
    grads_kv = grads[:, : 2 * width] + dot(partner_t[...], grad_far)
    grads = jnp.concatenate([grads_kv, grads[:, 2 * width :]], axis=1).astype(BF16)
    chunks[...] = grads.reshape(chunks.shape)
    for spot in range(SPOTS):
        near_out[spot, 0] = chunks[place_of(info.part, 0, spot)]
        far_out[spot, 0] = chunks[place_of(info.part, 1, spot)]
    bias_out[0] = jnp.broadcast_to(
        jnp.concatenate(
            [column_sum(grad_kv.astype(F32)), column_sum(grad_q.astype(F32))], axis=1
        ),
        bias_out.shape[1:],
    )


def settle_down_kernel(info, near, far, out):
    for half, source in enumerate((near, far)):
        for spot in range(SPOTS):
            out[place_of(info[1], half, spot)] = source[spot].astype(F32)


def settle_up_kernel(info, near, far, up_out, out_out, up_scratch, out_scratch):
    dim = up_out.shape[0]
    for half, source in enumerate((near, far)):
        for spot in range(SPOTS):
            place = place_of(info[1], half, spot)
            value = source[spot].astype(F32)
            up_scratch[place] = value[:, :dim]
            out_scratch[place] = value[:, dim:]
    up_out[...] = up_scratch[...].reshape(-1, dim).T
    shards = out_out.shape[0]
    turned = out_scratch[...].reshape(-1, dim).T.reshape(shards, -1, dim)
    for q in range(shards):
        out_out[info[2] ^ q] = turned[q]


def settle_input_kernel(info, near, far, out, scratch):
    width = out.shape[1]
    for half, source in enumerate((near, far)):
        for spot in range(SPOTS):
            scratch[place_of(info[1], half, spot)] = source[spot].astype(F32)
    turned = scratch[...].reshape(-1, scratch.shape[2]).T
    for i in range(3):
        out[(i + 1) % 3] = turned[i * width : (i + 1) * width]


def shape(dims, dtype):
    return jax.ShapeDtypeStruct(dims, dtype)


def whole(*dims):
    return pl.BlockSpec(dims, lambda *_: (0,) * len(dims))


def cost(flops, moved, slow=0):
    return pl.CostEstimate(flops=flops, bytes_accessed=moved, transcendentals=slow)


SMEM = pl.BlockSpec(memory_space=pltpu.SMEM)


def gathered_specs(near, first_shard):
    spots, _, piece, lanes = near.shape
    return [pl.BlockSpec((spots, 1, piece, lanes), lambda s: (0, s + first_shard - 1, 0, 0))] * 2


def attend(
    setting, count, info, tokens, partner, bias, out_weight, vectors, weights, carried, so_far
):
    heads, depth, first_shard, last = setting
    rows, dim = tokens.shape
    shards, width, _ = out_weight.shape
    lanes = 3 * width
    scratch = []
    if first_shard == 0:
        weight_specs = [whole(3, width, dim)]
    else:
        weight_specs = gathered_specs(weights[0], first_shard)
        scratch = [pltpu.VMEM((PARTS, dim // PARTS, lanes), BF16)]
    out_specs = [
        pl.BlockSpec((1, rows, lanes), lambda s: (s + first_shard, 0, 0)),
        whole(rows, dim) if last else pl.BlockSpec((1, rows, width), lambda s: (s, 0, 0)),
        pl.BlockSpec((1, 8, rows), lambda s: (s + first_shard, 0, 0)),
    ]
    out_shape = [
        shape((shards, rows, lanes), BF16),
        shape((rows, dim) if last else (count, rows, width), BF16),
        shape((shards, 8, rows), F32),
    ]
    fixed = 6 + len(weights) + len(carried)
    if last:
        out_specs += [whole(rows, dim)] * 2
        out_shape += [shape((rows, dim), F32), shape((rows, dim), BF16)]
        scratch = [pltpu.VMEM((8, 128), F32)] + scratch
    else:
        out_specs.append(whole(rows, dim))
        out_shape.append(shape((rows, dim), F32))
    return pl.pallas_call(
        functools.partial(attend_kernel, setting),
        grid=(count,),
        in_specs=[
            SMEM,
            whole(rows, dim),
            whole(rows, dim),
            pl.BlockSpec((1, 8, lanes), lambda s: (s + first_shard, 0, 0)),
            whole(shards, width, dim),
            whole(8, dim),
        ]
        + weight_specs
        + [whole(*value.shape) for value in carried]
        + [pl.BlockSpec(memory_space=pl.ANY)] * len(so_far),
        out_specs=out_specs,
        out_shape=out_shape,
        scratch_shapes=scratch,
        input_output_aliases={fixed + i: (0, 2)[i] for i in range(len(so_far))},
        compiler_params=PARAMS,
        cost_estimate=cost(
            count * (3 * rows * dim * dim + 4 * rows * rows * dim),
            count * 6 * rows * dim,
            count * heads * rows * rows,
        ),
        name="attend",
    )(info, tokens, partner, bias, out_weight, vectors, *weights, *carried, *so_far)


def feed_specs(near):
    spots, _, piece, lanes = near.shape
    other = pl.BlockSpec(
        (spots, 1, piece, lanes), lambda q: (0, jnp.maximum(q - 1, 0), 0, 0)
    )
    return [whole(PARTS, piece, lanes), other, other]


def feed_up(info, normed, weight, bias):
    rows, dim = normed.shape
    near = weight[1]
    shards = near.shape[1] + 1
    tile = SPOTS * near.shape[2]
    columns = pl.BlockSpec((rows, tile), lambda q: (0, q))
    return pl.pallas_call(
        feed_up_kernel,
        grid=(shards,),
        in_specs=[
            SMEM,
            whole(rows, dim),
            *feed_specs(near),
            whole(*bias.shape),
        ],
        out_specs=[columns] * 4,
        out_shape=[shape((rows, shards * tile), BF16)] * 2
        + [shape((rows, shards * tile), F32)] * 2,
        compiler_params=PARAMS,
        cost_estimate=cost(4 * rows * dim * tile * shards, 30 * rows * dim, rows * dim * 8),
        name="feed_up",
    )(info, normed, *weight, bias)


def feed_down(info, hidden, weight, rows_one, cotangent, vectors):
    rows, dim = rows_one.shape
    near = weight[1]
    shards = near.shape[1] + 1
    tile = SPOTS * near.shape[2]
    columns = pl.BlockSpec((rows, tile), lambda q: (0, q))
    return pl.pallas_call(
        feed_down_kernel,
        grid=(shards,),
        in_specs=[
            SMEM,
            columns,
            columns,
            *feed_specs(near),
            whole(rows, dim),
            whole(rows, dim),
            whole(8, dim),
        ],
        out_specs=[whole(rows, dim)] * 3 + [whole(8, dim)],
        out_shape=[
            shape((rows, dim), BF16),
            shape((rows, dim), F32),
            shape((rows, dim), BF16),
            shape((8, dim), F32),
        ],
        scratch_shapes=[pltpu.VMEM((rows, dim), F32)],
        compiler_params=PARAMS,
        cost_estimate=cost(4 * rows * dim * tile * shards, 20 * rows * dim),
        name="feed_down",
    )(info, *hidden, *weight, rows_one, cotangent, vectors)


def grad_pre_of(info, grad_branch, weight, slopes):
    rows, dim = grad_branch.shape
    near = weight[1]
    shards = near.shape[1] + 1
    tile = SPOTS * near.shape[2]
    columns = pl.BlockSpec((rows, tile), lambda q: (0, q))
    return pl.pallas_call(
        grad_pre_kernel,
        grid=(shards,),
        in_specs=[SMEM, whole(rows, dim), *feed_specs(near), columns, columns],
        out_specs=[columns, columns, whole(shards, PARTS, 8, near.shape[2])],
        out_shape=[
            shape((rows, shards * tile), BF16),
            shape((rows, shards * tile), BF16),
            shape((shards, PARTS, 8, near.shape[2]), F32),
        ],
        compiler_params=PARAMS,
        cost_estimate=cost(4 * rows * dim * tile * shards, 30 * rows * dim),
        name="grad_pre",
    )(info, grad_branch, *weight, *slopes)


def up_back(info, pres, weight, rows_one, grad_second, vectors):
    rows, dim = rows_one.shape
    near = weight[1]
    shards = near.shape[1] + 1
    tile = SPOTS * near.shape[2]
    columns = pl.BlockSpec((rows, tile), lambda q: (0, q))
    return pl.pallas_call(
        up_back_kernel,
        grid=(shards,),
        in_specs=[
            SMEM,
            columns,
            columns,
            *feed_specs(near),
            whole(rows, dim),
            whole(rows, dim),
            whole(8, dim),
        ],
        out_specs=[whole(rows, dim), whole(rows, dim), whole(8, dim)],
        out_shape=[shape((rows, dim), F32), shape((rows, dim), BF16), shape((8, dim), F32)],
        scratch_shapes=[pltpu.VMEM((rows, dim), F32)],
        compiler_params=PARAMS,
        cost_estimate=cost(4 * rows * dim * tile * shards, 24 * rows * dim),
        name="up_back",
    )(info, *pres, *weight, rows_one, grad_second, vectors)


def turn(tokens, partner):
    rows, dim = tokens.shape
    return pl.pallas_call(
        turn_kernel,
        out_shape=[shape((dim, rows), BF16)] * 2,
        compiler_params=PARAMS,
        cost_estimate=cost(rows * dim, 8 * rows * dim),
        name="turn",
    )(tokens, partner)


def row_grads(shards, mine, theirs, my_rows, their_rows, name):
    rows, dim = my_rows.shape
    tile = mine.shape[1] // shards
    piece = tile // SPOTS
    columns = pl.BlockSpec((rows, tile), lambda q: (0, q))
    out = pl.BlockSpec((1, piece, dim), lambda q: (q, 0, 0))
    return pl.pallas_call(
        row_grads_kernel,
        grid=(shards,),
        in_specs=[columns, columns, whole(rows, dim), whole(rows, dim)],
        out_specs=[out] * SPOTS,
        out_shape=[shape((shards, piece, dim), (F32, BF16)[spot & 1]) for spot in range(SPOTS)],
        compiler_params=PARAMS,
        cost_estimate=cost(4 * rows * dim * tile * shards, 20 * rows * dim),
        name=name,
    )(mine, theirs, my_rows, their_rows)


def out_grads(info, mine, theirs, my_context, their_context):
    rows, dim = mine.shape
    piece = dim // PARTS
    return pl.pallas_call(
        out_grads_kernel,
        in_specs=[SMEM] + [whole(rows, dim)] * 4,
        out_specs=[whole(2, piece, dim)] * 2,
        out_shape=[shape((2, piece, dim), F32), shape((2, piece, dim), BF16)],
        scratch_shapes=[pltpu.VMEM((2, PARTS, piece, rows), BF16)],
        compiler_params=PARAMS,
        cost_estimate=cost(2 * rows * dim * dim, 10 * rows * dim),
        name="out_grads",
    )(info, mine, theirs, my_context, their_context)


def attend_back(
    setting,
    info,
    tokens_t,
    partner_t,
    grad_proj,
    out_weight,
    own,
    near,
    far,
    qkvs,
    stats,
    carried,
    so_far,
):
    heads, depth, first_shard, count, shards = setting
    half = shards // 2
    slot = first_shard % half
    fixed = 9 + len(own) + len(carried)
    dim, rows = tokens_t.shape
    width = heads * depth
    lanes = 3 * width
    piece = dim // PARTS
    head_spot = heads * shards + 3
    own_specs = [] if first_shard else [whole(3, width, dim)]
    kernel = functools.partial(
        attend_back_kernel, (heads, depth, first_shard, bool(carried), len(so_far), shards)
    )

    def other(s, info):
        return (0, jnp.maximum(s + first_shard - 1, 0), 0, 0)

    parts_out = pl.BlockSpec((SPOTS, 1, piece, lanes), lambda s, info: (0, s + slot, 0, 0))
    return pl.pallas_call(
        kernel,
        grid_spec=pltpu.PrefetchScalarGridSpec(
            num_scalar_prefetch=1,
            grid=(count,),
            in_specs=[
                whole(dim, rows),
                whole(dim, rows),
                whole(rows, dim),
                pl.BlockSpec(
                    (1, width, dim), lambda s, info: (info[head_spot] ^ (s + first_shard), 0, 0)
                ),
            ]
            + own_specs
            + [pl.BlockSpec((SPOTS, 1, piece, lanes), other)] * 2
            + [
                pl.BlockSpec((1, rows, lanes), lambda s, info: (s + first_shard, 0, 0)),
                pl.BlockSpec((1, 8, rows), lambda s, info: (s + first_shard, 0, 0)),
            ]
            + [whole(rows, dim)] * len(carried)
            + [pl.BlockSpec(memory_space=pl.ANY)] * len(so_far),
            out_specs=[
                whole(rows, dim),
                whole(rows, dim),
                parts_out,
                parts_out,
                pl.BlockSpec(
                    (1, 8, lanes), lambda s, info: (info[head_spot] ^ (s + first_shard), 0, 0)
                ),
            ],
            scratch_shapes=[
                pltpu.VMEM((rows, dim), F32),
                pltpu.VMEM((PARTS, piece, lanes), BF16),
                pltpu.VMEM((PARTS, piece, lanes), BF16),
            ],
        ),
        out_shape=[
            shape((rows, dim), F32),
            shape((rows, dim), F32 if first_shard else BF16),
            shape((SPOTS, half, piece, lanes), BF16),
            shape((SPOTS, half, piece, lanes), BF16),
            shape((shards, 8, lanes), F32),
        ],
        input_output_aliases={
            fixed + i: 5 - len(so_far) + i for i in range(len(so_far))
        },
        compiler_params=PARAMS,
        cost_estimate=cost(
            count * (6 * rows * dim * dim + 10 * rows * rows * dim),
            count * 8 * rows * dim,
            count * heads * rows * rows,
        ),
        name="attend_back",
    )(
        info,
        tokens_t,
        partner_t,
        grad_proj,
        out_weight,
        *own,
        near,
        far,
        qkvs,
        stats,
        *carried,
        *so_far,
    )


class Mover:
    def __init__(self, batch_size, shards):
        self.batch_size, self.shards = batch_size, shards

    def batch(self, value, mask_of):
        perm = [(i, i ^ mask_of(i)) for i in range(self.batch_size)]
        return lax.ppermute(value, "batch", perm)

    def core(self, value):
        return self.batch(value, lambda i: CORE)

    def low(self, value):
        return self.batch(value, lambda i: 4 if i & 1 else 2)

    def high(self, value):
        return self.batch(value, lambda i: 2 if i & 1 else 4)

    def head(self, value, mask):
        return lax.ppermute(value, "head", [(i, i ^ mask) for i in range(self.shards)])

    def along(self, values, first=1):
        return [self.head(value, q) for q, value in enumerate(values, first)]

    def column(self, piece):
        return self.along([piece] * (self.shards - 1))

    def settle(self, total):
        total = total.astype(BF16)
        mask = PARTS
        while mask < self.batch_size:
            other = self.batch(total, lambda i, mask=mask: mask)
            total = (total.astype(F32) + other.astype(F32)).astype(BF16)
            mask *= 2
        return total

    def hops(self):
        steps, mask = [], 1
        while mask < self.batch_size:
            steps.append(lambda value, mask=mask: self.batch(value, lambda i: mask))
            mask *= 2
        mask = 1
        while mask < self.shards:
            steps.append(lambda value, mask=mask: self.head(value, mask))
            mask *= 2
        return steps


def after(value, *events):
    return lax.optimization_barrier((value, *events))[0]


def all_after(values, *events):
    return lax.optimization_barrier((*values, *events))[: len(values)]


def pair_of(first, second):
    return jnp.stack([first, second])


def four_of(pair, received):
    return jnp.concatenate([pair, received])


def shards_swapped(value, shards, mask):
    width = value.shape[1] // shards
    blocks = [value[:, (q ^ mask) * width : ((q ^ mask) + 1) * width] for q in range(shards)]
    return jnp.concatenate(blocks, axis=1)


def stack8(*rows):
    rows = [row.reshape(1, -1) for row in rows]
    return jnp.concatenate(rows + [jnp.zeros((8 - len(rows), rows[0].shape[1]), F32)], axis=0)


def local(
    batch_size,
    shards,
    tokens,
    lengths,
    block_swap,
    input_weight,
    input_bias,
    out_weight,
    out_bias,
    gain_one,
    shift_one,
    up_weight,
    up_bias,
    down_weight,
    down_bias,
    gain_two,
    shift_two,
    cotangent,
):
    move = Mover(batch_size, shards)
    heads = block_swap.shape[0]
    rows, dim = tokens.shape
    width = input_weight.shape[2]
    depth = width // heads
    hidden_own = up_weight.shape[1]
    piece = dim // PARTS
    batch_at, head_at = lax.axis_index("batch"), lax.axis_index("head")
    part = batch_at % PARTS
    blocks = SEQ_LEN // rows
    length = lax.dynamic_index_in_dim(lengths, head_at // blocks, 0, keepdims=False)
    block_at = head_at % blocks
    own_live = jnp.clip(length - block_at * rows, 0, rows)
    partner_live = jnp.clip(length - (blocks - 1 - block_at) * rows, 0, rows)

    input_piece = lax.dynamic_slice_in_dim(input_weight, part * piece, piece, 1)
    input_piece = jnp.concatenate([input_piece[1], input_piece[2], input_piece[0]], axis=1)
    small = jnp.concatenate([jnp.zeros((width,), F32), input_bias[1], input_bias[0]])
    high = lax.reduce_precision(small, 8, 7)
    middle = lax.reduce_precision(small - high, 8, 7)
    swaps = jnp.pad(block_swap.astype(F32), (0, 3 * width - heads))
    small = jnp.stack([high, middle, small - high - middle, swaps])
    small = jnp.pad(small, ((0, 12), (0, 0))).astype(BF16)
    input_column = move.column(jnp.concatenate([input_piece, small]))
    up_own = up_weight.T.reshape(PARTS, piece, dim)
    up_piece = lax.dynamic_index_in_dim(up_own, part, 0, keepdims=False)
    input_own = input_weight.transpose(0, 2, 1)
    down_own = down_weight.reshape(PARTS, piece, dim)
    down_piece = lax.dynamic_index_in_dim(down_own, part, 0, keepdims=False)
    short_info = jnp.stack([own_live, part, head_at]).astype(jnp.int32)
    up_bias_parts = up_bias.reshape(shards, PARTS, 1, piece)
    out_parts = out_weight.reshape(shards, width, dim)
    vectors_one = stack8(out_bias, gain_one, shift_one)
    vectors_two = stack8(gain_one, shift_one, down_bias, gain_two, shift_two)
    vectors_back = stack8(gain_one)
    *input_column, up_piece, tokens_sent = all_after(
        (*input_column, up_piece, tokens), vectors_one, vectors_two, down_piece
    )
    small = jnp.stack([small] + [value[piece:] for value in input_column]).astype(F32)
    input_column = jnp.stack([value[:piece] for value in input_column])
    partner = move.head(tokens_sent, 1)
    input_low = move.low(input_column)
    up_far = move.head(up_piece, 2)
    info = jnp.concatenate(
        [
            small[:, 3, :heads].reshape(-1).astype(jnp.int32),
            jnp.stack([own_live, partner_live, part, head_at]).astype(jnp.int32),
        ]
    )
    bias = (small[:, 0] + small[:, 1]) + small[:, 2]
    bias = jnp.broadcast_to(bias[:, None], (shards, 8, 3 * width))
    input_low, up_far = all_after((input_low, up_far), info, bias)
    input_pair = pair_of(input_column, input_low)
    input_high = move.high(input_pair)
    up_ends = pair_of(up_piece, up_far)
    up_others = move.head(up_ends, 1)
    input_high, up_others, partner = all_after((input_high, up_others, partner))
    input_near = four_of(input_pair, input_high)
    input_far = move.core(input_near)
    up_column = jnp.stack([up_others[0], up_ends[1], up_others[1]])
    up_low = move.low(up_column)
    down_far = move.head(after(down_piece, up_others), 2)
    def attend_shards(first_shard, count, last, weights, carried, so_far):
        return attend(
            (heads, depth, first_shard, last),
            count,
            info,
            tokens,
            partner,
            bias,
            out_parts,
            vectors_one,
            weights,
            carried,
            so_far,
        )

    qkv, context_0, stats, total = attend_shards(0, 1, False, [input_own], [], [])
    input_far, up_low, down_far, total, qkv, stats = all_after(
        (input_far, up_low, down_far, total, qkv, stats)
    )
    others = [input_near, input_far]
    up_pair = pair_of(up_column, up_low)
    up_high = move.high(up_pair)
    down_ends = pair_of(down_piece, down_far)
    down_others = move.head(down_ends, 1)
    total, down_ends, up_pair = all_after((total, down_ends, up_pair))
    qkv, context_1, stats, total = attend_shards(1, 2, False, others, [total], [qkv, stats])
    up_high, down_others, total, qkv, stats = all_after((up_high, down_others, total, qkv, stats))
    up_near = four_of(up_pair, up_high)
    up_far = move.core(up_near)
    down_column = jnp.stack([down_others[0], down_ends[1], down_others[1]])
    down_low = move.low(down_column)
    total, up_near, down_column = all_after((total, up_near, down_column))
    qkv, context, stats, rows_one, normed = attend_shards(
        3, 1, True, others, [total, context_0, context_1], [qkv, stats]
    )
    up_far, down_low, normed, context = all_after((up_far, down_low, normed, context))
    up_all = (up_own, up_near, up_far)
    down_pair = pair_of(down_column, down_low)
    down_high = move.high(down_pair)
    normed, down_pair = all_after((normed, down_pair))
    normed_received = move.core(normed)
    context_received = move.core(context)
    hidden_near, hidden_far, *slopes = feed_up(short_info, normed, up_all, up_bias_parts)
    hidden_received = move.core(hidden_far)
    down_near = four_of(down_pair, after(down_high, hidden_near))
    down_far = move.core(down_near)
    down_all = (down_own, down_near, down_far)
    mixed_out, grad_second, grad_branch, sums_two = feed_down(
        short_info, (hidden_near, hidden_far), down_all, rows_one, cotangent, vectors_two
    )

    branch_received = move.core(grad_branch)
    tokens_t, partner_t = turn(after(tokens, grad_branch), partner)
    branch_received, tokens_t, partner_t = all_after((branch_received, tokens_t, partner_t))
    down_mine, down_one, down_two, down_three = row_grads(
        shards,
        hidden_near,
        hidden_received,
        after(grad_branch, tokens_t),
        branch_received,
        "down_grads",
    )
    down_three = move.low(down_three)
    pre_near, pre_far, up_bias_sums = grad_pre_of(
        short_info, after(grad_branch, down_two), down_all, slopes
    )
    down_three, pre_near, pre_far, up_bias_sums = all_after(
        (down_three, pre_near, pre_far, up_bias_sums)
    )
    pre_received = move.core(pre_far)
    down_two = (down_two + down_three.astype(F32)).astype(BF16)
    down_high = move.high(down_two)
    grad_first, grad_proj, sums_one = up_back(
        short_info, (pre_near, pre_far), up_all, rows_one, after(grad_second, down_two), vectors_back
    )
    pre_received, down_high, grad_proj, grad_first, sums_one = all_after(
        (pre_received, down_high, grad_proj, grad_first, sums_one)
    )
    proj_received = move.core(grad_proj)
    down_one = move.low(after(down_one, down_high))

    def core_sum(mine, received):
        mine, received = (a.reshape(2, 2, *a.shape[1:]) for a in (mine, received))
        keep = mine[:, 0].astype(F32) + received[:, 0].astype(F32)
        return keep, (mine[:, 1].astype(F32) + received[:, 1].astype(F32)).astype(BF16)

    def fold_low(keep, received):
        return keep[0] + received[0].astype(F32), (keep[1] + received[1].astype(F32)).astype(BF16)

    def fold_high(own, received):
        total = own + received.astype(F32)
        return total[0::2], total[1::2].astype(BF16)

    def fold_near(own, received):
        return own[0] + received[0].astype(F32), (own[1] + received[1].astype(F32)).astype(BF16)

    def fold_last(own, received):
        return move.settle(own + received.astype(F32))

    up_mine, up_one, up_two, up_three = row_grads(
        shards, pre_near, pre_received, normed, normed_received, "up_grads"
    )
    proj_received, up_one, up_three = all_after((proj_received, up_one, up_three))
    up_three = move.low(up_three)
    out_keep, out_send = out_grads(
        short_info, after(grad_proj, up_one), proj_received, context, context_received
    )
    down_one, out_keep, out_send = all_after((down_one, out_keep, out_send))
    up_one = move.low(after(up_one, down_one))
    out_low = move.low(out_send)
    down_mine = down_mine + (down_one.astype(F32) + down_high.astype(F32))
    down_mine, down_next = down_mine[0::2], down_mine[1::2].astype(BF16)
    down_near = move.head(down_next, 1)

    def back(grad, first_shard, count, carried, so_far):
        return attend_back(
            (heads, depth, first_shard, count, shards),
            info,
            tokens_t,
            partner_t,
            grad,
            out_parts,
            [] if first_shard else [input_own],
            *others,
            qkv,
            stats,
            carried,
            so_far,
        )

    own_rows, partner_rows, late_near, late_far, late_bias = back(
        after(grad_proj, out_send, down_next), 2, 2, [], []
    )

    (
        down_near,
        up_one,
        up_three,
        out_low,
        own_rows,
        partner_rows,
        late_near,
        late_far,
        late_bias,
    ) = all_after(
        (
            down_near,
            up_one,
            up_three,
            out_low,
            own_rows,
            partner_rows,
            late_near,
            late_far,
            late_bias,
        )
    )
    up_next = (up_two + up_three.astype(F32)).astype(BF16)
    up_mine = up_mine + up_one.astype(F32)
    up_high = move.high(up_next)
    late_core = move.core(late_far)
    down_mine, down_next = fold_near(down_mine, after(down_near, up_next))
    down_last = move.head(down_next, 2)
    out_mine = out_keep[0] + out_low[0].astype(F32)
    out_next = (out_keep[1] + out_low[1].astype(F32)).astype(BF16)
    out_high = move.high(out_next)
    own_rows, partner_rows, *early = back(
        after(grad_proj, down_next, up_next, out_next), 1, 1, [own_rows, partner_rows], [late_bias]
    )

    up_high, down_last, late_core, out_high, own_rows, partner_rows, *early = all_after(
        (up_high, down_last, late_core, out_high, own_rows, partner_rows, *early)
    )
    up_mine, up_next = fold_high(up_mine, up_high)
    up_near = move.head(up_next, 1)
    late_keep, late_next = core_sum(late_near, late_core)
    late_low = move.low(late_next)
    down_total = fold_last(down_mine, down_last)
    down_low = move.low(down_total)
    out_next = (out_mine + out_high.astype(F32)).astype(BF16)
    out_near = move.head(out_next, 1)
    own_rows, partner_rows, early_near, early_far, early_bias = back(
        after(grad_proj, up_next, down_total, late_next, out_next),
        0,
        1,
        [own_rows, partner_rows],
        early,
    )

    up_near, down_low, late_low, out_near, own_rows, partner_rows = all_after(
        (up_near, down_low, late_low, out_near, own_rows, partner_rows), early_bias
    )
    early_near, early_far, early_bias = all_after((early_near, early_far, early_bias), up_near)

    early_core = move.core(early_far)
    up_mine, up_next = fold_near(up_mine, up_near)
    up_last = move.head(up_next, 2)
    late_mine, late_next = fold_low(late_keep, late_low)
    late_high = move.high(late_next)
    early_keep, early_next = core_sum(early_near, after(early_core, late_next, up_next))
    early_low = move.low(early_next)
    vectors = jnp.concatenate(
        [
            sums_one[:3],
            sums_two[:3],
            up_bias_sums[:, :, 0].reshape(shards, dim),
            jnp.pad(
                after(early_bias, early_next)[:, 0], ((0, 0), (0, dim - 3 * width))
            ),
        ]
    )
    hops = move.hops()

    def hop(value, sent, event):
        value = value + after(sent, event)
        return value, hops.pop(0)(value) if hops else None

    vectors_sent = hops.pop(0)(vectors)
    down_pair = pair_of(down_total, after(down_low, early_next))
    down_high = move.high(down_pair)
    out_near = shards_swapped(after(out_near, early_next), shards, 1)
    out_next = (out_next.astype(F32) + out_near.astype(F32)).astype(BF16)
    out_last = move.head(out_next, 2)
    vectors, vectors_sent = hop(vectors, vectors_sent, out_next)
    early_low = after(early_low, vectors)
    early_mine, early_next = fold_low(early_keep, early_low)
    early_high = move.high(early_next)
    from_partner = move.head(after(partner_rows, early_next), 1)
    late_mine = late_mine + after(late_high, early_next).astype(F32)
    vectors, vectors_sent = hop(vectors, vectors_sent, late_mine)
    early_mine = early_mine + after(early_high, vectors).astype(F32)
    input_next = jnp.stack([early_mine[1], late_mine[1]]).astype(BF16)
    input_near = move.head(input_next, 1)
    up_total = fold_last(up_mine, after(up_last, input_next))
    out_last = shards_swapped(after(out_last, input_next), shards, 2)
    out_total = move.settle(out_next.astype(F32) + out_last.astype(F32))
    up_total = jnp.concatenate([up_total, out_total], axis=1)
    up_low = move.low(up_total)
    input_mine, input_next = fold_near(
        jnp.stack([early_mine[0], late_mine[0]]), after(input_near, up_total)
    )
    input_last = move.head(input_next, 2)
    vectors, vectors_sent = hop(vectors, vectors_sent, input_next)
    up_pair = pair_of(up_total, after(up_low, vectors))
    up_high = move.high(up_pair)
    down_near = four_of(down_pair, after(down_high, up_pair))
    down_far = move.core(down_near)
    vectors, vectors_sent = hop(vectors, vectors_sent, down_near)
    input_total = fold_last(input_mine, after(input_last, down_near, vectors))
    input_low = move.low(input_total)
    grad_tokens = grad_first + own_rows + after(from_partner, input_total).astype(F32)
    input_pair = pair_of(input_total, after(input_low, grad_tokens))
    input_high = move.high(input_pair)
    up_near = four_of(up_pair, after(up_high, input_pair))
    up_far = move.core(up_near)
    while vectors_sent is not None:
        vectors, vectors_sent = hop(vectors, vectors_sent, input_pair)
    grad_down = pl.pallas_call(
        settle_down_kernel,
        in_specs=[SMEM] + [whole(4, piece, dim)] * 2,
        out_shape=shape((PARTS, piece, dim), F32),
        compiler_params=PARAMS,
        name="settle_down",
    )(short_info, after(down_near, up_near), down_far)
    grad_up, grad_out = pl.pallas_call(
        settle_up_kernel,
        in_specs=[SMEM] + [whole(4, piece, dim + shards * width)] * 2,
        out_shape=[shape((dim, hidden_own), F32), shape((shards, width, dim), F32)],
        scratch_shapes=[pltpu.VMEM((PARTS, piece, dim), F32)] * 2,
        compiler_params=PARAMS,
        name="settle_up",
    )(short_info, after(up_near, grad_down), up_far)
    input_near = four_of(input_pair, after(input_high, grad_up))
    input_done = (input_near, move.core(input_near))
    grad_input_bias = lax.dynamic_index_in_dim(vectors[10:], head_at, 0, keepdims=False)
    grad_input_bias = jnp.stack(
        [grad_input_bias[2 * width : 3 * width], grad_input_bias[width : 2 * width]]
    )
    grad_up_bias = lax.dynamic_index_in_dim(vectors[6:10], head_at, 0, keepdims=False)
    grad_input_weight = pl.pallas_call(
        settle_input_kernel,
        in_specs=[SMEM] + [whole(4, piece, 3 * width)] * 2,
        out_shape=shape((3, width, dim), F32),
        scratch_shapes=[pltpu.VMEM((PARTS, piece, 3 * width), F32)],
        compiler_params=PARAMS,
        name="settle_input",
    )(short_info, *input_done)
    return (
        mixed_out,
        grad_tokens,
        grad_input_weight.transpose(0, 2, 1),
        grad_input_bias,
        grad_out.reshape(dim, dim),
        vectors[0],
        vectors[1],
        vectors[2],
        grad_up,
        grad_up_bias,
        grad_down.reshape(hidden_own, dim),
        vectors[3],
        vectors[4],
        vectors[5],
    )


def solution(mesh):
    rows_spec = P(("batch", "head"), None)
    placed = (
        rows_spec,
        P("batch"),
        P("head"),
        P(None, None, "head"),
        P(None, "head"),
        P(),
        P(),
        P(),
        P(),
        P(None, "head"),
        P(),
        P("head", None),
        P(),
        P(),
        P(),
        rows_spec,
    )
    return jax.shard_map(
        functools.partial(local, mesh.shape["batch"], mesh.shape["head"]),
        mesh=mesh,
        in_specs=placed,
        out_specs=(
            rows_spec,
            rows_spec,
            P(None, None, "head"),
            P(None, "head"),
            P(),
            P(),
            P(),
            P(),
            P(None, "head"),
            P("head"),
            P("head", None),
            P(),
            P(),
            P(),
        ),
        check_vma=False,
    )
```

```python
import functools

import jax
import jax.numpy as jnp
from jax import lax
from jax.experimental import pallas as pl
from jax.experimental.pallas import tpu as pltpu
from jax.sharding import PartitionSpec as P

SEQ_LEN = 1024
EPSILON = 1e-05
F32 = jnp.float32
BF16 = jnp.bfloat16
VMEM_LIMIT = 18 * 1024 * 1024
PARAMS = pltpu.CompilerParams(vmem_limit_bytes=VMEM_LIMIT)
CORE = 1
PARTS = 8
SPOTS = 4


def dot(left_side, right_side, left_dim=1, right_dim=0):
    return lax.dot_general(
        left_side,
        right_side,
        (((left_dim,), (right_dim,)), ((), ())),
        preferred_element_type=F32,
    )


def unit_parts(values):
    centred = values - jnp.mean(values, axis=-1, keepdims=True)
    inverse = lax.rsqrt(jnp.mean(centred * centred, axis=-1, keepdims=True) + EPSILON)
    return centred * inverse, inverse


def norm_back(grad_rows, unit_rows, inverse, gain_row):
    scaled = grad_rows * gain_row
    return inverse * (
        scaled
        - jnp.mean(scaled, axis=-1, keepdims=True)
        - unit_rows * jnp.mean(scaled * unit_rows, axis=-1, keepdims=True)
    )


def column_sum(values):
    return jnp.sum(values, axis=0, keepdims=True)


def gelu_parts(inner):
    below = 0.5 + 0.5 * lax.erf(inner * 0.7071067811865476)
    bell = jnp.exp(inner * inner * -0.5) * 0.3989422804014327
    return inner * below, below + inner * bell


def row_chunks(rows, step):
    return [slice(i, i + step) for i in range(0, rows, step)]


def eight_sum(values):
    return sum(values[cut] for cut in row_chunks(values.shape[0], 8))


def lane_pick(values, depth):
    lane = lax.broadcasted_iota(jnp.int32, (1, len(values) * depth), 1)
    picked = jnp.full(lane.shape, values[0], jnp.int32)
    for j in range(1, len(values)):
        picked = jnp.where(lane >= j * depth, values[j], picked)
    return picked


def place_of(part, half, spot):
    seen = part ^ half
    core = seen & 1
    low, high = 2 + 2 * core, 4 - 2 * core
    return seen ^ (low * (spot & 1) + high * (spot >> 1))


class Info:
    def __init__(self, ref, heads, shards):
        self.ref, self.heads, self.base = ref, heads, heads * shards

    def swaps(self, shard):
        return [self.ref[shard * self.heads + j] for j in range(self.heads)]

    own_live = property(lambda self: self.ref[self.base])
    partner_live = property(lambda self: self.ref[self.base + 1])
    part = property(lambda self: self.ref[self.base + 2])
    head_at = property(lambda self: self.ref[self.base + 3])


def gathered(part, near, far, scratch):
    for spot in range(SPOTS):
        scratch[place_of(part, 0, spot)] = near[spot, 0]
        scratch[place_of(part, 1, spot)] = far[spot, 0]
    return scratch[...].reshape(-1, scratch.shape[2])


def attend_kernel(setting, info_ref, tokens, partner, bias, out_weight, vectors, *refs):
    heads, depth, first_shard, last = setting
    refs = list(refs)
    if first_shard == 0:
        turned = refs.pop(0)
        total_in = None
    else:
        near, far, total_in = refs[:3]
        del refs[:3]
    earlier = []
    if last:
        earlier = refs[:2]
        del refs[:2]
    if first_shard:
        del refs[:2]
    qkv_out, context_out, stats_out = refs[:3]
    step = pl.program_id(0)
    shard = first_shard + step
    info = Info(info_ref, heads, out_weight.shape[0])
    if first_shard:
        weight = gathered(info.part, near, far, refs.pop())
    total = refs.pop()
    swaps = info.swaps(shard)
    rows, dim = tokens.shape
    width = heads * depth
    x, xp = tokens[...], partner[...]
    if first_shard:
        own = dot(x, weight)
        other = dot(xp, weight[:, : 2 * width])
    else:
        kv_rows = jnp.concatenate([turned[1], turned[2]], axis=0)
        own = jnp.concatenate([dot(x, kv_rows, 1, 1), dot(x, turned[0], 1, 1)], axis=1)
        other = dot(xp, kv_rows, 1, 1)
    swapped = lane_pick(swaps + swaps, depth) == 1
    bias_row = bias[0, 0:1]
    kv, q = [], []
    for cut in row_chunks(rows, 32):
        mine = own[cut] + bias_row
        theirs = other[cut] + bias_row[:, : 2 * width]
        kv.append(jnp.where(swapped, theirs, mine[:, : 2 * width]).astype(BF16))
        q.append(mine[:, 2 * width :].astype(BF16) * (depth**-0.5))
    kv, q = jnp.concatenate(kv, axis=0), jnp.concatenate(q, axis=0)
    qkv_out[0, :, : 2 * width] = kv
    qkv_out[0, :, 2 * width :] = q
    stats = []
    pieces = []
    for j in range(heads):
        head = slice(j * depth, (j + 1) * depth)
        live = jnp.where(swaps[j] == 1, info.partner_live, info.own_live)
        anyone = jnp.where(live > 0, 1.0, 0.0).astype(F32)
        scores = dot(kv[:, head], q[:, head], 1, 1)
        masked, most = [], None
        for cut in row_chunks(rows, 32):
            index = cut.start + lax.broadcasted_iota(jnp.int32, (32, 1), 0)
            part = jnp.where(index < live, scores[cut], -1e30)
            masked.append(part)
            for tile in row_chunks(32, 8):
                most = part[tile] if most is None else jnp.maximum(most, part[tile])
        largest = jnp.max(most, axis=0, keepdims=True)
        largest = jnp.where(anyone > 0.5, largest, 0.0)
        total_rows = None
        for part in masked:
            weights = eight_sum(jnp.exp(part - largest))
            total_rows = weights if total_rows is None else total_rows + weights
        stat = largest + jnp.log(column_sum(total_rows) + (1.0 - anyone))
        mixing = [jnp.exp(part - stat).astype(BF16) for part in masked]
        stats.append(stat)
        values = kv[:, width + j * depth : width + (j + 1) * depth]
        pieces.append(dot(values, jnp.concatenate(mixing, axis=0), 0, 0))
    context = jnp.concatenate(pieces, axis=0).T.astype(BF16)
    stats_out[0] = jnp.concatenate(stats + [jnp.zeros((8 - heads, rows), F32)], axis=0)
    projected = dot(context, out_weight[info.head_at ^ shard])
    if not last:
        context_out[0] = context

        @pl.when(step == 0)
        def first():
            total[...] = projected if total_in is None else total_in[...] + projected

        @pl.when(step > 0)
        def later():
            total[...] += projected

        return

    context_out[...] = jnp.concatenate(
        [ref[q] for ref in earlier for q in range(ref.shape[0])] + [context], axis=1
    )
    rows_out, normed_out = refs[3:]
    for cut in row_chunks(rows, 16):
        values = x[cut].astype(F32) + ((total_in[cut] + projected[cut]) + vectors[0:1])
        rows_out[cut] = values
        unit, _ = unit_parts(values)
        normed_out[cut] = (unit * vectors[1:2] + vectors[2:3]).astype(BF16)


def tiles_of(part, own, near, far, run):
    @pl.when(pl.program_id(0) == 0)
    def mine():
        run(
            *(
                jnp.concatenate([own[place_of(part, half, spot)] for spot in range(SPOTS)], axis=0)
                for half in range(2)
            )
        )

    @pl.when(pl.program_id(0) > 0)
    def other():
        run(*(ref[:, 0].reshape(-1, ref.shape[3]) for ref in (near, far)))


def add_up(total, *partials):
    @pl.when(pl.program_id(0) == 0)
    def start():
        total[...] = sum(partials[1:], partials[0])

    @pl.when(pl.program_id(0) > 0)
    def later():
        total[...] = sum(partials, total[...])


def at_end(run):
    pl.when(pl.program_id(0) == pl.num_programs(0) - 1)(run)


def eight_rows(*rows):
    width = rows[0].shape[1]
    return jnp.concatenate([*rows, jnp.zeros((8 - len(rows), width), F32)], axis=0)


def feed_up_kernel(info, normed, own, near, far, bias, *outs):
    shard = info[2] ^ pl.program_id(0)

    def run(*tiles):
        for half, tile in enumerate(tiles):
            places = [place_of(info[1], half, spot) for spot in range(SPOTS)]
            bias_row = jnp.concatenate([bias[shard, place] for place in places], axis=1)
            pre = dot(normed[...], tile, 1, 1)
            for cut in row_chunks(pre.shape[0], 32):
                hidden, slope = gelu_parts(pre[cut] + bias_row)
                outs[half][cut] = hidden.astype(BF16)
                outs[half + 2][cut] = slope

    tiles_of(info[1], own, near, far, run)


def feed_down_kernel(
    info,
    near_hidden,
    far_hidden,
    own,
    near,
    far,
    rows_in,
    cotangent,
    vectors,
    mixed_out,
    second_out,
    grad_out,
    sums_out,
    total,
):
    def run(near_tile, far_tile):
        add_up(total, dot(near_hidden[...], near_tile), dot(far_hidden[...], far_tile))

    tiles_of(info[1], own, near, far, run)

    @at_end
    def finish():
        sums = [jnp.zeros((8, rows_in.shape[1]), F32)] * 3
        for cut in row_chunks(rows_in.shape[0], 16):
            unit_one, _ = unit_parts(rows_in[cut])
            first_norm = unit_one * vectors[0:1] + vectors[1:2]
            unit, inverse = unit_parts(first_norm + (total[cut] + vectors[2:3]))
            index = cut.start + lax.broadcasted_iota(jnp.int32, (16, 1), 0)
            mask = jnp.where(index < info[0], 1.0, 0.0).astype(F32)
            mixed_out[cut] = ((unit * vectors[3:4] + vectors[4:5]) * mask).astype(BF16)
            incoming = cotangent[cut].astype(F32) * mask
            grad = norm_back(incoming, unit, inverse, vectors[3:4])
            second_out[cut] = grad
            low = grad.astype(BF16)
            grad_out[cut] = low
            more = (low.astype(F32), incoming * unit, incoming)
            sums = [a + eight_sum(b) for a, b in zip(sums, more)]
        sums_out[...] = eight_rows(*(column_sum(a) for a in sums))


def grad_pre_kernel(
    info, grad_branch, own, near, far, near_slope, far_slope, near_out, far_out, bias_out
):
    def run(*tiles):
        for half, tile in enumerate(tiles):
            out, slope = (near_out, far_out)[half], (near_slope, far_slope)[half]
            grad = dot(grad_branch[...], tile, 1, 1)
            sums = jnp.zeros((8, grad.shape[1]), F32)
            for cut in row_chunks(grad.shape[0], 32):
                low = (grad[cut] * slope[cut]).astype(BF16)
                out[cut] = low
                sums = sums + eight_sum(low.astype(F32))
            sums = jnp.broadcast_to(column_sum(sums), sums.shape)
            width = bias_out.shape[3]
            for spot in range(SPOTS):
                row = sums[:, spot * width : (spot + 1) * width]
                bias_out[info[2] ^ pl.program_id(0), place_of(info[1], half, spot)] = row

    tiles_of(info[1], own, near, far, run)


def up_back_kernel(
    info,
    near_pre,
    far_pre,
    own,
    near,
    far,
    rows_in,
    second_in,
    vectors,
    first_out,
    proj_out,
    sums_out,
    total,
):
    def run(near_tile, far_tile):
        add_up(total, dot(near_pre[...], near_tile), dot(far_pre[...], far_tile))

    tiles_of(info[1], own, near, far, run)

    @at_end
    def finish():
        sums = [jnp.zeros((8, rows_in.shape[1]), F32)] * 3
        for cut in row_chunks(rows_in.shape[0], 16):
            unit, inverse = unit_parts(rows_in[cut])
            grad_normed = second_in[cut] + total[cut]
            grad = norm_back(grad_normed, unit, inverse, vectors[0:1])
            first_out[cut] = grad
            low = grad.astype(BF16)
            proj_out[cut] = low
            more = (low.astype(F32), grad_normed * unit, grad_normed)
            sums = [a + eight_sum(b) for a, b in zip(sums, more)]
        sums_out[...] = eight_rows(*(column_sum(a) for a in sums))


def turn_kernel(tokens, partner, tokens_out, partner_out):
    tokens_out[...] = tokens[...].T
    partner_out[...] = partner[...].T


def row_grads_kernel(mine, theirs, my_rows, their_rows, *outs):
    value = dot(mine[...], my_rows[...], 0, 0) + dot(theirs[...], their_rows[...], 0, 0)
    value = value.reshape(SPOTS, -1, value.shape[1])
    for spot, out in enumerate(outs):
        out[0] = value[spot].astype(out.dtype)


def out_grads_kernel(info, mine, theirs, my_context, their_context, keep_out, send_out, turned):
    value = 0.0
    for i, (grad, context) in enumerate(((mine, my_context), (theirs, their_context))):
        turned[i] = grad[...].T.reshape(turned.shape[1:])
        rows = [turned[i, place_of(info[1], 0, spot)] for spot in range(SPOTS)]
        value = value + dot(jnp.concatenate(rows, axis=0), context[...])
    value = value.reshape(SPOTS, -1, value.shape[1])
    for spot in range(SPOTS):
        out = (keep_out, send_out)[spot & 1]
        out[spot >> 1] = value[spot].astype(out.dtype)


def scatter_parts(part, value, chunks, near_out, far_out):
    chunks[...] = value.reshape(chunks.shape)
    for spot in range(SPOTS):
        near_out[spot, 0] = chunks[place_of(part, 0, spot)]
        far_out[spot, 0] = chunks[place_of(part, 1, spot)]


def attend_back_kernel(setting, info_ref, tokens_t, partner_t, grad_proj, out_weight, *refs):
    heads, depth, first_shard, carried, so_far, shards = setting
    refs = list(refs)
    if first_shard == 0:
        turned = refs.pop(0)
    near, far, qkv_in, stats_in = refs[:4]
    del refs[:4]
    if carried:
        own_in, partner_in = refs[:2]
        del refs[:2]
    del refs[:so_far]
    own_out, partner_out, near_out, far_out, bias_out, total, weight_scratch, chunks = refs
    step = pl.program_id(0)
    shard = first_shard + step
    info = Info(info_ref, heads, shards)
    if first_shard:
        gathered(info.part, near, far, weight_scratch)
    else:
        width = turned.shape[1]

        @pl.when(shard == 0)
        def own_weight():
            rows_kv = jnp.concatenate([turned[1], turned[2], turned[0]], axis=0)
            weight_scratch[...] = rows_kv.T.reshape(weight_scratch.shape)

        @pl.when(shard > 0)
        def other_weight():
            gathered(info.part, near, far, weight_scratch)

    weight = weight_scratch[...].reshape(-1, weight_scratch.shape[2])
    swaps = info.swaps(shard)
    dim, rows = tokens_t.shape
    width = heads * depth
    grad = dot(grad_proj[...], out_weight[0], 1, 1).astype(BF16)
    k, v, q = (qkv_in[0, :, i * width : (i + 1) * width] for i in range(3))
    stats = stats_in[0]
    gq, gk, gv = [], [], []
    for j in range(heads):
        head = slice(j * depth, (j + 1) * depth)
        stat = stats[j : j + 1, :]
        live = jnp.where(swaps[j] == 1, info.partner_live, info.own_live)
        scores = dot(k[:, head], q[:, head], 1, 1)
        grad_mix = dot(v[:, head], grad[:, head], 1, 1)
        chances, shared = [], jnp.zeros((8, rows), F32)
        for cut in row_chunks(rows, 32):
            index = cut.start + lax.broadcasted_iota(jnp.int32, (32, 1), 0)
            part = jnp.exp(jnp.where(index < live, scores[cut] - stat, -10000.0))
            chances.append(part)
            shared = shared + eight_sum(part * grad_mix[cut])
        shared = column_sum(shared)
        mixing = jnp.concatenate([part.astype(BF16) for part in chances], axis=0)
        grad_scores = jnp.concatenate(
            [
                (part * (grad_mix[cut] - shared)).astype(BF16)
                for part, cut in zip(chances, row_chunks(rows, 32))
            ],
            axis=0,
        )
        gk.append(dot(grad_scores, q[:, head]))
        gv.append(dot(mixing, grad[:, head]))
        gq.append(dot(k[:, head], grad_scores, 0, 0))
    grad_q = (jnp.concatenate(gq, axis=0).T * (depth**-0.5)).astype(BF16)
    grad_kv = jnp.concatenate(gk + gv, axis=1).astype(BF16)
    swapped = lane_pick(swaps + swaps, depth) == 1
    nothing = jnp.zeros((), BF16)
    grad_own = jnp.concatenate([jnp.where(swapped, nothing, grad_kv), grad_q], axis=1)
    grad_far = jnp.where(swapped, grad_kv, nothing)
    own = dot(grad_own, weight, 1, 1)
    other = dot(grad_far, weight[:, : 2 * width], 1, 1)

    @pl.when(step == 0)
    def first():
        own_out[...] = own_in[...] + own if carried else own
        total[...] = partner_in[...] + other if carried else other

    @pl.when(step > 0)
    def later():
        own_out[...] += own
        total[...] += other

    @at_end
    def finish():
        partner_out[...] = total[...].astype(partner_out.dtype)

    grads = dot(tokens_t[...], grad_own)
    grads_kv = grads[:, : 2 * width] + dot(partner_t[...], grad_far)
    grads = jnp.concatenate([grads_kv, grads[:, 2 * width :]], axis=1).astype(BF16)
    chunks[...] = grads.reshape(chunks.shape)
    for spot in range(SPOTS):
        near_out[spot, 0] = chunks[place_of(info.part, 0, spot)]
        far_out[spot, 0] = chunks[place_of(info.part, 1, spot)]
    bias_out[0] = jnp.broadcast_to(
        jnp.concatenate(
            [column_sum(grad_kv.astype(F32)), column_sum(grad_q.astype(F32))], axis=1
        ),
        bias_out.shape[1:],
    )


def settle_down_kernel(info, near, far, out):
    for half, source in enumerate((near, far)):
        for spot in range(SPOTS):
            out[place_of(info[1], half, spot)] = source[spot].astype(F32)


def settle_up_kernel(info, near, far, up_out, out_out, up_scratch, out_scratch):
    dim = up_out.shape[0]
    for half, source in enumerate((near, far)):
        for spot in range(SPOTS):
            place = place_of(info[1], half, spot)
            value = source[spot].astype(F32)
            up_scratch[place] = value[:, :dim]
            out_scratch[place] = value[:, dim:]
    up_out[...] = up_scratch[...].reshape(-1, dim).T
    shards = out_out.shape[0]
    turned = out_scratch[...].reshape(-1, dim).T.reshape(shards, -1, dim)
    for q in range(shards):
        out_out[info[2] ^ q] = turned[q]


def settle_input_kernel(info, near, far, out, scratch):
    width = out.shape[1]
    for half, source in enumerate((near, far)):
        for spot in range(SPOTS):
            scratch[place_of(info[1], half, spot)] = source[spot].astype(F32)
    turned = scratch[...].reshape(-1, scratch.shape[2]).T
    for i in range(3):
        out[(i + 1) % 3] = turned[i * width : (i + 1) * width]


def shape(dims, dtype):
    return jax.ShapeDtypeStruct(dims, dtype)


def whole(*dims):
    return pl.BlockSpec(dims, lambda *_: (0,) * len(dims))


def cost(flops, moved, slow=0):
    return pl.CostEstimate(flops=flops, bytes_accessed=moved, transcendentals=slow)


SMEM = pl.BlockSpec(memory_space=pltpu.SMEM)


def gathered_specs(near, first_shard):
    spots, _, piece, lanes = near.shape
    return [pl.BlockSpec((spots, 1, piece, lanes), lambda s: (0, s + first_shard - 1, 0, 0))] * 2


def attend(
    setting, count, info, tokens, partner, bias, out_weight, vectors, weights, carried, so_far
):
    heads, depth, first_shard, last = setting
    rows, dim = tokens.shape
    shards, width, _ = out_weight.shape
    lanes = 3 * width
    scratch = []
    if first_shard == 0:
        weight_specs = [whole(3, width, dim)]
    else:
        weight_specs = gathered_specs(weights[0], first_shard)
        scratch = [pltpu.VMEM((PARTS, dim // PARTS, lanes), BF16)]
    out_specs = [
        pl.BlockSpec((1, rows, lanes), lambda s: (s + first_shard, 0, 0)),
        whole(rows, dim) if last else pl.BlockSpec((1, rows, width), lambda s: (s, 0, 0)),
        pl.BlockSpec((1, 8, rows), lambda s: (s + first_shard, 0, 0)),
    ]
    out_shape = [
        shape((shards, rows, lanes), BF16),
        shape((rows, dim) if last else (count, rows, width), BF16),
        shape((shards, 8, rows), F32),
    ]
    fixed = 6 + len(weights) + len(carried)
    if last:
        out_specs += [whole(rows, dim)] * 2
        out_shape += [shape((rows, dim), F32), shape((rows, dim), BF16)]
        scratch = [pltpu.VMEM((8, 128), F32)] + scratch
    else:
        out_specs.append(whole(rows, dim))
        out_shape.append(shape((rows, dim), F32))
    return pl.pallas_call(
        functools.partial(attend_kernel, setting),
        grid=(count,),
        in_specs=[
            SMEM,
            whole(rows, dim),
            whole(rows, dim),
            pl.BlockSpec((1, 8, lanes), lambda s: (s + first_shard, 0, 0)),
            whole(shards, width, dim),
            whole(8, dim),
        ]
        + weight_specs
        + [whole(*value.shape) for value in carried]
        + [pl.BlockSpec(memory_space=pl.ANY)] * len(so_far),
        out_specs=out_specs,
        out_shape=out_shape,
        scratch_shapes=scratch,
        input_output_aliases={fixed + i: (0, 2)[i] for i in range(len(so_far))},
        compiler_params=PARAMS,
        cost_estimate=cost(
            count * (3 * rows * dim * dim + 4 * rows * rows * dim),
            count * 6 * rows * dim,
            count * heads * rows * rows,
        ),
        name="attend",
    )(info, tokens, partner, bias, out_weight, vectors, *weights, *carried, *so_far)


def feed_specs(near):
    spots, _, piece, lanes = near.shape
    other = pl.BlockSpec(
        (spots, 1, piece, lanes), lambda q: (0, jnp.maximum(q - 1, 0), 0, 0)
    )
    return [whole(PARTS, piece, lanes), other, other]


def feed_up(info, normed, weight, bias):
    rows, dim = normed.shape
    near = weight[1]
    shards = near.shape[1] + 1
    tile = SPOTS * near.shape[2]
    columns = pl.BlockSpec((rows, tile), lambda q: (0, q))
    return pl.pallas_call(
        feed_up_kernel,
        grid=(shards,),
        in_specs=[
            SMEM,
            whole(rows, dim),
            *feed_specs(near),
            whole(*bias.shape),
        ],
        out_specs=[columns] * 4,
        out_shape=[shape((rows, shards * tile), BF16)] * 2
        + [shape((rows, shards * tile), F32)] * 2,
        compiler_params=PARAMS,
        cost_estimate=cost(4 * rows * dim * tile * shards, 30 * rows * dim, rows * dim * 8),
        name="feed_up",
    )(info, normed, *weight, bias)


def feed_down(info, hidden, weight, rows_one, cotangent, vectors):
    rows, dim = rows_one.shape
    near = weight[1]
    shards = near.shape[1] + 1
    tile = SPOTS * near.shape[2]
    columns = pl.BlockSpec((rows, tile), lambda q: (0, q))
    return pl.pallas_call(
        feed_down_kernel,
        grid=(shards,),
        in_specs=[
            SMEM,
            columns,
            columns,
            *feed_specs(near),
            whole(rows, dim),
            whole(rows, dim),
            whole(8, dim),
        ],
        out_specs=[whole(rows, dim)] * 3 + [whole(8, dim)],
        out_shape=[
            shape((rows, dim), BF16),
            shape((rows, dim), F32),
            shape((rows, dim), BF16),
            shape((8, dim), F32),
        ],
        scratch_shapes=[pltpu.VMEM((rows, dim), F32)],
        compiler_params=PARAMS,
        cost_estimate=cost(4 * rows * dim * tile * shards, 20 * rows * dim),
        name="feed_down",
    )(info, *hidden, *weight, rows_one, cotangent, vectors)


def grad_pre_of(info, grad_branch, weight, slopes):
    rows, dim = grad_branch.shape
    near = weight[1]
    shards = near.shape[1] + 1
    tile = SPOTS * near.shape[2]
    columns = pl.BlockSpec((rows, tile), lambda q: (0, q))
    return pl.pallas_call(
        grad_pre_kernel,
        grid=(shards,),
        in_specs=[SMEM, whole(rows, dim), *feed_specs(near), columns, columns],
        out_specs=[columns, columns, whole(shards, PARTS, 8, near.shape[2])],
        out_shape=[
            shape((rows, shards * tile), BF16),
            shape((rows, shards * tile), BF16),
            shape((shards, PARTS, 8, near.shape[2]), F32),
        ],
        compiler_params=PARAMS,
        cost_estimate=cost(4 * rows * dim * tile * shards, 30 * rows * dim),
        name="grad_pre",
    )(info, grad_branch, *weight, *slopes)


def up_back(info, pres, weight, rows_one, grad_second, vectors):
    rows, dim = rows_one.shape
    near = weight[1]
    shards = near.shape[1] + 1
    tile = SPOTS * near.shape[2]
    columns = pl.BlockSpec((rows, tile), lambda q: (0, q))
    return pl.pallas_call(
        up_back_kernel,
        grid=(shards,),
        in_specs=[
            SMEM,
            columns,
            columns,
            *feed_specs(near),
            whole(rows, dim),
            whole(rows, dim),
            whole(8, dim),
        ],
        out_specs=[whole(rows, dim), whole(rows, dim), whole(8, dim)],
        out_shape=[shape((rows, dim), F32), shape((rows, dim), BF16), shape((8, dim), F32)],
        scratch_shapes=[pltpu.VMEM((rows, dim), F32)],
        compiler_params=PARAMS,
        cost_estimate=cost(4 * rows * dim * tile * shards, 24 * rows * dim),
        name="up_back",
    )(info, *pres, *weight, rows_one, grad_second, vectors)


def turn(tokens, partner):
    rows, dim = tokens.shape
    return pl.pallas_call(
        turn_kernel,
        out_shape=[shape((dim, rows), BF16)] * 2,
        compiler_params=PARAMS,
        cost_estimate=cost(rows * dim, 8 * rows * dim),
        name="turn",
    )(tokens, partner)


def row_grads(shards, mine, theirs, my_rows, their_rows, name):
    rows, dim = my_rows.shape
    tile = mine.shape[1] // shards
    piece = tile // SPOTS
    columns = pl.BlockSpec((rows, tile), lambda q: (0, q))
    out = pl.BlockSpec((1, piece, dim), lambda q: (q, 0, 0))
    return pl.pallas_call(
        row_grads_kernel,
        grid=(shards,),
        in_specs=[columns, columns, whole(rows, dim), whole(rows, dim)],
        out_specs=[out] * SPOTS,
        out_shape=[shape((shards, piece, dim), (F32, BF16)[spot & 1]) for spot in range(SPOTS)],
        compiler_params=PARAMS,
        cost_estimate=cost(4 * rows * dim * tile * shards, 20 * rows * dim),
        name=name,
    )(mine, theirs, my_rows, their_rows)


def out_grads(info, mine, theirs, my_context, their_context):
    rows, dim = mine.shape
    piece = dim // PARTS
    return pl.pallas_call(
        out_grads_kernel,
        in_specs=[SMEM] + [whole(rows, dim)] * 4,
        out_specs=[whole(2, piece, dim)] * 2,
        out_shape=[shape((2, piece, dim), F32), shape((2, piece, dim), BF16)],
        scratch_shapes=[pltpu.VMEM((2, PARTS, piece, rows), BF16)],
        compiler_params=PARAMS,
        cost_estimate=cost(2 * rows * dim * dim, 10 * rows * dim),
        name="out_grads",
    )(info, mine, theirs, my_context, their_context)


def attend_back(
    setting,
    info,
    tokens_t,
    partner_t,
    grad_proj,
    out_weight,
    own,
    near,
    far,
    qkvs,
    stats,
    carried,
    so_far,
):
    heads, depth, first_shard, count, shards = setting
    half = shards // 2
    slot = first_shard % half
    fixed = 9 + len(own) + len(carried)
    dim, rows = tokens_t.shape
    width = heads * depth
    lanes = 3 * width
    piece = dim // PARTS
    head_spot = heads * shards + 3
    own_specs = [] if first_shard else [whole(3, width, dim)]
    kernel = functools.partial(
        attend_back_kernel, (heads, depth, first_shard, bool(carried), len(so_far), shards)
    )

    def other(s, info):
        return (0, jnp.maximum(s + first_shard - 1, 0), 0, 0)

    parts_out = pl.BlockSpec((SPOTS, 1, piece, lanes), lambda s, info: (0, s + slot, 0, 0))
    return pl.pallas_call(
        kernel,
        grid_spec=pltpu.PrefetchScalarGridSpec(
            num_scalar_prefetch=1,
            grid=(count,),
            in_specs=[
                whole(dim, rows),
                whole(dim, rows),
                whole(rows, dim),
                pl.BlockSpec(
                    (1, width, dim), lambda s, info: (info[head_spot] ^ (s + first_shard), 0, 0)
                ),
            ]
            + own_specs
            + [pl.BlockSpec((SPOTS, 1, piece, lanes), other)] * 2
            + [
                pl.BlockSpec((1, rows, lanes), lambda s, info: (s + first_shard, 0, 0)),
                pl.BlockSpec((1, 8, rows), lambda s, info: (s + first_shard, 0, 0)),
            ]
            + [whole(rows, dim)] * len(carried)
            + [pl.BlockSpec(memory_space=pl.ANY)] * len(so_far),
            out_specs=[
                whole(rows, dim),
                whole(rows, dim),
                parts_out,
                parts_out,
                pl.BlockSpec(
                    (1, 8, lanes), lambda s, info: (info[head_spot] ^ (s + first_shard), 0, 0)
                ),
            ],
            scratch_shapes=[
                pltpu.VMEM((rows, dim), F32),
                pltpu.VMEM((PARTS, piece, lanes), BF16),
                pltpu.VMEM((PARTS, piece, lanes), BF16),
            ],
        ),
        out_shape=[
            shape((rows, dim), F32),
            shape((rows, dim), F32 if first_shard else BF16),
            shape((SPOTS, half, piece, lanes), BF16),
            shape((SPOTS, half, piece, lanes), BF16),
            shape((shards, 8, lanes), F32),
        ],
        input_output_aliases={
            fixed + i: 5 - len(so_far) + i for i in range(len(so_far))
        },
        compiler_params=PARAMS,
        cost_estimate=cost(
            count * (6 * rows * dim * dim + 10 * rows * rows * dim),
            count * 8 * rows * dim,
            count * heads * rows * rows,
        ),
        name="attend_back",
    )(
        info,
        tokens_t,
        partner_t,
        grad_proj,
        out_weight,
        *own,
        near,
        far,
        qkvs,
        stats,
        *carried,
        *so_far,
    )


class Mover:
    def __init__(self, batch_size, shards):
        self.batch_size, self.shards = batch_size, shards

    def batch(self, value, mask_of):
        perm = [(i, i ^ mask_of(i)) for i in range(self.batch_size)]
        return lax.ppermute(value, "batch", perm)

    def core(self, value):
        return self.batch(value, lambda i: CORE)

    def low(self, value):
        return self.batch(value, lambda i: 4 if i & 1 else 2)

    def high(self, value):
        return self.batch(value, lambda i: 2 if i & 1 else 4)

    def head(self, value, mask):
        return lax.ppermute(value, "head", [(i, i ^ mask) for i in range(self.shards)])

    def along(self, values, first=1):
        return [self.head(value, q) for q, value in enumerate(values, first)]

    def column(self, piece):
        return self.along([piece] * (self.shards - 1))

    def settle(self, total):
        total = total.astype(BF16)
        mask = PARTS
        while mask < self.batch_size:
            other = self.batch(total, lambda i, mask=mask: mask)
            total = (total.astype(F32) + other.astype(F32)).astype(BF16)
            mask *= 2
        return total

    def hops(self):
        steps, mask = [], 1
        while mask < self.shards:
            steps.append(lambda value, mask=mask: self.head(value, mask))
            mask *= 2
        mask = 1
        while mask < self.batch_size:
            steps.append(lambda value, mask=mask: self.batch(value, lambda i: mask))
            mask *= 2
        return steps


def after(value, *events):
    return lax.optimization_barrier((value, *events))[0]


def all_after(values, *events):
    return lax.optimization_barrier((*values, *events))[: len(values)]


def pair_of(first, second):
    return jnp.stack([first, second])


def four_of(pair, received):
    return jnp.concatenate([pair, received])


def shards_swapped(value, shards, mask):
    width = value.shape[1] // shards
    blocks = [value[:, (q ^ mask) * width : ((q ^ mask) + 1) * width] for q in range(shards)]
    return jnp.concatenate(blocks, axis=1)


def stack8(*rows):
    rows = [row.reshape(1, -1) for row in rows]
    return jnp.concatenate(rows + [jnp.zeros((8 - len(rows), rows[0].shape[1]), F32)], axis=0)


def local(
    batch_size,
    shards,
    tokens,
    lengths,
    block_swap,
    input_weight,
    input_bias,
    out_weight,
    out_bias,
    gain_one,
    shift_one,
    up_weight,
    up_bias,
    down_weight,
    down_bias,
    gain_two,
    shift_two,
    cotangent,
):
    move = Mover(batch_size, shards)
    heads = block_swap.shape[0]
    rows, dim = tokens.shape
    width = input_weight.shape[2]
    depth = width // heads
    hidden_own = up_weight.shape[1]
    piece = dim // PARTS
    batch_at, head_at = lax.axis_index("batch"), lax.axis_index("head")
    part = batch_at % PARTS
    blocks = SEQ_LEN // rows
    length = lax.dynamic_index_in_dim(lengths, head_at // blocks, 0, keepdims=False)
    block_at = head_at % blocks
    own_live = jnp.clip(length - block_at * rows, 0, rows)
    partner_live = jnp.clip(length - (blocks - 1 - block_at) * rows, 0, rows)

    input_piece = lax.dynamic_slice_in_dim(input_weight, part * piece, piece, 1)
    input_piece = jnp.concatenate([input_piece[1], input_piece[2], input_piece[0]], axis=1)
    small = jnp.concatenate([jnp.zeros((width,), F32), input_bias[1], input_bias[0]])
    high = lax.reduce_precision(small, 8, 7)
    middle = lax.reduce_precision(small - high, 8, 7)
    swaps = jnp.pad(block_swap.astype(F32), (0, 3 * width - heads))
    small = jnp.stack([high, middle, small - high - middle, swaps])
    small = jnp.pad(small, ((0, 12), (0, 0))).astype(BF16)
    input_column = move.column(jnp.concatenate([input_piece, small]))
    up_own = up_weight.T.reshape(PARTS, piece, dim)
    up_piece = lax.dynamic_index_in_dim(up_own, part, 0, keepdims=False)
    input_own = input_weight.transpose(0, 2, 1)
    down_own = down_weight.reshape(PARTS, piece, dim)
    down_piece = lax.dynamic_index_in_dim(down_own, part, 0, keepdims=False)
    short_info = jnp.stack([own_live, part, head_at]).astype(jnp.int32)
    up_bias_parts = up_bias.reshape(shards, PARTS, 1, piece)
    out_parts = out_weight.reshape(shards, width, dim)
    vectors_one = stack8(out_bias, gain_one, shift_one)
    vectors_two = stack8(gain_one, shift_one, down_bias, gain_two, shift_two)
    vectors_back = stack8(gain_one)
    *input_column, up_piece, tokens_sent = all_after(
        (*input_column, up_piece, tokens), vectors_one, vectors_two, down_piece
    )
    small = jnp.stack([small] + [value[piece:] for value in input_column]).astype(F32)
    input_column = jnp.stack([value[:piece] for value in input_column])
    partner = move.head(tokens_sent, 1)
    input_low = move.low(input_column)
    up_far = move.head(up_piece, 2)
    info = jnp.concatenate(
        [
            small[:, 3, :heads].reshape(-1).astype(jnp.int32),
            jnp.stack([own_live, partner_live, part, head_at]).astype(jnp.int32),
        ]
    )
    bias = (small[:, 0] + small[:, 1]) + small[:, 2]
    bias = jnp.broadcast_to(bias[:, None], (shards, 8, 3 * width))
    input_low, up_far = all_after((input_low, up_far), info, bias)
    input_pair = pair_of(input_column, input_low)
    input_high = move.high(input_pair)
    up_ends = pair_of(up_piece, up_far)
    up_others = move.head(up_ends, 1)
    input_high, up_others, partner = all_after((input_high, up_others, partner))
    input_near = four_of(input_pair, input_high)
    input_far = move.core(input_near)
    up_column = jnp.stack([up_others[0], up_ends[1], up_others[1]])
    up_low = move.low(up_column)
    down_far = move.head(after(down_piece, up_others), 2)
    def attend_shards(first_shard, count, last, weights, carried, so_far):
        return attend(
            (heads, depth, first_shard, last),
            count,
            info,
            tokens,
            partner,
            bias,
            out_parts,
            vectors_one,
            weights,
            carried,
            so_far,
        )

    qkv, context_0, stats, total = attend_shards(0, 1, False, [input_own], [], [])
    input_far, up_low, down_far, total, qkv, stats = all_after(
        (input_far, up_low, down_far, total, qkv, stats)
    )
    others = [input_near, input_far]
    up_pair = pair_of(up_column, up_low)
    up_high = move.high(up_pair)
    down_ends = pair_of(down_piece, down_far)
    down_others = move.head(down_ends, 1)
    total, down_ends, up_pair = all_after((total, down_ends, up_pair))
    qkv, context_1, stats, total = attend_shards(1, 2, False, others, [total], [qkv, stats])
    up_high, down_others, total, qkv, stats = all_after((up_high, down_others, total, qkv, stats))
    up_near = four_of(up_pair, up_high)
    up_far = move.core(up_near)
    down_column = jnp.stack([down_others[0], down_ends[1], down_others[1]])
    down_low = move.low(down_column)
    total, up_near, down_column = all_after((total, up_near, down_column))
    qkv, context, stats, rows_one, normed = attend_shards(
        3, 1, True, others, [total, context_0, context_1], [qkv, stats]
    )
    up_far, down_low, normed, context = all_after((up_far, down_low, normed, context))
    up_all = (up_own, up_near, up_far)
    down_pair = pair_of(down_column, down_low)
    down_high = move.high(down_pair)
    normed, down_pair = all_after((normed, down_pair))
    normed_received = move.core(normed)
    context_received = move.core(context)
    hidden_near, hidden_far, *slopes = feed_up(short_info, normed, up_all, up_bias_parts)
    hidden_received = move.core(hidden_far)
    down_near = four_of(down_pair, after(down_high, hidden_near))
    down_far = move.core(down_near)
    tokens_t, partner_t = turn(after(tokens, down_near), partner)
    down_far, tokens_t, partner_t = all_after((down_far, tokens_t, partner_t))
    down_all = (down_own, down_near, down_far)
    mixed_out, grad_second, grad_branch, sums_two = feed_down(
        short_info, (hidden_near, hidden_far), down_all, rows_one, cotangent, vectors_two
    )

    branch_received = move.core(grad_branch)
    down_mine, down_one, down_two, down_three = row_grads(
        shards,
        hidden_near,
        hidden_received,
        grad_branch,
        branch_received,
        "down_grads",
    )
    down_three = move.low(down_three)
    pre_near, pre_far, up_bias_sums = grad_pre_of(
        short_info, after(grad_branch, down_two), down_all, slopes
    )
    down_three, pre_near, pre_far, up_bias_sums = all_after(
        (down_three, pre_near, pre_far, up_bias_sums)
    )
    pre_received = move.core(pre_far)
    down_two = (down_two + down_three.astype(F32)).astype(BF16)
    down_high = move.high(down_two)
    grad_first, grad_proj, sums_one = up_back(
        short_info, (pre_near, pre_far), up_all, rows_one, after(grad_second, down_two), vectors_back
    )
    pre_received, down_high, grad_proj, grad_first, sums_one = all_after(
        (pre_received, down_high, grad_proj, grad_first, sums_one)
    )
    proj_received = move.core(grad_proj)
    down_one = move.low(after(down_one, down_high))

    def core_sum(mine, received):
        mine, received = (a.reshape(2, 2, *a.shape[1:]) for a in (mine, received))
        keep = mine[:, 0].astype(F32) + received[:, 0].astype(F32)
        return keep, (mine[:, 1].astype(F32) + received[:, 1].astype(F32)).astype(BF16)

    def fold_low(keep, received):
        return keep[0] + received[0].astype(F32), (keep[1] + received[1].astype(F32)).astype(BF16)

    def fold_high(own, received):
        total = own + received.astype(F32)
        return total[0::2], total[1::2].astype(BF16)

    def fold_near(own, received):
        return own[0] + received[0].astype(F32), (own[1] + received[1].astype(F32)).astype(BF16)

    def fold_last(own, received):
        return move.settle(own + received.astype(F32))

    up_mine, up_one, up_two, up_three = row_grads(
        shards, pre_near, pre_received, normed, normed_received, "up_grads"
    )
    proj_received, up_one, up_three = all_after((proj_received, up_one, up_three))
    up_three = move.low(up_three)
    out_keep, out_send = out_grads(
        short_info, after(grad_proj, up_one), proj_received, context, context_received
    )
    down_one, out_keep, out_send = all_after((down_one, out_keep, out_send))
    up_one = move.low(after(up_one, down_one))
    out_low = move.low(out_send)
    down_mine = down_mine + (down_one.astype(F32) + down_high.astype(F32))
    down_mine, down_next = down_mine[0::2], down_mine[1::2].astype(BF16)
    down_near = move.head(down_next, 1)

    def back(grad, first_shard, count, carried, so_far):
        return attend_back(
            (heads, depth, first_shard, count, shards),
            info,
            tokens_t,
            partner_t,
            grad,
            out_parts,
            [] if first_shard else [input_own],
            *others,
            qkv,
            stats,
            carried,
            so_far,
        )

    own_rows, partner_rows, late_near, late_far, late_bias = back(
        after(grad_proj, out_send, down_next), 2, 2, [], []
    )

    (
        down_near,
        up_one,
        up_three,
        out_low,
        own_rows,
        partner_rows,
        late_near,
        late_far,
        late_bias,
    ) = all_after(
        (
            down_near,
            up_one,
            up_three,
            out_low,
            own_rows,
            partner_rows,
            late_near,
            late_far,
            late_bias,
        )
    )
    up_next = (up_two + up_three.astype(F32)).astype(BF16)
    up_mine = up_mine + up_one.astype(F32)
    up_high = move.high(up_next)
    late_core = move.core(late_far)
    down_mine, down_next = fold_near(down_mine, after(down_near, up_next))
    down_last = move.head(down_next, 2)
    out_mine = out_keep[0] + out_low[0].astype(F32)
    out_next = (out_keep[1] + out_low[1].astype(F32)).astype(BF16)
    out_high = move.high(out_next)
    own_rows, partner_rows, *early = back(
        after(grad_proj, down_next, up_next, out_next), 1, 1, [own_rows, partner_rows], [late_bias]
    )

    up_high, down_last, late_core, out_high, own_rows, partner_rows, *early = all_after(
        (up_high, down_last, late_core, out_high, own_rows, partner_rows, *early)
    )
    up_mine, up_next = fold_high(up_mine, up_high)
    up_near = move.head(up_next, 1)
    late_keep, late_next = core_sum(late_near, late_core)
    late_low = move.low(late_next)
    down_total = fold_last(down_mine, down_last)
    down_low = move.low(down_total)
    out_next = (out_mine + out_high.astype(F32)).astype(BF16)
    out_near = move.head(out_next, 1)
    own_rows, partner_rows, early_near, early_far, early_bias = back(
        after(grad_proj, up_next, down_total, late_next, out_next),
        0,
        1,
        [own_rows, partner_rows],
        early,
    )

    up_near, down_low, late_low, out_near, own_rows, partner_rows = all_after(
        (up_near, down_low, late_low, out_near, own_rows, partner_rows), early_bias
    )
    early_near, early_far, early_bias = all_after((early_near, early_far, early_bias), up_near)

    early_core = move.core(early_far)
    partner_first = move.head(partner_rows[: rows // 2], 1)
    partner_second = move.head(partner_rows[rows // 2 :], 1)
    up_mine, up_next = fold_near(up_mine, up_near)
    up_last = move.head(up_next, 2)
    late_mine, late_next = fold_low(late_keep, late_low)
    late_high = move.high(late_next)
    early_keep, early_next = core_sum(early_near, after(early_core, late_next, up_next))
    early_low = move.low(early_next)
    vectors = jnp.concatenate(
        [
            sums_one[:3],
            sums_two[:3],
            up_bias_sums[:, :, 0].reshape(shards, dim),
            jnp.pad(
                after(early_bias, early_next)[:, 0], ((0, 0), (0, dim - 3 * width))
            ),
        ]
    )
    hops = move.hops()

    def hop(value, sent, event):
        value = value + after(sent, event)
        return value, hops.pop(0)(value) if hops else None

    vectors_sent = hops.pop(0)(vectors)
    down_pair = pair_of(down_total, after(down_low, early_next))
    down_high = move.high(down_pair)
    out_near = shards_swapped(after(out_near, early_next), shards, 1)
    out_next = (out_next.astype(F32) + out_near.astype(F32)).astype(BF16)
    out_last = move.head(out_next, 2)
    vectors, vectors_sent = hop(vectors, vectors_sent, out_next)
    early_low = after(early_low, vectors)
    early_mine, early_next = fold_low(early_keep, early_low)
    early_high = move.high(early_next)
    late_mine = late_mine + after(late_high, early_next).astype(F32)
    vectors, vectors_sent = hop(vectors, vectors_sent, late_mine)
    partner_first = after(partner_first, late_mine)
    early_mine = early_mine + after(early_high, vectors, partner_first).astype(F32)
    input_next = jnp.stack([early_mine[1], late_mine[1]]).astype(BF16)
    input_near = move.head(input_next, 1)
    partner_second = after(partner_second, input_next)
    up_total = fold_last(up_mine, after(up_last, partner_second))
    out_last = shards_swapped(after(out_last, input_next), shards, 2)
    out_total = move.settle(out_next.astype(F32) + out_last.astype(F32))
    up_total = jnp.concatenate([up_total, out_total], axis=1)
    up_low = move.low(up_total)
    input_mine, input_next = fold_near(
        jnp.stack([early_mine[0], late_mine[0]]), after(input_near, up_total)
    )
    input_last = move.head(input_next, 2)
    vectors, vectors_sent = hop(vectors, vectors_sent, input_next)
    up_pair = pair_of(up_total, after(up_low, vectors))
    up_high = move.high(up_pair)
    down_near = four_of(down_pair, after(down_high, up_pair))
    down_far = move.core(down_near)
    vectors, vectors_sent = hop(vectors, vectors_sent, down_near)
    input_total = fold_last(input_mine, after(input_last, down_near, vectors))
    input_low = move.low(input_total)
    from_partner = jnp.concatenate([partner_first, partner_second])
    grad_tokens = grad_first + own_rows + after(from_partner, input_total).astype(F32)
    input_pair = pair_of(input_total, after(input_low, grad_tokens))
    input_high = move.high(input_pair)
    up_near = four_of(up_pair, after(up_high, input_pair))
    up_far = move.core(up_near)
    while vectors_sent is not None:
        vectors, vectors_sent = hop(vectors, vectors_sent, input_pair)
    grad_down = pl.pallas_call(
        settle_down_kernel,
        in_specs=[SMEM] + [whole(4, piece, dim)] * 2,
        out_shape=shape((PARTS, piece, dim), F32),
        compiler_params=PARAMS,
        name="settle_down",
    )(short_info, after(down_near, up_near), down_far)
    grad_up, grad_out = pl.pallas_call(
        settle_up_kernel,
        in_specs=[SMEM] + [whole(4, piece, dim + shards * width)] * 2,
        out_shape=[shape((dim, hidden_own), F32), shape((shards, width, dim), F32)],
        scratch_shapes=[pltpu.VMEM((PARTS, piece, dim), F32)] * 2,
        compiler_params=PARAMS,
        name="settle_up",
    )(short_info, after(up_near, grad_down), up_far)
    input_near = four_of(input_pair, after(input_high, grad_up))
    input_done = (input_near, move.core(input_near))
    grad_input_bias = lax.dynamic_index_in_dim(vectors[10:], head_at, 0, keepdims=False)
    grad_input_bias = jnp.stack(
        [grad_input_bias[2 * width : 3 * width], grad_input_bias[width : 2 * width]]
    )
    grad_up_bias = lax.dynamic_index_in_dim(vectors[6:10], head_at, 0, keepdims=False)
    grad_input_weight = pl.pallas_call(
        settle_input_kernel,
        in_specs=[SMEM] + [whole(4, piece, 3 * width)] * 2,
        out_shape=shape((3, width, dim), F32),
        scratch_shapes=[pltpu.VMEM((PARTS, piece, 3 * width), F32)],
        compiler_params=PARAMS,
        name="settle_input",
    )(short_info, *input_done)
    return (
        mixed_out,
        grad_tokens,
        grad_input_weight.transpose(0, 2, 1),
        grad_input_bias,
        grad_out.reshape(dim, dim),
        vectors[0],
        vectors[1],
        vectors[2],
        grad_up,
        grad_up_bias,
        grad_down.reshape(hidden_own, dim),
        vectors[3],
        vectors[4],
        vectors[5],
    )


def solution(mesh):
    rows_spec = P(("batch", "head"), None)
    placed = (
        rows_spec,
        P("batch"),
        P("head"),
        P(None, None, "head"),
        P(None, "head"),
        P(),
        P(),
        P(),
        P(),
        P(None, "head"),
        P(),
        P("head", None),
        P(),
        P(),
        P(),
        rows_spec,
    )
    return jax.shard_map(
        functools.partial(local, mesh.shape["batch"], mesh.shape["head"]),
        mesh=mesh,
        in_specs=placed,
        out_specs=(
            rows_spec,
            rows_spec,
            P(None, None, "head"),
            P(None, "head"),
            P(),
            P(),
            P(),
            P(),
            P(None, "head"),
            P("head"),
            P("head", None),
            P(),
            P(),
            P(),
        ),
        check_vma=False,
    )
```

```python
import functools

import jax
import jax.numpy as jnp
from jax import lax
from jax.experimental import pallas as pl
from jax.experimental.pallas import tpu as pltpu
from jax.sharding import PartitionSpec as P

SEQ_LEN = 1024
EPSILON = 1e-05
F32 = jnp.float32
BF16 = jnp.bfloat16
VMEM_LIMIT = 18 * 1024 * 1024
PARAMS = pltpu.CompilerParams(vmem_limit_bytes=VMEM_LIMIT)
CORE = 1
PARTS = 8
SPOTS = 4


def dot(left_side, right_side, left_dim=1, right_dim=0):
    return lax.dot_general(
        left_side,
        right_side,
        (((left_dim,), (right_dim,)), ((), ())),
        preferred_element_type=F32,
    )


def unit_parts(values):
    centred = values - jnp.mean(values, axis=-1, keepdims=True)
    inverse = lax.rsqrt(jnp.mean(centred * centred, axis=-1, keepdims=True) + EPSILON)
    return centred * inverse, inverse


def norm_back(grad_rows, unit_rows, inverse, gain_row):
    scaled = grad_rows * gain_row
    return inverse * (
        scaled
        - jnp.mean(scaled, axis=-1, keepdims=True)
        - unit_rows * jnp.mean(scaled * unit_rows, axis=-1, keepdims=True)
    )


def column_sum(values):
    return jnp.sum(values, axis=0, keepdims=True)


def gelu_parts(inner):
    below = 0.5 + 0.5 * lax.erf(inner * 0.7071067811865476)
    bell = jnp.exp(inner * inner * -0.5) * 0.3989422804014327
    return inner * below, below + inner * bell


def row_chunks(rows, step):
    return [slice(i, i + step) for i in range(0, rows, step)]


def eight_sum(values):
    return sum(values[cut] for cut in row_chunks(values.shape[0], 8))


def lane_pick(values, depth):
    lane = lax.broadcasted_iota(jnp.int32, (1, len(values) * depth), 1)
    picked = jnp.full(lane.shape, values[0], jnp.int32)
    for j in range(1, len(values)):
        picked = jnp.where(lane >= j * depth, values[j], picked)
    return picked


def place_of(part, half, spot):
    seen = part ^ half
    core = seen & 1
    low, high = 2 + 2 * core, 4 - 2 * core
    return seen ^ (low * (spot & 1) + high * (spot >> 1))


class Info:
    def __init__(self, ref, heads, shards):
        self.ref, self.heads, self.base = ref, heads, heads * shards

    def swaps(self, shard):
        return [self.ref[shard * self.heads + j] for j in range(self.heads)]

    own_live = property(lambda self: self.ref[self.base])
    partner_live = property(lambda self: self.ref[self.base + 1])
    part = property(lambda self: self.ref[self.base + 2])
    head_at = property(lambda self: self.ref[self.base + 3])


def gathered(part, near, far, scratch):
    for spot in range(SPOTS):
        scratch[place_of(part, 0, spot)] = near[spot, 0]
        scratch[place_of(part, 1, spot)] = far[spot, 0]
    return scratch[...].reshape(-1, scratch.shape[2])


def attend_kernel(setting, info_ref, tokens, partner, bias, out_weight, vectors, *refs):
    heads, depth, first_shard, last = setting
    refs = list(refs)
    if first_shard == 0:
        turned = refs.pop(0)
        total_in = None
    else:
        near, far, total_in = refs[:3]
        del refs[:3]
    earlier = []
    if last:
        earlier = refs[:2]
        del refs[:2]
    if first_shard:
        del refs[:2]
    qkv_out, context_out, stats_out = refs[:3]
    step = pl.program_id(0)
    shard = first_shard + step
    info = Info(info_ref, heads, out_weight.shape[0])
    if first_shard:
        weight = gathered(info.part, near, far, refs.pop())
    total = refs.pop()
    swaps = info.swaps(shard)
    rows, dim = tokens.shape
    width = heads * depth
    x, xp = tokens[...], partner[...]
    if first_shard:
        own = dot(x, weight)
        other = dot(xp, weight[:, : 2 * width])
    else:
        kv_rows = jnp.concatenate([turned[1], turned[2]], axis=0)
        own = jnp.concatenate([dot(x, kv_rows, 1, 1), dot(x, turned[0], 1, 1)], axis=1)
        other = dot(xp, kv_rows, 1, 1)
    swapped = lane_pick(swaps + swaps, depth) == 1
    bias_row = bias[0, 0:1]
    kv, q = [], []
    for cut in row_chunks(rows, 32):
        mine = own[cut] + bias_row
        theirs = other[cut] + bias_row[:, : 2 * width]
        kv.append(jnp.where(swapped, theirs, mine[:, : 2 * width]).astype(BF16))
        q.append(mine[:, 2 * width :].astype(BF16) * (depth**-0.5))
    kv, q = jnp.concatenate(kv, axis=0), jnp.concatenate(q, axis=0)
    qkv_out[0, :, : 2 * width] = kv
    qkv_out[0, :, 2 * width :] = q
    stats = []
    pieces = []
    for j in range(heads):
        head = slice(j * depth, (j + 1) * depth)
        live = jnp.where(swaps[j] == 1, info.partner_live, info.own_live)
        anyone = jnp.where(live > 0, 1.0, 0.0).astype(F32)
        scores = dot(kv[:, head], q[:, head], 1, 1)
        masked, most = [], None
        for cut in row_chunks(rows, 32):
            index = cut.start + lax.broadcasted_iota(jnp.int32, (32, 1), 0)
            part = jnp.where(index < live, scores[cut], -1e30)
            masked.append(part)
            for tile in row_chunks(32, 8):
                most = part[tile] if most is None else jnp.maximum(most, part[tile])
        largest = jnp.max(most, axis=0, keepdims=True)
        largest = jnp.where(anyone > 0.5, largest, 0.0)
        total_rows = None
        for part in masked:
            weights = eight_sum(jnp.exp(part - largest))
            total_rows = weights if total_rows is None else total_rows + weights
        stat = largest + jnp.log(column_sum(total_rows) + (1.0 - anyone))
        mixing = [jnp.exp(part - stat).astype(BF16) for part in masked]
        stats.append(stat)
        values = kv[:, width + j * depth : width + (j + 1) * depth]
        pieces.append(dot(values, jnp.concatenate(mixing, axis=0), 0, 0))
    context = jnp.concatenate(pieces, axis=0).T.astype(BF16)
    stats_out[0] = jnp.concatenate(stats + [jnp.zeros((8 - heads, rows), F32)], axis=0)
    projected = dot(context, out_weight[info.head_at ^ shard])
    if not last:
        context_out[0] = context

        @pl.when(step == 0)
        def first():
            total[...] = projected if total_in is None else total_in[...] + projected

        @pl.when(step > 0)
        def later():
            total[...] += projected

        return

    context_out[...] = jnp.concatenate(
        [ref[q] for ref in earlier for q in range(ref.shape[0])] + [context], axis=1
    )
    rows_out, normed_out = refs[3:]
    for cut in row_chunks(rows, 16):
        values = x[cut].astype(F32) + ((total_in[cut] + projected[cut]) + vectors[0:1])
        rows_out[cut] = values
        unit, _ = unit_parts(values)
        normed_out[cut] = (unit * vectors[1:2] + vectors[2:3]).astype(BF16)


def tiles_of(part, own, near, far, run):
    @pl.when(pl.program_id(0) == 0)
    def mine():
        run(
            *(
                jnp.concatenate([own[place_of(part, half, spot)] for spot in range(SPOTS)], axis=0)
                for half in range(2)
            )
        )

    @pl.when(pl.program_id(0) > 0)
    def other():
        run(*(ref[:, 0].reshape(-1, ref.shape[3]) for ref in (near, far)))


def add_up(total, *partials):
    @pl.when(pl.program_id(0) == 0)
    def start():
        total[...] = sum(partials[1:], partials[0])

    @pl.when(pl.program_id(0) > 0)
    def later():
        total[...] = sum(partials, total[...])


def at_end(run):
    pl.when(pl.program_id(0) == pl.num_programs(0) - 1)(run)


def eight_rows(*rows):
    width = rows[0].shape[1]
    return jnp.concatenate([*rows, jnp.zeros((8 - len(rows), width), F32)], axis=0)


def feed_up_kernel(info, normed, own, near, far, bias, *outs):
    shard = info[2] ^ pl.program_id(0)

    def run(*tiles):
        for half, tile in enumerate(tiles):
            places = [place_of(info[1], half, spot) for spot in range(SPOTS)]
            bias_row = jnp.concatenate([bias[shard, place] for place in places], axis=1)
            pre = dot(normed[...], tile, 1, 1)
            for cut in row_chunks(pre.shape[0], 32):
                hidden, slope = gelu_parts(pre[cut] + bias_row)
                outs[half][cut] = hidden.astype(BF16)
                outs[half + 2][cut] = slope

    tiles_of(info[1], own, near, far, run)


def feed_down_kernel(
    info,
    near_hidden,
    far_hidden,
    own,
    near,
    far,
    rows_in,
    cotangent,
    vectors,
    mixed_out,
    second_out,
    grad_out,
    sums_out,
    total,
):
    def run(near_tile, far_tile):
        add_up(total, dot(near_hidden[...], near_tile), dot(far_hidden[...], far_tile))

    tiles_of(info[1], own, near, far, run)

    @at_end
    def finish():
        sums = [jnp.zeros((8, rows_in.shape[1]), F32)] * 3
        for cut in row_chunks(rows_in.shape[0], 16):
            unit_one, _ = unit_parts(rows_in[cut])
            first_norm = unit_one * vectors[0:1] + vectors[1:2]
            unit, inverse = unit_parts(first_norm + (total[cut] + vectors[2:3]))
            index = cut.start + lax.broadcasted_iota(jnp.int32, (16, 1), 0)
            mask = jnp.where(index < info[0], 1.0, 0.0).astype(F32)
            mixed_out[cut] = ((unit * vectors[3:4] + vectors[4:5]) * mask).astype(BF16)
            incoming = cotangent[cut].astype(F32) * mask
            grad = norm_back(incoming, unit, inverse, vectors[3:4])
            second_out[cut] = grad
            low = grad.astype(BF16)
            grad_out[cut] = low
            more = (low.astype(F32), incoming * unit, incoming)
            sums = [a + eight_sum(b) for a, b in zip(sums, more)]
        sums_out[...] = eight_rows(*(column_sum(a) for a in sums))


def grad_pre_kernel(
    info, grad_branch, own, near, far, near_slope, far_slope, near_out, far_out, bias_out
):
    def run(*tiles):
        for half, tile in enumerate(tiles):
            out, slope = (near_out, far_out)[half], (near_slope, far_slope)[half]
            grad = dot(grad_branch[...], tile, 1, 1)
            sums = jnp.zeros((8, grad.shape[1]), F32)
            for cut in row_chunks(grad.shape[0], 32):
                low = (grad[cut] * slope[cut]).astype(BF16)
                out[cut] = low
                sums = sums + eight_sum(low.astype(F32))
            sums = jnp.broadcast_to(column_sum(sums), sums.shape)
            width = bias_out.shape[3]
            for spot in range(SPOTS):
                row = sums[:, spot * width : (spot + 1) * width]
                bias_out[info[2] ^ pl.program_id(0), place_of(info[1], half, spot)] = row

    tiles_of(info[1], own, near, far, run)


def up_back_kernel(
    info,
    near_pre,
    far_pre,
    own,
    near,
    far,
    rows_in,
    second_in,
    vectors,
    first_out,
    proj_out,
    sums_out,
    total,
):
    def run(near_tile, far_tile):
        add_up(total, dot(near_pre[...], near_tile), dot(far_pre[...], far_tile))

    tiles_of(info[1], own, near, far, run)

    @at_end
    def finish():
        sums = [jnp.zeros((8, rows_in.shape[1]), F32)] * 3
        for cut in row_chunks(rows_in.shape[0], 16):
            unit, inverse = unit_parts(rows_in[cut])
            grad_normed = second_in[cut] + total[cut]
            grad = norm_back(grad_normed, unit, inverse, vectors[0:1])
            first_out[cut] = grad
            low = grad.astype(BF16)
            proj_out[cut] = low
            more = (low.astype(F32), grad_normed * unit, grad_normed)
            sums = [a + eight_sum(b) for a, b in zip(sums, more)]
        sums_out[...] = eight_rows(*(column_sum(a) for a in sums))


def turn_kernel(tokens, partner, tokens_out, partner_out):
    tokens_out[...] = tokens[...].T
    partner_out[...] = partner[...].T


def row_grads_kernel(mine, theirs, my_rows, their_rows, *outs):
    value = dot(mine[...], my_rows[...], 0, 0) + dot(theirs[...], their_rows[...], 0, 0)
    value = value.reshape(SPOTS, -1, value.shape[1])
    for spot, out in enumerate(outs):
        out[0] = value[spot].astype(out.dtype)


def out_grads_kernel(info, mine, theirs, my_context, their_context, keep_out, send_out, turned):
    value = 0.0
    for i, (grad, context) in enumerate(((mine, my_context), (theirs, their_context))):
        turned[i] = grad[...].T.reshape(turned.shape[1:])
        rows = [turned[i, place_of(info[1], 0, spot)] for spot in range(SPOTS)]
        value = value + dot(jnp.concatenate(rows, axis=0), context[...])
    value = value.reshape(SPOTS, -1, value.shape[1])
    for spot in range(SPOTS):
        out = (keep_out, send_out)[spot & 1]
        out[spot >> 1] = value[spot].astype(out.dtype)


def scatter_parts(part, value, chunks, near_out, far_out):
    chunks[...] = value.reshape(chunks.shape)
    for spot in range(SPOTS):
        near_out[spot, 0] = chunks[place_of(part, 0, spot)]
        far_out[spot, 0] = chunks[place_of(part, 1, spot)]


def attend_back_kernel(setting, info_ref, tokens_t, partner_t, grad_proj, out_weight, *refs):
    heads, depth, first_shard, carried, so_far, shards = setting
    refs = list(refs)
    if first_shard == 0:
        turned = refs.pop(0)
    near, far, qkv_in, stats_in = refs[:4]
    del refs[:4]
    if carried:
        own_in, partner_in = refs[:2]
        del refs[:2]
    del refs[:so_far]
    own_out, *partner_outs, near_out, far_out, bias_out, total, weight_scratch, chunks = refs
    step = pl.program_id(0)
    shard = first_shard + step
    info = Info(info_ref, heads, shards)
    if first_shard:
        gathered(info.part, near, far, weight_scratch)
    else:
        width = turned.shape[1]

        @pl.when(shard == 0)
        def own_weight():
            rows_kv = jnp.concatenate([turned[1], turned[2], turned[0]], axis=0)
            weight_scratch[...] = rows_kv.T.reshape(weight_scratch.shape)

        @pl.when(shard > 0)
        def other_weight():
            gathered(info.part, near, far, weight_scratch)

    weight = weight_scratch[...].reshape(-1, weight_scratch.shape[2])
    swaps = info.swaps(shard)
    dim, rows = tokens_t.shape
    width = heads * depth
    grad = dot(grad_proj[...], out_weight[0], 1, 1).astype(BF16)
    k, v, q = (qkv_in[0, :, i * width : (i + 1) * width] for i in range(3))
    stats = stats_in[0]
    gq, gk, gv = [], [], []
    for j in range(heads):
        head = slice(j * depth, (j + 1) * depth)
        stat = stats[j : j + 1, :]
        live = jnp.where(swaps[j] == 1, info.partner_live, info.own_live)
        scores = dot(k[:, head], q[:, head], 1, 1)
        grad_mix = dot(v[:, head], grad[:, head], 1, 1)
        chances, shared = [], jnp.zeros((8, rows), F32)
        for cut in row_chunks(rows, 32):
            index = cut.start + lax.broadcasted_iota(jnp.int32, (32, 1), 0)
            part = jnp.exp(jnp.where(index < live, scores[cut] - stat, -10000.0))
            chances.append(part)
            shared = shared + eight_sum(part * grad_mix[cut])
        shared = column_sum(shared)
        mixing = jnp.concatenate([part.astype(BF16) for part in chances], axis=0)
        grad_scores = jnp.concatenate(
            [
                (part * (grad_mix[cut] - shared)).astype(BF16)
                for part, cut in zip(chances, row_chunks(rows, 32))
            ],
            axis=0,
        )
        gk.append(dot(grad_scores, q[:, head]))
        gv.append(dot(mixing, grad[:, head]))
        gq.append(dot(k[:, head], grad_scores, 0, 0))
    grad_q = (jnp.concatenate(gq, axis=0).T * (depth**-0.5)).astype(BF16)
    grad_kv = jnp.concatenate(gk + gv, axis=1).astype(BF16)
    swapped = lane_pick(swaps + swaps, depth) == 1
    nothing = jnp.zeros((), BF16)
    grad_own = jnp.concatenate([jnp.where(swapped, nothing, grad_kv), grad_q], axis=1)
    grad_far = jnp.where(swapped, grad_kv, nothing)
    own = dot(grad_own, weight, 1, 1)
    other = dot(grad_far, weight[:, : 2 * width], 1, 1)

    @pl.when(step == 0)
    def first():
        own_out[...] = own_in[...] + own if carried else own
        total[...] = partner_in[...] + other if carried else other

    @pl.when(step > 0)
    def later():
        own_out[...] += own
        total[...] += other

    @at_end
    def finish():
        first = 0
        for out in partner_outs:
            out[...] = total[first : first + out.shape[0]].astype(out.dtype)
            first += out.shape[0]

    grads = dot(tokens_t[...], grad_own)
    grads_kv = grads[:, : 2 * width] + dot(partner_t[...], grad_far)
    grads = jnp.concatenate([grads_kv, grads[:, 2 * width :]], axis=1).astype(BF16)
    chunks[...] = grads.reshape(chunks.shape)
    for spot in range(SPOTS):
        near_out[spot, 0] = chunks[place_of(info.part, 0, spot)]
        far_out[spot, 0] = chunks[place_of(info.part, 1, spot)]
    bias_out[0] = jnp.broadcast_to(
        jnp.concatenate(
            [column_sum(grad_kv.astype(F32)), column_sum(grad_q.astype(F32))], axis=1
        ),
        bias_out.shape[1:],
    )


def settle_down_kernel(info, near, far, out):
    for half, source in enumerate((near, far)):
        for spot in range(SPOTS):
            out[place_of(info[1], half, spot)] = source[spot].astype(F32)


def settle_up_kernel(info, near, far, up_out, out_out, up_scratch, out_scratch):
    dim = up_out.shape[0]
    for half, source in enumerate((near, far)):
        for spot in range(SPOTS):
            place = place_of(info[1], half, spot)
            value = source[spot].astype(F32)
            up_scratch[place] = value[:, :dim]
            out_scratch[place] = value[:, dim:]
    up_out[...] = up_scratch[...].reshape(-1, dim).T
    shards = out_out.shape[0]
    turned = out_scratch[...].reshape(-1, dim).T.reshape(shards, -1, dim)
    for q in range(shards):
        out_out[info[2] ^ q] = turned[q]


def settle_input_kernel(info, near, far, out, scratch):
    width = out.shape[1]
    for half, source in enumerate((near, far)):
        for spot in range(SPOTS):
            scratch[place_of(info[1], half, spot)] = source[spot].astype(F32)
    turned = scratch[...].reshape(-1, scratch.shape[2]).T
    for i in range(3):
        out[(i + 1) % 3] = turned[i * width : (i + 1) * width]


def shape(dims, dtype):
    return jax.ShapeDtypeStruct(dims, dtype)


def whole(*dims):
    return pl.BlockSpec(dims, lambda *_: (0,) * len(dims))


def cost(flops, moved, slow=0):
    return pl.CostEstimate(flops=flops, bytes_accessed=moved, transcendentals=slow)


SMEM = pl.BlockSpec(memory_space=pltpu.SMEM)


def gathered_specs(near, first_shard):
    spots, _, piece, lanes = near.shape
    return [pl.BlockSpec((spots, 1, piece, lanes), lambda s: (0, s + first_shard - 1, 0, 0))] * 2


def attend(
    setting, count, info, tokens, partner, bias, out_weight, vectors, weights, carried, so_far
):
    heads, depth, first_shard, last = setting
    rows, dim = tokens.shape
    shards, width, _ = out_weight.shape
    lanes = 3 * width
    scratch = []
    if first_shard == 0:
        weight_specs = [whole(3, width, dim)]
    else:
        weight_specs = gathered_specs(weights[0], first_shard)
        scratch = [pltpu.VMEM((PARTS, dim // PARTS, lanes), BF16)]
    out_specs = [
        pl.BlockSpec((1, rows, lanes), lambda s: (s + first_shard, 0, 0)),
        whole(rows, dim) if last else pl.BlockSpec((1, rows, width), lambda s: (s, 0, 0)),
        pl.BlockSpec((1, 8, rows), lambda s: (s + first_shard, 0, 0)),
    ]
    out_shape = [
        shape((shards, rows, lanes), BF16),
        shape((rows, dim) if last else (count, rows, width), BF16),
        shape((shards, 8, rows), F32),
    ]
    fixed = 6 + len(weights) + len(carried)
    if last:
        out_specs += [whole(rows, dim)] * 2
        out_shape += [shape((rows, dim), F32), shape((rows, dim), BF16)]
        scratch = [pltpu.VMEM((8, 128), F32)] + scratch
    else:
        out_specs.append(whole(rows, dim))
        out_shape.append(shape((rows, dim), F32))
    return pl.pallas_call(
        functools.partial(attend_kernel, setting),
        grid=(count,),
        in_specs=[
            SMEM,
            whole(rows, dim),
            whole(rows, dim),
            pl.BlockSpec((1, 8, lanes), lambda s: (s + first_shard, 0, 0)),
            whole(shards, width, dim),
            whole(8, dim),
        ]
        + weight_specs
        + [whole(*value.shape) for value in carried]
        + [pl.BlockSpec(memory_space=pl.ANY)] * len(so_far),
        out_specs=out_specs,
        out_shape=out_shape,
        scratch_shapes=scratch,
        input_output_aliases={fixed + i: (0, 2)[i] for i in range(len(so_far))},
        compiler_params=PARAMS,
        cost_estimate=cost(
            count * (3 * rows * dim * dim + 4 * rows * rows * dim),
            count * 6 * rows * dim,
            count * heads * rows * rows,
        ),
        name="attend",
    )(info, tokens, partner, bias, out_weight, vectors, *weights, *carried, *so_far)


def feed_specs(near):
    spots, _, piece, lanes = near.shape
    other = pl.BlockSpec(
        (spots, 1, piece, lanes), lambda q: (0, jnp.maximum(q - 1, 0), 0, 0)
    )
    return [whole(PARTS, piece, lanes), other, other]


def feed_up(info, normed, weight, bias):
    rows, dim = normed.shape
    near = weight[1]
    shards = near.shape[1] + 1
    tile = SPOTS * near.shape[2]
    columns = pl.BlockSpec((rows, tile), lambda q: (0, q))
    return pl.pallas_call(
        feed_up_kernel,
        grid=(shards,),
        in_specs=[
            SMEM,
            whole(rows, dim),
            *feed_specs(near),
            whole(*bias.shape),
        ],
        out_specs=[columns] * 4,
        out_shape=[shape((rows, shards * tile), BF16)] * 2
        + [shape((rows, shards * tile), F32)] * 2,
        compiler_params=PARAMS,
        cost_estimate=cost(4 * rows * dim * tile * shards, 30 * rows * dim, rows * dim * 8),
        name="feed_up",
    )(info, normed, *weight, bias)


def feed_down(info, hidden, weight, rows_one, cotangent, vectors):
    rows, dim = rows_one.shape
    near = weight[1]
    shards = near.shape[1] + 1
    tile = SPOTS * near.shape[2]
    columns = pl.BlockSpec((rows, tile), lambda q: (0, q))
    return pl.pallas_call(
        feed_down_kernel,
        grid=(shards,),
        in_specs=[
            SMEM,
            columns,
            columns,
            *feed_specs(near),
            whole(rows, dim),
            whole(rows, dim),
            whole(8, dim),
        ],
        out_specs=[whole(rows, dim)] * 3 + [whole(8, dim)],
        out_shape=[
            shape((rows, dim), BF16),
            shape((rows, dim), F32),
            shape((rows, dim), BF16),
            shape((8, dim), F32),
        ],
        scratch_shapes=[pltpu.VMEM((rows, dim), F32)],
        compiler_params=PARAMS,
        cost_estimate=cost(4 * rows * dim * tile * shards, 20 * rows * dim),
        name="feed_down",
    )(info, *hidden, *weight, rows_one, cotangent, vectors)


def grad_pre_of(info, grad_branch, weight, slopes):
    rows, dim = grad_branch.shape
    near = weight[1]
    shards = near.shape[1] + 1
    tile = SPOTS * near.shape[2]
    columns = pl.BlockSpec((rows, tile), lambda q: (0, q))
    return pl.pallas_call(
        grad_pre_kernel,
        grid=(shards,),
        in_specs=[SMEM, whole(rows, dim), *feed_specs(near), columns, columns],
        out_specs=[columns, columns, whole(shards, PARTS, 8, near.shape[2])],
        out_shape=[
            shape((rows, shards * tile), BF16),
            shape((rows, shards * tile), BF16),
            shape((shards, PARTS, 8, near.shape[2]), F32),
        ],
        compiler_params=PARAMS,
        cost_estimate=cost(4 * rows * dim * tile * shards, 30 * rows * dim),
        name="grad_pre",
    )(info, grad_branch, *weight, *slopes)


def up_back(info, pres, weight, rows_one, grad_second, vectors):
    rows, dim = rows_one.shape
    near = weight[1]
    shards = near.shape[1] + 1
    tile = SPOTS * near.shape[2]
    columns = pl.BlockSpec((rows, tile), lambda q: (0, q))
    return pl.pallas_call(
        up_back_kernel,
        grid=(shards,),
        in_specs=[
            SMEM,
            columns,
            columns,
            *feed_specs(near),
            whole(rows, dim),
            whole(rows, dim),
            whole(8, dim),
        ],
        out_specs=[whole(rows, dim), whole(rows, dim), whole(8, dim)],
        out_shape=[shape((rows, dim), F32), shape((rows, dim), BF16), shape((8, dim), F32)],
        scratch_shapes=[pltpu.VMEM((rows, dim), F32)],
        compiler_params=PARAMS,
        cost_estimate=cost(4 * rows * dim * tile * shards, 24 * rows * dim),
        name="up_back",
    )(info, *pres, *weight, rows_one, grad_second, vectors)


def turn(tokens, partner):
    rows, dim = tokens.shape
    return pl.pallas_call(
        turn_kernel,
        out_shape=[shape((dim, rows), BF16)] * 2,
        compiler_params=PARAMS,
        cost_estimate=cost(rows * dim, 8 * rows * dim),
        name="turn",
    )(tokens, partner)


def row_grads(shards, mine, theirs, my_rows, their_rows, name):
    rows, dim = my_rows.shape
    tile = mine.shape[1] // shards
    piece = tile // SPOTS
    columns = pl.BlockSpec((rows, tile), lambda q: (0, q))
    out = pl.BlockSpec((1, piece, dim), lambda q: (q, 0, 0))
    return pl.pallas_call(
        row_grads_kernel,
        grid=(shards,),
        in_specs=[columns, columns, whole(rows, dim), whole(rows, dim)],
        out_specs=[out] * SPOTS,
        out_shape=[shape((shards, piece, dim), (F32, BF16)[spot & 1]) for spot in range(SPOTS)],
        compiler_params=PARAMS,
        cost_estimate=cost(4 * rows * dim * tile * shards, 20 * rows * dim),
        name=name,
    )(mine, theirs, my_rows, their_rows)


def out_grads(info, mine, theirs, my_context, their_context):
    rows, dim = mine.shape
    piece = dim // PARTS
    return pl.pallas_call(
        out_grads_kernel,
        in_specs=[SMEM] + [whole(rows, dim)] * 4,
        out_specs=[whole(2, piece, dim)] * 2,
        out_shape=[shape((2, piece, dim), F32), shape((2, piece, dim), BF16)],
        scratch_shapes=[pltpu.VMEM((2, PARTS, piece, rows), BF16)],
        compiler_params=PARAMS,
        cost_estimate=cost(2 * rows * dim * dim, 10 * rows * dim),
        name="out_grads",
    )(info, mine, theirs, my_context, their_context)


def attend_back(
    setting,
    info,
    tokens_t,
    partner_t,
    grad_proj,
    out_weight,
    own,
    near,
    far,
    qkvs,
    stats,
    carried,
    so_far,
):
    heads, depth, first_shard, count, shards = setting
    half = shards // 2
    slot = first_shard % half
    fixed = 9 + len(own) + len(carried)
    splits = 1 if first_shard else 2
    dim, rows = tokens_t.shape
    width = heads * depth
    lanes = 3 * width
    piece = dim // PARTS
    head_spot = heads * shards + 3
    own_specs = [] if first_shard else [whole(3, width, dim)]
    kernel = functools.partial(
        attend_back_kernel, (heads, depth, first_shard, bool(carried), len(so_far), shards)
    )

    def other(s, info):
        return (0, jnp.maximum(s + first_shard - 1, 0), 0, 0)

    parts_out = pl.BlockSpec((SPOTS, 1, piece, lanes), lambda s, info: (0, s + slot, 0, 0))
    return pl.pallas_call(
        kernel,
        grid_spec=pltpu.PrefetchScalarGridSpec(
            num_scalar_prefetch=1,
            grid=(count,),
            in_specs=[
                whole(dim, rows),
                whole(dim, rows),
                whole(rows, dim),
                pl.BlockSpec(
                    (1, width, dim), lambda s, info: (info[head_spot] ^ (s + first_shard), 0, 0)
                ),
            ]
            + own_specs
            + [pl.BlockSpec((SPOTS, 1, piece, lanes), other)] * 2
            + [
                pl.BlockSpec((1, rows, lanes), lambda s, info: (s + first_shard, 0, 0)),
                pl.BlockSpec((1, 8, rows), lambda s, info: (s + first_shard, 0, 0)),
            ]
            + [whole(rows, dim)] * len(carried)
            + [pl.BlockSpec(memory_space=pl.ANY)] * len(so_far),
            out_specs=[
                whole(rows, dim),
                *[whole(rows // splits, dim)] * splits,
                parts_out,
                parts_out,
                pl.BlockSpec(
                    (1, 8, lanes), lambda s, info: (info[head_spot] ^ (s + first_shard), 0, 0)
                ),
            ],
            scratch_shapes=[
                pltpu.VMEM((rows, dim), F32),
                pltpu.VMEM((PARTS, piece, lanes), BF16),
                pltpu.VMEM((PARTS, piece, lanes), BF16),
            ],
        ),
        out_shape=[
            shape((rows, dim), F32),
            *[shape((rows // splits, dim), F32 if first_shard else BF16)] * splits,
            shape((SPOTS, half, piece, lanes), BF16),
            shape((SPOTS, half, piece, lanes), BF16),
            shape((shards, 8, lanes), F32),
        ],
        input_output_aliases={
            fixed + i: 4 + splits - len(so_far) + i for i in range(len(so_far))
        },
        compiler_params=PARAMS,
        cost_estimate=cost(
            count * (6 * rows * dim * dim + 10 * rows * rows * dim),
            count * 8 * rows * dim,
            count * heads * rows * rows,
        ),
        name="attend_back",
    )(
        info,
        tokens_t,
        partner_t,
        grad_proj,
        out_weight,
        *own,
        near,
        far,
        qkvs,
        stats,
        *carried,
        *so_far,
    )


class Mover:
    def __init__(self, batch_size, shards):
        self.batch_size, self.shards = batch_size, shards

    def batch(self, value, mask_of):
        perm = [(i, i ^ mask_of(i)) for i in range(self.batch_size)]
        return lax.ppermute(value, "batch", perm)

    def core(self, value):
        return self.batch(value, lambda i: CORE)

    def low(self, value):
        return self.batch(value, lambda i: 4 if i & 1 else 2)

    def high(self, value):
        return self.batch(value, lambda i: 2 if i & 1 else 4)

    def head(self, value, mask):
        return lax.ppermute(value, "head", [(i, i ^ mask) for i in range(self.shards)])

    def along(self, values, first=1):
        return [self.head(value, q) for q, value in enumerate(values, first)]

    def column(self, piece):
        return self.along([piece] * (self.shards - 1))

    def settle(self, total):
        total = total.astype(BF16)
        mask = PARTS
        while mask < self.batch_size:
            other = self.batch(total, lambda i, mask=mask: mask)
            total = (total.astype(F32) + other.astype(F32)).astype(BF16)
            mask *= 2
        return total

    def hops(self):
        steps, mask = [self.core, self.low, self.high], 1
        while mask < self.shards:
            steps.append(lambda value, mask=mask: self.head(value, mask))
            mask *= 2
        mask = PARTS
        while mask < self.batch_size:
            steps.append(lambda value, mask=mask: self.batch(value, lambda i: mask))
            mask *= 2
        return steps


def after(value, *events):
    return lax.optimization_barrier((value, *events))[0]


def all_after(values, *events):
    return lax.optimization_barrier((*values, *events))[: len(values)]


def pair_of(first, second):
    return jnp.stack([first, second])


def four_of(pair, received):
    return jnp.concatenate([pair, received])


def shards_swapped(value, shards, mask):
    width = value.shape[1] // shards
    blocks = [value[:, (q ^ mask) * width : ((q ^ mask) + 1) * width] for q in range(shards)]
    return jnp.concatenate(blocks, axis=1)


def stack8(*rows):
    rows = [row.reshape(1, -1) for row in rows]
    return jnp.concatenate(rows + [jnp.zeros((8 - len(rows), rows[0].shape[1]), F32)], axis=0)


def local(
    batch_size,
    shards,
    tokens,
    lengths,
    block_swap,
    input_weight,
    input_bias,
    out_weight,
    out_bias,
    gain_one,
    shift_one,
    up_weight,
    up_bias,
    down_weight,
    down_bias,
    gain_two,
    shift_two,
    cotangent,
):
    move = Mover(batch_size, shards)
    heads = block_swap.shape[0]
    rows, dim = tokens.shape
    width = input_weight.shape[2]
    depth = width // heads
    hidden_own = up_weight.shape[1]
    piece = dim // PARTS
    batch_at, head_at = lax.axis_index("batch"), lax.axis_index("head")
    part = batch_at % PARTS
    blocks = SEQ_LEN // rows
    length = lax.dynamic_index_in_dim(lengths, head_at // blocks, 0, keepdims=False)
    block_at = head_at % blocks
    own_live = jnp.clip(length - block_at * rows, 0, rows)
    partner_live = jnp.clip(length - (blocks - 1 - block_at) * rows, 0, rows)

    input_piece = lax.dynamic_slice_in_dim(input_weight, part * piece, piece, 1)
    input_piece = jnp.concatenate([input_piece[1], input_piece[2], input_piece[0]], axis=1)
    small = jnp.concatenate([jnp.zeros((width,), F32), input_bias[1], input_bias[0]])
    high = lax.reduce_precision(small, 8, 7)
    middle = lax.reduce_precision(small - high, 8, 7)
    swaps = jnp.pad(block_swap.astype(F32), (0, 3 * width - heads))
    small = jnp.stack([high, middle, small - high - middle, swaps])
    small = jnp.pad(small, ((0, 12), (0, 0))).astype(BF16)
    input_column = move.column(jnp.concatenate([input_piece, small]))
    up_own = up_weight.T.reshape(PARTS, piece, dim)
    up_piece = lax.dynamic_index_in_dim(up_own, part, 0, keepdims=False)
    input_own = input_weight.transpose(0, 2, 1)
    down_own = down_weight.reshape(PARTS, piece, dim)
    down_piece = lax.dynamic_index_in_dim(down_own, part, 0, keepdims=False)
    short_info = jnp.stack([own_live, part, head_at]).astype(jnp.int32)
    up_bias_parts = up_bias.reshape(shards, PARTS, 1, piece)
    out_parts = out_weight.reshape(shards, width, dim)
    vectors_one = stack8(out_bias, gain_one, shift_one)
    vectors_two = stack8(gain_one, shift_one, down_bias, gain_two, shift_two)
    vectors_back = stack8(gain_one)
    *input_column, up_piece, tokens_sent = all_after(
        (*input_column, up_piece, tokens), vectors_one, vectors_two, down_piece
    )
    small = jnp.stack([small] + [value[piece:] for value in input_column]).astype(F32)
    input_column = jnp.stack([value[:piece] for value in input_column])
    partner = move.head(tokens_sent, 1)
    input_low = move.low(input_column)
    up_far = move.head(up_piece, 2)
    info = jnp.concatenate(
        [
            small[:, 3, :heads].reshape(-1).astype(jnp.int32),
            jnp.stack([own_live, partner_live, part, head_at]).astype(jnp.int32),
        ]
    )
    bias = (small[:, 0] + small[:, 1]) + small[:, 2]
    bias = jnp.broadcast_to(bias[:, None], (shards, 8, 3 * width))
    input_low, up_far = all_after((input_low, up_far), info, bias)
    input_pair = pair_of(input_column, input_low)
    input_high = move.high(input_pair)
    up_ends = pair_of(up_piece, up_far)
    up_others = move.head(up_ends, 1)
    input_high, up_others, partner = all_after((input_high, up_others, partner))
    input_near = four_of(input_pair, input_high)
    input_far = move.core(input_near)
    up_column = jnp.stack([up_others[0], up_ends[1], up_others[1]])
    up_low = move.low(up_column)
    down_far = move.head(after(down_piece, up_others), 2)
    def attend_shards(first_shard, count, last, weights, carried, so_far):
        return attend(
            (heads, depth, first_shard, last),
            count,
            info,
            tokens,
            partner,
            bias,
            out_parts,
            vectors_one,
            weights,
            carried,
            so_far,
        )

    qkv, context_0, stats, total = attend_shards(0, 1, False, [input_own], [], [])
    input_far, up_low, down_far, total, qkv, stats = all_after(
        (input_far, up_low, down_far, total, qkv, stats)
    )
    others = [input_near, input_far]
    up_pair = pair_of(up_column, up_low)
    up_high = move.high(up_pair)
    down_ends = pair_of(down_piece, down_far)
    down_others = move.head(down_ends, 1)
    total, down_ends, up_pair = all_after((total, down_ends, up_pair))
    qkv, context_1, stats, total = attend_shards(1, 2, False, others, [total], [qkv, stats])
    up_high, down_others, total, qkv, stats = all_after((up_high, down_others, total, qkv, stats))
    up_near = four_of(up_pair, up_high)
    up_far = move.core(up_near)
    down_column = jnp.stack([down_others[0], down_ends[1], down_others[1]])
    down_low = move.low(down_column)
    total, up_near, down_column = all_after((total, up_near, down_column))
    qkv, context, stats, rows_one, normed = attend_shards(
        3, 1, True, others, [total, context_0, context_1], [qkv, stats]
    )
    up_far, down_low, normed, context = all_after((up_far, down_low, normed, context))
    up_all = (up_own, up_near, up_far)
    down_pair = pair_of(down_column, down_low)
    down_high = move.high(down_pair)
    normed, down_pair = all_after((normed, down_pair))
    normed_received = move.core(normed)
    context_received = move.core(context)
    hidden_near, hidden_far, *slopes = feed_up(short_info, normed, up_all, up_bias_parts)
    hidden_received = move.core(hidden_far)
    down_near = four_of(down_pair, after(down_high, hidden_near))
    down_far = move.core(down_near)
    tokens_t, partner_t = turn(after(tokens, down_near), partner)
    down_far, tokens_t, partner_t = all_after((down_far, tokens_t, partner_t))
    down_all = (down_own, down_near, down_far)
    mixed_out, grad_second, grad_branch, sums_two = feed_down(
        short_info, (hidden_near, hidden_far), down_all, rows_one, cotangent, vectors_two
    )

    branch_received = move.core(grad_branch)
    down_mine, down_one, down_two, down_three = row_grads(
        shards,
        hidden_near,
        hidden_received,
        grad_branch,
        branch_received,
        "down_grads",
    )
    down_three = move.low(down_three)
    pre_near, pre_far, up_bias_sums = grad_pre_of(
        short_info, after(grad_branch, down_two), down_all, slopes
    )
    down_three, pre_near, pre_far, up_bias_sums = all_after(
        (down_three, pre_near, pre_far, up_bias_sums)
    )
    pre_received = move.core(pre_far)
    down_two = (down_two + down_three.astype(F32)).astype(BF16)
    down_high = move.high(down_two)
    grad_first, grad_proj, sums_one = up_back(
        short_info, (pre_near, pre_far), up_all, rows_one, after(grad_second, down_two), vectors_back
    )
    pre_received, down_high, grad_proj, grad_first, sums_one = all_after(
        (pre_received, down_high, grad_proj, grad_first, sums_one)
    )
    proj_received = move.core(grad_proj)
    down_one = move.low(after(down_one, down_high))

    def core_sum(mine, received):
        mine, received = (a.reshape(2, 2, *a.shape[1:]) for a in (mine, received))
        keep = [mine[i, 0].astype(F32) + received[i, 0].astype(F32) for i in range(2)]
        return keep, (mine[:, 1].astype(F32) + received[:, 1].astype(F32)).astype(BF16)

    def fold_low(keep, received):
        return keep[0] + received[0].astype(F32), (keep[1] + received[1].astype(F32)).astype(BF16)

    def fold_high(own, received):
        total = own + received.astype(F32)
        return total[0::2], total[1::2].astype(BF16)

    def fold_near(own, received):
        return own[0] + received[0].astype(F32), (own[1] + received[1].astype(F32)).astype(BF16)

    def fold_last(own, received):
        return move.settle(own + received.astype(F32))

    up_mine, up_one, up_two, up_three = row_grads(
        shards, pre_near, pre_received, normed, normed_received, "up_grads"
    )
    proj_received, up_one, up_three = all_after((proj_received, up_one, up_three))
    up_three = move.low(up_three)
    out_keep, out_send = out_grads(
        short_info, after(grad_proj, up_one), proj_received, context, context_received
    )
    down_one, out_keep, out_send = all_after((down_one, out_keep, out_send))
    up_one = move.low(after(up_one, down_one))
    out_low = move.low(out_send)
    down_mine = down_mine + (down_one.astype(F32) + down_high.astype(F32))
    down_mine, down_next = down_mine[0::2], down_mine[1::2].astype(BF16)
    down_near = move.head(down_next, 1)

    def back(grad, first_shard, count, carried, so_far):
        return attend_back(
            (heads, depth, first_shard, count, shards),
            info,
            tokens_t,
            partner_t,
            grad,
            out_parts,
            [] if first_shard else [input_own],
            *others,
            qkv,
            stats,
            carried,
            so_far,
        )

    own_rows, partner_rows, late_near, late_far, late_bias = back(
        after(grad_proj, out_send, down_next), 2, 2, [], []
    )

    (
        down_near,
        up_one,
        up_three,
        out_low,
        own_rows,
        partner_rows,
        late_near,
        late_far,
        late_bias,
    ) = all_after(
        (
            down_near,
            up_one,
            up_three,
            out_low,
            own_rows,
            partner_rows,
            late_near,
            late_far,
            late_bias,
        )
    )
    up_next = (up_two + up_three.astype(F32)).astype(BF16)
    up_mine = up_mine + up_one.astype(F32)
    up_high = move.high(up_next)
    late_core = move.core(late_far)
    down_mine, down_next = fold_near(down_mine, after(down_near, up_next))
    down_last = move.head(down_next, 2)
    out_mine = out_keep[0] + out_low[0].astype(F32)
    out_next = (out_keep[1] + out_low[1].astype(F32)).astype(BF16)
    out_high = move.high(out_next)
    own_rows, partner_rows, *early = back(
        after(grad_proj, down_next, up_next, out_next), 1, 1, [own_rows, partner_rows], [late_bias]
    )

    up_high, down_last, late_core, out_high, own_rows, partner_rows, *early = all_after(
        (up_high, down_last, late_core, out_high, own_rows, partner_rows, *early)
    )
    up_mine, up_next = fold_high(up_mine, up_high)
    up_near = move.head(up_next, 1)
    late_keep, late_next = core_sum(late_near, late_core)
    late_low = move.low(late_next)
    down_total = fold_last(down_mine, down_last)
    down_low = move.low(down_total)
    out_next = (out_mine + out_high.astype(F32)).astype(BF16)
    out_near = move.head(out_next, 1)
    own_rows, partner_first, partner_second, early_near, early_far, early_bias = back(
        after(grad_proj, up_next, down_total, late_next, out_next),
        0,
        1,
        [own_rows, partner_rows],
        early,
    )

    up_near, down_low, late_low, out_near, own_rows, partner_first, partner_second = all_after(
        (up_near, down_low, late_low, out_near, own_rows, partner_first, partner_second), early_bias
    )
    early_near, early_far, early_bias = all_after((early_near, early_far, early_bias), up_near)

    early_core = move.core(early_far)
    up_mine, up_next = fold_near(up_mine, up_near)
    up_last = move.head(up_next, 2)
    late_mine, late_next = fold_low(late_keep, late_low)
    late_high = move.high(late_next)
    out_near = shards_swapped(out_near, shards, 1)
    out_next = (out_next.astype(F32) + out_near.astype(F32)).astype(BF16)
    out_last = move.head(out_next, 2)
    vectors = jnp.concatenate(
        [
            sums_one[:3],
            sums_two[:3],
            up_bias_sums[:, :, 0].reshape(shards, dim),
            jnp.pad(early_bias[:, 0], ((0, 0), (0, dim - 3 * width))),
        ]
    )
    hops = move.hops()

    def hop(value, sent, event):
        value = value + after(sent, event)
        return value, hops.pop(0)(value) if hops else None

    vectors_sent = hops.pop(0)(vectors)
    early_keep, early_next = core_sum(
        early_near, after(early_core, late_next, up_next, vectors, out_next)
    )
    early_low = move.low(early_next)
    vectors, vectors_sent = hop(vectors, vectors_sent, early_next)
    late_mine = late_mine + after(late_high, vectors).astype(F32)
    partner_first = move.head(after(partner_first, late_mine), 1)
    down_pair = pair_of(down_total, after(down_low, late_mine))
    down_high = move.high(down_pair)
    early_mine, early_next = fold_low(early_keep, after(early_low, down_pair))
    early_high = move.high(early_next)
    vectors, vectors_sent = hop(vectors, vectors_sent, early_next)
    up_total = fold_last(up_mine, after(up_last, vectors))
    out_last = shards_swapped(after(out_last, up_total), shards, 2)
    out_total = move.settle(out_next.astype(F32) + out_last.astype(F32))
    up_total = jnp.concatenate([up_total, out_total], axis=1)
    up_low = move.low(up_total)
    down_near = four_of(down_pair, after(down_high, up_total))
    down_far = move.core(down_near)
    early_mine = early_mine + after(early_high, down_near).astype(F32)
    input_next = jnp.stack([early_mine[1], late_mine[1]]).astype(BF16)
    input_near = move.head(input_next, 1)
    vectors, vectors_sent = hop(vectors, vectors_sent, input_next)
    partner_second = move.head(after(partner_second, input_next), 1)
    up_pair = pair_of(up_total, after(up_low, vectors))
    up_high = move.high(up_pair)
    down_far = after(down_far, up_pair)
    input_mine, input_next = fold_near(
        jnp.stack([early_mine[0], late_mine[0]]), after(input_near, up_pair)
    )
    input_last = move.head(input_next, 2)
    grad_down = pl.pallas_call(
        settle_down_kernel,
        in_specs=[SMEM] + [whole(4, piece, dim)] * 2,
        out_shape=shape((PARTS, piece, dim), F32),
        compiler_params=PARAMS,
        name="settle_down",
    )(short_info, after(down_near, input_next), down_far)
    input_last, vectors_sent, partner_first = all_after(
        (input_last, vectors_sent, partner_first), grad_down
    )
    input_total = fold_last(input_mine, input_last)
    input_low = move.low(input_total)
    vectors, vectors_sent = hop(vectors, vectors_sent, input_total)
    up_near = four_of(up_pair, after(up_high, input_total))
    up_far = move.core(up_near)
    from_partner = jnp.concatenate([partner_first, after(partner_second, up_near)])
    grad_tokens = grad_first + own_rows + from_partner.astype(F32)
    input_low, vectors_sent = all_after((input_low, vectors_sent), grad_tokens)
    input_pair = pair_of(input_total, input_low)
    input_high = move.high(input_pair)
    while vectors_sent is not None:
        vectors, vectors_sent = hop(vectors, vectors_sent, input_pair)
    input_near = four_of(input_pair, after(input_high, vectors))
    input_far = move.core(input_near)
    grad_up, grad_out = pl.pallas_call(
        settle_up_kernel,
        in_specs=[SMEM] + [whole(4, piece, dim + shards * width)] * 2,
        out_shape=[shape((dim, hidden_own), F32), shape((shards, width, dim), F32)],
        scratch_shapes=[pltpu.VMEM((PARTS, piece, dim), F32)] * 2,
        compiler_params=PARAMS,
        name="settle_up",
    )(short_info, after(up_near, input_near), up_far)
    grad_input_bias = lax.dynamic_index_in_dim(vectors[10:], head_at, 0, keepdims=False)
    grad_input_bias = jnp.stack(
        [grad_input_bias[2 * width : 3 * width], grad_input_bias[width : 2 * width]]
    )
    grad_up_bias = lax.dynamic_index_in_dim(vectors[6:10], head_at, 0, keepdims=False)
    grad_input_weight = pl.pallas_call(
        settle_input_kernel,
        in_specs=[SMEM] + [whole(4, piece, 3 * width)] * 2,
        out_shape=shape((3, width, dim), F32),
        scratch_shapes=[pltpu.VMEM((PARTS, piece, 3 * width), F32)],
        compiler_params=PARAMS,
        name="settle_input",
    )(short_info, after(input_near, grad_up), input_far)
    return (
        mixed_out,
        grad_tokens,
        grad_input_weight.transpose(0, 2, 1),
        grad_input_bias,
        grad_out.reshape(dim, dim),
        vectors[0],
        vectors[1],
        vectors[2],
        grad_up,
        grad_up_bias,
        grad_down.reshape(hidden_own, dim),
        vectors[3],
        vectors[4],
        vectors[5],
    )


def solution(mesh):
    rows_spec = P(("batch", "head"), None)
    placed = (
        rows_spec,
        P("batch"),
        P("head"),
        P(None, None, "head"),
        P(None, "head"),
        P(),
        P(),
        P(),
        P(),
        P(None, "head"),
        P(),
        P("head", None),
        P(),
        P(),
        P(),
        rows_spec,
    )
    return jax.shard_map(
        functools.partial(local, mesh.shape["batch"], mesh.shape["head"]),
        mesh=mesh,
        in_specs=placed,
        out_specs=(
            rows_spec,
            rows_spec,
            P(None, None, "head"),
            P(None, "head"),
            P(),
            P(),
            P(),
            P(),
            P(None, "head"),
            P("head"),
            P("head", None),
            P(),
            P(),
            P(),
        ),
        check_vma=False,
    )
```

```python
import functools

import jax
import jax.numpy as jnp
from jax import lax
from jax.experimental import pallas as pl
from jax.experimental.pallas import tpu as pltpu
from jax.sharding import PartitionSpec as P

SEQ_LEN = 1024
EPSILON = 1e-05
F32 = jnp.float32
BF16 = jnp.bfloat16
VMEM_LIMIT = 18 * 1024 * 1024
PARAMS = pltpu.CompilerParams(vmem_limit_bytes=VMEM_LIMIT)
CORE = 1
PARTS = 8
SPOTS = 4


def dot(left_side, right_side, left_dim=1, right_dim=0):
    return lax.dot_general(
        left_side,
        right_side,
        (((left_dim,), (right_dim,)), ((), ())),
        preferred_element_type=F32,
    )


def unit_parts(values):
    centred = values - jnp.mean(values, axis=-1, keepdims=True)
    inverse = lax.rsqrt(jnp.mean(centred * centred, axis=-1, keepdims=True) + EPSILON)
    return centred * inverse, inverse


def norm_back(grad_rows, unit_rows, inverse, gain_row):
    scaled = grad_rows * gain_row
    return inverse * (
        scaled
        - jnp.mean(scaled, axis=-1, keepdims=True)
        - unit_rows * jnp.mean(scaled * unit_rows, axis=-1, keepdims=True)
    )


def column_sum(values):
    return jnp.sum(values, axis=0, keepdims=True)


def gelu_parts(inner):
    below = 0.5 + 0.5 * lax.erf(inner * 0.7071067811865476)
    bell = jnp.exp(inner * inner * -0.5) * 0.3989422804014327
    return inner * below, below + inner * bell


def row_chunks(rows, step):
    return [slice(i, i + step) for i in range(0, rows, step)]


def eight_sum(values):
    return sum(values[cut] for cut in row_chunks(values.shape[0], 8))


def lane_pick(values, depth):
    lane = lax.broadcasted_iota(jnp.int32, (1, len(values) * depth), 1)
    picked = jnp.full(lane.shape, values[0], jnp.int32)
    for j in range(1, len(values)):
        picked = jnp.where(lane >= j * depth, values[j], picked)
    return picked


def place_of(part, half, spot):
    seen = part ^ half
    core = seen & 1
    low, high = 2 + 2 * core, 4 - 2 * core
    return seen ^ (low * (spot & 1) + high * (spot >> 1))


class Info:
    def __init__(self, ref, heads, shards):
        self.ref, self.heads, self.base = ref, heads, heads * shards

    def swaps(self, shard):
        return [self.ref[shard * self.heads + j] for j in range(self.heads)]

    own_live = property(lambda self: self.ref[self.base])
    partner_live = property(lambda self: self.ref[self.base + 1])
    part = property(lambda self: self.ref[self.base + 2])
    head_at = property(lambda self: self.ref[self.base + 3])


def gathered(part, near, far, scratch):
    for spot in range(SPOTS):
        scratch[place_of(part, 0, spot)] = near[spot, 0]
        scratch[place_of(part, 1, spot)] = far[spot, 0]
    return scratch[...].reshape(-1, scratch.shape[2])


def attend_kernel(setting, info_ref, tokens, partner, bias, out_weight, vectors, *refs):
    heads, depth, first_shard, last = setting
    refs = list(refs)
    if first_shard == 0:
        turned = refs.pop(0)
        total_in = None
    else:
        near, far, total_in = refs[:3]
        del refs[:3]
    earlier = []
    if last:
        earlier = refs[:2]
        del refs[:2]
    if first_shard:
        del refs[:2]
    qkv_out, context_out, stats_out = refs[:3]
    step = pl.program_id(0)
    shard = first_shard + step
    info = Info(info_ref, heads, out_weight.shape[0])
    if first_shard:
        weight = gathered(info.part, near, far, refs.pop())
    total = refs.pop()
    swaps = info.swaps(shard)
    rows, dim = tokens.shape
    width = heads * depth
    x, xp = tokens[...], partner[...]
    if first_shard:
        own = dot(x, weight)
        other = dot(xp, weight[:, : 2 * width])
    else:
        kv_rows = jnp.concatenate([turned[1], turned[2]], axis=0)
        own = jnp.concatenate([dot(x, kv_rows, 1, 1), dot(x, turned[0], 1, 1)], axis=1)
        other = dot(xp, kv_rows, 1, 1)
    swapped = lane_pick(swaps + swaps, depth) == 1
    bias_row = bias[0, 0:1]
    kv, q = [], []
    for cut in row_chunks(rows, 32):
        mine = own[cut] + bias_row
        theirs = other[cut] + bias_row[:, : 2 * width]
        kv.append(jnp.where(swapped, theirs, mine[:, : 2 * width]).astype(BF16))
        q.append(mine[:, 2 * width :].astype(BF16) * (depth**-0.5))
    kv, q = jnp.concatenate(kv, axis=0), jnp.concatenate(q, axis=0)
    qkv_out[0, :, : 2 * width] = kv
    qkv_out[0, :, 2 * width :] = q
    stats = []
    pieces = []
    for j in range(heads):
        head = slice(j * depth, (j + 1) * depth)
        live = jnp.where(swaps[j] == 1, info.partner_live, info.own_live)
        anyone = jnp.where(live > 0, 1.0, 0.0).astype(F32)
        scores = dot(kv[:, head], q[:, head], 1, 1)
        masked, most = [], None
        for cut in row_chunks(rows, 32):
            index = cut.start + lax.broadcasted_iota(jnp.int32, (32, 1), 0)
            part = jnp.where(index < live, scores[cut], -1e30)
            masked.append(part)
            for tile in row_chunks(32, 8):
                most = part[tile] if most is None else jnp.maximum(most, part[tile])
        largest = jnp.max(most, axis=0, keepdims=True)
        largest = jnp.where(anyone > 0.5, largest, 0.0)
        total_rows = None
        for part in masked:
            weights = eight_sum(jnp.exp(part - largest))
            total_rows = weights if total_rows is None else total_rows + weights
        stat = largest + jnp.log(column_sum(total_rows) + (1.0 - anyone))
        mixing = [jnp.exp(part - stat).astype(BF16) for part in masked]
        stats.append(stat)
        values = kv[:, width + j * depth : width + (j + 1) * depth]
        pieces.append(dot(values, jnp.concatenate(mixing, axis=0), 0, 0))
    context = jnp.concatenate(pieces, axis=0).T.astype(BF16)
    stats_out[0] = jnp.concatenate(stats + [jnp.zeros((8 - heads, rows), F32)], axis=0)
    projected = dot(context, out_weight[info.head_at ^ shard])
    if not last:
        context_out[0] = context

        @pl.when(step == 0)
        def first():
            total[...] = projected if total_in is None else total_in[...] + projected

        @pl.when(step > 0)
        def later():
            total[...] += projected

        return

    context_out[...] = jnp.concatenate(
        [ref[q] for ref in earlier for q in range(ref.shape[0])] + [context], axis=1
    )
    rows_out, normed_out = refs[3:]
    for cut in row_chunks(rows, 16):
        values = x[cut].astype(F32) + ((total_in[cut] + projected[cut]) + vectors[0:1])
        rows_out[cut] = values
        unit, _ = unit_parts(values)
        normed_out[cut] = (unit * vectors[1:2] + vectors[2:3]).astype(BF16)


def tiles_of(part, own, near, far, run):
    @pl.when(pl.program_id(0) == 0)
    def mine():
        run(
            *(
                jnp.concatenate([own[place_of(part, half, spot)] for spot in range(SPOTS)], axis=0)
                for half in range(2)
            )
        )

    @pl.when(pl.program_id(0) > 0)
    def other():
        run(*(ref[:, 0].reshape(-1, ref.shape[3]) for ref in (near, far)))


def add_up(total, *partials):
    @pl.when(pl.program_id(0) == 0)
    def start():
        total[...] = sum(partials[1:], partials[0])

    @pl.when(pl.program_id(0) > 0)
    def later():
        total[...] = sum(partials, total[...])


def at_end(run):
    pl.when(pl.program_id(0) == pl.num_programs(0) - 1)(run)


def eight_rows(*rows):
    width = rows[0].shape[1]
    return jnp.concatenate([*rows, jnp.zeros((8 - len(rows), width), F32)], axis=0)


def feed_up_kernel(info, normed, own, near, far, bias, *outs):
    shard = info[2] ^ pl.program_id(0)

    def run(*tiles):
        for half, tile in enumerate(tiles):
            places = [place_of(info[1], half, spot) for spot in range(SPOTS)]
            bias_row = jnp.concatenate([bias[shard, place] for place in places], axis=1)
            pre = dot(normed[...], tile, 1, 1)
            for cut in row_chunks(pre.shape[0], 32):
                hidden, slope = gelu_parts(pre[cut] + bias_row)
                outs[half][cut] = hidden.astype(BF16)
                outs[half + 2][cut] = slope

    tiles_of(info[1], own, near, far, run)


def feed_down_kernel(
    info,
    near_hidden,
    far_hidden,
    own,
    near,
    far,
    rows_in,
    cotangent,
    vectors,
    mixed_out,
    second_out,
    grad_out,
    sums_out,
    total,
):
    def run(near_tile, far_tile):
        add_up(total, dot(near_hidden[...], near_tile), dot(far_hidden[...], far_tile))

    tiles_of(info[1], own, near, far, run)

    @at_end
    def finish():
        sums = [jnp.zeros((8, rows_in.shape[1]), F32)] * 3
        for cut in row_chunks(rows_in.shape[0], 16):
            unit_one, _ = unit_parts(rows_in[cut])
            first_norm = unit_one * vectors[0:1] + vectors[1:2]
            unit, inverse = unit_parts(first_norm + (total[cut] + vectors[2:3]))
            index = cut.start + lax.broadcasted_iota(jnp.int32, (16, 1), 0)
            mask = jnp.where(index < info[0], 1.0, 0.0).astype(F32)
            mixed_out[cut] = ((unit * vectors[3:4] + vectors[4:5]) * mask).astype(BF16)
            incoming = cotangent[cut].astype(F32) * mask
            grad = norm_back(incoming, unit, inverse, vectors[3:4])
            second_out[cut] = grad
            low = grad.astype(BF16)
            grad_out[cut] = low
            more = (low.astype(F32), incoming * unit, incoming)
            sums = [a + eight_sum(b) for a, b in zip(sums, more)]
        sums_out[...] = eight_rows(*(column_sum(a) for a in sums))


def grad_pre_kernel(
    info, grad_branch, own, near, far, near_slope, far_slope, near_out, far_out, bias_out
):
    def run(*tiles):
        for half, tile in enumerate(tiles):
            out, slope = (near_out, far_out)[half], (near_slope, far_slope)[half]
            grad = dot(grad_branch[...], tile, 1, 1)
            sums = jnp.zeros((8, grad.shape[1]), F32)
            for cut in row_chunks(grad.shape[0], 32):
                low = (grad[cut] * slope[cut]).astype(BF16)
                out[cut] = low
                sums = sums + eight_sum(low.astype(F32))
            sums = jnp.broadcast_to(column_sum(sums), sums.shape)
            width = bias_out.shape[3]
            for spot in range(SPOTS):
                row = sums[:, spot * width : (spot + 1) * width]
                bias_out[info[2] ^ pl.program_id(0), place_of(info[1], half, spot)] = row

    tiles_of(info[1], own, near, far, run)


def up_back_kernel(
    info,
    near_pre,
    far_pre,
    own,
    near,
    far,
    rows_in,
    second_in,
    vectors,
    first_out,
    proj_out,
    sums_out,
    total,
):
    def run(near_tile, far_tile):
        add_up(total, dot(near_pre[...], near_tile), dot(far_pre[...], far_tile))

    tiles_of(info[1], own, near, far, run)

    @at_end
    def finish():
        sums = [jnp.zeros((8, rows_in.shape[1]), F32)] * 3
        for cut in row_chunks(rows_in.shape[0], 16):
            unit, inverse = unit_parts(rows_in[cut])
            grad_normed = second_in[cut] + total[cut]
            grad = norm_back(grad_normed, unit, inverse, vectors[0:1])
            first_out[cut] = grad
            low = grad.astype(BF16)
            proj_out[cut] = low
            more = (low.astype(F32), grad_normed * unit, grad_normed)
            sums = [a + eight_sum(b) for a, b in zip(sums, more)]
        sums_out[...] = eight_rows(*(column_sum(a) for a in sums))


def turn_kernel(tokens, partner, tokens_out, partner_out):
    tokens_out[...] = tokens[...].T
    partner_out[...] = partner[...].T


def row_grads_kernel(mine, theirs, my_rows, their_rows, *outs):
    value = dot(mine[...], my_rows[...], 0, 0) + dot(theirs[...], their_rows[...], 0, 0)
    value = value.reshape(SPOTS, -1, value.shape[1])
    for spot, out in enumerate(outs):
        out[0] = value[spot].astype(out.dtype)


def out_grads_kernel(info, mine, theirs, my_context, their_context, keep_out, send_out, turned):
    value = 0.0
    for i, (grad, context) in enumerate(((mine, my_context), (theirs, their_context))):
        turned[i] = grad[...].T.reshape(turned.shape[1:])
        rows = [turned[i, place_of(info[1], 0, spot)] for spot in range(SPOTS)]
        value = value + dot(jnp.concatenate(rows, axis=0), context[...])
    value = value.reshape(SPOTS, -1, value.shape[1])
    for spot in range(SPOTS):
        out = (keep_out, send_out)[spot & 1]
        out[spot >> 1] = value[spot].astype(out.dtype)


def scatter_parts(part, value, chunks, near_out, far_out):
    chunks[...] = value.reshape(chunks.shape)
    for spot in range(SPOTS):
        near_out[spot, 0] = chunks[place_of(part, 0, spot)]
        far_out[spot, 0] = chunks[place_of(part, 1, spot)]


def attend_back_kernel(setting, info_ref, tokens_t, partner_t, grad_proj, out_weight, *refs):
    heads, depth, first_shard, carried, so_far, shards = setting
    refs = list(refs)
    if first_shard == 0:
        turned = refs.pop(0)
    near, far, qkv_in, stats_in = refs[:4]
    del refs[:4]
    if carried:
        own_in, partner_in = refs[:2]
        del refs[:2]
    del refs[:so_far]
    own_out, *partner_outs, near_out, far_out, bias_out, total, weight_scratch, chunks = refs
    step = pl.program_id(0)
    shard = first_shard + step
    info = Info(info_ref, heads, shards)
    if first_shard:
        gathered(info.part, near, far, weight_scratch)
    else:
        width = turned.shape[1]

        @pl.when(shard == 0)
        def own_weight():
            rows_kv = jnp.concatenate([turned[1], turned[2], turned[0]], axis=0)
            weight_scratch[...] = rows_kv.T.reshape(weight_scratch.shape)

        @pl.when(shard > 0)
        def other_weight():
            gathered(info.part, near, far, weight_scratch)

    weight = weight_scratch[...].reshape(-1, weight_scratch.shape[2])
    swaps = info.swaps(shard)
    dim, rows = tokens_t.shape
    width = heads * depth
    grad = dot(grad_proj[...], out_weight[0], 1, 1).astype(BF16)
    k, v, q = (qkv_in[0, :, i * width : (i + 1) * width] for i in range(3))
    stats = stats_in[0]
    gq, gk, gv = [], [], []
    for j in range(heads):
        head = slice(j * depth, (j + 1) * depth)
        stat = stats[j : j + 1, :]
        live = jnp.where(swaps[j] == 1, info.partner_live, info.own_live)
        scores = dot(k[:, head], q[:, head], 1, 1)
        grad_mix = dot(v[:, head], grad[:, head], 1, 1)
        chances, shared = [], jnp.zeros((8, rows), F32)
        for cut in row_chunks(rows, 32):
            index = cut.start + lax.broadcasted_iota(jnp.int32, (32, 1), 0)
            part = jnp.exp(jnp.where(index < live, scores[cut] - stat, -10000.0))
            chances.append(part)
            shared = shared + eight_sum(part * grad_mix[cut])
        shared = column_sum(shared)
        mixing = jnp.concatenate([part.astype(BF16) for part in chances], axis=0)
        grad_scores = jnp.concatenate(
            [
                (part * (grad_mix[cut] - shared)).astype(BF16)
                for part, cut in zip(chances, row_chunks(rows, 32))
            ],
            axis=0,
        )
        gk.append(dot(grad_scores, q[:, head]))
        gv.append(dot(mixing, grad[:, head]))
        gq.append(dot(k[:, head], grad_scores, 0, 0))
    grad_q = (jnp.concatenate(gq, axis=0).T * (depth**-0.5)).astype(BF16)
    grad_kv = jnp.concatenate(gk + gv, axis=1).astype(BF16)
    swapped = lane_pick(swaps + swaps, depth) == 1
    nothing = jnp.zeros((), BF16)
    grad_own = jnp.concatenate([jnp.where(swapped, nothing, grad_kv), grad_q], axis=1)
    grad_far = jnp.where(swapped, grad_kv, nothing)
    own = dot(grad_own, weight, 1, 1)
    other = dot(grad_far, weight[:, : 2 * width], 1, 1)

    @pl.when(step == 0)
    def first():
        own_out[...] = own_in[...] + own if carried else own
        total[...] = partner_in[...] + other if carried else other

    @pl.when(step > 0)
    def later():
        own_out[...] += own
        total[...] += other

    @at_end
    def finish():
        first = 0
        for out in partner_outs:
            out[...] = total[first : first + out.shape[0]].astype(out.dtype)
            first += out.shape[0]

    grads = dot(tokens_t[...], grad_own)
    grads_kv = grads[:, : 2 * width] + dot(partner_t[...], grad_far)
    grads = jnp.concatenate([grads_kv, grads[:, 2 * width :]], axis=1).astype(BF16)
    chunks[...] = grads.reshape(chunks.shape)
    for spot in range(SPOTS):
        near_out[spot, 0] = chunks[place_of(info.part, 0, spot)]
        far_out[spot, 0] = chunks[place_of(info.part, 1, spot)]
    bias_out[0] = jnp.broadcast_to(
        jnp.concatenate(
            [column_sum(grad_kv.astype(F32)), column_sum(grad_q.astype(F32))], axis=1
        ),
        bias_out.shape[1:],
    )


def settle_down_kernel(info, near, far, out):
    for half, source in enumerate((near, far)):
        for spot in range(SPOTS):
            out[place_of(info[1], half, spot)] = source[spot].astype(F32)


def settle_up_kernel(info, near, far, up_out, out_out, up_scratch, out_scratch):
    dim = up_out.shape[0]
    for half, source in enumerate((near, far)):
        for spot in range(SPOTS):
            place = place_of(info[1], half, spot)
            value = source[spot].astype(F32)
            up_scratch[place] = value[:, :dim]
            out_scratch[place] = value[:, dim:]
    up_out[...] = up_scratch[...].reshape(-1, dim).T
    shards = out_out.shape[0]
    turned = out_scratch[...].reshape(-1, dim).T.reshape(shards, -1, dim)
    for q in range(shards):
        out_out[info[2] ^ q] = turned[q]


def settle_input_kernel(info, near, far, out, scratch):
    width = out.shape[1]
    for half, source in enumerate((near, far)):
        for spot in range(SPOTS):
            scratch[place_of(info[1], half, spot)] = source[spot].astype(F32)
    turned = scratch[...].reshape(-1, scratch.shape[2]).T
    for i in range(3):
        out[(i + 1) % 3] = turned[i * width : (i + 1) * width]


def shape(dims, dtype):
    return jax.ShapeDtypeStruct(dims, dtype)


def whole(*dims):
    return pl.BlockSpec(dims, lambda *_: (0,) * len(dims))


def cost(flops, moved, slow=0):
    return pl.CostEstimate(flops=flops, bytes_accessed=moved, transcendentals=slow)


SMEM = pl.BlockSpec(memory_space=pltpu.SMEM)


def gathered_specs(near, first_shard):
    spots, _, piece, lanes = near.shape
    return [pl.BlockSpec((spots, 1, piece, lanes), lambda s: (0, s + first_shard - 1, 0, 0))] * 2


def attend(
    setting, count, info, tokens, partner, bias, out_weight, vectors, weights, carried, so_far
):
    heads, depth, first_shard, last = setting
    rows, dim = tokens.shape
    shards, width, _ = out_weight.shape
    lanes = 3 * width
    scratch = []
    if first_shard == 0:
        weight_specs = [whole(3, width, dim)]
    else:
        weight_specs = gathered_specs(weights[0], first_shard)
        scratch = [pltpu.VMEM((PARTS, dim // PARTS, lanes), BF16)]
    out_specs = [
        pl.BlockSpec((1, rows, lanes), lambda s: (s + first_shard, 0, 0)),
        whole(rows, dim) if last else pl.BlockSpec((1, rows, width), lambda s: (s, 0, 0)),
        pl.BlockSpec((1, 8, rows), lambda s: (s + first_shard, 0, 0)),
    ]
    out_shape = [
        shape((shards, rows, lanes), BF16),
        shape((rows, dim) if last else (count, rows, width), BF16),
        shape((shards, 8, rows), F32),
    ]
    fixed = 6 + len(weights) + len(carried)
    if last:
        out_specs += [whole(rows, dim)] * 2
        out_shape += [shape((rows, dim), F32), shape((rows, dim), BF16)]
        scratch = [pltpu.VMEM((8, 128), F32)] + scratch
    else:
        out_specs.append(whole(rows, dim))
        out_shape.append(shape((rows, dim), F32))
    return pl.pallas_call(
        functools.partial(attend_kernel, setting),
        grid=(count,),
        in_specs=[
            SMEM,
            whole(rows, dim),
            whole(rows, dim),
            pl.BlockSpec((1, 8, lanes), lambda s: (s + first_shard, 0, 0)),
            whole(shards, width, dim),
            whole(8, dim),
        ]
        + weight_specs
        + [whole(*value.shape) for value in carried]
        + [pl.BlockSpec(memory_space=pl.ANY)] * len(so_far),
        out_specs=out_specs,
        out_shape=out_shape,
        scratch_shapes=scratch,
        input_output_aliases={fixed + i: (0, 2)[i] for i in range(len(so_far))},
        compiler_params=PARAMS,
        cost_estimate=cost(
            count * (3 * rows * dim * dim + 4 * rows * rows * dim),
            count * 6 * rows * dim,
            count * heads * rows * rows,
        ),
        name="attend",
    )(info, tokens, partner, bias, out_weight, vectors, *weights, *carried, *so_far)


def feed_specs(near):
    spots, _, piece, lanes = near.shape
    other = pl.BlockSpec(
        (spots, 1, piece, lanes), lambda q: (0, jnp.maximum(q - 1, 0), 0, 0)
    )
    return [whole(PARTS, piece, lanes), other, other]


def feed_up(info, normed, weight, bias):
    rows, dim = normed.shape
    near = weight[1]
    shards = near.shape[1] + 1
    tile = SPOTS * near.shape[2]
    columns = pl.BlockSpec((rows, tile), lambda q: (0, q))
    return pl.pallas_call(
        feed_up_kernel,
        grid=(shards,),
        in_specs=[
            SMEM,
            whole(rows, dim),
            *feed_specs(near),
            whole(*bias.shape),
        ],
        out_specs=[columns] * 4,
        out_shape=[shape((rows, shards * tile), BF16)] * 2
        + [shape((rows, shards * tile), F32)] * 2,
        compiler_params=PARAMS,
        cost_estimate=cost(4 * rows * dim * tile * shards, 30 * rows * dim, rows * dim * 8),
        name="feed_up",
    )(info, normed, *weight, bias)


def feed_down(info, hidden, weight, rows_one, cotangent, vectors):
    rows, dim = rows_one.shape
    near = weight[1]
    shards = near.shape[1] + 1
    tile = SPOTS * near.shape[2]
    columns = pl.BlockSpec((rows, tile), lambda q: (0, q))
    return pl.pallas_call(
        feed_down_kernel,
        grid=(shards,),
        in_specs=[
            SMEM,
            columns,
            columns,
            *feed_specs(near),
            whole(rows, dim),
            whole(rows, dim),
            whole(8, dim),
        ],
        out_specs=[whole(rows, dim)] * 3 + [whole(8, dim)],
        out_shape=[
            shape((rows, dim), BF16),
            shape((rows, dim), F32),
            shape((rows, dim), BF16),
            shape((8, dim), F32),
        ],
        scratch_shapes=[pltpu.VMEM((rows, dim), F32)],
        compiler_params=PARAMS,
        cost_estimate=cost(4 * rows * dim * tile * shards, 20 * rows * dim),
        name="feed_down",
    )(info, *hidden, *weight, rows_one, cotangent, vectors)


def grad_pre_of(info, grad_branch, weight, slopes):
    rows, dim = grad_branch.shape
    near = weight[1]
    shards = near.shape[1] + 1
    tile = SPOTS * near.shape[2]
    columns = pl.BlockSpec((rows, tile), lambda q: (0, q))
    return pl.pallas_call(
        grad_pre_kernel,
        grid=(shards,),
        in_specs=[SMEM, whole(rows, dim), *feed_specs(near), columns, columns],
        out_specs=[columns, columns, whole(shards, PARTS, 8, near.shape[2])],
        out_shape=[
            shape((rows, shards * tile), BF16),
            shape((rows, shards * tile), BF16),
            shape((shards, PARTS, 8, near.shape[2]), F32),
        ],
        compiler_params=PARAMS,
        cost_estimate=cost(4 * rows * dim * tile * shards, 30 * rows * dim),
        name="grad_pre",
    )(info, grad_branch, *weight, *slopes)


def up_back(info, pres, weight, rows_one, grad_second, vectors):
    rows, dim = rows_one.shape
    near = weight[1]
    shards = near.shape[1] + 1
    tile = SPOTS * near.shape[2]
    columns = pl.BlockSpec((rows, tile), lambda q: (0, q))
    return pl.pallas_call(
        up_back_kernel,
        grid=(shards,),
        in_specs=[
            SMEM,
            columns,
            columns,
            *feed_specs(near),
            whole(rows, dim),
            whole(rows, dim),
            whole(8, dim),
        ],
        out_specs=[whole(rows, dim), whole(rows, dim), whole(8, dim)],
        out_shape=[shape((rows, dim), F32), shape((rows, dim), BF16), shape((8, dim), F32)],
        scratch_shapes=[pltpu.VMEM((rows, dim), F32)],
        compiler_params=PARAMS,
        cost_estimate=cost(4 * rows * dim * tile * shards, 24 * rows * dim),
        name="up_back",
    )(info, *pres, *weight, rows_one, grad_second, vectors)


def turn(tokens, partner):
    rows, dim = tokens.shape
    return pl.pallas_call(
        turn_kernel,
        out_shape=[shape((dim, rows), BF16)] * 2,
        compiler_params=PARAMS,
        cost_estimate=cost(rows * dim, 8 * rows * dim),
        name="turn",
    )(tokens, partner)


def row_grads(shards, mine, theirs, my_rows, their_rows, name):
    rows, dim = my_rows.shape
    tile = mine.shape[1] // shards
    piece = tile // SPOTS
    columns = pl.BlockSpec((rows, tile), lambda q: (0, q))
    out = pl.BlockSpec((1, piece, dim), lambda q: (q, 0, 0))
    return pl.pallas_call(
        row_grads_kernel,
        grid=(shards,),
        in_specs=[columns, columns, whole(rows, dim), whole(rows, dim)],
        out_specs=[out] * SPOTS,
        out_shape=[shape((shards, piece, dim), (F32, BF16)[spot & 1]) for spot in range(SPOTS)],
        compiler_params=PARAMS,
        cost_estimate=cost(4 * rows * dim * tile * shards, 20 * rows * dim),
        name=name,
    )(mine, theirs, my_rows, their_rows)


def out_grads(info, mine, theirs, my_context, their_context):
    rows, dim = mine.shape
    piece = dim // PARTS
    return pl.pallas_call(
        out_grads_kernel,
        in_specs=[SMEM] + [whole(rows, dim)] * 4,
        out_specs=[whole(2, piece, dim)] * 2,
        out_shape=[shape((2, piece, dim), F32), shape((2, piece, dim), BF16)],
        scratch_shapes=[pltpu.VMEM((2, PARTS, piece, rows), BF16)],
        compiler_params=PARAMS,
        cost_estimate=cost(2 * rows * dim * dim, 10 * rows * dim),
        name="out_grads",
    )(info, mine, theirs, my_context, their_context)


def attend_back(
    setting,
    info,
    tokens_t,
    partner_t,
    grad_proj,
    out_weight,
    own,
    near,
    far,
    qkvs,
    stats,
    carried,
    so_far,
):
    heads, depth, first_shard, count, shards = setting
    half = shards // 2
    slot = first_shard % half
    fixed = 9 + len(own) + len(carried)
    splits = 1 if first_shard else 2
    dim, rows = tokens_t.shape
    width = heads * depth
    lanes = 3 * width
    piece = dim // PARTS
    head_spot = heads * shards + 3
    own_specs = [] if first_shard else [whole(3, width, dim)]
    kernel = functools.partial(
        attend_back_kernel, (heads, depth, first_shard, bool(carried), len(so_far), shards)
    )

    def other(s, info):
        return (0, jnp.maximum(s + first_shard - 1, 0), 0, 0)

    parts_out = pl.BlockSpec((SPOTS, 1, piece, lanes), lambda s, info: (0, s + slot, 0, 0))
    return pl.pallas_call(
        kernel,
        grid_spec=pltpu.PrefetchScalarGridSpec(
            num_scalar_prefetch=1,
            grid=(count,),
            in_specs=[
                whole(dim, rows),
                whole(dim, rows),
                whole(rows, dim),
                pl.BlockSpec(
                    (1, width, dim), lambda s, info: (info[head_spot] ^ (s + first_shard), 0, 0)
                ),
            ]
            + own_specs
            + [pl.BlockSpec((SPOTS, 1, piece, lanes), other)] * 2
            + [
                pl.BlockSpec((1, rows, lanes), lambda s, info: (s + first_shard, 0, 0)),
                pl.BlockSpec((1, 8, rows), lambda s, info: (s + first_shard, 0, 0)),
            ]
            + [whole(rows, dim)] * len(carried)
            + [pl.BlockSpec(memory_space=pl.ANY)] * len(so_far),
            out_specs=[
                whole(rows, dim),
                *[whole(rows // splits, dim)] * splits,
                parts_out,
                parts_out,
                pl.BlockSpec(
                    (1, 8, lanes), lambda s, info: (info[head_spot] ^ (s + first_shard), 0, 0)
                ),
            ],
            scratch_shapes=[
                pltpu.VMEM((rows, dim), F32),
                pltpu.VMEM((PARTS, piece, lanes), BF16),
                pltpu.VMEM((PARTS, piece, lanes), BF16),
            ],
        ),
        out_shape=[
            shape((rows, dim), F32),
            *[shape((rows // splits, dim), F32 if first_shard else BF16)] * splits,
            shape((SPOTS, half, piece, lanes), BF16),
            shape((SPOTS, half, piece, lanes), BF16),
            shape((shards, 8, lanes), F32),
        ],
        input_output_aliases={
            fixed + i: 4 + splits - len(so_far) + i for i in range(len(so_far))
        },
        compiler_params=PARAMS,
        cost_estimate=cost(
            count * (6 * rows * dim * dim + 10 * rows * rows * dim),
            count * 8 * rows * dim,
            count * heads * rows * rows,
        ),
        name="attend_back",
    )(
        info,
        tokens_t,
        partner_t,
        grad_proj,
        out_weight,
        *own,
        near,
        far,
        qkvs,
        stats,
        *carried,
        *so_far,
    )


class Mover:
    def __init__(self, batch_size, shards):
        self.batch_size, self.shards = batch_size, shards

    def batch(self, value, mask_of):
        perm = [(i, i ^ mask_of(i)) for i in range(self.batch_size)]
        return lax.ppermute(value, "batch", perm)

    def core(self, value):
        return self.batch(value, lambda i: CORE)

    def low(self, value):
        return self.batch(value, lambda i: 4 if i & 1 else 2)

    def high(self, value):
        return self.batch(value, lambda i: 2 if i & 1 else 4)

    def head(self, value, mask):
        return lax.ppermute(value, "head", [(i, i ^ mask) for i in range(self.shards)])

    def along(self, values, first=1):
        return [self.head(value, q) for q, value in enumerate(values, first)]

    def column(self, piece):
        return self.along([piece] * (self.shards - 1))

    def settle(self, total):
        total = total.astype(BF16)
        mask = PARTS
        while mask < self.batch_size:
            other = self.batch(total, lambda i, mask=mask: mask)
            total = (total.astype(F32) + other.astype(F32)).astype(BF16)
            mask *= 2
        return total

    def hops(self):
        steps, mask = [self.core, self.low, self.high], 1
        while mask < self.shards:
            steps.append(lambda value, mask=mask: self.head(value, mask))
            mask *= 2
        mask = PARTS
        while mask < self.batch_size:
            steps.append(lambda value, mask=mask: self.batch(value, lambda i: mask))
            mask *= 2
        return steps


def after(value, *events):
    return lax.optimization_barrier((value, *events))[0]


def all_after(values, *events):
    return lax.optimization_barrier((*values, *events))[: len(values)]


def pair_of(first, second):
    return jnp.stack([first, second])


def four_of(pair, received):
    return jnp.concatenate([pair, received])


def shards_swapped(value, shards, mask):
    width = value.shape[1] // shards
    blocks = [value[:, (q ^ mask) * width : ((q ^ mask) + 1) * width] for q in range(shards)]
    return jnp.concatenate(blocks, axis=1)


def stack8(*rows):
    rows = [row.reshape(1, -1) for row in rows]
    return jnp.concatenate(rows + [jnp.zeros((8 - len(rows), rows[0].shape[1]), F32)], axis=0)


def local(
    batch_size,
    shards,
    tokens,
    lengths,
    block_swap,
    input_weight,
    input_bias,
    out_weight,
    out_bias,
    gain_one,
    shift_one,
    up_weight,
    up_bias,
    down_weight,
    down_bias,
    gain_two,
    shift_two,
    cotangent,
):
    move = Mover(batch_size, shards)
    heads = block_swap.shape[0]
    rows, dim = tokens.shape
    width = input_weight.shape[2]
    depth = width // heads
    hidden_own = up_weight.shape[1]
    piece = dim // PARTS
    batch_at, head_at = lax.axis_index("batch"), lax.axis_index("head")
    part = batch_at % PARTS
    blocks = SEQ_LEN // rows
    length = lax.dynamic_index_in_dim(lengths, head_at // blocks, 0, keepdims=False)
    block_at = head_at % blocks
    own_live = jnp.clip(length - block_at * rows, 0, rows)
    partner_live = jnp.clip(length - (blocks - 1 - block_at) * rows, 0, rows)

    input_piece = lax.dynamic_slice_in_dim(input_weight, part * piece, piece, 1)
    input_piece = jnp.concatenate([input_piece[1], input_piece[2], input_piece[0]], axis=1)
    small = jnp.concatenate([jnp.zeros((width,), F32), input_bias[1], input_bias[0]])
    high = lax.reduce_precision(small, 8, 7)
    middle = lax.reduce_precision(small - high, 8, 7)
    swaps = jnp.pad(block_swap.astype(F32), (0, 3 * width - heads))
    small = jnp.stack([high, middle, small - high - middle, swaps])
    small = jnp.pad(small, ((0, 12), (0, 0))).astype(BF16)
    input_column = move.column(jnp.concatenate([input_piece, small]))
    up_own = up_weight.T.reshape(PARTS, piece, dim)
    up_piece = lax.dynamic_index_in_dim(up_own, part, 0, keepdims=False)
    input_own = input_weight.transpose(0, 2, 1)
    down_own = down_weight.reshape(PARTS, piece, dim)
    down_piece = lax.dynamic_index_in_dim(down_own, part, 0, keepdims=False)
    short_info = jnp.stack([own_live, part, head_at]).astype(jnp.int32)
    up_bias_parts = up_bias.reshape(shards, PARTS, 1, piece)
    out_parts = out_weight.reshape(shards, width, dim)
    vectors_one = stack8(out_bias, gain_one, shift_one)
    vectors_two = stack8(gain_one, shift_one, down_bias, gain_two, shift_two)
    vectors_back = stack8(gain_one)
    *input_column, up_piece, tokens_sent = all_after(
        (*input_column, up_piece, tokens), vectors_one, vectors_two, down_piece
    )
    small = jnp.stack([small] + [value[piece:] for value in input_column]).astype(F32)
    input_column = jnp.stack([value[:piece] for value in input_column])
    partner = move.head(tokens_sent, 1)
    input_low = move.low(input_column)
    up_far = move.head(up_piece, 2)
    info = jnp.concatenate(
        [
            small[:, 3, :heads].reshape(-1).astype(jnp.int32),
            jnp.stack([own_live, partner_live, part, head_at]).astype(jnp.int32),
        ]
    )
    bias = (small[:, 0] + small[:, 1]) + small[:, 2]
    bias = jnp.broadcast_to(bias[:, None], (shards, 8, 3 * width))
    input_low, up_far = all_after((input_low, up_far), info, bias)
    input_pair = pair_of(input_column, input_low)
    input_high = move.high(input_pair)
    input_high, partner = all_after((input_high, partner))
    input_near = four_of(input_pair, input_high)
    input_far = move.core(input_near)
    up_ends = pair_of(up_piece, after(up_far, partner))
    up_others = move.head(up_ends, 1)

    def attend_shards(first_shard, count, last, weights, carried, so_far):
        return attend(
            (heads, depth, first_shard, last),
            count,
            info,
            tokens,
            partner,
            bias,
            out_parts,
            vectors_one,
            weights,
            carried,
            so_far,
        )

    qkv, context_0, stats, total = attend_shards(0, 1, False, [input_own], [], [])
    input_far, up_others, total, qkv, stats = all_after(
        (input_far, up_others, total, qkv, stats)
    )
    others = [input_near, input_far]
    up_column = jnp.stack([up_others[0], up_ends[1], up_others[1]])
    up_low = move.low(up_column)
    down_far = move.head(after(down_piece, total), 2)
    total, up_column = all_after((total, up_column))
    qkv, context_1, stats, total = attend_shards(1, 2, False, others, [total], [qkv, stats])
    up_low, down_far, total, qkv, stats = all_after((up_low, down_far, total, qkv, stats))
    up_pair = pair_of(up_column, up_low)
    up_high = move.high(up_pair)
    down_ends = pair_of(down_piece, down_far)
    down_others = move.head(down_ends, 1)
    total, up_pair, down_ends = all_after((total, up_pair, down_ends))
    qkv, context, stats, rows_one, normed = attend_shards(
        3, 1, True, others, [total, context_0, context_1], [qkv, stats]
    )
    up_high, down_others, normed, context = all_after((up_high, down_others, normed, context))
    up_near = four_of(up_pair, up_high)
    up_far = move.core(up_near)
    down_column = jnp.stack([down_others[0], down_ends[1], down_others[1]])
    down_low = move.low(down_column)
    up_far, down_low = all_after((up_far, down_low))
    up_all = (up_own, up_near, up_far)
    down_pair = pair_of(down_column, down_low)
    down_high = move.high(down_pair)
    normed, down_pair = all_after((normed, down_pair))
    normed_received = move.core(normed)
    context_received = move.core(context)
    hidden_near, hidden_far, *slopes = feed_up(short_info, normed, up_all, up_bias_parts)
    hidden_received = move.core(hidden_far)
    down_near = four_of(down_pair, after(down_high, hidden_near))
    down_far = move.core(down_near)
    tokens_t, partner_t = turn(after(tokens, down_near), partner)
    down_far, tokens_t, partner_t = all_after((down_far, tokens_t, partner_t))
    down_all = (down_own, down_near, down_far)
    mixed_out, grad_second, grad_branch, sums_two = feed_down(
        short_info, (hidden_near, hidden_far), down_all, rows_one, cotangent, vectors_two
    )

    branch_received = move.core(grad_branch)
    down_mine, down_one, down_two, down_three = row_grads(
        shards,
        hidden_near,
        hidden_received,
        grad_branch,
        branch_received,
        "down_grads",
    )
    down_three = move.low(down_three)
    pre_near, pre_far, up_bias_sums = grad_pre_of(
        short_info, after(grad_branch, down_two), down_all, slopes
    )
    down_three, pre_near, pre_far, up_bias_sums = all_after(
        (down_three, pre_near, pre_far, up_bias_sums)
    )
    pre_received = move.core(pre_far)
    down_two = (down_two + down_three.astype(F32)).astype(BF16)
    down_high = move.high(down_two)
    grad_first, grad_proj, sums_one = up_back(
        short_info, (pre_near, pre_far), up_all, rows_one, after(grad_second, down_two), vectors_back
    )
    pre_received, down_high, grad_proj, grad_first, sums_one = all_after(
        (pre_received, down_high, grad_proj, grad_first, sums_one)
    )
    proj_received = move.core(grad_proj)
    down_one = move.low(after(down_one, down_high))

    def core_sum(mine, received):
        mine, received = (a.reshape(2, 2, *a.shape[1:]) for a in (mine, received))
        keep = [mine[i, 0].astype(F32) + received[i, 0].astype(F32) for i in range(2)]
        return keep, (mine[:, 1].astype(F32) + received[:, 1].astype(F32)).astype(BF16)

    def fold_low(keep, received):
        return keep[0] + received[0].astype(F32), (keep[1] + received[1].astype(F32)).astype(BF16)

    def fold_high(own, received):
        total = own + received.astype(F32)
        return total[0::2], total[1::2].astype(BF16)

    def fold_near(own, received):
        return own[0] + received[0].astype(F32), (own[1] + received[1].astype(F32)).astype(BF16)

    def fold_last(own, received):
        return move.settle(own + received.astype(F32))

    up_mine, up_one, up_two, up_three = row_grads(
        shards, pre_near, pre_received, normed, normed_received, "up_grads"
    )
    proj_received, up_one, up_three = all_after((proj_received, up_one, up_three))
    up_three = move.low(up_three)
    out_keep, out_send = out_grads(
        short_info, after(grad_proj, up_one), proj_received, context, context_received
    )
    down_one, out_keep, out_send = all_after((down_one, out_keep, out_send))
    up_one = move.low(after(up_one, down_one))
    out_low = move.low(out_send)
    down_mine = down_mine + (down_one.astype(F32) + down_high.astype(F32))
    down_mine, down_next = down_mine[0::2], down_mine[1::2].astype(BF16)
    down_near = move.head(down_next, 1)

    def back(grad, first_shard, count, carried, so_far):
        return attend_back(
            (heads, depth, first_shard, count, shards),
            info,
            tokens_t,
            partner_t,
            grad,
            out_parts,
            [] if first_shard else [input_own],
            *others,
            qkv,
            stats,
            carried,
            so_far,
        )

    own_rows, partner_rows, late_near, late_far, late_bias = back(
        after(grad_proj, out_send, down_next), 2, 2, [], []
    )

    (
        down_near,
        up_one,
        up_three,
        out_low,
        own_rows,
        partner_rows,
        late_near,
        late_far,
        late_bias,
    ) = all_after(
        (
            down_near,
            up_one,
            up_three,
            out_low,
            own_rows,
            partner_rows,
            late_near,
            late_far,
            late_bias,
        )
    )
    up_next = (up_two + up_three.astype(F32)).astype(BF16)
    up_mine = up_mine + up_one.astype(F32)
    up_high = move.high(up_next)
    late_core = move.core(late_far)
    down_mine, down_next = fold_near(down_mine, after(down_near, up_next))
    down_last = move.head(down_next, 2)
    out_mine = out_keep[0] + out_low[0].astype(F32)
    out_next = (out_keep[1] + out_low[1].astype(F32)).astype(BF16)
    out_high = move.high(out_next)
    own_rows, partner_rows, *early = back(
        after(grad_proj, down_next, up_next, out_next), 1, 1, [own_rows, partner_rows], [late_bias]
    )

    up_high, down_last, late_core, out_high, own_rows, partner_rows, *early = all_after(
        (up_high, down_last, late_core, out_high, own_rows, partner_rows, *early)
    )
    up_mine, up_next = fold_high(up_mine, up_high)
    up_near = move.head(up_next, 1)
    late_keep, late_next = core_sum(late_near, late_core)
    late_low = move.low(late_next)
    down_total = fold_last(down_mine, down_last)
    down_low = move.low(down_total)
    out_next = (out_mine + out_high.astype(F32)).astype(BF16)
    out_near = move.head(out_next, 1)
    own_rows, partner_first, partner_second, early_near, early_far, early_bias = back(
        after(grad_proj, up_next, down_total, late_next, out_next),
        0,
        1,
        [own_rows, partner_rows],
        early,
    )

    up_near, down_low, late_low, out_near, own_rows, partner_first, partner_second = all_after(
        (up_near, down_low, late_low, out_near, own_rows, partner_first, partner_second), early_bias
    )
    early_near, early_far, early_bias = all_after((early_near, early_far, early_bias), up_near)

    early_core = move.core(early_far)
    up_mine, up_next = fold_near(up_mine, up_near)
    up_last = move.head(up_next, 2)
    late_mine, late_next = fold_low(late_keep, late_low)
    late_high = move.high(late_next)
    out_near = shards_swapped(out_near, shards, 1)
    out_next = (out_next.astype(F32) + out_near.astype(F32)).astype(BF16)
    out_last = move.head(out_next, 2)
    vectors = jnp.concatenate(
        [
            sums_one[:3],
            sums_two[:3],
            up_bias_sums[:, :, 0].reshape(shards, dim),
            jnp.pad(early_bias[:, 0], ((0, 0), (0, dim - 3 * width))),
        ]
    )
    hops = move.hops()

    def hop(value, sent, event):
        value = value + after(sent, event)
        return value, hops.pop(0)(value) if hops else None

    vectors_sent = hops.pop(0)(vectors)
    early_keep, early_next = core_sum(
        early_near, after(early_core, late_next, up_next, vectors, out_next)
    )
    early_low = move.low(early_next)
    vectors, vectors_sent = hop(vectors, vectors_sent, early_next)
    late_mine = late_mine + after(late_high, vectors).astype(F32)
    partner_first = move.head(after(partner_first, late_mine), 1)
    early_mine, early_next = fold_low(early_keep, after(early_low, late_mine))
    early_high = move.high(early_next)
    vectors, vectors_sent = hop(vectors, vectors_sent, early_next)
    up_total = fold_last(up_mine, after(up_last, vectors))
    out_last = shards_swapped(after(out_last, up_total), shards, 2)
    out_total = move.settle(out_next.astype(F32) + out_last.astype(F32))
    up_total = jnp.concatenate([up_total, out_total], axis=1)
    up_low = move.low(up_total)
    early_mine = early_mine + after(early_high, up_total).astype(F32)
    input_next = jnp.stack([early_mine[1], late_mine[1]]).astype(BF16)
    input_near = move.head(input_next, 1)
    vectors, vectors_sent = hop(vectors, vectors_sent, input_next)
    partner_second = move.head(after(partner_second, input_next), 1)
    up_pair = pair_of(up_total, after(up_low, vectors))
    up_high = move.high(up_pair)
    down_pair = pair_of(down_total, after(down_low, up_pair))
    down_high = move.high(down_pair)
    input_mine, input_next = fold_near(
        jnp.stack([early_mine[0], late_mine[0]]), after(input_near, up_pair)
    )
    input_last = move.head(input_next, 2)
    input_last, vectors_sent, partner_first = all_after(
        (input_last, vectors_sent, partner_first), down_pair
    )
    input_total = fold_last(input_mine, input_last)
    input_low = move.low(input_total)
    vectors, vectors_sent = hop(vectors, vectors_sent, input_total)
    up_near = four_of(up_pair, after(up_high, input_total))
    up_far = move.core(up_near)
    down_near = four_of(down_pair, after(down_high, up_near))
    down_far = move.core(down_near)
    from_partner = jnp.concatenate([partner_first, after(partner_second, down_near)])
    grad_tokens = grad_first + own_rows + from_partner.astype(F32)
    input_low, vectors_sent = all_after((input_low, vectors_sent), grad_tokens)
    input_pair = pair_of(input_total, input_low)
    input_high = move.high(input_pair)
    while vectors_sent is not None:
        vectors, vectors_sent = hop(vectors, vectors_sent, input_pair)
    grad_down = pl.pallas_call(
        settle_down_kernel,
        in_specs=[SMEM] + [whole(4, piece, dim)] * 2,
        out_shape=shape((PARTS, piece, dim), F32),
        compiler_params=PARAMS,
        name="settle_down",
    )(short_info, after(down_near, input_pair), down_far)
    input_near = four_of(input_pair, after(input_high, grad_down, vectors))
    input_far = move.core(input_near)
    grad_up, grad_out = pl.pallas_call(
        settle_up_kernel,
        in_specs=[SMEM] + [whole(4, piece, dim + shards * width)] * 2,
        out_shape=[shape((dim, hidden_own), F32), shape((shards, width, dim), F32)],
        scratch_shapes=[pltpu.VMEM((PARTS, piece, dim), F32)] * 2,
        compiler_params=PARAMS,
        name="settle_up",
    )(short_info, after(up_near, input_near), up_far)
    grad_input_bias = lax.dynamic_index_in_dim(vectors[10:], head_at, 0, keepdims=False)
    grad_input_bias = jnp.stack(
        [grad_input_bias[2 * width : 3 * width], grad_input_bias[width : 2 * width]]
    )
    grad_up_bias = lax.dynamic_index_in_dim(vectors[6:10], head_at, 0, keepdims=False)
    grad_input_weight = pl.pallas_call(
        settle_input_kernel,
        in_specs=[SMEM] + [whole(4, piece, 3 * width)] * 2,
        out_shape=shape((3, width, dim), F32),
        scratch_shapes=[pltpu.VMEM((PARTS, piece, 3 * width), F32)],
        compiler_params=PARAMS,
        name="settle_input",
    )(short_info, after(input_near, grad_up), input_far)
    return (
        mixed_out,
        grad_tokens,
        grad_input_weight.transpose(0, 2, 1),
        grad_input_bias,
        grad_out.reshape(dim, dim),
        vectors[0],
        vectors[1],
        vectors[2],
        grad_up,
        grad_up_bias,
        grad_down.reshape(hidden_own, dim),
        vectors[3],
        vectors[4],
        vectors[5],
    )


def solution(mesh):
    rows_spec = P(("batch", "head"), None)
    placed = (
        rows_spec,
        P("batch"),
        P("head"),
        P(None, None, "head"),
        P(None, "head"),
        P(),
        P(),
        P(),
        P(),
        P(None, "head"),
        P(),
        P("head", None),
        P(),
        P(),
        P(),
        rows_spec,
    )
    return jax.shard_map(
        functools.partial(local, mesh.shape["batch"], mesh.shape["head"]),
        mesh=mesh,
        in_specs=placed,
        out_specs=(
            rows_spec,
            rows_spec,
            P(None, None, "head"),
            P(None, "head"),
            P(),
            P(),
            P(),
            P(),
            P(None, "head"),
            P("head"),
            P("head", None),
            P(),
            P(),
            P(),
        ),
        check_vma=False,
    )
```

```python
import functools

import jax
import jax.numpy as jnp
from jax import lax
from jax.experimental import pallas as pl
from jax.experimental.pallas import tpu as pltpu
from jax.sharding import PartitionSpec as P

SEQ_LEN = 1024
EPSILON = 1e-05
F32 = jnp.float32
BF16 = jnp.bfloat16
VMEM_LIMIT = 18 * 1024 * 1024
PARAMS = pltpu.CompilerParams(vmem_limit_bytes=VMEM_LIMIT)
CORE = 1
PARTS = 8
SPOTS = 4


def dot(left_side, right_side, left_dim=1, right_dim=0):
    return lax.dot_general(
        left_side,
        right_side,
        (((left_dim,), (right_dim,)), ((), ())),
        preferred_element_type=F32,
    )


def unit_parts(values):
    centred = values - jnp.mean(values, axis=-1, keepdims=True)
    inverse = lax.rsqrt(jnp.mean(centred * centred, axis=-1, keepdims=True) + EPSILON)
    return centred * inverse, inverse


def norm_back(grad_rows, unit_rows, inverse, gain_row):
    scaled = grad_rows * gain_row
    return inverse * (
        scaled
        - jnp.mean(scaled, axis=-1, keepdims=True)
        - unit_rows * jnp.mean(scaled * unit_rows, axis=-1, keepdims=True)
    )


def column_sum(values):
    return jnp.sum(values, axis=0, keepdims=True)


def gelu_parts(inner):
    below = 0.5 + 0.5 * lax.erf(inner * 0.7071067811865476)
    bell = jnp.exp(inner * inner * -0.5) * 0.3989422804014327
    return inner * below, below + inner * bell


def row_chunks(rows, step):
    return [slice(i, i + step) for i in range(0, rows, step)]


def eight_sum(values):
    return sum(values[cut] for cut in row_chunks(values.shape[0], 8))


def lane_pick(values, depth):
    lane = lax.broadcasted_iota(jnp.int32, (1, len(values) * depth), 1)
    picked = jnp.full(lane.shape, values[0], jnp.int32)
    for j in range(1, len(values)):
        picked = jnp.where(lane >= j * depth, values[j], picked)
    return picked


def place_of(part, half, spot):
    seen = part ^ half
    core = seen & 1
    low, high = 2 + 2 * core, 4 - 2 * core
    return seen ^ (low * (spot & 1) + high * (spot >> 1))


class Info:
    def __init__(self, ref, heads, shards):
        self.ref, self.heads, self.base = ref, heads, heads * shards

    def swaps(self, shard):
        return [self.ref[shard * self.heads + j] for j in range(self.heads)]

    own_live = property(lambda self: self.ref[self.base])
    partner_live = property(lambda self: self.ref[self.base + 1])
    part = property(lambda self: self.ref[self.base + 2])
    head_at = property(lambda self: self.ref[self.base + 3])


def gathered(part, near, far, scratch):
    for spot in range(SPOTS):
        scratch[place_of(part, 0, spot)] = near[spot, 0]
        scratch[place_of(part, 1, spot)] = far[spot, 0]
    return scratch[...].reshape(-1, scratch.shape[2])


def attend_kernel(setting, info_ref, tokens, partner, bias, out_weight, vectors, *refs):
    heads, depth, first_shard, last = setting
    refs = list(refs)
    if first_shard == 0:
        turned = refs.pop(0)
        total_in = None
    else:
        near, far, total_in = refs[:3]
        del refs[:3]
    earlier = []
    if last:
        earlier = refs[:2]
        del refs[:2]
    if first_shard:
        del refs[:2]
    qkv_out, context_out, stats_out = refs[:3]
    step = pl.program_id(0)
    shard = first_shard + step
    info = Info(info_ref, heads, out_weight.shape[0])
    if first_shard:
        weight = gathered(info.part, near, far, refs.pop())
    total = refs.pop()
    swaps = info.swaps(shard)
    rows, dim = tokens.shape
    width = heads * depth
    x, xp = tokens[...], partner[...]
    if first_shard:
        own = dot(x, weight)
        other = dot(xp, weight[:, : 2 * width])
    else:
        kv_rows = jnp.concatenate([turned[1], turned[2]], axis=0)
        own = jnp.concatenate([dot(x, kv_rows, 1, 1), dot(x, turned[0], 1, 1)], axis=1)
        other = dot(xp, kv_rows, 1, 1)
    swapped = lane_pick(swaps + swaps, depth) == 1
    bias_row = bias[0, 0:1]
    kv, q = [], []
    for cut in row_chunks(rows, 32):
        mine = own[cut] + bias_row
        theirs = other[cut] + bias_row[:, : 2 * width]
        kv.append(jnp.where(swapped, theirs, mine[:, : 2 * width]).astype(BF16))
        q.append(mine[:, 2 * width :].astype(BF16) * (depth**-0.5))
    kv, q = jnp.concatenate(kv, axis=0), jnp.concatenate(q, axis=0)
    qkv_out[0, :, : 2 * width] = kv
    qkv_out[0, :, 2 * width :] = q
    stats = []
    pieces = []
    for j in range(heads):
        head = slice(j * depth, (j + 1) * depth)
        live = jnp.where(swaps[j] == 1, info.partner_live, info.own_live)
        anyone = jnp.where(live > 0, 1.0, 0.0).astype(F32)
        scores = dot(kv[:, head], q[:, head], 1, 1)
        masked, most = [], None
        for cut in row_chunks(rows, 32):
            index = cut.start + lax.broadcasted_iota(jnp.int32, (32, 1), 0)
            part = jnp.where(index < live, scores[cut], -1e30)
            masked.append(part)
            for tile in row_chunks(32, 8):
                most = part[tile] if most is None else jnp.maximum(most, part[tile])
        largest = jnp.max(most, axis=0, keepdims=True)
        largest = jnp.where(anyone > 0.5, largest, 0.0)
        total_rows = None
        for part in masked:
            weights = eight_sum(jnp.exp(part - largest))
            total_rows = weights if total_rows is None else total_rows + weights
        stat = largest + jnp.log(column_sum(total_rows) + (1.0 - anyone))
        mixing = [jnp.exp(part - stat).astype(BF16) for part in masked]
        stats.append(stat)
        values = kv[:, width + j * depth : width + (j + 1) * depth]
        pieces.append(dot(values, jnp.concatenate(mixing, axis=0), 0, 0))
    context = jnp.concatenate(pieces, axis=0).T.astype(BF16)
    stats_out[0] = jnp.concatenate(stats + [jnp.zeros((8 - heads, rows), F32)], axis=0)
    projected = dot(context, out_weight[info.head_at ^ shard])
    if not last:
        context_out[0] = context

        @pl.when(step == 0)
        def first():
            total[...] = projected if total_in is None else total_in[...] + projected

        @pl.when(step > 0)
        def later():
            total[...] += projected

        return

    context_out[...] = jnp.concatenate(
        [ref[q] for ref in earlier for q in range(ref.shape[0])] + [context], axis=1
    )
    rows_out, normed_out = refs[3:]
    for cut in row_chunks(rows, 16):
        values = x[cut].astype(F32) + ((total_in[cut] + projected[cut]) + vectors[0:1])
        rows_out[cut] = values
        unit, _ = unit_parts(values)
        normed_out[cut] = (unit * vectors[1:2] + vectors[2:3]).astype(BF16)


def tiles_of(part, own, near, far, run):
    @pl.when(pl.program_id(0) == 0)
    def mine():
        run(
            *(
                jnp.concatenate([own[place_of(part, half, spot)] for spot in range(SPOTS)], axis=0)
                for half in range(2)
            )
        )

    @pl.when(pl.program_id(0) > 0)
    def other():
        run(*(ref[:, 0].reshape(-1, ref.shape[3]) for ref in (near, far)))


def add_up(total, *partials):
    @pl.when(pl.program_id(0) == 0)
    def start():
        total[...] = sum(partials[1:], partials[0])

    @pl.when(pl.program_id(0) > 0)
    def later():
        total[...] = sum(partials, total[...])


def at_end(run):
    pl.when(pl.program_id(0) == pl.num_programs(0) - 1)(run)


def eight_rows(*rows):
    width = rows[0].shape[1]
    return jnp.concatenate([*rows, jnp.zeros((8 - len(rows), width), F32)], axis=0)


def feed_up_kernel(info, normed, own, near, far, bias, *outs):
    shard = info[2] ^ pl.program_id(0)

    def run(*tiles):
        for half, tile in enumerate(tiles):
            places = [place_of(info[1], half, spot) for spot in range(SPOTS)]
            bias_row = jnp.concatenate([bias[shard, place] for place in places], axis=1)
            pre = dot(normed[...], tile, 1, 1)
            for cut in row_chunks(pre.shape[0], 32):
                hidden, slope = gelu_parts(pre[cut] + bias_row)
                outs[half][cut] = hidden.astype(BF16)
                outs[half + 2][cut] = slope

    tiles_of(info[1], own, near, far, run)


def feed_down_kernel(
    info,
    near_hidden,
    far_hidden,
    own,
    near,
    far,
    rows_in,
    cotangent,
    vectors,
    mixed_out,
    second_out,
    grad_out,
    sums_out,
    total,
):
    def run(near_tile, far_tile):
        add_up(total, dot(near_hidden[...], near_tile), dot(far_hidden[...], far_tile))

    tiles_of(info[1], own, near, far, run)

    @at_end
    def finish():
        sums = [jnp.zeros((8, rows_in.shape[1]), F32)] * 3
        for cut in row_chunks(rows_in.shape[0], 16):
            unit_one, _ = unit_parts(rows_in[cut])
            first_norm = unit_one * vectors[0:1] + vectors[1:2]
            unit, inverse = unit_parts(first_norm + (total[cut] + vectors[2:3]))
            index = cut.start + lax.broadcasted_iota(jnp.int32, (16, 1), 0)
            mask = jnp.where(index < info[0], 1.0, 0.0).astype(F32)
            mixed_out[cut] = ((unit * vectors[3:4] + vectors[4:5]) * mask).astype(BF16)
            incoming = cotangent[cut].astype(F32) * mask
            grad = norm_back(incoming, unit, inverse, vectors[3:4])
            second_out[cut] = grad
            low = grad.astype(BF16)
            grad_out[cut] = low
            more = (low.astype(F32), incoming * unit, incoming)
            sums = [a + eight_sum(b) for a, b in zip(sums, more)]
        sums_out[...] = eight_rows(*(column_sum(a) for a in sums))


def grad_pre_kernel(
    info, grad_branch, own, near, far, near_slope, far_slope, near_out, far_out, bias_out
):
    def run(*tiles):
        for half, tile in enumerate(tiles):
            out, slope = (near_out, far_out)[half], (near_slope, far_slope)[half]
            grad = dot(grad_branch[...], tile, 1, 1)
            sums = jnp.zeros((8, grad.shape[1]), F32)
            for cut in row_chunks(grad.shape[0], 32):
                low = (grad[cut] * slope[cut]).astype(BF16)
                out[cut] = low
                sums = sums + eight_sum(low.astype(F32))
            sums = jnp.broadcast_to(column_sum(sums), sums.shape)
            width = bias_out.shape[3]
            for spot in range(SPOTS):
                row = sums[:, spot * width : (spot + 1) * width]
                bias_out[info[2] ^ pl.program_id(0), place_of(info[1], half, spot)] = row

    tiles_of(info[1], own, near, far, run)


def up_back_kernel(
    info,
    near_pre,
    far_pre,
    own,
    near,
    far,
    rows_in,
    second_in,
    vectors,
    first_out,
    proj_out,
    sums_out,
    total,
):
    def run(near_tile, far_tile):
        add_up(total, dot(near_pre[...], near_tile), dot(far_pre[...], far_tile))

    tiles_of(info[1], own, near, far, run)

    @at_end
    def finish():
        sums = [jnp.zeros((8, rows_in.shape[1]), F32)] * 3
        for cut in row_chunks(rows_in.shape[0], 16):
            unit, inverse = unit_parts(rows_in[cut])
            grad_normed = second_in[cut] + total[cut]
            grad = norm_back(grad_normed, unit, inverse, vectors[0:1])
            first_out[cut] = grad
            low = grad.astype(BF16)
            proj_out[cut] = low
            more = (low.astype(F32), grad_normed * unit, grad_normed)
            sums = [a + eight_sum(b) for a, b in zip(sums, more)]
        sums_out[...] = eight_rows(*(column_sum(a) for a in sums))


def turn_kernel(tokens, partner, tokens_out, partner_out):
    tokens_out[...] = tokens[...].T
    partner_out[...] = partner[...].T


def row_grads_kernel(mine, theirs, my_rows, their_rows, *outs):
    value = dot(mine[...], my_rows[...], 0, 0) + dot(theirs[...], their_rows[...], 0, 0)
    value = value.reshape(SPOTS, -1, value.shape[1])
    for spot, out in enumerate(outs):
        out[0] = value[spot].astype(out.dtype)


def out_grads_kernel(info, mine, theirs, my_context, their_context, keep_out, send_out, turned):
    value = 0.0
    for i, (grad, context) in enumerate(((mine, my_context), (theirs, their_context))):
        turned[i] = grad[...].T.reshape(turned.shape[1:])
        rows = [turned[i, place_of(info[1], 0, spot)] for spot in range(SPOTS)]
        value = value + dot(jnp.concatenate(rows, axis=0), context[...])
    value = value.reshape(SPOTS, -1, value.shape[1])
    for spot in range(SPOTS):
        out = (keep_out, send_out)[spot & 1]
        out[spot >> 1] = value[spot].astype(out.dtype)


def scatter_parts(part, value, chunks, near_out, far_out):
    chunks[...] = value.reshape(chunks.shape)
    for spot in range(SPOTS):
        near_out[spot, 0] = chunks[place_of(part, 0, spot)]
        far_out[spot, 0] = chunks[place_of(part, 1, spot)]


def attend_back_kernel(setting, info_ref, tokens_t, partner_t, grad_proj, out_weight, *refs):
    heads, depth, first_shard, carried, so_far, shards = setting
    refs = list(refs)
    if first_shard == 0:
        turned = refs.pop(0)
    near, far, qkv_in, stats_in = refs[:4]
    del refs[:4]
    if carried:
        own_in, partner_in = refs[:2]
        del refs[:2]
    del refs[:so_far]
    own_out, *partner_outs, near_out, far_out, bias_out, total, weight_scratch, chunks = refs
    step = pl.program_id(0)
    shard = first_shard + step
    info = Info(info_ref, heads, shards)
    if first_shard:
        gathered(info.part, near, far, weight_scratch)
    else:
        width = turned.shape[1]

        @pl.when(shard == 0)
        def own_weight():
            rows_kv = jnp.concatenate([turned[1], turned[2], turned[0]], axis=0)
            weight_scratch[...] = rows_kv.T.reshape(weight_scratch.shape)

        @pl.when(shard > 0)
        def other_weight():
            gathered(info.part, near, far, weight_scratch)

    weight = weight_scratch[...].reshape(-1, weight_scratch.shape[2])
    swaps = info.swaps(shard)
    dim, rows = tokens_t.shape
    width = heads * depth
    grad = dot(grad_proj[...], out_weight[0], 1, 1).astype(BF16)
    k, v, q = (qkv_in[0, :, i * width : (i + 1) * width] for i in range(3))
    stats = stats_in[0]
    gq, gk, gv = [], [], []
    for j in range(heads):
        head = slice(j * depth, (j + 1) * depth)
        stat = stats[j : j + 1, :]
        live = jnp.where(swaps[j] == 1, info.partner_live, info.own_live)
        scores = dot(k[:, head], q[:, head], 1, 1)
        grad_mix = dot(v[:, head], grad[:, head], 1, 1)
        chances, shared = [], jnp.zeros((8, rows), F32)
        for cut in row_chunks(rows, 32):
            index = cut.start + lax.broadcasted_iota(jnp.int32, (32, 1), 0)
            part = jnp.exp(jnp.where(index < live, scores[cut] - stat, -10000.0))
            chances.append(part)
            shared = shared + eight_sum(part * grad_mix[cut])
        shared = column_sum(shared)
        mixing = jnp.concatenate([part.astype(BF16) for part in chances], axis=0)
        grad_scores = jnp.concatenate(
            [
                (part * (grad_mix[cut] - shared)).astype(BF16)
                for part, cut in zip(chances, row_chunks(rows, 32))
            ],
            axis=0,
        )
        gk.append(dot(grad_scores, q[:, head]))
        gv.append(dot(mixing, grad[:, head]))
        gq.append(dot(k[:, head], grad_scores, 0, 0))
    grad_q = (jnp.concatenate(gq, axis=0).T * (depth**-0.5)).astype(BF16)
    grad_kv = jnp.concatenate(gk + gv, axis=1).astype(BF16)
    swapped = lane_pick(swaps + swaps, depth) == 1
    nothing = jnp.zeros((), BF16)
    grad_own = jnp.concatenate([jnp.where(swapped, nothing, grad_kv), grad_q], axis=1)
    grad_far = jnp.where(swapped, grad_kv, nothing)
    own = dot(grad_own, weight, 1, 1)
    other = dot(grad_far, weight[:, : 2 * width], 1, 1)

    @pl.when(step == 0)
    def first():
        own_out[...] = own_in[...] + own if carried else own
        total[...] = partner_in[...] + other if carried else other

    @pl.when(step > 0)
    def later():
        own_out[...] += own
        total[...] += other

    @at_end
    def finish():
        first = 0
        for out in partner_outs:
            out[...] = total[first : first + out.shape[0]].astype(out.dtype)
            first += out.shape[0]

    grads = dot(tokens_t[...], grad_own)
    grads_kv = grads[:, : 2 * width] + dot(partner_t[...], grad_far)
    grads = jnp.concatenate([grads_kv, grads[:, 2 * width :]], axis=1).astype(BF16)
    chunks[...] = grads.reshape(chunks.shape)
    for spot in range(SPOTS):
        near_out[spot, 0] = chunks[place_of(info.part, 0, spot)]
        far_out[spot, 0] = chunks[place_of(info.part, 1, spot)]
    bias_out[0] = jnp.broadcast_to(
        jnp.concatenate(
            [column_sum(grad_kv.astype(F32)), column_sum(grad_q.astype(F32))], axis=1
        ),
        bias_out.shape[1:],
    )


def settle_down_kernel(info, near, far, out):
    for half, source in enumerate((near, far)):
        for spot in range(SPOTS):
            out[place_of(info[1], half, spot)] = source[spot].astype(F32)


def settle_up_kernel(info, near, far, up_out, out_out, up_scratch, out_scratch):
    dim = up_out.shape[0]
    for half, source in enumerate((near, far)):
        for spot in range(SPOTS):
            place = place_of(info[1], half, spot)
            value = source[spot].astype(F32)
            up_scratch[place] = value[:, :dim]
            out_scratch[place] = value[:, dim:]
    up_out[...] = up_scratch[...].reshape(-1, dim).T
    shards = out_out.shape[0]
    turned = out_scratch[...].reshape(-1, dim).T.reshape(shards, -1, dim)
    for q in range(shards):
        out_out[info[2] ^ q] = turned[q]


def settle_input_kernel(info, near, far, out, scratch):
    width = out.shape[1]
    for half, source in enumerate((near, far)):
        for spot in range(SPOTS):
            scratch[place_of(info[1], half, spot)] = source[spot].astype(F32)
    turned = scratch[...].reshape(-1, scratch.shape[2]).T
    for i in range(3):
        out[(i + 1) % 3] = turned[i * width : (i + 1) * width]


def shape(dims, dtype):
    return jax.ShapeDtypeStruct(dims, dtype)


def whole(*dims):
    return pl.BlockSpec(dims, lambda *_: (0,) * len(dims))


def cost(flops, moved, slow=0):
    return pl.CostEstimate(flops=flops, bytes_accessed=moved, transcendentals=slow)


SMEM = pl.BlockSpec(memory_space=pltpu.SMEM)


def gathered_specs(near, first_shard):
    spots, _, piece, lanes = near.shape
    return [pl.BlockSpec((spots, 1, piece, lanes), lambda s: (0, s + first_shard - 1, 0, 0))] * 2


def attend(
    setting, count, info, tokens, partner, bias, out_weight, vectors, weights, carried, so_far
):
    heads, depth, first_shard, last = setting
    rows, dim = tokens.shape
    shards, width, _ = out_weight.shape
    lanes = 3 * width
    scratch = []
    if first_shard == 0:
        weight_specs = [whole(3, width, dim)]
    else:
        weight_specs = gathered_specs(weights[0], first_shard)
        scratch = [pltpu.VMEM((PARTS, dim // PARTS, lanes), BF16)]
    out_specs = [
        pl.BlockSpec((1, rows, lanes), lambda s: (s + first_shard, 0, 0)),
        whole(rows, dim) if last else pl.BlockSpec((1, rows, width), lambda s: (s, 0, 0)),
        pl.BlockSpec((1, 8, rows), lambda s: (s + first_shard, 0, 0)),
    ]
    out_shape = [
        shape((shards, rows, lanes), BF16),
        shape((rows, dim) if last else (count, rows, width), BF16),
        shape((shards, 8, rows), F32),
    ]
    fixed = 6 + len(weights) + len(carried)
    if last:
        out_specs += [whole(rows, dim)] * 2
        out_shape += [shape((rows, dim), F32), shape((rows, dim), BF16)]
        scratch = [pltpu.VMEM((8, 128), F32)] + scratch
    else:
        out_specs.append(whole(rows, dim))
        out_shape.append(shape((rows, dim), F32))
    return pl.pallas_call(
        functools.partial(attend_kernel, setting),
        grid=(count,),
        in_specs=[
            SMEM,
            whole(rows, dim),
            whole(rows, dim),
            pl.BlockSpec((1, 8, lanes), lambda s: (s + first_shard, 0, 0)),
            whole(shards, width, dim),
            whole(8, dim),
        ]
        + weight_specs
        + [whole(*value.shape) for value in carried]
        + [pl.BlockSpec(memory_space=pl.ANY)] * len(so_far),
        out_specs=out_specs,
        out_shape=out_shape,
        scratch_shapes=scratch,
        input_output_aliases={fixed + i: (0, 2)[i] for i in range(len(so_far))},
        compiler_params=PARAMS,
        cost_estimate=cost(
            count * (3 * rows * dim * dim + 4 * rows * rows * dim),
            count * 6 * rows * dim,
            count * heads * rows * rows,
        ),
        name="attend",
    )(info, tokens, partner, bias, out_weight, vectors, *weights, *carried, *so_far)


def feed_specs(near):
    spots, _, piece, lanes = near.shape
    other = pl.BlockSpec(
        (spots, 1, piece, lanes), lambda q: (0, jnp.maximum(q - 1, 0), 0, 0)
    )
    return [whole(PARTS, piece, lanes), other, other]


def feed_up(info, normed, weight, bias):
    rows, dim = normed.shape
    near = weight[1]
    shards = near.shape[1] + 1
    tile = SPOTS * near.shape[2]
    columns = pl.BlockSpec((rows, tile), lambda q: (0, q))
    return pl.pallas_call(
        feed_up_kernel,
        grid=(shards,),
        in_specs=[
            SMEM,
            whole(rows, dim),
            *feed_specs(near),
            whole(*bias.shape),
        ],
        out_specs=[columns] * 4,
        out_shape=[shape((rows, shards * tile), BF16)] * 2
        + [shape((rows, shards * tile), F32)] * 2,
        compiler_params=PARAMS,
        cost_estimate=cost(4 * rows * dim * tile * shards, 30 * rows * dim, rows * dim * 8),
        name="feed_up",
    )(info, normed, *weight, bias)


def feed_down(info, hidden, weight, rows_one, cotangent, vectors):
    rows, dim = rows_one.shape
    near = weight[1]
    shards = near.shape[1] + 1
    tile = SPOTS * near.shape[2]
    columns = pl.BlockSpec((rows, tile), lambda q: (0, q))
    return pl.pallas_call(
        feed_down_kernel,
        grid=(shards,),
        in_specs=[
            SMEM,
            columns,
            columns,
            *feed_specs(near),
            whole(rows, dim),
            whole(rows, dim),
            whole(8, dim),
        ],
        out_specs=[whole(rows, dim)] * 3 + [whole(8, dim)],
        out_shape=[
            shape((rows, dim), BF16),
            shape((rows, dim), F32),
            shape((rows, dim), BF16),
            shape((8, dim), F32),
        ],
        scratch_shapes=[pltpu.VMEM((rows, dim), F32)],
        compiler_params=PARAMS,
        cost_estimate=cost(4 * rows * dim * tile * shards, 20 * rows * dim),
        name="feed_down",
    )(info, *hidden, *weight, rows_one, cotangent, vectors)


def grad_pre_of(info, grad_branch, weight, slopes):
    rows, dim = grad_branch.shape
    near = weight[1]
    shards = near.shape[1] + 1
    tile = SPOTS * near.shape[2]
    columns = pl.BlockSpec((rows, tile), lambda q: (0, q))
    return pl.pallas_call(
        grad_pre_kernel,
        grid=(shards,),
        in_specs=[SMEM, whole(rows, dim), *feed_specs(near), columns, columns],
        out_specs=[columns, columns, whole(shards, PARTS, 8, near.shape[2])],
        out_shape=[
            shape((rows, shards * tile), BF16),
            shape((rows, shards * tile), BF16),
            shape((shards, PARTS, 8, near.shape[2]), F32),
        ],
        compiler_params=PARAMS,
        cost_estimate=cost(4 * rows * dim * tile * shards, 30 * rows * dim),
        name="grad_pre",
    )(info, grad_branch, *weight, *slopes)


def up_back(info, pres, weight, rows_one, grad_second, vectors):
    rows, dim = rows_one.shape
    near = weight[1]
    shards = near.shape[1] + 1
    tile = SPOTS * near.shape[2]
    columns = pl.BlockSpec((rows, tile), lambda q: (0, q))
    return pl.pallas_call(
        up_back_kernel,
        grid=(shards,),
        in_specs=[
            SMEM,
            columns,
            columns,
            *feed_specs(near),
            whole(rows, dim),
            whole(rows, dim),
            whole(8, dim),
        ],
        out_specs=[whole(rows, dim), whole(rows, dim), whole(8, dim)],
        out_shape=[shape((rows, dim), F32), shape((rows, dim), BF16), shape((8, dim), F32)],
        scratch_shapes=[pltpu.VMEM((rows, dim), F32)],
        compiler_params=PARAMS,
        cost_estimate=cost(4 * rows * dim * tile * shards, 24 * rows * dim),
        name="up_back",
    )(info, *pres, *weight, rows_one, grad_second, vectors)


def turn(tokens, partner):
    rows, dim = tokens.shape
    return pl.pallas_call(
        turn_kernel,
        out_shape=[shape((dim, rows), BF16)] * 2,
        compiler_params=PARAMS,
        cost_estimate=cost(rows * dim, 8 * rows * dim),
        name="turn",
    )(tokens, partner)


def row_grads(shards, mine, theirs, my_rows, their_rows, name):
    rows, dim = my_rows.shape
    tile = mine.shape[1] // shards
    piece = tile // SPOTS
    columns = pl.BlockSpec((rows, tile), lambda q: (0, q))
    out = pl.BlockSpec((1, piece, dim), lambda q: (q, 0, 0))
    return pl.pallas_call(
        row_grads_kernel,
        grid=(shards,),
        in_specs=[columns, columns, whole(rows, dim), whole(rows, dim)],
        out_specs=[out] * SPOTS,
        out_shape=[shape((shards, piece, dim), (F32, BF16)[spot & 1]) for spot in range(SPOTS)],
        compiler_params=PARAMS,
        cost_estimate=cost(4 * rows * dim * tile * shards, 20 * rows * dim),
        name=name,
    )(mine, theirs, my_rows, their_rows)


def out_grads(info, mine, theirs, my_context, their_context):
    rows, dim = mine.shape
    piece = dim // PARTS
    return pl.pallas_call(
        out_grads_kernel,
        in_specs=[SMEM] + [whole(rows, dim)] * 4,
        out_specs=[whole(2, piece, dim)] * 2,
        out_shape=[shape((2, piece, dim), F32), shape((2, piece, dim), BF16)],
        scratch_shapes=[pltpu.VMEM((2, PARTS, piece, rows), BF16)],
        compiler_params=PARAMS,
        cost_estimate=cost(2 * rows * dim * dim, 10 * rows * dim),
        name="out_grads",
    )(info, mine, theirs, my_context, their_context)


def attend_back(
    setting,
    info,
    tokens_t,
    partner_t,
    grad_proj,
    out_weight,
    own,
    near,
    far,
    qkvs,
    stats,
    carried,
    so_far,
):
    heads, depth, first_shard, count, shards = setting
    half = shards // 2
    slot = first_shard % half
    fixed = 9 + len(own) + len(carried)
    splits = 1 if first_shard else 2
    dim, rows = tokens_t.shape
    width = heads * depth
    lanes = 3 * width
    piece = dim // PARTS
    head_spot = heads * shards + 3
    own_specs = [] if first_shard else [whole(3, width, dim)]
    kernel = functools.partial(
        attend_back_kernel, (heads, depth, first_shard, bool(carried), len(so_far), shards)
    )

    def other(s, info):
        return (0, jnp.maximum(s + first_shard - 1, 0), 0, 0)

    parts_out = pl.BlockSpec((SPOTS, 1, piece, lanes), lambda s, info: (0, s + slot, 0, 0))
    return pl.pallas_call(
        kernel,
        grid_spec=pltpu.PrefetchScalarGridSpec(
            num_scalar_prefetch=1,
            grid=(count,),
            in_specs=[
                whole(dim, rows),
                whole(dim, rows),
                whole(rows, dim),
                pl.BlockSpec(
                    (1, width, dim), lambda s, info: (info[head_spot] ^ (s + first_shard), 0, 0)
                ),
            ]
            + own_specs
            + [pl.BlockSpec((SPOTS, 1, piece, lanes), other)] * 2
            + [
                pl.BlockSpec((1, rows, lanes), lambda s, info: (s + first_shard, 0, 0)),
                pl.BlockSpec((1, 8, rows), lambda s, info: (s + first_shard, 0, 0)),
            ]
            + [whole(rows, dim)] * len(carried)
            + [pl.BlockSpec(memory_space=pl.ANY)] * len(so_far),
            out_specs=[
                whole(rows, dim),
                *[whole(rows // splits, dim)] * splits,
                parts_out,
                parts_out,
                pl.BlockSpec(
                    (1, 8, lanes), lambda s, info: (info[head_spot] ^ (s + first_shard), 0, 0)
                ),
            ],
            scratch_shapes=[
                pltpu.VMEM((rows, dim), F32),
                pltpu.VMEM((PARTS, piece, lanes), BF16),
                pltpu.VMEM((PARTS, piece, lanes), BF16),
            ],
        ),
        out_shape=[
            shape((rows, dim), F32),
            *[shape((rows // splits, dim), F32 if first_shard else BF16)] * splits,
            shape((SPOTS, half, piece, lanes), BF16),
            shape((SPOTS, half, piece, lanes), BF16),
            shape((shards, 8, lanes), F32),
        ],
        input_output_aliases={
            fixed + i: 4 + splits - len(so_far) + i for i in range(len(so_far))
        },
        compiler_params=PARAMS,
        cost_estimate=cost(
            count * (6 * rows * dim * dim + 10 * rows * rows * dim),
            count * 8 * rows * dim,
            count * heads * rows * rows,
        ),
        name="attend_back",
    )(
        info,
        tokens_t,
        partner_t,
        grad_proj,
        out_weight,
        *own,
        near,
        far,
        qkvs,
        stats,
        *carried,
        *so_far,
    )


class Mover:
    def __init__(self, batch_size, shards):
        self.batch_size, self.shards = batch_size, shards

    def batch(self, value, mask_of):
        perm = [(i, i ^ mask_of(i)) for i in range(self.batch_size)]
        return lax.ppermute(value, "batch", perm)

    def core(self, value):
        return self.batch(value, lambda i: CORE)

    def low(self, value):
        return self.batch(value, lambda i: 4 if i & 1 else 2)

    def high(self, value):
        return self.batch(value, lambda i: 2 if i & 1 else 4)

    def head(self, value, mask):
        return lax.ppermute(value, "head", [(i, i ^ mask) for i in range(self.shards)])

    def along(self, values, first=1):
        return [self.head(value, q) for q, value in enumerate(values, first)]

    def column(self, piece):
        return self.along([piece] * (self.shards - 1))

    def settle(self, total):
        total = total.astype(BF16)
        mask = PARTS
        while mask < self.batch_size:
            other = self.batch(total, lambda i, mask=mask: mask)
            total = (total.astype(F32) + other.astype(F32)).astype(BF16)
            mask *= 2
        return total

    def hops(self):
        steps, mask = [self.core, self.low, self.high], 1
        while mask < self.shards:
            steps.append(lambda value, mask=mask: self.head(value, mask))
            mask *= 2
        mask = PARTS
        while mask < self.batch_size:
            steps.append(lambda value, mask=mask: self.batch(value, lambda i: mask))
            mask *= 2
        return steps


def after(value, *events):
    return lax.optimization_barrier((value, *events))[0]


def all_after(values, *events):
    return lax.optimization_barrier((*values, *events))[: len(values)]


def pair_of(first, second):
    return jnp.stack([first, second])


def four_of(pair, received):
    return jnp.concatenate([pair, received])


def shards_swapped(value, shards, mask):
    width = value.shape[1] // shards
    blocks = [value[:, (q ^ mask) * width : ((q ^ mask) + 1) * width] for q in range(shards)]
    return jnp.concatenate(blocks, axis=1)


def stack8(*rows):
    rows = [row.reshape(1, -1) for row in rows]
    return jnp.concatenate(rows + [jnp.zeros((8 - len(rows), rows[0].shape[1]), F32)], axis=0)


def local(
    batch_size,
    shards,
    tokens,
    lengths,
    block_swap,
    input_weight,
    input_bias,
    out_weight,
    out_bias,
    gain_one,
    shift_one,
    up_weight,
    up_bias,
    down_weight,
    down_bias,
    gain_two,
    shift_two,
    cotangent,
):
    move = Mover(batch_size, shards)
    heads = block_swap.shape[0]
    rows, dim = tokens.shape
    width = input_weight.shape[2]
    depth = width // heads
    hidden_own = up_weight.shape[1]
    piece = dim // PARTS
    batch_at, head_at = lax.axis_index("batch"), lax.axis_index("head")
    part = batch_at % PARTS
    blocks = SEQ_LEN // rows
    length = lax.dynamic_index_in_dim(lengths, head_at // blocks, 0, keepdims=False)
    block_at = head_at % blocks
    own_live = jnp.clip(length - block_at * rows, 0, rows)
    partner_live = jnp.clip(length - (blocks - 1 - block_at) * rows, 0, rows)

    input_piece = lax.dynamic_slice_in_dim(input_weight, part * piece, piece, 1)
    input_piece = jnp.concatenate([input_piece[1], input_piece[2], input_piece[0]], axis=1)
    small = jnp.concatenate([jnp.zeros((width,), F32), input_bias[1], input_bias[0]])
    high = lax.reduce_precision(small, 8, 7)
    middle = lax.reduce_precision(small - high, 8, 7)
    swaps = jnp.pad(block_swap.astype(F32), (0, 3 * width - heads))
    small = jnp.stack([high, middle, small - high - middle, swaps])
    small = jnp.pad(small, ((0, 12), (0, 0))).astype(BF16)
    input_column = move.column(jnp.concatenate([input_piece, small]))
    up_own = up_weight.T.reshape(PARTS, piece, dim)
    up_piece = lax.dynamic_index_in_dim(up_own, part, 0, keepdims=False)
    input_own = input_weight.transpose(0, 2, 1)
    down_own = down_weight.reshape(PARTS, piece, dim)
    down_piece = lax.dynamic_index_in_dim(down_own, part, 0, keepdims=False)
    short_info = jnp.stack([own_live, part, head_at]).astype(jnp.int32)
    up_bias_parts = up_bias.reshape(shards, PARTS, 1, piece)
    out_parts = out_weight.reshape(shards, width, dim)
    vectors_one = stack8(out_bias, gain_one, shift_one)
    vectors_two = stack8(gain_one, shift_one, down_bias, gain_two, shift_two)
    vectors_back = stack8(gain_one)
    *input_column, up_piece, tokens_sent = all_after(
        (*input_column, up_piece, tokens), vectors_one, vectors_two, down_piece
    )
    small = jnp.stack([small] + [value[piece:] for value in input_column]).astype(F32)
    input_column = jnp.stack([value[:piece] for value in input_column])
    partner = move.head(tokens_sent, 1)
    input_low = move.low(input_column)
    up_far = move.head(up_piece, 2)
    info = jnp.concatenate(
        [
            small[:, 3, :heads].reshape(-1).astype(jnp.int32),
            jnp.stack([own_live, partner_live, part, head_at]).astype(jnp.int32),
        ]
    )
    bias = (small[:, 0] + small[:, 1]) + small[:, 2]
    bias = jnp.broadcast_to(bias[:, None], (shards, 8, 3 * width))
    input_low, up_far = all_after((input_low, up_far), info, bias)
    input_pair = pair_of(input_column, input_low)
    input_high = move.high(input_pair)
    input_high, partner = all_after((input_high, partner))
    input_near = four_of(input_pair, input_high)
    input_far = move.core(input_near)
    up_ends = pair_of(up_piece, after(up_far, partner))
    up_others = move.head(up_ends, 1)
    down_far = move.head(after(down_piece, partner), 2)

    def attend_shards(first_shard, count, last, weights, carried, so_far):
        return attend(
            (heads, depth, first_shard, last),
            count,
            info,
            tokens,
            partner,
            bias,
            out_parts,
            vectors_one,
            weights,
            carried,
            so_far,
        )

    qkv, context_0, stats, total = attend_shards(0, 1, False, [input_own], [], [])
    input_far, up_others, down_far, total, qkv, stats = all_after(
        (input_far, up_others, down_far, total, qkv, stats)
    )
    others = [input_near, input_far]
    up_column = jnp.stack([up_others[0], up_ends[1], up_others[1]])
    up_low = move.low(up_column)
    down_ends = pair_of(down_piece, down_far)
    down_others = move.head(down_ends, 1)
    total, up_column, down_ends = all_after((total, up_column, down_ends))
    qkv, context_1, stats, total = attend_shards(1, 2, False, others, [total], [qkv, stats])
    up_low, down_others, total, qkv, stats = all_after((up_low, down_others, total, qkv, stats))
    up_pair = pair_of(up_column, up_low)
    up_high = move.high(up_pair)
    down_column = jnp.stack([down_others[0], down_ends[1], down_others[1]])
    down_low = move.low(down_column)
    total, up_pair, down_column = all_after((total, up_pair, down_column))
    qkv, context, stats, rows_one, normed = attend_shards(
        3, 1, True, others, [total, context_0, context_1], [qkv, stats]
    )
    up_high, down_low, normed, context = all_after((up_high, down_low, normed, context))
    up_near = four_of(up_pair, up_high)
    up_far = move.core(up_near)
    up_all = (up_own, up_near, up_far)
    down_pair = pair_of(down_column, down_low)
    down_high = move.high(down_pair)
    normed, down_pair = all_after((normed, down_pair))
    normed_received = move.core(normed)
    context_received = move.core(context)
    hidden_near, hidden_far, *slopes = feed_up(short_info, normed, up_all, up_bias_parts)
    hidden_received = move.core(hidden_far)
    down_near = four_of(down_pair, after(down_high, hidden_near))
    down_far = move.core(down_near)
    tokens_t, partner_t = turn(after(tokens, down_near), partner)
    down_far, tokens_t, partner_t = all_after((down_far, tokens_t, partner_t))
    down_all = (down_own, down_near, down_far)
    mixed_out, grad_second, grad_branch, sums_two = feed_down(
        short_info, (hidden_near, hidden_far), down_all, rows_one, cotangent, vectors_two
    )

    branch_received = move.core(grad_branch)
    down_mine, down_one, down_two, down_three = row_grads(
        shards,
        hidden_near,
        hidden_received,
        grad_branch,
        branch_received,
        "down_grads",
    )
    down_three = move.low(down_three)
    pre_near, pre_far, up_bias_sums = grad_pre_of(
        short_info, after(grad_branch, down_two), down_all, slopes
    )
    down_three, pre_near, pre_far, up_bias_sums = all_after(
        (down_three, pre_near, pre_far, up_bias_sums)
    )
    pre_received = move.core(pre_far)
    down_two = (down_two + down_three.astype(F32)).astype(BF16)
    down_high = move.high(down_two)
    grad_first, grad_proj, sums_one = up_back(
        short_info, (pre_near, pre_far), up_all, rows_one, after(grad_second, down_two), vectors_back
    )
    pre_received, down_high, grad_proj, grad_first, sums_one = all_after(
        (pre_received, down_high, grad_proj, grad_first, sums_one)
    )
    proj_received = move.core(grad_proj)
    down_one = move.low(after(down_one, down_high))

    def core_sum(mine, received):
        mine, received = (a.reshape(2, 2, *a.shape[1:]) for a in (mine, received))
        keep = [mine[i, 0].astype(F32) + received[i, 0].astype(F32) for i in range(2)]
        return keep, (mine[:, 1].astype(F32) + received[:, 1].astype(F32)).astype(BF16)

    def fold_low(keep, received):
        return keep[0] + received[0].astype(F32), (keep[1] + received[1].astype(F32)).astype(BF16)

    def fold_high(own, received):
        total = own + received.astype(F32)
        return total[0::2], total[1::2].astype(BF16)

    def fold_near(own, received):
        return own[0] + received[0].astype(F32), (own[1] + received[1].astype(F32)).astype(BF16)

    def fold_last(own, received):
        return move.settle(own + received.astype(F32))

    up_mine, up_one, up_two, up_three = row_grads(
        shards, pre_near, pre_received, normed, normed_received, "up_grads"
    )
    proj_received, up_one, up_three = all_after((proj_received, up_one, up_three))
    up_three = move.low(up_three)
    out_keep, out_send = out_grads(
        short_info, after(grad_proj, up_one), proj_received, context, context_received
    )
    down_one, out_keep, out_send = all_after((down_one, out_keep, out_send))
    up_one = move.low(after(up_one, down_one))
    out_low = move.low(out_send)
    down_mine = down_mine + (down_one.astype(F32) + down_high.astype(F32))
    down_mine, down_next = down_mine[0::2], down_mine[1::2].astype(BF16)
    down_near = move.head(down_next, 1)

    def back(grad, first_shard, count, carried, so_far):
        return attend_back(
            (heads, depth, first_shard, count, shards),
            info,
            tokens_t,
            partner_t,
            grad,
            out_parts,
            [] if first_shard else [input_own],
            *others,
            qkv,
            stats,
            carried,
            so_far,
        )

    own_rows, partner_rows, late_near, late_far, late_bias = back(
        after(grad_proj, out_send, down_next), 2, 2, [], []
    )

    (
        down_near,
        up_one,
        up_three,
        out_low,
        own_rows,
        partner_rows,
        late_near,
        late_far,
        late_bias,
    ) = all_after(
        (
            down_near,
            up_one,
            up_three,
            out_low,
            own_rows,
            partner_rows,
            late_near,
            late_far,
            late_bias,
        )
    )
    up_next = (up_two + up_three.astype(F32)).astype(BF16)
    up_mine = up_mine + up_one.astype(F32)
    up_high = move.high(up_next)
    late_core = move.core(late_far)
    down_mine, down_next = fold_near(down_mine, after(down_near, up_next))
    down_last = move.head(down_next, 2)
    out_mine = out_keep[0] + out_low[0].astype(F32)
    out_next = (out_keep[1] + out_low[1].astype(F32)).astype(BF16)
    out_high = move.high(out_next)
    own_rows, partner_rows, *early = back(
        after(grad_proj, down_next, up_next, out_next), 1, 1, [own_rows, partner_rows], [late_bias]
    )

    up_high, down_last, late_core, out_high, own_rows, partner_rows, *early = all_after(
        (up_high, down_last, late_core, out_high, own_rows, partner_rows, *early)
    )
    up_mine, up_next = fold_high(up_mine, up_high)
    up_near = move.head(up_next, 1)
    late_keep, late_next = core_sum(late_near, late_core)
    late_low = move.low(late_next)
    down_total = fold_last(down_mine, down_last)
    down_low = move.low(down_total)
    out_next = (out_mine + out_high.astype(F32)).astype(BF16)
    out_near = move.head(out_next, 1)
    own_rows, partner_first, partner_second, early_near, early_far, early_bias = back(
        after(grad_proj, up_next, down_total, late_next, out_next),
        0,
        1,
        [own_rows, partner_rows],
        early,
    )

    up_near, down_low, late_low, out_near, own_rows, partner_first, partner_second = all_after(
        (up_near, down_low, late_low, out_near, own_rows, partner_first, partner_second), early_bias
    )
    early_near, early_far, early_bias = all_after((early_near, early_far, early_bias), up_near)

    early_core = move.core(early_far)
    late_mine, late_next = fold_low(late_keep, late_low)
    late_high = move.high(late_next)
    vectors = jnp.concatenate(
        [
            sums_one[:3],
            sums_two[:3],
            up_bias_sums[:, :, 0].reshape(shards, dim),
            jnp.pad(early_bias[:, 0], ((0, 0), (0, dim - 3 * width))),
        ]
    )
    hops = move.hops()

    def hop(value, sent, event):
        value = value + after(sent, event)
        return value, hops.pop(0)(value) if hops else None

    vectors_sent = hops.pop(0)(vectors)
    early_keep, early_next = core_sum(
        early_near, after(early_core, late_next, vectors)
    )
    early_low = move.low(early_next)
    up_mine, up_next = fold_near(up_mine, after(up_near, early_next))
    up_last = move.head(up_next, 2)
    out_near = shards_swapped(after(out_near, early_next), shards, 1)
    out_next = (out_next.astype(F32) + out_near.astype(F32)).astype(BF16)
    out_last = move.head(out_next, 2)
    vectors, vectors_sent = hop(vectors, vectors_sent, out_next)
    late_mine = late_mine + after(late_high, vectors).astype(F32)
    partner_first = move.head(after(partner_first, late_mine), 1)
    early_mine, early_next = fold_low(early_keep, after(early_low, late_mine))
    early_high = move.high(early_next)
    vectors, vectors_sent = hop(vectors, vectors_sent, early_next)
    up_total = fold_last(up_mine, after(up_last, vectors))
    out_last = shards_swapped(after(out_last, up_total), shards, 2)
    out_total = move.settle(out_next.astype(F32) + out_last.astype(F32))
    up_total = jnp.concatenate([up_total, out_total], axis=1)
    up_low = move.low(up_total)
    early_mine = early_mine + after(early_high, up_total).astype(F32)
    input_next = jnp.stack([early_mine[1], late_mine[1]]).astype(BF16)
    input_near = move.head(input_next, 1)
    vectors, vectors_sent = hop(vectors, vectors_sent, input_next)
    up_pair = pair_of(up_total, after(up_low, vectors))
    up_high = move.high(up_pair)
    down_pair = pair_of(down_total, after(down_low, up_pair))
    down_high = move.high(down_pair)
    input_mine, input_next = fold_near(
        jnp.stack([early_mine[0], late_mine[0]]), after(input_near, up_pair)
    )
    input_last = move.head(input_next, 2)
    partner_second = move.head(after(partner_second, input_next), 1)
    input_last, vectors_sent, partner_first = all_after(
        (input_last, vectors_sent, partner_first), down_pair
    )
    input_total = fold_last(input_mine, input_last)
    input_low = move.low(input_total)
    vectors, vectors_sent = hop(vectors, vectors_sent, input_total)
    up_near = four_of(up_pair, after(up_high, input_total))
    up_far = move.core(up_near)
    down_near = four_of(down_pair, after(down_high, up_near))
    down_far = move.core(down_near)
    input_low, vectors_sent, partner_second = all_after(
        (input_low, vectors_sent, partner_second), down_near
    )
    input_pair = pair_of(input_total, input_low)
    input_high = move.high(input_pair)
    while vectors_sent is not None:
        vectors, vectors_sent = hop(vectors, vectors_sent, input_pair)
    grad_down = pl.pallas_call(
        settle_down_kernel,
        in_specs=[SMEM] + [whole(4, piece, dim)] * 2,
        out_shape=shape((PARTS, piece, dim), F32),
        compiler_params=PARAMS,
        name="settle_down",
    )(short_info, after(down_near, input_pair), down_far)
    grad_input_bias = lax.dynamic_index_in_dim(vectors[10:], head_at, 0, keepdims=False)
    grad_input_bias = jnp.stack(
        [grad_input_bias[2 * width : 3 * width], grad_input_bias[width : 2 * width]]
    )
    grad_up_bias = lax.dynamic_index_in_dim(vectors[6:10], head_at, 0, keepdims=False)
    input_high, grad_input_bias, grad_up_bias = all_after(
        (input_high, grad_input_bias, grad_up_bias), grad_down
    )
    from_partner = jnp.concatenate([partner_first, partner_second])
    input_near = four_of(input_pair, input_high)
    input_far = move.core(input_near)
    grad_tokens = grad_first + own_rows + from_partner.astype(F32)
    grad_up, grad_out = pl.pallas_call(
        settle_up_kernel,
        in_specs=[SMEM] + [whole(4, piece, dim + shards * width)] * 2,
        out_shape=[shape((dim, hidden_own), F32), shape((shards, width, dim), F32)],
        scratch_shapes=[pltpu.VMEM((PARTS, piece, dim), F32)] * 2,
        compiler_params=PARAMS,
        name="settle_up",
    )(short_info, after(up_near, input_near, grad_tokens), up_far)
    grad_input_weight = pl.pallas_call(
        settle_input_kernel,
        in_specs=[SMEM] + [whole(4, piece, 3 * width)] * 2,
        out_shape=shape((3, width, dim), F32),
        scratch_shapes=[pltpu.VMEM((PARTS, piece, 3 * width), F32)],
        compiler_params=PARAMS,
        name="settle_input",
    )(short_info, after(input_near, grad_up), input_far)
    return (
        mixed_out,
        grad_tokens,
        grad_input_weight.transpose(0, 2, 1),
        grad_input_bias,
        grad_out.reshape(dim, dim),
        vectors[0],
        vectors[1],
        vectors[2],
        grad_up,
        grad_up_bias,
        grad_down.reshape(hidden_own, dim),
        vectors[3],
        vectors[4],
        vectors[5],
    )


def solution(mesh):
    rows_spec = P(("batch", "head"), None)
    placed = (
        rows_spec,
        P("batch"),
        P("head"),
        P(None, None, "head"),
        P(None, "head"),
        P(),
        P(),
        P(),
        P(),
        P(None, "head"),
        P(),
        P("head", None),
        P(),
        P(),
        P(),
        rows_spec,
    )
    return jax.shard_map(
        functools.partial(local, mesh.shape["batch"], mesh.shape["head"]),
        mesh=mesh,
        in_specs=placed,
        out_specs=(
            rows_spec,
            rows_spec,
            P(None, None, "head"),
            P(None, "head"),
            P(),
            P(),
            P(),
            P(),
            P(None, "head"),
            P("head"),
            P("head", None),
            P(),
            P(),
            P(),
        ),
        check_vma=False,
    )
```

```python
import functools

import jax
import jax.numpy as jnp
from jax import lax
from jax.experimental import pallas as pl
from jax.experimental.pallas import tpu as pltpu
from jax.sharding import PartitionSpec as P

SEQ_LEN = 1024
EPSILON = 1e-05
F32 = jnp.float32
BF16 = jnp.bfloat16
VMEM_LIMIT = 18 * 1024 * 1024
PARAMS = pltpu.CompilerParams(vmem_limit_bytes=VMEM_LIMIT)
CORE = 1
PARTS = 8
SPOTS = 4


def dot(left_side, right_side, left_dim=1, right_dim=0):
    return lax.dot_general(
        left_side,
        right_side,
        (((left_dim,), (right_dim,)), ((), ())),
        preferred_element_type=F32,
    )


def unit_parts(values):
    centred = values - jnp.mean(values, axis=-1, keepdims=True)
    inverse = lax.rsqrt(jnp.mean(centred * centred, axis=-1, keepdims=True) + EPSILON)
    return centred * inverse, inverse


def norm_back(grad_rows, unit_rows, inverse, gain_row):
    scaled = grad_rows * gain_row
    return inverse * (
        scaled
        - jnp.mean(scaled, axis=-1, keepdims=True)
        - unit_rows * jnp.mean(scaled * unit_rows, axis=-1, keepdims=True)
    )


def column_sum(values):
    return jnp.sum(values, axis=0, keepdims=True)


def gelu_parts(inner):
    below = 0.5 + 0.5 * lax.erf(inner * 0.7071067811865476)
    bell = jnp.exp(inner * inner * -0.5) * 0.3989422804014327
    return inner * below, below + inner * bell


def row_chunks(rows, step):
    return [slice(i, i + step) for i in range(0, rows, step)]


def eight_sum(values):
    return sum(values[cut] for cut in row_chunks(values.shape[0], 8))


def lane_pick(values, depth):
    lane = lax.broadcasted_iota(jnp.int32, (1, len(values) * depth), 1)
    picked = jnp.full(lane.shape, values[0], jnp.int32)
    for j in range(1, len(values)):
        picked = jnp.where(lane >= j * depth, values[j], picked)
    return picked


def place_of(part, half, spot):
    seen = part ^ half
    core = seen & 1
    low, high = 2 + 2 * core, 4 - 2 * core
    return seen ^ (low * (spot & 1) + high * (spot >> 1))


class Info:
    def __init__(self, ref, heads, shards):
        self.ref, self.heads, self.base = ref, heads, heads * shards

    def swaps(self, shard):
        return [self.ref[shard * self.heads + j] for j in range(self.heads)]

    own_live = property(lambda self: self.ref[self.base])
    partner_live = property(lambda self: self.ref[self.base + 1])
    part = property(lambda self: self.ref[self.base + 2])
    head_at = property(lambda self: self.ref[self.base + 3])


def gathered(part, near, far, scratch):
    for spot in range(SPOTS):
        scratch[place_of(part, 0, spot)] = near[spot, 0]
        scratch[place_of(part, 1, spot)] = far[spot, 0]
    return scratch[...].reshape(-1, scratch.shape[2])


def attend_kernel(setting, info_ref, tokens, partner, bias, out_weight, vectors, *refs):
    heads, depth, first_shard, last = setting
    refs = list(refs)
    if first_shard == 0:
        turned = refs.pop(0)
        total_in = None
    else:
        near, far, total_in = refs[:3]
        del refs[:3]
    earlier = []
    if last:
        earlier = refs[:2]
        del refs[:2]
    if first_shard:
        del refs[:2]
    qkv_out, context_out, stats_out = refs[:3]
    step = pl.program_id(0)
    shard = first_shard + step
    info = Info(info_ref, heads, out_weight.shape[0])
    if first_shard:
        weight = gathered(info.part, near, far, refs.pop())
    total = refs.pop()
    swaps = info.swaps(shard)
    rows, dim = tokens.shape
    width = heads * depth
    x, xp = tokens[...], partner[...]
    if first_shard:
        own = dot(x, weight)
        other = dot(xp, weight[:, : 2 * width])
    else:
        kv_rows = jnp.concatenate([turned[1], turned[2]], axis=0)
        own = jnp.concatenate([dot(x, kv_rows, 1, 1), dot(x, turned[0], 1, 1)], axis=1)
        other = dot(xp, kv_rows, 1, 1)
    swapped = lane_pick(swaps + swaps, depth) == 1
    bias_row = bias[0, 0:1]
    kv, q = [], []
    for cut in row_chunks(rows, 32):
        mine = own[cut] + bias_row
        theirs = other[cut] + bias_row[:, : 2 * width]
        kv.append(jnp.where(swapped, theirs, mine[:, : 2 * width]).astype(BF16))
        q.append(mine[:, 2 * width :].astype(BF16) * (depth**-0.5))
    kv, q = jnp.concatenate(kv, axis=0), jnp.concatenate(q, axis=0)
    qkv_out[0, :, : 2 * width] = kv
    qkv_out[0, :, 2 * width :] = q
    stats = []
    pieces = []
    for j in range(heads):
        head = slice(j * depth, (j + 1) * depth)
        live = jnp.where(swaps[j] == 1, info.partner_live, info.own_live)
        anyone = jnp.where(live > 0, 1.0, 0.0).astype(F32)
        scores = dot(kv[:, head], q[:, head], 1, 1)
        masked, most = [], None
        for cut in row_chunks(rows, 32):
            index = cut.start + lax.broadcasted_iota(jnp.int32, (32, 1), 0)
            part = jnp.where(index < live, scores[cut], -1e30)
            masked.append(part)
            for tile in row_chunks(32, 8):
                most = part[tile] if most is None else jnp.maximum(most, part[tile])
        largest = jnp.max(most, axis=0, keepdims=True)
        largest = jnp.where(anyone > 0.5, largest, 0.0)
        total_rows = None
        for part in masked:
            weights = eight_sum(jnp.exp(part - largest))
            total_rows = weights if total_rows is None else total_rows + weights
        stat = largest + jnp.log(column_sum(total_rows) + (1.0 - anyone))
        mixing = [jnp.exp(part - stat).astype(BF16) for part in masked]
        stats.append(stat)
        values = kv[:, width + j * depth : width + (j + 1) * depth]
        pieces.append(dot(values, jnp.concatenate(mixing, axis=0), 0, 0))
    context = jnp.concatenate(pieces, axis=0).T.astype(BF16)
    stats_out[0] = jnp.concatenate(stats + [jnp.zeros((8 - heads, rows), F32)], axis=0)
    projected = dot(context, out_weight[info.head_at ^ shard])
    if not last:
        context_out[0] = context

        @pl.when(step == 0)
        def first():
            total[...] = projected if total_in is None else total_in[...] + projected

        @pl.when(step > 0)
        def later():
            total[...] += projected

        return

    context_out[...] = jnp.concatenate(
        [ref[q] for ref in earlier for q in range(ref.shape[0])] + [context], axis=1
    )
    rows_out, normed_out = refs[3:]
    for cut in row_chunks(rows, 16):
        values = x[cut].astype(F32) + ((total_in[cut] + projected[cut]) + vectors[0:1])
        rows_out[cut] = values
        unit, _ = unit_parts(values)
        normed_out[cut] = (unit * vectors[1:2] + vectors[2:3]).astype(BF16)


def tiles_of(part, own, near, far, run):
    @pl.when(pl.program_id(0) == 0)
    def mine():
        run(
            *(
                jnp.concatenate([own[place_of(part, half, spot)] for spot in range(SPOTS)], axis=0)
                for half in range(2)
            )
        )

    @pl.when(pl.program_id(0) > 0)
    def other():
        run(*(ref[:, 0].reshape(-1, ref.shape[3]) for ref in (near, far)))


def add_up(total, *partials):
    @pl.when(pl.program_id(0) == 0)
    def start():
        total[...] = sum(partials[1:], partials[0])

    @pl.when(pl.program_id(0) > 0)
    def later():
        total[...] = sum(partials, total[...])


def at_end(run):
    pl.when(pl.program_id(0) == pl.num_programs(0) - 1)(run)


def eight_rows(*rows):
    width = rows[0].shape[1]
    return jnp.concatenate([*rows, jnp.zeros((8 - len(rows), width), F32)], axis=0)


def feed_up_kernel(info, normed, own, near, far, bias, *outs):
    shard = info[2] ^ pl.program_id(0)

    def run(*tiles):
        for half, tile in enumerate(tiles):
            places = [place_of(info[1], half, spot) for spot in range(SPOTS)]
            bias_row = jnp.concatenate([bias[shard, place] for place in places], axis=1)
            pre = dot(normed[...], tile, 1, 1)
            for cut in row_chunks(pre.shape[0], 32):
                hidden, slope = gelu_parts(pre[cut] + bias_row)
                outs[half][cut] = hidden.astype(BF16)
                outs[half + 2][cut] = slope

    tiles_of(info[1], own, near, far, run)


def feed_down_kernel(
    info,
    near_hidden,
    far_hidden,
    own,
    near,
    far,
    rows_in,
    cotangent,
    vectors,
    mixed_out,
    second_out,
    grad_out,
    sums_out,
    total,
):
    def run(near_tile, far_tile):
        add_up(total, dot(near_hidden[...], near_tile), dot(far_hidden[...], far_tile))

    tiles_of(info[1], own, near, far, run)

    @at_end
    def finish():
        sums = [jnp.zeros((8, rows_in.shape[1]), F32)] * 3
        for cut in row_chunks(rows_in.shape[0], 16):
            unit_one, _ = unit_parts(rows_in[cut])
            first_norm = unit_one * vectors[0:1] + vectors[1:2]
            unit, inverse = unit_parts(first_norm + (total[cut] + vectors[2:3]))
            index = cut.start + lax.broadcasted_iota(jnp.int32, (16, 1), 0)
            mask = jnp.where(index < info[0], 1.0, 0.0).astype(F32)
            mixed_out[cut] = ((unit * vectors[3:4] + vectors[4:5]) * mask).astype(BF16)
            incoming = cotangent[cut].astype(F32) * mask
            grad = norm_back(incoming, unit, inverse, vectors[3:4])
            second_out[cut] = grad
            low = grad.astype(BF16)
            grad_out[cut] = low
            more = (low.astype(F32), incoming * unit, incoming)
            sums = [a + eight_sum(b) for a, b in zip(sums, more)]
        sums_out[...] = eight_rows(*(column_sum(a) for a in sums))


def grad_pre_kernel(
    info, grad_branch, own, near, far, near_slope, far_slope, near_out, far_out, bias_out
):
    def run(*tiles):
        for half, tile in enumerate(tiles):
            out, slope = (near_out, far_out)[half], (near_slope, far_slope)[half]
            grad = dot(grad_branch[...], tile, 1, 1)
            sums = jnp.zeros((8, grad.shape[1]), F32)
            for cut in row_chunks(grad.shape[0], 32):
                low = (grad[cut] * slope[cut]).astype(BF16)
                out[cut] = low
                sums = sums + eight_sum(low.astype(F32))
            sums = jnp.broadcast_to(column_sum(sums), sums.shape)
            width = bias_out.shape[3]
            for spot in range(SPOTS):
                row = sums[:, spot * width : (spot + 1) * width]
                bias_out[info[2] ^ pl.program_id(0), place_of(info[1], half, spot)] = row

    tiles_of(info[1], own, near, far, run)


def up_back_kernel(
    info,
    near_pre,
    far_pre,
    own,
    near,
    far,
    rows_in,
    second_in,
    vectors,
    first_out,
    proj_out,
    sums_out,
    total,
):
    def run(near_tile, far_tile):
        add_up(total, dot(near_pre[...], near_tile), dot(far_pre[...], far_tile))

    tiles_of(info[1], own, near, far, run)

    @at_end
    def finish():
        sums = [jnp.zeros((8, rows_in.shape[1]), F32)] * 3
        for cut in row_chunks(rows_in.shape[0], 16):
            unit, inverse = unit_parts(rows_in[cut])
            grad_normed = second_in[cut] + total[cut]
            grad = norm_back(grad_normed, unit, inverse, vectors[0:1])
            first_out[cut] = grad
            low = grad.astype(BF16)
            proj_out[cut] = low
            more = (low.astype(F32), grad_normed * unit, grad_normed)
            sums = [a + eight_sum(b) for a, b in zip(sums, more)]
        sums_out[...] = eight_rows(*(column_sum(a) for a in sums))


def turn_kernel(tokens, partner, tokens_out, partner_out):
    tokens_out[...] = tokens[...].T
    partner_out[...] = partner[...].T


def row_grads_kernel(mine, theirs, my_rows, their_rows, *outs):
    value = dot(mine[...], my_rows[...], 0, 0) + dot(theirs[...], their_rows[...], 0, 0)
    value = value.reshape(SPOTS, -1, value.shape[1])
    for spot, out in enumerate(outs):
        out[0] = value[spot].astype(out.dtype)


def out_grads_kernel(info, mine, theirs, my_context, their_context, keep_out, send_out, turned):
    value = 0.0
    for i, (grad, context) in enumerate(((mine, my_context), (theirs, their_context))):
        turned[i] = grad[...].T.reshape(turned.shape[1:])
        rows = [turned[i, place_of(info[1], 0, spot)] for spot in range(SPOTS)]
        value = value + dot(jnp.concatenate(rows, axis=0), context[...])
    value = value.reshape(SPOTS, -1, value.shape[1])
    for spot in range(SPOTS):
        out = (keep_out, send_out)[spot & 1]
        out[spot >> 1] = value[spot].astype(out.dtype)


def scatter_parts(part, value, chunks, near_out, far_out):
    chunks[...] = value.reshape(chunks.shape)
    for spot in range(SPOTS):
        near_out[spot, 0] = chunks[place_of(part, 0, spot)]
        far_out[spot, 0] = chunks[place_of(part, 1, spot)]


def attend_back_kernel(setting, info_ref, tokens_t, partner_t, grad_proj, out_weight, *refs):
    heads, depth, first_shard, carried, so_far, shards = setting
    refs = list(refs)
    if first_shard == 0:
        turned = refs.pop(0)
    near, far, qkv_in, stats_in = refs[:4]
    del refs[:4]
    if carried:
        own_in, partner_in = refs[:2]
        del refs[:2]
    del refs[:so_far]
    own_out, *partner_outs, near_out, far_out, bias_out, total, weight_scratch, chunks = refs
    step = pl.program_id(0)
    shard = first_shard + step
    info = Info(info_ref, heads, shards)
    if first_shard:
        gathered(info.part, near, far, weight_scratch)
    else:
        width = turned.shape[1]

        @pl.when(shard == 0)
        def own_weight():
            rows_kv = jnp.concatenate([turned[1], turned[2], turned[0]], axis=0)
            weight_scratch[...] = rows_kv.T.reshape(weight_scratch.shape)

        @pl.when(shard > 0)
        def other_weight():
            gathered(info.part, near, far, weight_scratch)

    weight = weight_scratch[...].reshape(-1, weight_scratch.shape[2])
    swaps = info.swaps(shard)
    dim, rows = tokens_t.shape
    width = heads * depth
    grad = dot(grad_proj[...], out_weight[0], 1, 1).astype(BF16)
    k, v, q = (qkv_in[0, :, i * width : (i + 1) * width] for i in range(3))
    stats = stats_in[0]
    gq, gk, gv = [], [], []
    for j in range(heads):
        head = slice(j * depth, (j + 1) * depth)
        stat = stats[j : j + 1, :]
        live = jnp.where(swaps[j] == 1, info.partner_live, info.own_live)
        scores = dot(k[:, head], q[:, head], 1, 1)
        grad_mix = dot(v[:, head], grad[:, head], 1, 1)
        chances, shared = [], jnp.zeros((8, rows), F32)
        for cut in row_chunks(rows, 32):
            index = cut.start + lax.broadcasted_iota(jnp.int32, (32, 1), 0)
            part = jnp.exp(jnp.where(index < live, scores[cut] - stat, -10000.0))
            chances.append(part)
            shared = shared + eight_sum(part * grad_mix[cut])
        shared = column_sum(shared)
        mixing = jnp.concatenate([part.astype(BF16) for part in chances], axis=0)
        grad_scores = jnp.concatenate(
            [
                (part * (grad_mix[cut] - shared)).astype(BF16)
                for part, cut in zip(chances, row_chunks(rows, 32))
            ],
            axis=0,
        )
        gk.append(dot(grad_scores, q[:, head]))
        gv.append(dot(mixing, grad[:, head]))
        gq.append(dot(k[:, head], grad_scores, 0, 0))
    grad_q = (jnp.concatenate(gq, axis=0).T * (depth**-0.5)).astype(BF16)
    grad_kv = jnp.concatenate(gk + gv, axis=1).astype(BF16)
    swapped = lane_pick(swaps + swaps, depth) == 1
    nothing = jnp.zeros((), BF16)
    grad_own = jnp.concatenate([jnp.where(swapped, nothing, grad_kv), grad_q], axis=1)
    grad_far = jnp.where(swapped, grad_kv, nothing)
    own = dot(grad_own, weight, 1, 1)
    other = dot(grad_far, weight[:, : 2 * width], 1, 1)

    @pl.when(step == 0)
    def first():
        own_out[...] = own_in[...] + own if carried else own
        total[...] = partner_in[...] + other if carried else other

    @pl.when(step > 0)
    def later():
        own_out[...] += own
        total[...] += other

    @at_end
    def finish():
        first = 0
        for out in partner_outs:
            out[...] = total[first : first + out.shape[0]].astype(out.dtype)
            first += out.shape[0]

    grads = dot(tokens_t[...], grad_own)
    grads_kv = grads[:, : 2 * width] + dot(partner_t[...], grad_far)
    grads = jnp.concatenate([grads_kv, grads[:, 2 * width :]], axis=1).astype(BF16)
    chunks[...] = grads.reshape(chunks.shape)
    for spot in range(SPOTS):
        near_out[spot, 0] = chunks[place_of(info.part, 0, spot)]
        far_out[spot, 0] = chunks[place_of(info.part, 1, spot)]
    bias_out[0] = jnp.broadcast_to(
        jnp.concatenate(
            [column_sum(grad_kv.astype(F32)), column_sum(grad_q.astype(F32))], axis=1
        ),
        bias_out.shape[1:],
    )


def settle_down_kernel(info, near, far, out):
    for half, source in enumerate((near, far)):
        for spot in range(SPOTS):
            out[place_of(info[1], half, spot)] = source[spot].astype(F32)


def settle_up_kernel(info, near, far, up_out, out_out, up_scratch, out_scratch):
    dim = up_out.shape[0]
    for half, source in enumerate((near, far)):
        for spot in range(SPOTS):
            place = place_of(info[1], half, spot)
            value = source[spot].astype(F32)
            up_scratch[place] = value[:, :dim]
            out_scratch[place] = value[:, dim:]
    up_out[...] = up_scratch[...].reshape(-1, dim).T
    shards = out_out.shape[0]
    turned = out_scratch[...].reshape(-1, dim).T.reshape(shards, -1, dim)
    for q in range(shards):
        out_out[info[2] ^ q] = turned[q]


def settle_input_kernel(info, near, far, out, scratch):
    width = out.shape[1]
    for half, source in enumerate((near, far)):
        for spot in range(SPOTS):
            scratch[place_of(info[1], half, spot)] = source[spot].astype(F32)
    turned = scratch[...].reshape(-1, scratch.shape[2]).T
    for i in range(3):
        out[(i + 1) % 3] = turned[i * width : (i + 1) * width]


def shape(dims, dtype):
    return jax.ShapeDtypeStruct(dims, dtype)


def whole(*dims):
    return pl.BlockSpec(dims, lambda *_: (0,) * len(dims))


def cost(flops, moved, slow=0):
    return pl.CostEstimate(flops=flops, bytes_accessed=moved, transcendentals=slow)


SMEM = pl.BlockSpec(memory_space=pltpu.SMEM)


def gathered_specs(near, first_shard):
    spots, _, piece, lanes = near.shape
    return [pl.BlockSpec((spots, 1, piece, lanes), lambda s: (0, s + first_shard - 1, 0, 0))] * 2


def attend(
    setting, count, info, tokens, partner, bias, out_weight, vectors, weights, carried, so_far
):
    heads, depth, first_shard, last = setting
    rows, dim = tokens.shape
    shards, width, _ = out_weight.shape
    lanes = 3 * width
    scratch = []
    if first_shard == 0:
        weight_specs = [whole(3, width, dim)]
    else:
        weight_specs = gathered_specs(weights[0], first_shard)
        scratch = [pltpu.VMEM((PARTS, dim // PARTS, lanes), BF16)]
    out_specs = [
        pl.BlockSpec((1, rows, lanes), lambda s: (s + first_shard, 0, 0)),
        whole(rows, dim) if last else pl.BlockSpec((1, rows, width), lambda s: (s, 0, 0)),
        pl.BlockSpec((1, 8, rows), lambda s: (s + first_shard, 0, 0)),
    ]
    out_shape = [
        shape((shards, rows, lanes), BF16),
        shape((rows, dim) if last else (count, rows, width), BF16),
        shape((shards, 8, rows), F32),
    ]
    fixed = 6 + len(weights) + len(carried)
    if last:
        out_specs += [whole(rows, dim)] * 2
        out_shape += [shape((rows, dim), F32), shape((rows, dim), BF16)]
        scratch = [pltpu.VMEM((8, 128), F32)] + scratch
    else:
        out_specs.append(whole(rows, dim))
        out_shape.append(shape((rows, dim), F32))
    return pl.pallas_call(
        functools.partial(attend_kernel, setting),
        grid=(count,),
        in_specs=[
            SMEM,
            whole(rows, dim),
            whole(rows, dim),
            pl.BlockSpec((1, 8, lanes), lambda s: (s + first_shard, 0, 0)),
            whole(shards, width, dim),
            whole(8, dim),
        ]
        + weight_specs
        + [whole(*value.shape) for value in carried]
        + [pl.BlockSpec(memory_space=pl.ANY)] * len(so_far),
        out_specs=out_specs,
        out_shape=out_shape,
        scratch_shapes=scratch,
        input_output_aliases={fixed + i: (0, 2)[i] for i in range(len(so_far))},
        compiler_params=PARAMS,
        cost_estimate=cost(
            count * (3 * rows * dim * dim + 4 * rows * rows * dim),
            count * 6 * rows * dim,
            count * heads * rows * rows,
        ),
        name="attend",
    )(info, tokens, partner, bias, out_weight, vectors, *weights, *carried, *so_far)


def feed_specs(near):
    spots, _, piece, lanes = near.shape
    other = pl.BlockSpec(
        (spots, 1, piece, lanes), lambda q: (0, jnp.maximum(q - 1, 0), 0, 0)
    )
    return [whole(PARTS, piece, lanes), other, other]


def feed_up(info, normed, weight, bias):
    rows, dim = normed.shape
    near = weight[1]
    shards = near.shape[1] + 1
    tile = SPOTS * near.shape[2]
    columns = pl.BlockSpec((rows, tile), lambda q: (0, q))
    return pl.pallas_call(
        feed_up_kernel,
        grid=(shards,),
        in_specs=[
            SMEM,
            whole(rows, dim),
            *feed_specs(near),
            whole(*bias.shape),
        ],
        out_specs=[columns] * 4,
        out_shape=[shape((rows, shards * tile), BF16)] * 2
        + [shape((rows, shards * tile), F32)] * 2,
        compiler_params=PARAMS,
        cost_estimate=cost(4 * rows * dim * tile * shards, 30 * rows * dim, rows * dim * 8),
        name="feed_up",
    )(info, normed, *weight, bias)


def feed_down(info, hidden, weight, rows_one, cotangent, vectors):
    rows, dim = rows_one.shape
    near = weight[1]
    shards = near.shape[1] + 1
    tile = SPOTS * near.shape[2]
    columns = pl.BlockSpec((rows, tile), lambda q: (0, q))
    return pl.pallas_call(
        feed_down_kernel,
        grid=(shards,),
        in_specs=[
            SMEM,
            columns,
            columns,
            *feed_specs(near),
            whole(rows, dim),
            whole(rows, dim),
            whole(8, dim),
        ],
        out_specs=[whole(rows, dim)] * 3 + [whole(8, dim)],
        out_shape=[
            shape((rows, dim), BF16),
            shape((rows, dim), F32),
            shape((rows, dim), BF16),
            shape((8, dim), F32),
        ],
        scratch_shapes=[pltpu.VMEM((rows, dim), F32)],
        compiler_params=PARAMS,
        cost_estimate=cost(4 * rows * dim * tile * shards, 20 * rows * dim),
        name="feed_down",
    )(info, *hidden, *weight, rows_one, cotangent, vectors)


def grad_pre_of(info, grad_branch, weight, slopes):
    rows, dim = grad_branch.shape
    near = weight[1]
    shards = near.shape[1] + 1
    tile = SPOTS * near.shape[2]
    columns = pl.BlockSpec((rows, tile), lambda q: (0, q))
    return pl.pallas_call(
        grad_pre_kernel,
        grid=(shards,),
        in_specs=[SMEM, whole(rows, dim), *feed_specs(near), columns, columns],
        out_specs=[columns, columns, whole(shards, PARTS, 8, near.shape[2])],
        out_shape=[
            shape((rows, shards * tile), BF16),
            shape((rows, shards * tile), BF16),
            shape((shards, PARTS, 8, near.shape[2]), F32),
        ],
        compiler_params=PARAMS,
        cost_estimate=cost(4 * rows * dim * tile * shards, 30 * rows * dim),
        name="grad_pre",
    )(info, grad_branch, *weight, *slopes)


def up_back(info, pres, weight, rows_one, grad_second, vectors):
    rows, dim = rows_one.shape
    near = weight[1]
    shards = near.shape[1] + 1
    tile = SPOTS * near.shape[2]
    columns = pl.BlockSpec((rows, tile), lambda q: (0, q))
    return pl.pallas_call(
        up_back_kernel,
        grid=(shards,),
        in_specs=[
            SMEM,
            columns,
            columns,
            *feed_specs(near),
            whole(rows, dim),
            whole(rows, dim),
            whole(8, dim),
        ],
        out_specs=[whole(rows, dim), whole(rows, dim), whole(8, dim)],
        out_shape=[shape((rows, dim), F32), shape((rows, dim), BF16), shape((8, dim), F32)],
        scratch_shapes=[pltpu.VMEM((rows, dim), F32)],
        compiler_params=PARAMS,
        cost_estimate=cost(4 * rows * dim * tile * shards, 24 * rows * dim),
        name="up_back",
    )(info, *pres, *weight, rows_one, grad_second, vectors)


def turn(tokens, partner):
    rows, dim = tokens.shape
    return pl.pallas_call(
        turn_kernel,
        out_shape=[shape((dim, rows), BF16)] * 2,
        compiler_params=PARAMS,
        cost_estimate=cost(rows * dim, 8 * rows * dim),
        name="turn",
    )(tokens, partner)


def row_grads(shards, mine, theirs, my_rows, their_rows, name):
    rows, dim = my_rows.shape
    tile = mine.shape[1] // shards
    piece = tile // SPOTS
    columns = pl.BlockSpec((rows, tile), lambda q: (0, q))
    out = pl.BlockSpec((1, piece, dim), lambda q: (q, 0, 0))
    return pl.pallas_call(
        row_grads_kernel,
        grid=(shards,),
        in_specs=[columns, columns, whole(rows, dim), whole(rows, dim)],
        out_specs=[out] * SPOTS,
        out_shape=[shape((shards, piece, dim), (F32, BF16)[spot & 1]) for spot in range(SPOTS)],
        compiler_params=PARAMS,
        cost_estimate=cost(4 * rows * dim * tile * shards, 20 * rows * dim),
        name=name,
    )(mine, theirs, my_rows, their_rows)


def out_grads(info, mine, theirs, my_context, their_context):
    rows, dim = mine.shape
    piece = dim // PARTS
    return pl.pallas_call(
        out_grads_kernel,
        in_specs=[SMEM] + [whole(rows, dim)] * 4,
        out_specs=[whole(2, piece, dim)] * 2,
        out_shape=[shape((2, piece, dim), F32), shape((2, piece, dim), BF16)],
        scratch_shapes=[pltpu.VMEM((2, PARTS, piece, rows), BF16)],
        compiler_params=PARAMS,
        cost_estimate=cost(2 * rows * dim * dim, 10 * rows * dim),
        name="out_grads",
    )(info, mine, theirs, my_context, their_context)


def attend_back(
    setting,
    info,
    tokens_t,
    partner_t,
    grad_proj,
    out_weight,
    own,
    near,
    far,
    qkvs,
    stats,
    carried,
    so_far,
):
    heads, depth, first_shard, count, shards = setting
    half = shards // 2
    slot = first_shard % half
    fixed = 9 + len(own) + len(carried)
    splits = 1 if first_shard else 2
    dim, rows = tokens_t.shape
    width = heads * depth
    lanes = 3 * width
    piece = dim // PARTS
    head_spot = heads * shards + 3
    own_specs = [] if first_shard else [whole(3, width, dim)]
    kernel = functools.partial(
        attend_back_kernel, (heads, depth, first_shard, bool(carried), len(so_far), shards)
    )

    def other(s, info):
        return (0, jnp.maximum(s + first_shard - 1, 0), 0, 0)

    parts_out = pl.BlockSpec((SPOTS, 1, piece, lanes), lambda s, info: (0, s + slot, 0, 0))
    return pl.pallas_call(
        kernel,
        grid_spec=pltpu.PrefetchScalarGridSpec(
            num_scalar_prefetch=1,
            grid=(count,),
            in_specs=[
                whole(dim, rows),
                whole(dim, rows),
                whole(rows, dim),
                pl.BlockSpec(
                    (1, width, dim), lambda s, info: (info[head_spot] ^ (s + first_shard), 0, 0)
                ),
            ]
            + own_specs
            + [pl.BlockSpec((SPOTS, 1, piece, lanes), other)] * 2
            + [
                pl.BlockSpec((1, rows, lanes), lambda s, info: (s + first_shard, 0, 0)),
                pl.BlockSpec((1, 8, rows), lambda s, info: (s + first_shard, 0, 0)),
            ]
            + [whole(rows, dim)] * len(carried)
            + [pl.BlockSpec(memory_space=pl.ANY)] * len(so_far),
            out_specs=[
                whole(rows, dim),
                *[whole(rows // splits, dim)] * splits,
                parts_out,
                parts_out,
                pl.BlockSpec(
                    (1, 8, lanes), lambda s, info: (info[head_spot] ^ (s + first_shard), 0, 0)
                ),
            ],
            scratch_shapes=[
                pltpu.VMEM((rows, dim), F32),
                pltpu.VMEM((PARTS, piece, lanes), BF16),
                pltpu.VMEM((PARTS, piece, lanes), BF16),
            ],
        ),
        out_shape=[
            shape((rows, dim), F32),
            *[shape((rows // splits, dim), F32 if first_shard else BF16)] * splits,
            shape((SPOTS, half, piece, lanes), BF16),
            shape((SPOTS, half, piece, lanes), BF16),
            shape((shards, 8, lanes), F32),
        ],
        input_output_aliases={
            fixed + i: 4 + splits - len(so_far) + i for i in range(len(so_far))
        },
        compiler_params=PARAMS,
        cost_estimate=cost(
            count * (6 * rows * dim * dim + 10 * rows * rows * dim),
            count * 8 * rows * dim,
            count * heads * rows * rows,
        ),
        name="attend_back",
    )(
        info,
        tokens_t,
        partner_t,
        grad_proj,
        out_weight,
        *own,
        near,
        far,
        qkvs,
        stats,
        *carried,
        *so_far,
    )


class Mover:
    def __init__(self, batch_size, shards):
        self.batch_size, self.shards = batch_size, shards

    def batch(self, value, mask_of):
        perm = [(i, i ^ mask_of(i)) for i in range(self.batch_size)]
        return lax.ppermute(value, "batch", perm)

    def core(self, value):
        return self.batch(value, lambda i: CORE)

    def low(self, value):
        return self.batch(value, lambda i: 4 if i & 1 else 2)

    def high(self, value):
        return self.batch(value, lambda i: 2 if i & 1 else 4)

    def head(self, value, mask):
        return lax.ppermute(value, "head", [(i, i ^ mask) for i in range(self.shards)])

    def along(self, values, first=1):
        return [self.head(value, q) for q, value in enumerate(values, first)]

    def column(self, piece):
        return self.along([piece] * (self.shards - 1))

    def settle(self, total):
        total = total.astype(BF16)
        mask = PARTS
        while mask < self.batch_size:
            other = self.batch(total, lambda i, mask=mask: mask)
            total = (total.astype(F32) + other.astype(F32)).astype(BF16)
            mask *= 2
        return total

    def hops(self):
        steps, mask = [self.core, self.low, self.high], 1
        while mask < self.shards:
            steps.append(lambda value, mask=mask: self.head(value, mask))
            mask *= 2
        mask = PARTS
        while mask < self.batch_size:
            steps.append(lambda value, mask=mask: self.batch(value, lambda i: mask))
            mask *= 2
        return steps


def after(value, *events):
    return lax.optimization_barrier((value, *events))[0]


def all_after(values, *events):
    return lax.optimization_barrier((*values, *events))[: len(values)]


def pair_of(first, second):
    return jnp.stack([first, second])


def four_of(pair, received):
    return jnp.concatenate([pair, received])


def shards_swapped(value, shards, mask):
    width = value.shape[1] // shards
    blocks = [value[:, (q ^ mask) * width : ((q ^ mask) + 1) * width] for q in range(shards)]
    return jnp.concatenate(blocks, axis=1)


def stack8(*rows):
    rows = [row.reshape(1, -1) for row in rows]
    return jnp.concatenate(rows + [jnp.zeros((8 - len(rows), rows[0].shape[1]), F32)], axis=0)


def local(
    batch_size,
    shards,
    tokens,
    lengths,
    block_swap,
    input_weight,
    input_bias,
    out_weight,
    out_bias,
    gain_one,
    shift_one,
    up_weight,
    up_bias,
    down_weight,
    down_bias,
    gain_two,
    shift_two,
    cotangent,
):
    move = Mover(batch_size, shards)
    heads = block_swap.shape[0]
    rows, dim = tokens.shape
    width = input_weight.shape[2]
    depth = width // heads
    hidden_own = up_weight.shape[1]
    piece = dim // PARTS
    batch_at, head_at = lax.axis_index("batch"), lax.axis_index("head")
    part = batch_at % PARTS
    blocks = SEQ_LEN // rows
    length = lax.dynamic_index_in_dim(lengths, head_at // blocks, 0, keepdims=False)
    block_at = head_at % blocks
    own_live = jnp.clip(length - block_at * rows, 0, rows)
    partner_live = jnp.clip(length - (blocks - 1 - block_at) * rows, 0, rows)

    input_piece = lax.dynamic_slice_in_dim(input_weight, part * piece, piece, 1)
    input_piece = jnp.concatenate([input_piece[1], input_piece[2], input_piece[0]], axis=1)
    small = jnp.concatenate([jnp.zeros((width,), F32), input_bias[1], input_bias[0]])
    high = lax.reduce_precision(small, 8, 7)
    middle = lax.reduce_precision(small - high, 8, 7)
    swaps = jnp.pad(block_swap.astype(F32), (0, 3 * width - heads))
    small = jnp.stack([high, middle, small - high - middle, swaps])
    small = jnp.pad(small, ((0, 12), (0, 0))).astype(BF16)
    input_column = move.column(jnp.concatenate([input_piece, small]))
    up_own = up_weight.T.reshape(PARTS, piece, dim)
    up_piece = lax.dynamic_index_in_dim(up_own, part, 0, keepdims=False)
    input_own = input_weight.transpose(0, 2, 1)
    down_own = down_weight.reshape(PARTS, piece, dim)
    down_piece = lax.dynamic_index_in_dim(down_own, part, 0, keepdims=False)
    short_info = jnp.stack([own_live, part, head_at]).astype(jnp.int32)
    up_bias_parts = up_bias.reshape(shards, PARTS, 1, piece)
    out_parts = out_weight.reshape(shards, width, dim)
    vectors_one = stack8(out_bias, gain_one, shift_one)
    vectors_two = stack8(gain_one, shift_one, down_bias, gain_two, shift_two)
    vectors_back = stack8(gain_one)
    *input_column, up_piece, tokens_sent = all_after(
        (*input_column, up_piece, tokens), vectors_one, vectors_two, down_piece
    )
    small = jnp.stack([small] + [value[piece:] for value in input_column]).astype(F32)
    input_column = jnp.stack([value[:piece] for value in input_column])
    partner = move.head(tokens_sent, 1)
    input_low = move.low(input_column)
    up_far = move.head(up_piece, 2)
    info = jnp.concatenate(
        [
            small[:, 3, :heads].reshape(-1).astype(jnp.int32),
            jnp.stack([own_live, partner_live, part, head_at]).astype(jnp.int32),
        ]
    )
    bias = (small[:, 0] + small[:, 1]) + small[:, 2]
    bias = jnp.broadcast_to(bias[:, None], (shards, 8, 3 * width))
    input_low, up_far = all_after((input_low, up_far), info, bias)
    input_pair = pair_of(input_column, input_low)
    input_high = move.high(input_pair)
    input_high, partner = all_after((input_high, partner))
    input_near = four_of(input_pair, input_high)
    input_far = move.core(input_near)
    up_ends = pair_of(up_piece, after(up_far, partner))
    up_others = move.head(up_ends, 1)
    down_far = move.head(after(down_piece, partner), 2)

    def attend_shards(first_shard, count, last, weights, carried, so_far):
        return attend(
            (heads, depth, first_shard, last),
            count,
            info,
            tokens,
            partner,
            bias,
            out_parts,
            vectors_one,
            weights,
            carried,
            so_far,
        )

    qkv, context_0, stats, total = attend_shards(0, 1, False, [input_own], [], [])
    input_far, up_others, down_far, total, qkv, stats = all_after(
        (input_far, up_others, down_far, total, qkv, stats)
    )
    others = [input_near, input_far]
    up_column = jnp.stack([up_others[0], up_ends[1], up_others[1]])
    up_low = move.low(up_column)
    down_ends = pair_of(down_piece, down_far)
    down_others = move.head(down_ends, 1)
    total, up_column, down_ends = all_after((total, up_column, down_ends))
    qkv, context_1, stats, total = attend_shards(1, 2, False, others, [total], [qkv, stats])
    up_low, down_others, total, qkv, stats = all_after((up_low, down_others, total, qkv, stats))
    up_pair = pair_of(up_column, up_low)
    up_high = move.high(up_pair)
    down_column = jnp.stack([down_others[0], down_ends[1], down_others[1]])
    down_low = move.low(down_column)
    total, up_pair, down_column = all_after((total, up_pair, down_column))
    qkv, context, stats, rows_one, normed = attend_shards(
        3, 1, True, others, [total, context_0, context_1], [qkv, stats]
    )
    up_high, down_low, normed, context = all_after((up_high, down_low, normed, context))
    up_near = four_of(up_pair, up_high)
    up_far = move.core(up_near)
    up_all = (up_own, up_near, up_far)
    down_pair = pair_of(down_column, down_low)
    down_high = move.high(down_pair)
    normed, down_pair = all_after((normed, down_pair))
    normed_received = move.core(normed)
    context_received = move.core(context)
    hidden_near, hidden_far, *slopes = feed_up(short_info, normed, up_all, up_bias_parts)
    hidden_received = move.core(hidden_far)
    down_near = four_of(down_pair, after(down_high, hidden_near))
    down_far = move.core(down_near)
    tokens_t, partner_t = turn(after(tokens, down_near), partner)
    down_far, tokens_t, partner_t = all_after((down_far, tokens_t, partner_t))
    down_all = (down_own, down_near, down_far)
    mixed_out, grad_second, grad_branch, sums_two = feed_down(
        short_info, (hidden_near, hidden_far), down_all, rows_one, cotangent, vectors_two
    )

    branch_received = move.core(grad_branch)
    down_mine, down_one, down_two, down_three = row_grads(
        shards,
        hidden_near,
        hidden_received,
        grad_branch,
        branch_received,
        "down_grads",
    )
    down_three = move.low(down_three)
    pre_near, pre_far, up_bias_sums = grad_pre_of(
        short_info, after(grad_branch, down_two), down_all, slopes
    )
    down_three, pre_near, pre_far, up_bias_sums = all_after(
        (down_three, pre_near, pre_far, up_bias_sums)
    )
    pre_received = move.core(pre_far)
    down_two = (down_two + down_three.astype(F32)).astype(BF16)
    down_high = move.high(down_two)
    grad_first, grad_proj, sums_one = up_back(
        short_info, (pre_near, pre_far), up_all, rows_one, after(grad_second, down_two), vectors_back
    )
    pre_received, down_high, grad_proj, grad_first, sums_one = all_after(
        (pre_received, down_high, grad_proj, grad_first, sums_one)
    )
    proj_received = move.core(grad_proj)
    down_one = move.low(after(down_one, down_high))

    def core_sum(mine, received):
        mine, received = (a.reshape(2, 2, *a.shape[1:]) for a in (mine, received))
        keep = [mine[i, 0].astype(F32) + received[i, 0].astype(F32) for i in range(2)]
        return keep, (mine[:, 1].astype(F32) + received[:, 1].astype(F32)).astype(BF16)

    def fold_low(keep, received):
        return keep[0] + received[0].astype(F32), (keep[1] + received[1].astype(F32)).astype(BF16)

    def fold_high(own, received):
        total = own + received.astype(F32)
        return total[0::2], total[1::2].astype(BF16)

    def fold_near(own, received):
        return own[0] + received[0].astype(F32), (own[1] + received[1].astype(F32)).astype(BF16)

    def fold_last(own, received):
        return move.settle(own + received.astype(F32))

    up_mine, up_one, up_two, up_three = row_grads(
        shards, pre_near, pre_received, normed, normed_received, "up_grads"
    )
    proj_received, up_one, up_three = all_after((proj_received, up_one, up_three))
    up_three = move.low(up_three)
    out_keep, out_send = out_grads(
        short_info, after(grad_proj, up_one), proj_received, context, context_received
    )
    down_one, out_keep, out_send = all_after((down_one, out_keep, out_send))
    up_one = move.low(after(up_one, down_one))
    out_low = move.low(out_send)
    down_mine = down_mine + (down_one.astype(F32) + down_high.astype(F32))
    down_mine, down_next = down_mine[0::2], down_mine[1::2].astype(BF16)
    down_near = move.head(down_next, 1)

    def back(grad, first_shard, count, carried, so_far):
        return attend_back(
            (heads, depth, first_shard, count, shards),
            info,
            tokens_t,
            partner_t,
            grad,
            out_parts,
            [] if first_shard else [input_own],
            *others,
            qkv,
            stats,
            carried,
            so_far,
        )

    own_rows, partner_rows, late_near, late_far, late_bias = back(
        after(grad_proj, out_send, down_next), 2, 2, [], []
    )

    (
        down_near,
        up_three,
        out_low,
        own_rows,
        partner_rows,
        late_near,
        late_far,
        late_bias,
    ) = all_after(
        (
            down_near,
            up_three,
            out_low,
            own_rows,
            partner_rows,
            late_near,
            late_far,
            late_bias,
        )
    )
    up_next = (up_two + up_three.astype(F32)).astype(BF16)
    up_high = move.high(up_next)
    late_core = move.core(late_far)
    down_mine, down_next = fold_near(down_mine, after(down_near, up_next))
    down_last = move.head(down_next, 2)
    out_mine = out_keep[0] + out_low[0].astype(F32)
    out_next = (out_keep[1] + out_low[1].astype(F32)).astype(BF16)
    out_high = move.high(out_next)
    own_rows, partner_rows, *early = back(
        after(grad_proj, down_next, up_next, out_next), 1, 1, [own_rows, partner_rows], [late_bias]
    )

    up_one, up_high, down_last, late_core, out_high, own_rows, partner_rows, *early = all_after(
        (up_one, up_high, down_last, late_core, out_high, own_rows, partner_rows, *early)
    )
    up_mine, up_next = fold_high(up_mine + up_one.astype(F32), up_high)
    up_near = move.head(up_next, 1)
    late_keep, late_next = core_sum(late_near, late_core)
    late_low = move.low(late_next)
    down_total = fold_last(down_mine, down_last)
    down_low = move.low(down_total)
    out_next = (out_mine + out_high.astype(F32)).astype(BF16)
    out_near = move.head(out_next, 1)
    own_rows, partner_first, partner_second, early_near, early_far, early_bias = back(
        after(grad_proj, up_next, down_total, late_next, out_next),
        0,
        1,
        [own_rows, partner_rows],
        early,
    )

    up_near, down_low, late_low, out_near, own_rows, partner_first, partner_second = all_after(
        (up_near, down_low, late_low, out_near, own_rows, partner_first, partner_second), early_bias
    )
    early_near, early_far, early_bias = all_after((early_near, early_far, early_bias), up_near)

    early_core = move.core(early_far)
    up_mine, up_next = fold_near(up_mine, up_near)
    up_last = move.head(up_next, 2)
    late_mine, late_next = fold_low(late_keep, late_low)
    late_high = move.high(late_next)
    out_near = shards_swapped(out_near, shards, 1)
    out_next = (out_next.astype(F32) + out_near.astype(F32)).astype(BF16)
    out_last = move.head(out_next, 2)
    vectors = jnp.concatenate(
        [
            sums_one[:3],
            sums_two[:3],
            up_bias_sums[:, :, 0].reshape(shards, dim),
            jnp.pad(early_bias[:, 0], ((0, 0), (0, dim - 3 * width))),
        ]
    )
    hops = move.hops()

    def hop(value, sent, event):
        value = value + after(sent, event)
        return value, hops.pop(0)(value) if hops else None

    vectors_sent = hops.pop(0)(vectors)
    early_keep, early_next = core_sum(
        early_near, after(early_core, late_next, up_next, vectors, out_next)
    )
    early_low = move.low(early_next)
    vectors, vectors_sent = hop(vectors, vectors_sent, early_next)
    late_mine = late_mine + after(late_high, vectors).astype(F32)
    partner_first = move.head(after(partner_first, late_mine), 1)
    early_mine, early_next = fold_low(early_keep, after(early_low, late_mine))
    early_high = move.high(early_next)
    vectors, vectors_sent = hop(vectors, vectors_sent, early_next)
    up_total = fold_last(up_mine, after(up_last, vectors))
    out_last = shards_swapped(after(out_last, up_total), shards, 2)
    out_total = move.settle(out_next.astype(F32) + out_last.astype(F32))
    up_total = jnp.concatenate([up_total, out_total], axis=1)
    up_low = move.low(up_total)
    early_mine = early_mine + after(early_high, up_total).astype(F32)
    input_next = jnp.stack([early_mine[1], late_mine[1]]).astype(BF16)
    input_near = move.head(input_next, 1)
    vectors, vectors_sent = hop(vectors, vectors_sent, input_next)
    up_pair = pair_of(up_total, after(up_low, vectors))
    up_high = move.high(up_pair)
    down_pair = pair_of(down_total, after(down_low, up_pair))
    down_high = move.high(down_pair)
    input_mine, input_next = fold_near(
        jnp.stack([early_mine[0], late_mine[0]]), after(input_near, up_pair)
    )
    input_last = move.head(input_next, 2)
    partner_second = move.head(after(partner_second, input_next), 1)
    input_last, vectors_sent, partner_first = all_after(
        (input_last, vectors_sent, partner_first), down_pair
    )
    input_total = fold_last(input_mine, input_last)
    input_low = move.low(input_total)
    vectors, vectors_sent = hop(vectors, vectors_sent, input_total)
    up_near = four_of(up_pair, after(up_high, input_total))
    up_far = move.core(up_near)
    down_near = four_of(down_pair, after(down_high, up_near))
    down_far = move.core(down_near)
    input_low = after(input_low, down_near)
    input_pair = pair_of(input_total, input_low)
    input_high = move.high(input_pair)
    grad_down = pl.pallas_call(
        settle_down_kernel,
        in_specs=[SMEM] + [whole(4, piece, dim)] * 2,
        out_shape=shape((PARTS, piece, dim), F32),
        compiler_params=PARAMS,
        name="settle_down",
    )(short_info, after(down_near, input_pair), down_far)
    while vectors_sent is not None:
        vectors, vectors_sent = hop(vectors, vectors_sent, grad_down)
    grad_input_bias = lax.dynamic_index_in_dim(vectors[10:], head_at, 0, keepdims=False)
    grad_input_bias = jnp.stack(
        [grad_input_bias[2 * width : 3 * width], grad_input_bias[width : 2 * width]]
    )
    grad_up_bias = lax.dynamic_index_in_dim(vectors[6:10], head_at, 0, keepdims=False)
    input_high, grad_input_bias, grad_up_bias = all_after(
        (input_high, grad_input_bias, grad_up_bias), grad_down
    )
    input_near = four_of(input_pair, input_high)
    input_far = move.core(input_near)
    from_partner = jnp.concatenate([partner_first, after(partner_second, input_near)])
    grad_tokens = grad_first + own_rows + from_partner.astype(F32)
    grad_up, grad_out = pl.pallas_call(
        settle_up_kernel,
        in_specs=[SMEM] + [whole(4, piece, dim + shards * width)] * 2,
        out_shape=[shape((dim, hidden_own), F32), shape((shards, width, dim), F32)],
        scratch_shapes=[pltpu.VMEM((PARTS, piece, dim), F32)] * 2,
        compiler_params=PARAMS,
        name="settle_up",
    )(short_info, after(up_near, input_near, grad_tokens), up_far)
    grad_input_weight = pl.pallas_call(
        settle_input_kernel,
        in_specs=[SMEM] + [whole(4, piece, 3 * width)] * 2,
        out_shape=shape((3, width, dim), F32),
        scratch_shapes=[pltpu.VMEM((PARTS, piece, 3 * width), F32)],
        compiler_params=PARAMS,
        name="settle_input",
    )(short_info, after(input_near, grad_up), input_far)
    return (
        mixed_out,
        grad_tokens,
        grad_input_weight.transpose(0, 2, 1),
        grad_input_bias,
        grad_out.reshape(dim, dim),
        vectors[0],
        vectors[1],
        vectors[2],
        grad_up,
        grad_up_bias,
        grad_down.reshape(hidden_own, dim),
        vectors[3],
        vectors[4],
        vectors[5],
    )


def solution(mesh):
    rows_spec = P(("batch", "head"), None)
    placed = (
        rows_spec,
        P("batch"),
        P("head"),
        P(None, None, "head"),
        P(None, "head"),
        P(),
        P(),
        P(),
        P(),
        P(None, "head"),
        P(),
        P("head", None),
        P(),
        P(),
        P(),
        rows_spec,
    )
    return jax.shard_map(
        functools.partial(local, mesh.shape["batch"], mesh.shape["head"]),
        mesh=mesh,
        in_specs=placed,
        out_specs=(
            rows_spec,
            rows_spec,
            P(None, None, "head"),
            P(None, "head"),
            P(),
            P(),
            P(),
            P(),
            P(None, "head"),
            P("head"),
            P("head", None),
            P(),
            P(),
            P(),
        ),
        check_vma=False,
    )
```

```python
import functools

import jax
import jax.numpy as jnp
from jax import lax
from jax.experimental import pallas as pl
from jax.experimental.pallas import tpu as pltpu
from jax.sharding import PartitionSpec as P

SEQ_LEN = 1024
EPSILON = 1e-05
F32 = jnp.float32
BF16 = jnp.bfloat16
VMEM_LIMIT = 18 * 1024 * 1024
PARAMS = pltpu.CompilerParams(vmem_limit_bytes=VMEM_LIMIT)
CORE = 1
PARTS = 8
SPOTS = 4


def dot(left_side, right_side, left_dim=1, right_dim=0):
    return lax.dot_general(
        left_side,
        right_side,
        (((left_dim,), (right_dim,)), ((), ())),
        preferred_element_type=F32,
    )


def unit_parts(values):
    centred = values - jnp.mean(values, axis=-1, keepdims=True)
    inverse = lax.rsqrt(jnp.mean(centred * centred, axis=-1, keepdims=True) + EPSILON)
    return centred * inverse, inverse


def norm_back(grad_rows, unit_rows, inverse, gain_row):
    scaled = grad_rows * gain_row
    return inverse * (
        scaled
        - jnp.mean(scaled, axis=-1, keepdims=True)
        - unit_rows * jnp.mean(scaled * unit_rows, axis=-1, keepdims=True)
    )


def column_sum(values):
    return jnp.sum(values, axis=0, keepdims=True)


def gelu_parts(inner):
    below = 0.5 + 0.5 * lax.erf(inner * 0.7071067811865476)
    bell = jnp.exp(inner * inner * -0.5) * 0.3989422804014327
    return inner * below, below + inner * bell


def row_chunks(rows, step):
    return [slice(i, i + step) for i in range(0, rows, step)]


def eight_sum(values):
    return sum(values[cut] for cut in row_chunks(values.shape[0], 8))


def lane_pick(values, depth):
    lane = lax.broadcasted_iota(jnp.int32, (1, len(values) * depth), 1)
    picked = jnp.full(lane.shape, values[0], jnp.int32)
    for j in range(1, len(values)):
        picked = jnp.where(lane >= j * depth, values[j], picked)
    return picked


def place_of(part, half, spot):
    seen = part ^ half
    core = seen & 1
    low, high = 2 + 2 * core, 4 - 2 * core
    return seen ^ (low * (spot & 1) + high * (spot >> 1))


class Info:
    def __init__(self, ref, heads, shards):
        self.ref, self.heads, self.base = ref, heads, heads * shards

    def swaps(self, shard):
        return [self.ref[shard * self.heads + j] for j in range(self.heads)]

    own_live = property(lambda self: self.ref[self.base])
    partner_live = property(lambda self: self.ref[self.base + 1])
    part = property(lambda self: self.ref[self.base + 2])
    head_at = property(lambda self: self.ref[self.base + 3])


def gathered(part, near, far, scratch):
    for spot in range(SPOTS):
        scratch[place_of(part, 0, spot)] = near[spot, 0]
        scratch[place_of(part, 1, spot)] = far[spot, 0]
    return scratch[...].reshape(-1, scratch.shape[2])


def attend_kernel(setting, info_ref, tokens, partner, bias, out_weight, vectors, *refs):
    heads, depth, first_shard, last = setting
    refs = list(refs)
    if first_shard == 0:
        turned = refs.pop(0)
        total_in = None
    else:
        near, far, total_in = refs[:3]
        del refs[:3]
    earlier = []
    if last:
        earlier = refs[:2]
        del refs[:2]
    if first_shard:
        del refs[:2]
    qkv_out, context_out, stats_out = refs[:3]
    step = pl.program_id(0)
    shard = first_shard + step
    info = Info(info_ref, heads, out_weight.shape[0])
    if first_shard:
        weight = gathered(info.part, near, far, refs.pop())
    total = refs.pop()
    swaps = info.swaps(shard)
    rows, dim = tokens.shape
    width = heads * depth
    x, xp = tokens[...], partner[...]
    if first_shard:
        own = dot(x, weight)
        other = dot(xp, weight[:, : 2 * width])
    else:
        kv_rows = jnp.concatenate([turned[1], turned[2]], axis=0)
        own = jnp.concatenate([dot(x, kv_rows, 1, 1), dot(x, turned[0], 1, 1)], axis=1)
        other = dot(xp, kv_rows, 1, 1)
    swapped = lane_pick(swaps + swaps, depth) == 1
    bias_row = bias[0, 0:1]
    kv, q = [], []
    for cut in row_chunks(rows, 32):
        mine = own[cut] + bias_row
        theirs = other[cut] + bias_row[:, : 2 * width]
        kv.append(jnp.where(swapped, theirs, mine[:, : 2 * width]).astype(BF16))
        q.append(mine[:, 2 * width :].astype(BF16) * (depth**-0.5))
    kv, q = jnp.concatenate(kv, axis=0), jnp.concatenate(q, axis=0)
    qkv_out[0, :, : 2 * width] = kv
    qkv_out[0, :, 2 * width :] = q
    stats = []
    pieces = []
    for j in range(heads):
        head = slice(j * depth, (j + 1) * depth)
        live = jnp.where(swaps[j] == 1, info.partner_live, info.own_live)
        anyone = jnp.where(live > 0, 1.0, 0.0).astype(F32)
        scores = dot(kv[:, head], q[:, head], 1, 1)
        masked, most = [], None
        for cut in row_chunks(rows, 32):
            index = cut.start + lax.broadcasted_iota(jnp.int32, (32, 1), 0)
            part = jnp.where(index < live, scores[cut], -1e30)
            masked.append(part)
            for tile in row_chunks(32, 8):
                most = part[tile] if most is None else jnp.maximum(most, part[tile])
        largest = jnp.max(most, axis=0, keepdims=True)
        largest = jnp.where(anyone > 0.5, largest, 0.0)
        total_rows = None
        for part in masked:
            weights = eight_sum(jnp.exp(part - largest))
            total_rows = weights if total_rows is None else total_rows + weights
        stat = largest + jnp.log(column_sum(total_rows) + (1.0 - anyone))
        mixing = [jnp.exp(part - stat).astype(BF16) for part in masked]
        stats.append(stat)
        values = kv[:, width + j * depth : width + (j + 1) * depth]
        pieces.append(dot(values, jnp.concatenate(mixing, axis=0), 0, 0))
    context = jnp.concatenate(pieces, axis=0).T.astype(BF16)
    stats_out[0] = jnp.concatenate(stats + [jnp.zeros((8 - heads, rows), F32)], axis=0)
    projected = dot(context, out_weight[info.head_at ^ shard])
    if not last:
        context_out[0] = context

        @pl.when(step == 0)
        def first():
            total[...] = projected if total_in is None else total_in[...] + projected

        @pl.when(step > 0)
        def later():
            total[...] += projected

        return

    context_out[...] = jnp.concatenate(
        [ref[q] for ref in earlier for q in range(ref.shape[0])] + [context], axis=1
    )
    rows_out, normed_out = refs[3:]
    for cut in row_chunks(rows, 16):
        values = x[cut].astype(F32) + ((total_in[cut] + projected[cut]) + vectors[0:1])
        rows_out[cut] = values
        unit, _ = unit_parts(values)
        normed_out[cut] = (unit * vectors[1:2] + vectors[2:3]).astype(BF16)


def tiles_of(part, own, near, far, run):
    @pl.when(pl.program_id(0) == 0)
    def mine():
        run(
            *(
                jnp.concatenate([own[place_of(part, half, spot)] for spot in range(SPOTS)], axis=0)
                for half in range(2)
            )
        )

    @pl.when(pl.program_id(0) > 0)
    def other():
        run(*(ref[:, 0].reshape(-1, ref.shape[3]) for ref in (near, far)))


def add_up(total, *partials):
    @pl.when(pl.program_id(0) == 0)
    def start():
        total[...] = sum(partials[1:], partials[0])

    @pl.when(pl.program_id(0) > 0)
    def later():
        total[...] = sum(partials, total[...])


def at_end(run):
    pl.when(pl.program_id(0) == pl.num_programs(0) - 1)(run)


def eight_rows(*rows):
    width = rows[0].shape[1]
    return jnp.concatenate([*rows, jnp.zeros((8 - len(rows), width), F32)], axis=0)


def feed_up_kernel(info, normed, own, near, far, bias, *outs):
    shard = info[2] ^ pl.program_id(0)

    def run(*tiles):
        for half, tile in enumerate(tiles):
            places = [place_of(info[1], half, spot) for spot in range(SPOTS)]
            bias_row = jnp.concatenate([bias[shard, place] for place in places], axis=1)
            pre = dot(normed[...], tile, 1, 1)
            for cut in row_chunks(pre.shape[0], 32):
                hidden, slope = gelu_parts(pre[cut] + bias_row)
                outs[half][cut] = hidden.astype(BF16)
                outs[half + 2][cut] = slope

    tiles_of(info[1], own, near, far, run)


def feed_down_kernel(
    info,
    near_hidden,
    far_hidden,
    own,
    near,
    far,
    rows_in,
    cotangent,
    vectors,
    mixed_out,
    second_out,
    grad_out,
    sums_out,
    total,
):
    def run(near_tile, far_tile):
        add_up(total, dot(near_hidden[...], near_tile), dot(far_hidden[...], far_tile))

    tiles_of(info[1], own, near, far, run)

    @at_end
    def finish():
        sums = [jnp.zeros((8, rows_in.shape[1]), F32)] * 3
        for cut in row_chunks(rows_in.shape[0], 16):
            unit_one, _ = unit_parts(rows_in[cut])
            first_norm = unit_one * vectors[0:1] + vectors[1:2]
            unit, inverse = unit_parts(first_norm + (total[cut] + vectors[2:3]))
            index = cut.start + lax.broadcasted_iota(jnp.int32, (16, 1), 0)
            mask = jnp.where(index < info[0], 1.0, 0.0).astype(F32)
            mixed_out[cut] = ((unit * vectors[3:4] + vectors[4:5]) * mask).astype(BF16)
            incoming = cotangent[cut].astype(F32) * mask
            grad = norm_back(incoming, unit, inverse, vectors[3:4])
            second_out[cut] = grad
            low = grad.astype(BF16)
            grad_out[cut] = low
            more = (low.astype(F32), incoming * unit, incoming)
            sums = [a + eight_sum(b) for a, b in zip(sums, more)]
        sums_out[...] = eight_rows(*(column_sum(a) for a in sums))


def grad_pre_kernel(
    info, grad_branch, own, near, far, near_slope, far_slope, near_out, far_out, bias_out
):
    def run(*tiles):
        for half, tile in enumerate(tiles):
            out, slope = (near_out, far_out)[half], (near_slope, far_slope)[half]
            grad = dot(grad_branch[...], tile, 1, 1)
            sums = jnp.zeros((8, grad.shape[1]), F32)
            for cut in row_chunks(grad.shape[0], 32):
                low = (grad[cut] * slope[cut]).astype(BF16)
                out[cut] = low
                sums = sums + eight_sum(low.astype(F32))
            sums = jnp.broadcast_to(column_sum(sums), sums.shape)
            width = bias_out.shape[3]
            for spot in range(SPOTS):
                row = sums[:, spot * width : (spot + 1) * width]
                bias_out[info[2] ^ pl.program_id(0), place_of(info[1], half, spot)] = row

    tiles_of(info[1], own, near, far, run)


def up_back_kernel(
    info,
    near_pre,
    far_pre,
    own,
    near,
    far,
    rows_in,
    second_in,
    vectors,
    first_out,
    proj_out,
    sums_out,
    total,
):
    def run(near_tile, far_tile):
        add_up(total, dot(near_pre[...], near_tile), dot(far_pre[...], far_tile))

    tiles_of(info[1], own, near, far, run)

    @at_end
    def finish():
        sums = [jnp.zeros((8, rows_in.shape[1]), F32)] * 3
        for cut in row_chunks(rows_in.shape[0], 16):
            unit, inverse = unit_parts(rows_in[cut])
            grad_normed = second_in[cut] + total[cut]
            grad = norm_back(grad_normed, unit, inverse, vectors[0:1])
            first_out[cut] = grad
            low = grad.astype(BF16)
            proj_out[cut] = low
            more = (low.astype(F32), grad_normed * unit, grad_normed)
            sums = [a + eight_sum(b) for a, b in zip(sums, more)]
        sums_out[...] = eight_rows(*(column_sum(a) for a in sums))


def turn_kernel(tokens, partner, tokens_out, partner_out):
    tokens_out[...] = tokens[...].T
    partner_out[...] = partner[...].T


def row_grads_kernel(mine, theirs, my_rows, their_rows, *outs):
    value = dot(mine[...], my_rows[...], 0, 0) + dot(theirs[...], their_rows[...], 0, 0)
    value = value.reshape(SPOTS, -1, value.shape[1])
    for spot, out in enumerate(outs):
        out[0] = value[spot].astype(out.dtype)


def out_grads_kernel(info, mine, theirs, my_context, their_context, keep_out, send_out, turned):
    value = 0.0
    for i, (grad, context) in enumerate(((mine, my_context), (theirs, their_context))):
        turned[i] = grad[...].T.reshape(turned.shape[1:])
        rows = [turned[i, place_of(info[1], 0, spot)] for spot in range(SPOTS)]
        value = value + dot(jnp.concatenate(rows, axis=0), context[...])
    value = value.reshape(SPOTS, -1, value.shape[1])
    for spot in range(SPOTS):
        out = (keep_out, send_out)[spot & 1]
        out[spot >> 1] = value[spot].astype(out.dtype)


def scatter_parts(part, value, chunks, near_out, far_out):
    chunks[...] = value.reshape(chunks.shape)
    for spot in range(SPOTS):
        near_out[spot, 0] = chunks[place_of(part, 0, spot)]
        far_out[spot, 0] = chunks[place_of(part, 1, spot)]


def attend_back_kernel(setting, info_ref, tokens_t, partner_t, grad_proj, out_weight, *refs):
    heads, depth, first_shard, carried, so_far, shards = setting
    refs = list(refs)
    if first_shard == 0:
        turned = refs.pop(0)
    near, far, qkv_in, stats_in = refs[:4]
    del refs[:4]
    if carried:
        own_in, partner_in = refs[:2]
        del refs[:2]
    del refs[:so_far]
    own_out, *partner_outs, near_out, far_out, bias_out, total, weight_scratch, chunks = refs
    step = pl.program_id(0)
    shard = first_shard + step
    info = Info(info_ref, heads, shards)
    if first_shard:
        gathered(info.part, near, far, weight_scratch)
    else:
        width = turned.shape[1]

        @pl.when(shard == 0)
        def own_weight():
            rows_kv = jnp.concatenate([turned[1], turned[2], turned[0]], axis=0)
            weight_scratch[...] = rows_kv.T.reshape(weight_scratch.shape)

        @pl.when(shard > 0)
        def other_weight():
            gathered(info.part, near, far, weight_scratch)

    weight = weight_scratch[...].reshape(-1, weight_scratch.shape[2])
    swaps = info.swaps(shard)
    dim, rows = tokens_t.shape
    width = heads * depth
    grad = dot(grad_proj[...], out_weight[0], 1, 1).astype(BF16)
    k, v, q = (qkv_in[0, :, i * width : (i + 1) * width] for i in range(3))
    stats = stats_in[0]
    gq, gk, gv = [], [], []
    for j in range(heads):
        head = slice(j * depth, (j + 1) * depth)
        stat = stats[j : j + 1, :]
        live = jnp.where(swaps[j] == 1, info.partner_live, info.own_live)
        scores = dot(k[:, head], q[:, head], 1, 1)
        grad_mix = dot(v[:, head], grad[:, head], 1, 1)
        chances, shared = [], jnp.zeros((8, rows), F32)
        for cut in row_chunks(rows, 32):
            index = cut.start + lax.broadcasted_iota(jnp.int32, (32, 1), 0)
            part = jnp.exp(jnp.where(index < live, scores[cut] - stat, -10000.0))
            chances.append(part)
            shared = shared + eight_sum(part * grad_mix[cut])
        shared = column_sum(shared)
        mixing = jnp.concatenate([part.astype(BF16) for part in chances], axis=0)
        grad_scores = jnp.concatenate(
            [
                (part * (grad_mix[cut] - shared)).astype(BF16)
                for part, cut in zip(chances, row_chunks(rows, 32))
            ],
            axis=0,
        )
        gk.append(dot(grad_scores, q[:, head]))
        gv.append(dot(mixing, grad[:, head]))
        gq.append(dot(k[:, head], grad_scores, 0, 0))
    grad_q = (jnp.concatenate(gq, axis=0).T * (depth**-0.5)).astype(BF16)
    grad_kv = jnp.concatenate(gk + gv, axis=1).astype(BF16)
    swapped = lane_pick(swaps + swaps, depth) == 1
    nothing = jnp.zeros((), BF16)
    grad_own = jnp.concatenate([jnp.where(swapped, nothing, grad_kv), grad_q], axis=1)
    grad_far = jnp.where(swapped, grad_kv, nothing)
    own = dot(grad_own, weight, 1, 1)
    other = dot(grad_far, weight[:, : 2 * width], 1, 1)

    @pl.when(step == 0)
    def first():
        own_out[...] = own_in[...] + own if carried else own
        total[...] = partner_in[...] + other if carried else other

    @pl.when(step > 0)
    def later():
        own_out[...] += own
        total[...] += other

    @at_end
    def finish():
        first = 0
        for out in partner_outs:
            out[...] = total[first : first + out.shape[0]].astype(out.dtype)
            first += out.shape[0]

    grads = dot(tokens_t[...], grad_own)
    grads_kv = grads[:, : 2 * width] + dot(partner_t[...], grad_far)
    grads = jnp.concatenate([grads_kv, grads[:, 2 * width :]], axis=1).astype(BF16)
    chunks[...] = grads.reshape(chunks.shape)
    for spot in range(SPOTS):
        near_out[spot, 0] = chunks[place_of(info.part, 0, spot)]
        far_out[spot, 0] = chunks[place_of(info.part, 1, spot)]
    bias_out[0] = jnp.broadcast_to(
        jnp.concatenate(
            [column_sum(grad_kv.astype(F32)), column_sum(grad_q.astype(F32))], axis=1
        ),
        bias_out.shape[1:],
    )


def settle_down_kernel(info, near, far, out):
    for half, source in enumerate((near, far)):
        for spot in range(SPOTS):
            out[place_of(info[1], half, spot)] = source[spot].astype(F32)


def settle_up_kernel(info, near, far, up_out, out_out, up_scratch, out_scratch):
    dim = up_out.shape[0]
    for half, source in enumerate((near, far)):
        for spot in range(SPOTS):
            place = place_of(info[1], half, spot)
            value = source[spot].astype(F32)
            up_scratch[place] = value[:, :dim]
            out_scratch[place] = value[:, dim:]
    up_out[...] = up_scratch[...].reshape(-1, dim).T
    shards = out_out.shape[0]
    turned = out_scratch[...].reshape(-1, dim).T.reshape(shards, -1, dim)
    for q in range(shards):
        out_out[info[2] ^ q] = turned[q]


def settle_input_kernel(info, near, far, out, scratch):
    width = out.shape[1]
    for half, source in enumerate((near, far)):
        for spot in range(SPOTS):
            scratch[place_of(info[1], half, spot)] = source[spot].astype(F32)
    turned = scratch[...].reshape(-1, scratch.shape[2]).T
    for i in range(3):
        out[(i + 1) % 3] = turned[i * width : (i + 1) * width]


def shape(dims, dtype):
    return jax.ShapeDtypeStruct(dims, dtype)


def whole(*dims):
    return pl.BlockSpec(dims, lambda *_: (0,) * len(dims))


def cost(flops, moved, slow=0):
    return pl.CostEstimate(flops=flops, bytes_accessed=moved, transcendentals=slow)


SMEM = pl.BlockSpec(memory_space=pltpu.SMEM)


def gathered_specs(near, first_shard):
    spots, _, piece, lanes = near.shape
    return [pl.BlockSpec((spots, 1, piece, lanes), lambda s: (0, s + first_shard - 1, 0, 0))] * 2


def attend(
    setting, count, info, tokens, partner, bias, out_weight, vectors, weights, carried, so_far
):
    heads, depth, first_shard, last = setting
    rows, dim = tokens.shape
    shards, width, _ = out_weight.shape
    lanes = 3 * width
    scratch = []
    if first_shard == 0:
        weight_specs = [whole(3, width, dim)]
    else:
        weight_specs = gathered_specs(weights[0], first_shard)
        scratch = [pltpu.VMEM((PARTS, dim // PARTS, lanes), BF16)]
    out_specs = [
        pl.BlockSpec((1, rows, lanes), lambda s: (s + first_shard, 0, 0)),
        whole(rows, dim) if last else pl.BlockSpec((1, rows, width), lambda s: (s, 0, 0)),
        pl.BlockSpec((1, 8, rows), lambda s: (s + first_shard, 0, 0)),
    ]
    out_shape = [
        shape((shards, rows, lanes), BF16),
        shape((rows, dim) if last else (count, rows, width), BF16),
        shape((shards, 8, rows), F32),
    ]
    fixed = 6 + len(weights) + len(carried)
    if last:
        out_specs += [whole(rows, dim)] * 2
        out_shape += [shape((rows, dim), F32), shape((rows, dim), BF16)]
        scratch = [pltpu.VMEM((8, 128), F32)] + scratch
    else:
        out_specs.append(whole(rows, dim))
        out_shape.append(shape((rows, dim), F32))
    return pl.pallas_call(
        functools.partial(attend_kernel, setting),
        grid=(count,),
        in_specs=[
            SMEM,
            whole(rows, dim),
            whole(rows, dim),
            pl.BlockSpec((1, 8, lanes), lambda s: (s + first_shard, 0, 0)),
            whole(shards, width, dim),
            whole(8, dim),
        ]
        + weight_specs
        + [whole(*value.shape) for value in carried]
        + [pl.BlockSpec(memory_space=pl.ANY)] * len(so_far),
        out_specs=out_specs,
        out_shape=out_shape,
        scratch_shapes=scratch,
        input_output_aliases={fixed + i: (0, 2)[i] for i in range(len(so_far))},
        compiler_params=PARAMS,
        cost_estimate=cost(
            count * (3 * rows * dim * dim + 4 * rows * rows * dim),
            count * 6 * rows * dim,
            count * heads * rows * rows,
        ),
        name="attend",
    )(info, tokens, partner, bias, out_weight, vectors, *weights, *carried, *so_far)


def feed_specs(near):
    spots, _, piece, lanes = near.shape
    other = pl.BlockSpec(
        (spots, 1, piece, lanes), lambda q: (0, jnp.maximum(q - 1, 0), 0, 0)
    )
    return [whole(PARTS, piece, lanes), other, other]


def feed_up(info, normed, weight, bias):
    rows, dim = normed.shape
    near = weight[1]
    shards = near.shape[1] + 1
    tile = SPOTS * near.shape[2]
    columns = pl.BlockSpec((rows, tile), lambda q: (0, q))
    return pl.pallas_call(
        feed_up_kernel,
        grid=(shards,),
        in_specs=[
            SMEM,
            whole(rows, dim),
            *feed_specs(near),
            whole(*bias.shape),
        ],
        out_specs=[columns] * 4,
        out_shape=[shape((rows, shards * tile), BF16)] * 2
        + [shape((rows, shards * tile), F32)] * 2,
        compiler_params=PARAMS,
        cost_estimate=cost(4 * rows * dim * tile * shards, 30 * rows * dim, rows * dim * 8),
        name="feed_up",
    )(info, normed, *weight, bias)


def feed_down(info, hidden, weight, rows_one, cotangent, vectors):
    rows, dim = rows_one.shape
    near = weight[1]
    shards = near.shape[1] + 1
    tile = SPOTS * near.shape[2]
    columns = pl.BlockSpec((rows, tile), lambda q: (0, q))
    return pl.pallas_call(
        feed_down_kernel,
        grid=(shards,),
        in_specs=[
            SMEM,
            columns,
            columns,
            *feed_specs(near),
            whole(rows, dim),
            whole(rows, dim),
            whole(8, dim),
        ],
        out_specs=[whole(rows, dim)] * 3 + [whole(8, dim)],
        out_shape=[
            shape((rows, dim), BF16),
            shape((rows, dim), F32),
            shape((rows, dim), BF16),
            shape((8, dim), F32),
        ],
        scratch_shapes=[pltpu.VMEM((rows, dim), F32)],
        compiler_params=PARAMS,
        cost_estimate=cost(4 * rows * dim * tile * shards, 20 * rows * dim),
        name="feed_down",
    )(info, *hidden, *weight, rows_one, cotangent, vectors)


def grad_pre_of(info, grad_branch, weight, slopes):
    rows, dim = grad_branch.shape
    near = weight[1]
    shards = near.shape[1] + 1
    tile = SPOTS * near.shape[2]
    columns = pl.BlockSpec((rows, tile), lambda q: (0, q))
    return pl.pallas_call(
        grad_pre_kernel,
        grid=(shards,),
        in_specs=[SMEM, whole(rows, dim), *feed_specs(near), columns, columns],
        out_specs=[columns, columns, whole(shards, PARTS, 8, near.shape[2])],
        out_shape=[
            shape((rows, shards * tile), BF16),
            shape((rows, shards * tile), BF16),
            shape((shards, PARTS, 8, near.shape[2]), F32),
        ],
        compiler_params=PARAMS,
        cost_estimate=cost(4 * rows * dim * tile * shards, 30 * rows * dim),
        name="grad_pre",
    )(info, grad_branch, *weight, *slopes)


def up_back(info, pres, weight, rows_one, grad_second, vectors):
    rows, dim = rows_one.shape
    near = weight[1]
    shards = near.shape[1] + 1
    tile = SPOTS * near.shape[2]
    columns = pl.BlockSpec((rows, tile), lambda q: (0, q))
    return pl.pallas_call(
        up_back_kernel,
        grid=(shards,),
        in_specs=[
            SMEM,
            columns,
            columns,
            *feed_specs(near),
            whole(rows, dim),
            whole(rows, dim),
            whole(8, dim),
        ],
        out_specs=[whole(rows, dim), whole(rows, dim), whole(8, dim)],
        out_shape=[shape((rows, dim), F32), shape((rows, dim), BF16), shape((8, dim), F32)],
        scratch_shapes=[pltpu.VMEM((rows, dim), F32)],
        compiler_params=PARAMS,
        cost_estimate=cost(4 * rows * dim * tile * shards, 24 * rows * dim),
        name="up_back",
    )(info, *pres, *weight, rows_one, grad_second, vectors)


def turn(tokens, partner):
    rows, dim = tokens.shape
    return pl.pallas_call(
        turn_kernel,
        out_shape=[shape((dim, rows), BF16)] * 2,
        compiler_params=PARAMS,
        cost_estimate=cost(rows * dim, 8 * rows * dim),
        name="turn",
    )(tokens, partner)


def row_grads(shards, mine, theirs, my_rows, their_rows, name):
    rows, dim = my_rows.shape
    tile = mine.shape[1] // shards
    piece = tile // SPOTS
    columns = pl.BlockSpec((rows, tile), lambda q: (0, q))
    out = pl.BlockSpec((1, piece, dim), lambda q: (q, 0, 0))
    return pl.pallas_call(
        row_grads_kernel,
        grid=(shards,),
        in_specs=[columns, columns, whole(rows, dim), whole(rows, dim)],
        out_specs=[out] * SPOTS,
        out_shape=[shape((shards, piece, dim), (F32, BF16)[spot & 1]) for spot in range(SPOTS)],
        compiler_params=PARAMS,
        cost_estimate=cost(4 * rows * dim * tile * shards, 20 * rows * dim),
        name=name,
    )(mine, theirs, my_rows, their_rows)


def out_grads(info, mine, theirs, my_context, their_context):
    rows, dim = mine.shape
    piece = dim // PARTS
    return pl.pallas_call(
        out_grads_kernel,
        in_specs=[SMEM] + [whole(rows, dim)] * 4,
        out_specs=[whole(2, piece, dim)] * 2,
        out_shape=[shape((2, piece, dim), F32), shape((2, piece, dim), BF16)],
        scratch_shapes=[pltpu.VMEM((2, PARTS, piece, rows), BF16)],
        compiler_params=PARAMS,
        cost_estimate=cost(2 * rows * dim * dim, 10 * rows * dim),
        name="out_grads",
    )(info, mine, theirs, my_context, their_context)


def attend_back(
    setting,
    info,
    tokens_t,
    partner_t,
    grad_proj,
    out_weight,
    own,
    near,
    far,
    qkvs,
    stats,
    carried,
    so_far,
):
    heads, depth, first_shard, count, shards = setting
    half = shards // 2
    slot = first_shard % half
    fixed = 9 + len(own) + len(carried)
    splits = 1 if first_shard else 2
    dim, rows = tokens_t.shape
    width = heads * depth
    lanes = 3 * width
    piece = dim // PARTS
    head_spot = heads * shards + 3
    own_specs = [] if first_shard else [whole(3, width, dim)]
    kernel = functools.partial(
        attend_back_kernel, (heads, depth, first_shard, bool(carried), len(so_far), shards)
    )

    def other(s, info):
        return (0, jnp.maximum(s + first_shard - 1, 0), 0, 0)

    parts_out = pl.BlockSpec((SPOTS, 1, piece, lanes), lambda s, info: (0, s + slot, 0, 0))
    return pl.pallas_call(
        kernel,
        grid_spec=pltpu.PrefetchScalarGridSpec(
            num_scalar_prefetch=1,
            grid=(count,),
            in_specs=[
                whole(dim, rows),
                whole(dim, rows),
                whole(rows, dim),
                pl.BlockSpec(
                    (1, width, dim), lambda s, info: (info[head_spot] ^ (s + first_shard), 0, 0)
                ),
            ]
            + own_specs
            + [pl.BlockSpec((SPOTS, 1, piece, lanes), other)] * 2
            + [
                pl.BlockSpec((1, rows, lanes), lambda s, info: (s + first_shard, 0, 0)),
                pl.BlockSpec((1, 8, rows), lambda s, info: (s + first_shard, 0, 0)),
            ]
            + [whole(rows, dim)] * len(carried)
            + [pl.BlockSpec(memory_space=pl.ANY)] * len(so_far),
            out_specs=[
                whole(rows, dim),
                *[whole(rows // splits, dim)] * splits,
                parts_out,
                parts_out,
                pl.BlockSpec(
                    (1, 8, lanes), lambda s, info: (info[head_spot] ^ (s + first_shard), 0, 0)
                ),
            ],
            scratch_shapes=[
                pltpu.VMEM((rows, dim), F32),
                pltpu.VMEM((PARTS, piece, lanes), BF16),
                pltpu.VMEM((PARTS, piece, lanes), BF16),
            ],
        ),
        out_shape=[
            shape((rows, dim), F32),
            *[shape((rows // splits, dim), F32 if first_shard else BF16)] * splits,
            shape((SPOTS, half, piece, lanes), BF16),
            shape((SPOTS, half, piece, lanes), BF16),
            shape((shards, 8, lanes), F32),
        ],
        input_output_aliases={
            fixed + i: 4 + splits - len(so_far) + i for i in range(len(so_far))
        },
        compiler_params=PARAMS,
        cost_estimate=cost(
            count * (6 * rows * dim * dim + 10 * rows * rows * dim),
            count * 8 * rows * dim,
            count * heads * rows * rows,
        ),
        name="attend_back",
    )(
        info,
        tokens_t,
        partner_t,
        grad_proj,
        out_weight,
        *own,
        near,
        far,
        qkvs,
        stats,
        *carried,
        *so_far,
    )


class Mover:
    def __init__(self, batch_size, shards):
        self.batch_size, self.shards = batch_size, shards

    def batch(self, value, mask_of):
        perm = [(i, i ^ mask_of(i)) for i in range(self.batch_size)]
        return lax.ppermute(value, "batch", perm)

    def core(self, value):
        return self.batch(value, lambda i: CORE)

    def low(self, value):
        return self.batch(value, lambda i: 4 if i & 1 else 2)

    def high(self, value):
        return self.batch(value, lambda i: 2 if i & 1 else 4)

    def head(self, value, mask):
        return lax.ppermute(value, "head", [(i, i ^ mask) for i in range(self.shards)])

    def along(self, values, first=1):
        return [self.head(value, q) for q, value in enumerate(values, first)]

    def column(self, piece):
        return self.along([piece] * (self.shards - 1))

    def settle(self, total):
        total = total.astype(BF16)
        mask = PARTS
        while mask < self.batch_size:
            other = self.batch(total, lambda i, mask=mask: mask)
            total = (total.astype(F32) + other.astype(F32)).astype(BF16)
            mask *= 2
        return total

    def hops(self):
        steps, mask = [self.core, self.low, self.high], 1
        while mask < self.shards:
            steps.append(lambda value, mask=mask: self.head(value, mask))
            mask *= 2
        mask = PARTS
        while mask < self.batch_size:
            steps.append(lambda value, mask=mask: self.batch(value, lambda i: mask))
            mask *= 2
        return steps


def after(value, *events):
    return lax.optimization_barrier((value, *events))[0]


def all_after(values, *events):
    return lax.optimization_barrier((*values, *events))[: len(values)]


def pair_of(first, second):
    return jnp.stack([first, second])


def four_of(pair, received):
    return jnp.concatenate([pair, received])


def shards_swapped(value, shards, mask):
    width = value.shape[1] // shards
    blocks = [value[:, (q ^ mask) * width : ((q ^ mask) + 1) * width] for q in range(shards)]
    return jnp.concatenate(blocks, axis=1)


def stack8(*rows):
    rows = [row.reshape(1, -1) for row in rows]
    return jnp.concatenate(rows + [jnp.zeros((8 - len(rows), rows[0].shape[1]), F32)], axis=0)


def local(
    batch_size,
    shards,
    tokens,
    lengths,
    block_swap,
    input_weight,
    input_bias,
    out_weight,
    out_bias,
    gain_one,
    shift_one,
    up_weight,
    up_bias,
    down_weight,
    down_bias,
    gain_two,
    shift_two,
    cotangent,
):
    move = Mover(batch_size, shards)
    heads = block_swap.shape[0]
    rows, dim = tokens.shape
    width = input_weight.shape[2]
    depth = width // heads
    hidden_own = up_weight.shape[1]
    piece = dim // PARTS
    batch_at, head_at = lax.axis_index("batch"), lax.axis_index("head")
    part = batch_at % PARTS
    blocks = SEQ_LEN // rows
    length = lax.dynamic_index_in_dim(lengths, head_at // blocks, 0, keepdims=False)
    block_at = head_at % blocks
    own_live = jnp.clip(length - block_at * rows, 0, rows)
    partner_live = jnp.clip(length - (blocks - 1 - block_at) * rows, 0, rows)

    input_piece = lax.dynamic_slice_in_dim(input_weight, part * piece, piece, 1)
    input_piece = jnp.concatenate([input_piece[1], input_piece[2], input_piece[0]], axis=1)
    small = jnp.concatenate([jnp.zeros((width,), F32), input_bias[1], input_bias[0]])
    high = lax.reduce_precision(small, 8, 7)
    middle = lax.reduce_precision(small - high, 8, 7)
    swaps = jnp.pad(block_swap.astype(F32), (0, 3 * width - heads))
    small = jnp.stack([high, middle, small - high - middle, swaps])
    small = jnp.pad(small, ((0, 12), (0, 0))).astype(BF16)
    input_column = move.column(jnp.concatenate([input_piece, small]))
    up_own = up_weight.T.reshape(PARTS, piece, dim)
    up_piece = lax.dynamic_index_in_dim(up_own, part, 0, keepdims=False)
    input_own = input_weight.transpose(0, 2, 1)
    down_own = down_weight.reshape(PARTS, piece, dim)
    down_piece = lax.dynamic_index_in_dim(down_own, part, 0, keepdims=False)
    short_info = jnp.stack([own_live, part, head_at]).astype(jnp.int32)
    up_bias_parts = up_bias.reshape(shards, PARTS, 1, piece)
    out_parts = out_weight.reshape(shards, width, dim)
    vectors_one = stack8(out_bias, gain_one, shift_one)
    vectors_two = stack8(gain_one, shift_one, down_bias, gain_two, shift_two)
    vectors_back = stack8(gain_one)
    *input_column, up_piece, tokens_sent = all_after(
        (*input_column, up_piece, tokens), vectors_one, vectors_two, down_piece
    )
    small = jnp.stack([small] + [value[piece:] for value in input_column]).astype(F32)
    input_column = jnp.stack([value[:piece] for value in input_column])
    partner = move.head(tokens_sent, 1)
    input_low = move.low(input_column)
    up_far = move.head(up_piece, 2)
    info = jnp.concatenate(
        [
            small[:, 3, :heads].reshape(-1).astype(jnp.int32),
            jnp.stack([own_live, partner_live, part, head_at]).astype(jnp.int32),
        ]
    )
    bias = (small[:, 0] + small[:, 1]) + small[:, 2]
    bias = jnp.broadcast_to(bias[:, None], (shards, 8, 3 * width))
    input_low, up_far = all_after((input_low, up_far), info, bias)
    input_pair = pair_of(input_column, input_low)
    input_high = move.high(input_pair)
    input_high, partner = all_after((input_high, partner))
    input_near = four_of(input_pair, input_high)
    input_far = move.core(input_near)
    up_ends = pair_of(up_piece, after(up_far, partner))
    up_others = move.head(up_ends, 1)
    down_far = move.head(after(down_piece, partner), 2)

    def attend_shards(first_shard, count, last, weights, carried, so_far):
        return attend(
            (heads, depth, first_shard, last),
            count,
            info,
            tokens,
            partner,
            bias,
            out_parts,
            vectors_one,
            weights,
            carried,
            so_far,
        )

    qkv, context_0, stats, total = attend_shards(0, 1, False, [input_own], [], [])
    input_far, up_others, down_far, total, qkv, stats = all_after(
        (input_far, up_others, down_far, total, qkv, stats)
    )
    others = [input_near, input_far]
    up_column = jnp.stack([up_others[0], up_ends[1], up_others[1]])
    up_low = move.low(up_column)
    down_ends = pair_of(down_piece, down_far)
    down_others = move.head(down_ends, 1)
    total, up_column, down_ends = all_after((total, up_column, down_ends))
    qkv, context_1, stats, total = attend_shards(1, 2, False, others, [total], [qkv, stats])
    up_low, down_others, total, qkv, stats = all_after((up_low, down_others, total, qkv, stats))
    up_pair = pair_of(up_column, up_low)
    up_high = move.high(up_pair)
    down_column = jnp.stack([down_others[0], down_ends[1], down_others[1]])
    down_low = move.low(down_column)
    total, up_pair, down_column = all_after((total, up_pair, down_column))
    qkv, context, stats, rows_one, normed = attend_shards(
        3, 1, True, others, [total, context_0, context_1], [qkv, stats]
    )
    up_high, down_low, normed, context = all_after((up_high, down_low, normed, context))
    up_near = four_of(up_pair, up_high)
    up_far = move.core(up_near)
    up_all = (up_own, up_near, up_far)
    down_pair = pair_of(down_column, down_low)
    down_high = move.high(down_pair)
    normed, down_pair = all_after((normed, down_pair))
    normed_received = move.core(normed)
    context_received = move.core(context)
    hidden_near, hidden_far, *slopes = feed_up(short_info, normed, up_all, up_bias_parts)
    hidden_received = move.core(hidden_far)
    down_near = four_of(down_pair, after(down_high, hidden_near))
    down_far = move.core(down_near)
    tokens_t, partner_t = turn(after(tokens, down_near), partner)
    down_far, tokens_t, partner_t = all_after((down_far, tokens_t, partner_t))
    down_all = (down_own, down_near, down_far)
    mixed_out, grad_second, grad_branch, sums_two = feed_down(
        short_info, (hidden_near, hidden_far), down_all, rows_one, cotangent, vectors_two
    )

    branch_received = move.core(grad_branch)
    down_mine, down_one, down_two, down_three = row_grads(
        shards,
        hidden_near,
        hidden_received,
        grad_branch,
        branch_received,
        "down_grads",
    )
    down_three = move.low(down_three)
    pre_near, pre_far, up_bias_sums = grad_pre_of(
        short_info, after(grad_branch, down_two), down_all, slopes
    )
    down_three, pre_near, pre_far, up_bias_sums = all_after(
        (down_three, pre_near, pre_far, up_bias_sums)
    )
    pre_received = move.core(pre_far)
    down_two = (down_two + down_three.astype(F32)).astype(BF16)
    down_high = move.high(down_two)
    grad_first, grad_proj, sums_one = up_back(
        short_info, (pre_near, pre_far), up_all, rows_one, after(grad_second, down_two), vectors_back
    )
    pre_received, down_high, grad_proj, grad_first, sums_one = all_after(
        (pre_received, down_high, grad_proj, grad_first, sums_one)
    )
    proj_received = move.core(grad_proj)
    down_one = move.low(after(down_one, down_high))

    def core_sum(mine, received):
        mine, received = (a.reshape(2, 2, *a.shape[1:]) for a in (mine, received))
        keep = [mine[i, 0].astype(F32) + received[i, 0].astype(F32) for i in range(2)]
        return keep, (mine[:, 1].astype(F32) + received[:, 1].astype(F32)).astype(BF16)

    def fold_low(keep, received):
        return keep[0] + received[0].astype(F32), (keep[1] + received[1].astype(F32)).astype(BF16)

    def fold_high(own, received):
        total = own + received.astype(F32)
        return total[0::2], total[1::2].astype(BF16)

    def fold_near(own, received):
        return own[0] + received[0].astype(F32), (own[1] + received[1].astype(F32)).astype(BF16)

    def fold_last(own, received):
        return move.settle(own + received.astype(F32))

    up_mine, up_one, up_two, up_three = row_grads(
        shards, pre_near, pre_received, normed, normed_received, "up_grads"
    )
    proj_received, up_one, up_three = all_after((proj_received, up_one, up_three))
    up_three = move.low(up_three)
    out_keep, out_send = out_grads(
        short_info, after(grad_proj, up_one), proj_received, context, context_received
    )
    down_one, out_keep, out_send = all_after((down_one, out_keep, out_send))
    up_one = move.low(after(up_one, down_one))
    out_low = move.low(out_send)
    down_mine = down_mine + (down_one.astype(F32) + down_high.astype(F32))
    down_mine, down_next = down_mine[0::2], down_mine[1::2].astype(BF16)
    down_near = move.head(down_next, 1)

    def back(grad, first_shard, count, carried, so_far):
        return attend_back(
            (heads, depth, first_shard, count, shards),
            info,
            tokens_t,
            partner_t,
            grad,
            out_parts,
            [] if first_shard else [input_own],
            *others,
            qkv,
            stats,
            carried,
            so_far,
        )

    own_rows, partner_rows, late_near, late_far, late_bias = back(
        after(grad_proj, out_send, down_next), 2, 2, [], []
    )

    (
        down_near,
        up_three,
        out_low,
        own_rows,
        partner_rows,
        late_near,
        late_far,
        late_bias,
    ) = all_after(
        (
            down_near,
            up_three,
            out_low,
            own_rows,
            partner_rows,
            late_near,
            late_far,
            late_bias,
        )
    )
    up_next = (up_two + up_three.astype(F32)).astype(BF16)
    up_high = move.high(up_next)
    late_core = move.core(late_far)
    down_mine, down_next = fold_near(down_mine, after(down_near, up_next))
    down_last = move.head(down_next, 2)
    out_mine = out_keep[0] + out_low[0].astype(F32)
    out_next = (out_keep[1] + out_low[1].astype(F32)).astype(BF16)
    out_high = move.high(out_next)
    own_rows, partner_rows, *early = back(
        after(grad_proj, down_next, up_next, out_next), 1, 1, [own_rows, partner_rows], [late_bias]
    )

    up_one, up_high, down_last, late_core, out_high, own_rows, partner_rows, *early = all_after(
        (up_one, up_high, down_last, late_core, out_high, own_rows, partner_rows, *early)
    )
    up_mine, up_next = fold_high(up_mine + up_one.astype(F32), up_high)
    up_near = move.head(up_next, 1)
    late_keep, late_next = core_sum(late_near, late_core)
    late_low = move.low(late_next)
    down_total = fold_last(down_mine, down_last)
    down_low = move.low(down_total)
    out_next = (out_mine + out_high.astype(F32)).astype(BF16)
    out_near = move.head(out_next, 1)
    own_rows, partner_first, partner_second, early_near, early_far, early_bias = back(
        after(grad_proj, up_next, down_total, late_next, out_next),
        0,
        1,
        [own_rows, partner_rows],
        early,
    )

    up_near, down_low, late_low, out_near, own_rows, partner_first, partner_second = all_after(
        (up_near, down_low, late_low, out_near, own_rows, partner_first, partner_second), early_bias
    )
    early_near, early_far, early_bias = all_after((early_near, early_far, early_bias), up_near)

    early_core = move.core(early_far)
    up_mine, up_next = fold_near(up_mine, up_near)
    up_last = move.head(up_next, 2)
    late_mine, late_next = fold_low(late_keep, late_low)
    late_high = move.high(late_next)
    out_near = shards_swapped(out_near, shards, 1)
    out_next = (out_next.astype(F32) + out_near.astype(F32)).astype(BF16)
    out_last = move.head(out_next, 2)
    vectors = jnp.concatenate(
        [
            sums_one[:3],
            sums_two[:3],
            up_bias_sums[:, :, 0].reshape(shards, dim),
            jnp.pad(early_bias[:, 0], ((0, 0), (0, dim - 3 * width))),
        ]
    )
    hops = move.hops()

    def hop(value, sent, event):
        value = value + after(sent, event)
        return value, hops.pop(0)(value) if hops else None

    vectors_sent = hops.pop(0)(vectors)
    early_keep, early_next = core_sum(
        early_near, after(early_core, late_next, up_next, vectors, out_next)
    )
    early_low = move.low(early_next)
    vectors, vectors_sent = hop(vectors, vectors_sent, early_next)
    late_mine = late_mine + after(late_high, vectors).astype(F32)
    partner_first = move.head(after(partner_first, late_mine), 1)
    early_mine, early_next = fold_low(early_keep, after(early_low, late_mine))
    early_high = move.high(early_next)
    down_pair = pair_of(down_total, after(down_low, early_next))
    down_high = move.high(down_pair)
    vectors, vectors_sent = hop(vectors, vectors_sent, early_next)
    up_total = fold_last(up_mine, after(up_last, vectors))
    out_last = shards_swapped(after(out_last, up_total), shards, 2)
    out_total = move.settle(out_next.astype(F32) + out_last.astype(F32))
    up_total = jnp.concatenate([up_total, out_total], axis=1)
    up_low = move.low(up_total)
    early_mine = early_mine + after(early_high, up_total).astype(F32)
    input_next = jnp.stack([early_mine[1], late_mine[1]]).astype(BF16)
    input_near = move.head(input_next, 1)
    vectors, vectors_sent = hop(vectors, vectors_sent, input_next)
    down_near = four_of(down_pair, after(down_high, vectors))
    down_far = move.core(down_near)
    up_pair = pair_of(up_total, after(up_low, down_near))
    up_high = move.high(up_pair)
    input_mine, input_next = fold_near(
        jnp.stack([early_mine[0], late_mine[0]]), after(input_near, up_pair)
    )
    input_last = move.head(input_next, 2)
    partner_second = move.head(after(partner_second, input_next), 1)
    grad_down = pl.pallas_call(
        settle_down_kernel,
        in_specs=[SMEM] + [whole(4, piece, dim)] * 2,
        out_shape=shape((PARTS, piece, dim), F32),
        compiler_params=PARAMS,
        name="settle_down",
    )(short_info, after(down_near, input_next), down_far)
    input_last, vectors_sent, partner_first = all_after(
        (input_last, vectors_sent, partner_first), grad_down
    )
    input_total = fold_last(input_mine, input_last)
    input_low = move.low(input_total)
    vectors, vectors_sent = hop(vectors, vectors_sent, input_total)
    up_near = four_of(up_pair, after(up_high, input_total))
    up_far = move.core(up_near)
    input_low = after(input_low, up_near)
    input_pair = pair_of(input_total, input_low)
    input_high = move.high(input_pair)
    while vectors_sent is not None:
        vectors, vectors_sent = hop(vectors, vectors_sent, input_pair)
    grad_input_bias = lax.dynamic_index_in_dim(vectors[10:], head_at, 0, keepdims=False)
    grad_input_bias = jnp.stack(
        [grad_input_bias[2 * width : 3 * width], grad_input_bias[width : 2 * width]]
    )
    grad_up_bias = lax.dynamic_index_in_dim(vectors[6:10], head_at, 0, keepdims=False)
    input_high, grad_input_bias, grad_up_bias = all_after(
        (input_high, grad_input_bias, grad_up_bias)
    )
    input_near = four_of(input_pair, input_high)
    input_far = move.core(input_near)
    from_partner = jnp.concatenate([partner_first, after(partner_second, input_near)])
    grad_tokens = grad_first + own_rows + from_partner.astype(F32)
    grad_up, grad_out = pl.pallas_call(
        settle_up_kernel,
        in_specs=[SMEM] + [whole(4, piece, dim + shards * width)] * 2,
        out_shape=[shape((dim, hidden_own), F32), shape((shards, width, dim), F32)],
        scratch_shapes=[pltpu.VMEM((PARTS, piece, dim), F32)] * 2,
        compiler_params=PARAMS,
        name="settle_up",
    )(short_info, after(up_near, input_near, grad_tokens), up_far)
    grad_input_weight = pl.pallas_call(
        settle_input_kernel,
        in_specs=[SMEM] + [whole(4, piece, 3 * width)] * 2,
        out_shape=shape((3, width, dim), F32),
        scratch_shapes=[pltpu.VMEM((PARTS, piece, 3 * width), F32)],
        compiler_params=PARAMS,
        name="settle_input",
    )(short_info, after(input_near, grad_up), input_far)
    return (
        mixed_out,
        grad_tokens,
        grad_input_weight.transpose(0, 2, 1),
        grad_input_bias,
        grad_out.reshape(dim, dim),
        vectors[0],
        vectors[1],
        vectors[2],
        grad_up,
        grad_up_bias,
        grad_down.reshape(hidden_own, dim),
        vectors[3],
        vectors[4],
        vectors[5],
    )


def solution(mesh):
    rows_spec = P(("batch", "head"), None)
    placed = (
        rows_spec,
        P("batch"),
        P("head"),
        P(None, None, "head"),
        P(None, "head"),
        P(),
        P(),
        P(),
        P(),
        P(None, "head"),
        P(),
        P("head", None),
        P(),
        P(),
        P(),
        rows_spec,
    )
    return jax.shard_map(
        functools.partial(local, mesh.shape["batch"], mesh.shape["head"]),
        mesh=mesh,
        in_specs=placed,
        out_specs=(
            rows_spec,
            rows_spec,
            P(None, None, "head"),
            P(None, "head"),
            P(),
            P(),
            P(),
            P(),
            P(None, "head"),
            P("head"),
            P("head", None),
            P(),
            P(),
            P(),
        ),
        check_vma=False,
    )
```
